32 devices in a mesh: seq: 8 (over z, y), exp: 4 (over x, core).
Axes of the slice: x: 2, y: 2, z: 4, core: 2. Of those that a mesh axis runs over, the one named last changes fastest.
Arguments:
- tokens: bfloat16 [4, 2048, 768], P('exp', 'seq'), may hold values from -6 to 6
- cotangent: bfloat16 [4, 2048, 768], P('exp', 'seq'), may hold values from -6 to 6
- segment_ids: int32 [4, 2048], P('exp', 'seq'), may hold values from 0 to 2, as said below
- expert_ids: int32 [4, 2048, 1], P('exp', 'seq'), may hold values from 0 to 3; in each aligned block of 256 rows (0 to 255, 256 to 511, ..., all dimensions but the last counted through in order) at most 128 rows name the same one
- projection: float32 [768, 2304], P(('seq', 'exp')), may hold values from -0.21875 to 0.21875
- output_weight: float32 [768, 768], P(('seq', 'exp')), may hold values from -1.25 to 1.25
- expert_up: float32 [4, 3072, 768], P('exp', 'seq'), may hold values from -0.28867513 to 0.28867513
- expert_down: float32 [4, 3072, 768], P('exp', 'seq'), may hold values from -0.14433757 to 0.14433757
- norm_gains: float32 [2, 768], replicated, may hold values from 0.3 to 2.8
- projection_first: float32 [768, 2304], P(('seq', 'exp')), may hold values from -0.00036621094 to 0.00036621094
- projection_second: float32 [768, 2304], P(('seq', 'exp')), may hold values from 4.756598e-10 to 1.9026392e-09
- output_first: float32 [768, 768], P(('seq', 'exp')), may hold values from -0.00036621094 to 0.00036621094
- output_second: float32 [768, 768], P(('seq', 'exp')), may hold values from 4.756598e-10 to 1.9026392e-09
- up_first: float32 [4, 3072, 768], P('exp', 'seq'), may hold values from -0.00036621094 to 0.00036621094
- up_second: float32 [4, 3072, 768], P('exp', 'seq'), may hold values from 4.756598e-10 to 1.9026392e-09
- down_first: float32 [4, 3072, 768], P('exp', 'seq'), may hold values from -0.00036621094 to 0.00036621094
- down_second: float32 [4, 3072, 768], P('exp', 'seq'), may hold values from 4.756598e-10 to 1.9026392e-09
- gains_first: float32 [2, 768], replicated, may hold values from -0.0014648438 to 0.0014648438
- gains_second: float32 [2, 768], replicated, may hold values from 7.5352045e-09 to 3.061177e-08
Outputs:
- block_output: bfloat16 [4, 2048, 768], P('exp', 'seq')
- input_grad: float32 [4, 2048, 768], P('exp', 'seq')
- grad_norm: float32 [], replicated
- projection_grad: float32 [768, 2304], P(('seq', 'exp'))
- projection_moment: float32 [768, 2304], P(('seq', 'exp'))
- projection_square: float32 [768, 2304], P(('seq', 'exp'))
- projection_new: float32 [768, 2304], P(('seq', 'exp'))
- output_grad: float32 [768, 768], P(('seq', 'exp'))
- output_moment: float32 [768, 768], P(('seq', 'exp'))
- output_square: float32 [768, 768], P(('seq', 'exp'))
- output_new: float32 [768, 768], P(('seq', 'exp'))
- up_grad: float32 [4, 3072, 768], P('exp', 'seq')
- up_moment: float32 [4, 3072, 768], P('exp', 'seq')
- up_square: float32 [4, 3072, 768], P('exp', 'seq')
- up_new: float32 [4, 3072, 768], P('exp', 'seq')
- down_grad: float32 [4, 3072, 768], P('exp', 'seq')
- down_moment: float32 [4, 3072, 768], P('exp', 'seq')
- down_square: float32 [4, 3072, 768], P('exp', 'seq')
- down_new: float32 [4, 3072, 768], P('exp', 'seq')
- gains_grad: float32 [2, 768], replicated
- gains_moment: float32 [2, 768], replicated
- gains_square: float32 [2, 768], replicated
- gains_new: float32 [2, 768], replicated
The draws below stay inside these ranges and needn't reach their ends.
Inputs may be any that keep to these rules, and one draw needn't show every extreme that they name: `segment_ids`: never falling along a row; document 1 begins within the first 256 positions of its row and ends within the last 256. `expert_ids`: in the 256 rows of one device no expert is named by more than 128 tokens.
All inputs are finite; a program needn't handle non-finite values.
Results may differ from the reference program's by a relative error of at most 0.018.
Values may be sent and summed in bfloat16 or wider, within the bound.
No kernel may reach another device: no remote copies, remote signals or barrier semaphores. Data moves between devices by JAX's collectives and lax.ppermute only.
A program may use at most 512 MiB of HBM per device.

```python
import math
import jax
import jax.numpy as jnp
import numpy as np
from jax import lax

D = 768
HEADS = 12
HEAD_DIM = 64
FF = 3072
TOK_DEV = 256
CAP = 128
ROW = 2048
GROUPS = 4
EXPERTS = 4
STEP = 10


def rising(count, ratio):
    return ratio ** (jnp.arange(count, dtype=jnp.float32) / max(count - 1, 1))


def shaped(entries, ratio):
    expert_scale = 0.75 * rising(EXPERTS, ratio)
    unit_scale = 0.75 * rising(FF, ratio)
    return entries * expert_scale[:, None, None] * unit_scale[None, :, None]


def draw_segment_ids(key, part):
    key = jax.random.fold_in(key, 11)
    first_key, second_key = jax.random.split(key)
    begin = jax.random.randint(first_key, (GROUPS, 1), 1, TOK_DEV)
    finish = jax.random.randint(second_key, (GROUPS, 1), ROW - TOK_DEV + 1, ROW)
    place = jnp.arange(ROW, dtype=jnp.int32)[None, :]
    return (place >= begin).astype(jnp.int32) + (place >= finish).astype(jnp.int32)


def draw_norm_gains(key, part):
    key = jax.random.fold_in(key, 23)
    base = 0.6 * rising(D, 3.0)
    noise = jnp.clip(0.1 * jax.random.normal(key, (2, D), jnp.float32), -0.3, 0.3)
    return base[None, :] * (1.0 + noise)


def draw_expert_up(key, part):
    key = jax.random.fold_in(key, 31)
    entries = jax.random.truncated_normal(key, -4.0, 4.0, (EXPERTS, FF, D), jnp.float32)
    ratio = 1.8
    return shaped(entries, ratio) * D ** (-0.5)


def draw_expert_down(key, part):
    key = jax.random.fold_in(key, 37)
    entries = jax.random.truncated_normal(key, -4.0, 4.0, (EXPERTS, FF, D), jnp.float32)
    ratio = 1.8
    return shaped(entries, ratio) * FF ** (-0.5)


def block_scale(rng, shape, cuts, low, top_value):
    def one(axis_at, shards_of):
        heights = jax.random.uniform(jax.random.fold_in(jax.random.fold_in(rng, 6), axis_at), (shards_of,), jnp.float32, low / len(cuts), top_value / len(cuts))
        return jnp.repeat(jnp.exp(heights), shape[axis_at] // shards_of).reshape((-1,) + (1,) * (len(shape) - axis_at - 1))

    level = one(*cuts[0])
    for cut in cuts[1:]:
        level = level * one(*cut)
    return level


def assign_block(key, own, number, rows, number_of, top, reach, skew):
    ranking = jax.random.permutation(key, number_of)
    packed, usual = shares(number_of, rows * top, reach, skew, True), shares(number_of, rows * top, reach, skew, False)
    places = jnp.arange(number_of)

    def named(lengths, turn):
        used = int((lengths > 0).sum())
        fixed = max(1, used // 4)
        moved = fixed + (places - fixed + turn * (used - fixed)) % max(1, number_of - fixed)
        return jnp.zeros((number_of,), jnp.int32).at[ranking[jnp.where(places < fixed, places, moved)]].set(jnp.asarray(lengths, jnp.int32))

    lengths = jnp.where(number % 4 == 0, named(packed, number // 4), named(usual, number - number // 4 - 1))
    mixed = jax.random.permutation(jax.random.fold_in(own, 3), number_of)
    donor, receiver = mixed[0:number_of // 2 * 2:2], mixed[1:number_of // 2 * 2:2]
    slack = jnp.minimum(lengths[donor] - 1, reach - lengths[receiver]) // 2
    slack = jnp.where((donor == ranking[0]) | (receiver == ranking[0]) | (lengths[receiver] == 0), 0, jnp.maximum(slack, 0))
    moved = jax.random.randint(jax.random.fold_in(own, 4), (number_of // 2,), 0, 1 << 20) % (slack + 1)
    lengths = lengths.at[donor].add(-moved).at[receiver].add(moved)
    members = jnp.searchsorted(jnp.cumsum(lengths), jnp.arange(rows * top), side="right").astype(jnp.int32)
    listing = members.reshape(top, rows).T
    listing = listing[jax.random.permutation(jax.random.fold_in(own, 1), rows)]
    turn = jax.random.randint(jax.random.fold_in(own, 2), (rows, 1), 0, top)
    return jnp.take_along_axis(listing, (jnp.arange(top)[None, :] + turn) % top, axis=1)


def shares(count, total, limit, lean, full):
    loads = [(1 << 20) // math.isqrt(grade ** lean) + 1 for grade in range(1, count + 1)]
    largest = limit if full else min(limit, max(-(-total // count), total * loads[0] // sum(loads)))
    least = 1 if total - largest >= count - 1 else 0
    holding, surplus = [largest] + [least] * (count - 1), total - largest - least * (count - 1)
    while surplus > 0:
        free = [i for i in range(1, count) if holding[i] < largest] or [i for i in range(1, count) if holding[i] < limit]
        pool, budget = sum([loads[i] for i in free]), surplus
        for i in free:
            addition = min(limit - holding[i], max(1, budget * loads[i] // pool), surplus)
            holding[i] = holding[i] + addition
            surplus = surplus - addition
    return np.array(holding)


def bell_draw(rng, shape, scale, limit, shards=(), kind=jnp.bfloat16):
    drawn = jax.random.normal(rng, shape, jnp.float32) * scale
    if len(shards) > 0:
        drawn = block_scale(rng, shape, shards, -0.22, 0.18) * drawn
    return jnp.clip(drawn, min=-limit, max=limit).astype(kind)


def setup_inputs(seed: int = 0) -> dict:
    streams_of = jax.random.split(jax.random.key(seed), 20)
    tokens = bell_draw(streams_of[0], (GROUPS, ROW, D), 1.0, 6.0, ((0, 4), (1, 8)))
    cotangent = bell_draw(streams_of[1], (GROUPS, ROW, D), 1.0, 6.0, ((0, 4), (1, 8)))
    segment_ids = draw_segment_ids(jax.random.fold_in(streams_of[19], 71), 0)
    expert_ids_keys = jax.random.split(jax.random.fold_in(streams_of[3], 1), GROUPS * ROW // TOK_DEV)
    expert_ids_turns = jax.random.permutation(jax.random.fold_in(streams_of[3], 3), GROUPS * ROW // TOK_DEV)
    expert_ids = jax.vmap(lambda own, number: assign_block(jax.random.fold_in(streams_of[3], 2), own, number, TOK_DEV, EXPERTS, 1, CAP, 1))(expert_ids_keys, expert_ids_turns).reshape((GROUPS, ROW, 1))
    projection = bell_draw(streams_of[4], (D, 3 * D), D ** -0.5, 0.21875, ((0, 32),), jnp.float32)
    output_weight = bell_draw(streams_of[5], (D, D), (D // 32) ** -0.5, 1.25, ((0, 32),), jnp.float32)
    expert_up = draw_expert_up(jax.random.fold_in(streams_of[19], 71), 0)
    expert_down = draw_expert_down(jax.random.fold_in(streams_of[19], 71), 0)
    norm_gains = draw_norm_gains(jax.random.fold_in(streams_of[19], 71), 0)
    projection_first = bell_draw(streams_of[9], (D, 3 * D), (0.11 * (4 * D * D + 2 * EXPERTS * FF * D) ** -0.5), 0.00036621094, ((0, 32),), jnp.float32)
    projection_second = jnp.clip(jnp.exp(math.log(1.902639157336239e-09) - 1.3862944 * jax.random.uniform(streams_of[10], (D, 3 * D), jnp.float32) ** block_scale(streams_of[10], (D, 3 * D), ((0, 32),), -0.2, 0.2)), 4.756597893340597e-10, 1.902639157336239e-09)
    output_first = bell_draw(streams_of[11], (D, D), (0.11 * (4 * D * D + 2 * EXPERTS * FF * D) ** -0.5), 0.00036621094, ((0, 32),), jnp.float32)
    output_second = jnp.clip(jnp.exp(math.log(1.902639157336239e-09) - 1.3862944 * jax.random.uniform(streams_of[12], (D, D), jnp.float32) ** block_scale(streams_of[12], (D, D), ((0, 32),), -0.2, 0.2)), 4.756597893340597e-10, 1.902639157336239e-09)
    up_first = bell_draw(streams_of[13], (EXPERTS, FF, D), (0.11 * (4 * D * D + 2 * EXPERTS * FF * D) ** -0.5), 0.00036621094, ((0, 4), (1, 8)), jnp.float32)
    up_second = jnp.clip(jnp.exp(math.log(1.902639157336239e-09) - 1.3862944 * jax.random.uniform(streams_of[14], (EXPERTS, FF, D), jnp.float32) ** block_scale(streams_of[14], (EXPERTS, FF, D), ((0, 4), (1, 8)), -0.2, 0.2)), 4.756597893340597e-10, 1.902639157336239e-09)
    down_first = bell_draw(streams_of[15], (EXPERTS, FF, D), (0.11 * (4 * D * D + 2 * EXPERTS * FF * D) ** -0.5), 0.00036621094, ((0, 4), (1, 8)), jnp.float32)
    down_second = jnp.clip(jnp.exp(math.log(1.902639157336239e-09) - 1.3862944 * jax.random.uniform(streams_of[16], (EXPERTS, FF, D), jnp.float32) ** block_scale(streams_of[16], (EXPERTS, FF, D), ((0, 4), (1, 8)), -0.2, 0.2)), 4.756597893340597e-10, 1.902639157336239e-09)
    gains_first = bell_draw(streams_of[17], (2, D), (0.44 * (4 * D * D + 2 * EXPERTS * FF * D) ** -0.5), 0.0014648438, (), jnp.float32)
    gains_second = jnp.clip(jnp.exp(jax.random.uniform(streams_of[18], (2, D), jnp.float32, math.log(7.535204460396017e-09), math.log(3.061176911955954e-08))), 7.535204460396017e-09, 3.061176911955954e-08)
    return {"tokens": tokens, "cotangent": cotangent, "segment_ids": segment_ids, "expert_ids": expert_ids, "projection": projection, "output_weight": output_weight, "expert_up": expert_up, "expert_down": expert_down, "norm_gains": norm_gains, "projection_first": projection_first, "projection_second": projection_second, "output_first": output_first, "output_second": output_second, "up_first": up_first, "up_second": up_second, "down_first": down_first, "down_second": down_second, "gains_first": gains_first, "gains_second": gains_second}


EPSILON = 1e-05
CLIP = 1.0
BETA_ONE = 0.9
BETA_TWO = 0.99
ADAM_FLOOR = 1e-08
DECAY = 0.1
RATE_MATRIX = 0.04
RATE_OUTPUT = 0.1
RATE_GAIN = 0.5
HIGHEST = lax.Precision.HIGHEST

@jax.custom_vjp
def low(v):
    return lax.optimization_barrier(v.astype(jnp.bfloat16)).astype(jnp.float32)

@jax.custom_vjp
def low_back(v):
    return v

def low_keep(v):
    return (low(v), None)

def low_pass(kept, grad):
    return (grad,)

def back_keep(v):
    return (v, None)

def back_low(kept, grad):
    return (low(grad),)
low.defvjp(low_keep, low_pass)
low_back.defvjp(back_keep, back_low)

def normalize(values, gain):
    scaling = lax.rsqrt(lax.optimization_barrier(jnp.mean(values * values, axis=-1, keepdims=True)) + EPSILON)
    return values * scaling * gain

def group_attention(operands):
    query, keys, values, segments = operands
    block = 512 if ROW % 512 == 0 else ROW
    count = ROW // block
    scaling = HEAD_DIM ** (-0.5)
    key_heads = keys.reshape(ROW, HEADS, HEAD_DIM)
    value_heads = values.reshape(ROW, HEADS, HEAD_DIM)
    key_place = jnp.arange(ROW, dtype=jnp.int32)

    def one_block(item):
        query_block, segment_block, start = item
        query_place = start + jnp.arange(block, dtype=jnp.int32)
        scores = jnp.einsum('qhd,khd->hqk', query_block.reshape(block, HEADS, HEAD_DIM), key_heads, precision=HIGHEST) * scaling
        scores = low_back(scores)
        allowed = (segment_block[:, None] == segments[None, :]) & (key_place[None, :] <= query_place[:, None])
        scores = jnp.where(allowed[None], scores, -1e+30)
        top = lax.optimization_barrier(jnp.max(scores, axis=-1, keepdims=True))
        expd = jnp.where(allowed[None], jnp.exp(scores - top), 0.0)
        attend_weights = low(expd / lax.optimization_barrier(jnp.sum(expd, axis=-1, keepdims=True)))
        mixed = jnp.einsum('hqk,khd->qhd', attend_weights, value_heads, precision=HIGHEST)
        return mixed.reshape(block, HEADS * HEAD_DIM)
    starts = jnp.arange(count, dtype=jnp.int32) * block
    result = lax.map(jax.checkpoint(one_block), (query.reshape(count, block, HEADS * HEAD_DIM), segments.reshape(count, block), starts))
    return result.reshape(ROW, HEADS * HEAD_DIM)

def forward(inputs, projection, output_weight, expert_up, expert_down, norm_gains, segment_ids, expert_ids):
    attend_in = low(normalize(inputs, norm_gains[0]))
    projected = jnp.dot(attend_in.reshape(-1, D), low(projection), precision=HIGHEST)
    projected = low(low_back(projected)).reshape(GROUPS, ROW, 3 * D)
    query = projected[:, :, :D]
    keys = projected[:, :, D:2 * D]
    values = projected[:, :, 2 * D:]
    mixed = lax.map(group_attention, (query, keys, values, segment_ids))
    mixed = low(low_back(mixed))
    branch = low_back(jnp.dot(mixed.reshape(-1, D), low(output_weight), precision=HIGHEST)).reshape(GROUPS, ROW, D)
    middle = inputs + branch
    expert_in = low(low_back(normalize(middle, norm_gains[1]))).reshape(-1, D)
    chosen = expert_ids.reshape(-1)

    def expert_step(total, item):
        up_matrix, down_matrix, index = item
        hidden = low_back(jnp.dot(expert_in, low(up_matrix).T, precision=HIGHEST))
        active = low(jax.nn.gelu(hidden))
        produced = low(low_back(jnp.dot(active, low(down_matrix), precision=HIGHEST)))
        return (total + jnp.where((chosen == index)[:, None], produced, 0.0), None)
    beginning = jnp.zeros_like(expert_in)
    experts_sum, unused = lax.scan(jax.checkpoint(expert_step), beginning, (expert_up, expert_down, jnp.arange(EXPERTS, dtype=jnp.int32)))
    return middle + experts_sum.reshape(GROUPS, ROW, D)

def adam_update(weight, grad, first, second, factor, rate, decay):
    clipped = grad * factor
    first_new = BETA_ONE * first + (1.0 - BETA_ONE) * clipped
    second_new = BETA_TWO * second + (1.0 - BETA_TWO) * clipped * clipped
    first_hat = first_new / (1.0 - BETA_ONE ** STEP)
    second_hat = second_new / (1.0 - BETA_TWO ** STEP)
    weight_new = weight - rate * (first_hat / (jnp.sqrt(second_hat) + ADAM_FLOOR) + decay * weight)
    return (first_new, second_new, weight_new)

def reference(tokens, cotangent, segment_ids, expert_ids, projection, output_weight, expert_up, expert_down, norm_gains, projection_first, projection_second, output_first, output_second, up_first, up_second, down_first, down_second, gains_first, gains_second):

    def wrapped(inputs, proj_weight, out_weight, up_weight, down_weight, gain_values):
        return forward(inputs, proj_weight, out_weight, up_weight, down_weight, gain_values, segment_ids, expert_ids)
    result, pull = jax.vjp(wrapped, tokens.astype(jnp.float32), projection, output_weight, expert_up, expert_down, norm_gains)
    gradients = pull(cotangent.astype(jnp.float32))
    input_grad, projection_grad, output_grad, up_grad, down_grad, gains_grad = gradients
    square = jnp.sum(projection_grad * projection_grad) + jnp.sum(output_grad * output_grad)
    square = square + jnp.sum(up_grad * up_grad) + jnp.sum(down_grad * down_grad) + jnp.sum(gains_grad * gains_grad)
    grad_norm = jnp.sqrt(square)
    factor = jnp.minimum(1.0, CLIP / (grad_norm + 1e-06))
    projection_moment, projection_square, projection_new = adam_update(projection, projection_grad, projection_first, projection_second, factor, RATE_MATRIX, DECAY)
    output_moment, output_square, output_new = adam_update(output_weight, output_grad, output_first, output_second, factor, RATE_OUTPUT, DECAY)
    up_moment, up_square, up_new = adam_update(expert_up, up_grad, up_first, up_second, factor, RATE_MATRIX, DECAY)
    down_moment, down_square, down_new = adam_update(expert_down, down_grad, down_first, down_second, factor, RATE_MATRIX, DECAY)
    gains_moment, gains_square, gains_new = adam_update(norm_gains, gains_grad, gains_first, gains_second, factor, RATE_GAIN, 0.0)
    return (result.astype(jnp.bfloat16), input_grad, grad_norm, projection_grad, projection_moment, projection_square, projection_new, output_grad, output_moment, output_square, output_new, up_grad, up_moment, up_square, up_new, down_grad, down_moment, down_square, down_new, gains_grad, gains_moment, gains_square, gains_new)
```

```python
import functools
import math

import jax
import jax.numpy as jnp
import numpy as np
from jax import lax
from jax.experimental import pallas as pl
from jax.experimental.pallas import tpu as pltpu
from jax.sharding import Mesh
from jax.sharding import PartitionSpec as P

HEADS = 12
CAP = 128
STEP = 10


EPSILON = 1e-05
CLIP = 1.0
BETA_ONE = 0.9
BETA_TWO = 0.99
ADAM_FLOOR = 1e-08
DECAY = 0.1
RATE_MATRIX = 0.04
RATE_OUTPUT = 0.1
RATE_GAIN = 0.5

SEQ = ("hi", "lo", "in")
EXP = ("exp",)
ALL = SEQ + EXP
TEAM = ("lo",)
SHARE = ("hi", "in")
LANES = 128
HALF = 64
FAR = -1e30
BF16 = jnp.bfloat16
F32 = jnp.float32
VMEM_LIMIT = 60 * 1024 * 1024


def head_plan(count):
    whole = math.lcm(HEADS, count)
    units, parts = whole // count, whole // HEADS
    first = np.zeros((count,), np.int64)
    active = np.zeros((count, 2, count), np.int32)
    for device in range(count):
        first[device] = min(units * device // parts, HEADS - 2)
        for unit in range(units * device, units * (device + 1)):
            slot = unit // parts - first[device]
            for block in range(count):
                turn = block % (2 * parts)
                if min(turn, 2 * parts - 1 - turn) == unit % parts:
                    active[device, slot, block] = 1
    return first, active


def three_parts(value):
    high = value.astype(BF16).astype(F32)
    middle = (value - high).astype(BF16).astype(F32)
    return high, middle, value - high - middle


def contract(left, right, left_axis, right_axis):
    return lax.dot_general(
        left, right, (((left_axis,), (right_axis,)), ((), ())), preferred_element_type=F32
    )


def attend_kernel(active_ref, qkv_ref, low_ref, full_ref, stat_ref, mixed_ref, *, block, chunk):
    at = pl.program_id(0)
    rows = pl.ds(pl.multiple_of(at * block, block), block)
    lane = lax.broadcasted_iota(jnp.int32, (block, LANES), 1)
    last = lax.div(at * block, chunk)
    for slot in range(2):
        spare = HALF - HALF * slot
        own = (lane < HALF) if slot == 0 else (lane >= HALF)
        columns = slice(slot * LANES, (slot + 1) * LANES)

        @pl.when(active_ref[slot, at] != 0)
        def _():
            query = qkv_ref[rows, columns]

            def step(index, carry, edge):
                top, weighted = carry
                place = pl.ds(pl.multiple_of(index * chunk, chunk), chunk)
                keys = qkv_ref[place, 2 * LANES + slot * LANES : 3 * LANES + slot * LANES]
                values = qkv_ref[place, 4 * LANES + slot * LANES : 5 * LANES + slot * LANES]
                scores = contract(query, keys, 1, 1)
                if edge:
                    key_at = index * chunk + lax.broadcasted_iota(jnp.int32, (block, chunk), 1)
                    query_at = at * block + lax.broadcasted_iota(jnp.int32, (block, chunk), 0)
                    scores = jnp.where(key_at <= query_at, scores, FAR)
                new_top = jnp.maximum(top, jnp.max(scores, axis=1, keepdims=True))
                weights = jnp.exp(scores - new_top).astype(BF16)
                weighted = weighted * jnp.exp(top - new_top) + contract(weights, values, 1, 0)
                return new_top, weighted

            carry = (jnp.full((block, 1), FAR, F32), jnp.zeros((block, LANES), F32))
            carry = lax.fori_loop(0, last, lambda index, state: step(index, state, False), carry)
            top, weighted = step(last, carry, True)
            total = weighted[:, spare : spare + 1]
            mixed_ref[slot] = jnp.where(own, weighted / total, 0.0)
            log_total = top + jnp.log(total)
            high, middle, small = three_parts(log_total)
            extra = jnp.where(lane == spare + 3, -high, 0.0)
            extra = jnp.where(lane == spare + 4, -middle, extra)
            extra = jnp.where(lane == spare + 5, -small, extra)
            stat_ref[:, columns] = (query.astype(F32) + extra).astype(BF16)

        @pl.when(active_ref[slot, at] == 0)
        def _():
            mixed_ref[slot] = jnp.zeros((block, LANES), F32)
            stat_ref[:, columns] = jnp.zeros((block, LANES), BF16)

    mixed = mixed_ref[0] + mixed_ref[1]
    full_ref[...] = mixed
    low_ref[...] = mixed.astype(BF16)


def attend_back_kernel(
    active_ref,
    qkv_ref,
    stat_ref,
    grad_ref,
    mixed_ref,
    out_ref,
    key_sum_ref,
    value_sum_ref,
    query_sum_ref,
    *,
    block,
    chunk,
    scaling,
):
    at = pl.program_id(0)
    rows = pl.ds(pl.multiple_of(at * block, block), block)
    lane = lax.broadcasted_iota(jnp.int32, (block, LANES), 1)
    last = lax.div(at * block, chunk)

    @pl.when(at == 0)
    def _():
        key_sum_ref[...] = jnp.zeros_like(key_sum_ref)
        value_sum_ref[...] = jnp.zeros_like(value_sum_ref)

    for slot in range(2):
        spare = HALF - HALF * slot
        own = (lane < HALF) if slot == 0 else (lane >= HALF)
        columns = slice(slot * LANES, (slot + 1) * LANES)
        query_sum_ref[slot] = jnp.zeros((block, LANES), F32)

        @pl.when(active_ref[slot, at] != 0)
        def _():
            query = stat_ref[:, columns]
            grad = grad_ref[...].astype(F32)
            delta = jnp.sum(jnp.where(own, grad * mixed_ref[...], 0.0), axis=1, keepdims=True)
            high, middle, small = three_parts(delta)
            extra = jnp.where(lane == spare, -high, 0.0)
            extra = jnp.where(lane == spare + 1, -middle, extra)
            extra = jnp.where(lane == spare + 2, -small, extra)
            grad_low = jnp.where(own, grad, extra).astype(BF16)

            def step(index, edge):
                place = pl.ds(pl.multiple_of(index * chunk, chunk), chunk)
                keys = qkv_ref[place, 2 * LANES + slot * LANES : 3 * LANES + slot * LANES]
                values = qkv_ref[place, 4 * LANES + slot * LANES : 5 * LANES + slot * LANES]
                scores = contract(keys, query, 1, 1)
                if edge:
                    key_at = index * chunk + lax.broadcasted_iota(jnp.int32, (chunk, block), 0)
                    query_at = at * block + lax.broadcasted_iota(jnp.int32, (chunk, block), 1)
                    scores = jnp.where(key_at <= query_at, scores, FAR)
                weights = jnp.exp(scores)
                grad_weights = contract(values, grad_low, 1, 1)
                grad_scores = (weights * grad_weights).astype(BF16)
                value_sum_ref[slot, place, :] += contract(weights.astype(BF16), grad_low, 1, 0)
                key_sum_ref[slot, place, :] += contract(grad_scores, query, 1, 0)
                query_sum_ref[slot] += contract(grad_scores, keys, 0, 0)

            @pl.loop(0, last)
            def _(index):
                step(index, False)

            step(last, True)

    first_half = lane < HALF
    query_grad = jnp.where(first_half, query_sum_ref[0], query_sum_ref[1]) * scaling
    out_ref[rows, :LANES] = query_grad.astype(BF16)

    @pl.when(at == pl.num_programs(0) - 1)
    def _():
        @pl.loop(0, pl.num_programs(0))
        def _(index):
            place = pl.ds(pl.multiple_of(index * block, block), block)
            key_grad = jnp.where(first_half, key_sum_ref[0, place, :], key_sum_ref[1, place, :])
            value_grad = jnp.where(
                first_half, value_sum_ref[0, place, :], value_sum_ref[1, place, :]
            )
            out_ref[place, LANES : 2 * LANES] = key_grad.astype(BF16)
            out_ref[place, 2 * LANES :] = value_grad.astype(BF16)


def attend(active, qkv, block):
    length = qkv.shape[0]
    count = length // block
    pairs = length * length * 3 // 4
    return pl.pallas_call(
        functools.partial(attend_kernel, block=block, chunk=2 * block),
        grid_spec=pltpu.PrefetchScalarGridSpec(
            num_scalar_prefetch=1,
            grid=(count,),
            in_specs=[
                pl.BlockSpec(qkv.shape, lambda i, a: (0, 0), pipeline_mode=pl.Buffered(1)),
            ],
            out_specs=[
                pl.BlockSpec((block, LANES), lambda i, a: (i, 0)),
                pl.BlockSpec((block, LANES), lambda i, a: (i, 0)),
                pl.BlockSpec((block, 2 * LANES), lambda i, a: (i, 0)),
            ],
            scratch_shapes=[pltpu.VMEM((2, block, LANES), F32)],
        ),
        out_shape=[
            jax.ShapeDtypeStruct((length, LANES), BF16),
            jax.ShapeDtypeStruct((length, LANES), F32),
            jax.ShapeDtypeStruct((length, 2 * LANES), BF16),
        ],
        compiler_params=pltpu.CompilerParams(vmem_limit_bytes=VMEM_LIMIT),
        cost_estimate=pl.CostEstimate(
            flops=pairs * 4 * LANES, bytes_accessed=length * 2 * 10 * LANES, transcendentals=pairs
        ),
    )(active, qkv)


def attend_back(active, qkv, stat, grad, mixed, block, scaling):
    length = qkv.shape[0]
    count = length // block
    pairs = length * length * 3 // 4
    return pl.pallas_call(
        functools.partial(attend_back_kernel, block=block, chunk=2 * block, scaling=scaling),
        grid_spec=pltpu.PrefetchScalarGridSpec(
            num_scalar_prefetch=1,
            grid=(count,),
            in_specs=[
                pl.BlockSpec(qkv.shape, lambda i, a: (0, 0), pipeline_mode=pl.Buffered(1)),
                pl.BlockSpec((block, 2 * LANES), lambda i, a: (i, 0)),
                pl.BlockSpec((block, LANES), lambda i, a: (i, 0)),
                pl.BlockSpec((block, LANES), lambda i, a: (i, 0)),
            ],
            out_specs=pl.BlockSpec(
                (length, 3 * LANES), lambda i, a: (0, 0), pipeline_mode=pl.Buffered(1)
            ),
            scratch_shapes=[
                pltpu.VMEM((2, length, LANES), F32),
                pltpu.VMEM((2, length, LANES), F32),
                pltpu.VMEM((2, block, LANES), F32),
            ],
        ),
        out_shape=jax.ShapeDtypeStruct((length, 3 * LANES), BF16),
        compiler_params=pltpu.CompilerParams(vmem_limit_bytes=VMEM_LIMIT),
        cost_estimate=pl.CostEstimate(
            flops=pairs * 10 * LANES, bytes_accessed=length * 2 * 15 * LANES, transcendentals=pairs
        ),
    )(active, qkv, stat, grad, mixed)


def adam_update(weight, grad, first, second, factor, rate, decay):
    clipped = grad * factor
    first_new = BETA_ONE * first + (1.0 - BETA_ONE) * clipped
    second_new = BETA_TWO * second + (1.0 - BETA_TWO) * clipped * clipped
    first_hat = first_new / (1.0 - BETA_ONE**STEP)
    second_hat = second_new / (1.0 - BETA_TWO**STEP)
    weight_new = weight - rate * (first_hat / (jnp.sqrt(second_hat) + ADAM_FLOOR) + decay * weight)
    return (first_new, second_new, weight_new)


def spread_sum(value):
    count = lax.axis_size(ALL)
    copies = jnp.broadcast_to(value[None], (count, *value.shape))
    return jnp.sum(lax.all_to_all(copies, ALL, split_axis=0, concat_axis=0, tiled=True), axis=0)


def lane_table(kind):
    table = np.zeros((3, 2, LANES), np.float32)
    for slot in range(2):
        spare = HALF - HALF * slot
        for segment in range(3):
            for other in range(3):
                if kind == "query":
                    table[segment, slot, spare + other] = 0.0 if other == segment else FAR
                elif kind == "key":
                    table[segment, slot, spare + other] = 1.0 if other == segment else 0.0
                    table[segment, slot, spare + 3 + other] = 1.0
                else:
                    table[segment, slot, spare + other] = 1.0
    return table.reshape(3, 2 * LANES)


def body(
    tokens,
    cotangent,
    segment_ids,
    expert_ids,
    projection,
    output_weight,
    expert_up,
    expert_down,
    norm_gains,
    projection_first,
    projection_second,
    output_first,
    output_second,
    up_first,
    up_second,
    down_first,
    down_second,
    gains_first,
    gains_second,
):
    inputs = tokens[0].astype(F32)
    upstream = cotangent[0].astype(F32)
    row_count = inputs.shape[0]
    width = inputs.shape[1]
    head_size = width // HEADS
    scaling = head_size ** (-0.5)
    count = lax.axis_size(SEQ)
    groups = lax.axis_size("exp")
    team = lax.axis_size(TEAM)
    position = lax.axis_index(SEQ)
    length = count * row_count
    weight_rows = projection.shape[0]
    first_heads, active_table = head_plan(count)
    starts = [int(head) * head_size for head in first_heads]
    active = lax.dynamic_index_in_dim(jnp.asarray(active_table), position, 0, keepdims=False)
    gain_first = norm_gains[0]
    gain_second = norm_gains[1]
    used = active_table.any(axis=2)

    scale_first = lax.rsqrt(jnp.mean(inputs * inputs, axis=-1, keepdims=True) + EPSILON)
    normed_first = inputs * scale_first
    attend_in = (normed_first * gain_first).astype(BF16)
    row_in = lax.all_gather(attend_in, SEQ, axis=0, tiled=True)
    projection_low = projection.astype(BF16)
    pieces = [
        jnp.concatenate(
            [projection_low[:, k * width + s : k * width + s + LANES] for k in range(3)], axis=1
        )
        for s in starts
    ]
    sent_columns = jnp.broadcast_to(
        jnp.stack(pieces)[:, None], (count, groups, weight_rows, 3 * LANES)
    ).reshape(count * groups, weight_rows, 3 * LANES)
    columns = lax.all_to_all(sent_columns, ALL, split_axis=0, concat_axis=0, tiled=True).reshape(
        width, 3, 2, head_size
    )
    blank = jnp.zeros((width, 3, 1, head_size), BF16)
    padded = jnp.stack(
        [
            jnp.concatenate([columns[:, :, :1], blank], axis=2),
            jnp.concatenate([blank, columns[:, :, 1:]], axis=2),
        ],
        axis=2,
    ).reshape(width, 6 * LANES)
    segments = lax.all_gather(segment_ids[0].astype(BF16), SEQ, axis=0, tiled=True)
    output_full = lax.all_gather(output_weight.astype(BF16), ALL, axis=0, tiled=True)

    slots = groups * CAP
    chosen = expert_ids[0, :, 0]
    one_hot = (chosen[:, None] == jnp.arange(groups, dtype=jnp.int32)[None, :]).astype(jnp.int32)
    rank = jnp.sum(jnp.cumsum(one_hot, axis=0) * one_hot, axis=1) - 1
    target = chosen * CAP + rank
    placing = (target[:, None] == jnp.arange(slots, dtype=jnp.int32)[None, :]).astype(BF16)

    def dispatch(values):
        outgoing = jnp.einsum("ts,td->sd", placing, values, preferred_element_type=F32)
        outgoing = outgoing.astype(BF16).reshape(1, groups, CAP, width)
        outgoing = jnp.broadcast_to(outgoing, (team, groups, CAP, width))
        return lax.all_to_all(
            outgoing.reshape(team * groups, CAP, width),
            TEAM + EXP,
            split_axis=0,
            concat_axis=0,
            tiled=True,
        ).reshape(team * slots, width)

    def combine(values):
        returned = lax.all_to_all(
            values.reshape(team * groups, CAP, width),
            TEAM + EXP,
            split_axis=0,
            concat_axis=0,
            tiled=True,
        ).reshape(team, slots, width)
        return jnp.einsum("ts,jsd->td", placing, returned, preferred_element_type=F32)

    grad_arrived = dispatch(cotangent[0])

    weights_full = lax.all_gather(
        jnp.concatenate([expert_up[0], expert_down[0]], axis=1).astype(BF16),
        SHARE,
        axis=0,
        tiled=True,
    )
    up_matrix = weights_full[:, :width]
    down_matrix = weights_full[:, width:]
    projection_full = lax.all_gather(projection_low, ALL, axis=0, tiled=True)

    tables = [lane_table(kind) for kind in ("query", "key", "value")]
    table = jnp.asarray(np.concatenate(tables, axis=1), BF16)
    documents = segments[:, None]
    extra = jnp.where(documents == 0, table[0], jnp.where(documents == 1, table[1], table[2]))
    scales = np.ones((6 * LANES,), np.float32)
    scales[: 2 * LANES] = scaling
    qkv = jnp.dot(row_in, padded, preferred_element_type=F32).astype(BF16)
    qkv = qkv * jnp.asarray(scales, BF16) + extra
    mixed_low, mixed_full, stat = attend(active, qkv, row_count)

    def place_heads():
        index = np.arange(LANES)
        matrix = np.zeros((count, LANES, width), np.float32)
        for device in range(count):
            for slot in range(2):
                if used[device, slot]:
                    own = index[slot * HALF : (slot + 1) * HALF]
                    matrix[device, own, starts[device] + own] = 1.0
        return jnp.asarray(matrix, BF16)

    head_places = place_heads()

    def to_tokens(values):
        return lax.all_to_all(
            values.reshape(count, row_count, values.shape[1]),
            SEQ,
            split_axis=0,
            concat_axis=0,
            tiled=True,
        )

    attend_out = jnp.einsum(
        "jtc,jcd->td", to_tokens(mixed_low), head_places, preferred_element_type=F32
    ).astype(BF16)
    branch = jnp.dot(attend_out, output_full, preferred_element_type=F32)
    middle = inputs + branch
    scale_second = lax.rsqrt(jnp.mean(middle * middle, axis=-1, keepdims=True) + EPSILON)
    normed_second = middle * scale_second
    expert_in = (normed_second * gain_second).astype(BF16)

    arrived = dispatch(expert_in)
    hidden = jnp.einsum("sd,hd->sh", arrived, up_matrix, preferred_element_type=F32)
    active_units = jax.nn.gelu(hidden).astype(BF16)
    grad_active = jnp.einsum("sd,hd->sh", grad_arrived, down_matrix, preferred_element_type=F32)
    unused, gelu_pull = jax.vjp(jax.nn.gelu, hidden)
    grad_hidden = gelu_pull(grad_active)[0].astype(BF16)
    grad_slots = jnp.einsum("sh,hd->sd", grad_hidden, up_matrix, preferred_element_type=F32)
    grad_expert_in = combine(grad_slots.astype(BF16))
    produced = jnp.einsum("sh,hd->sd", active_units, down_matrix, preferred_element_type=F32)
    expert_part = combine(produced.astype(BF16))
    block_output = (middle + expert_part).astype(BF16)[None]
    up_term = jnp.einsum("sh,sd->hd", grad_hidden, arrived, preferred_element_type=F32)
    down_term = jnp.einsum("sh,sd->hd", active_units, grad_arrived, preferred_element_type=F32)
    expert_sum = lax.psum_scatter(
        jnp.concatenate([up_term.astype(BF16), down_term.astype(BF16)], axis=1),
        SHARE,
        scatter_dimension=0,
        tiled=True,
    ).astype(F32)
    up_grad = expert_sum[:, :width][None]
    down_grad = expert_sum[:, width:][None]

    scaled_second = grad_expert_in * gain_second
    gain_second_part = jnp.sum(grad_expert_in * normed_second, axis=0)
    grad_middle = scale_second * (
        scaled_second
        - normed_second * jnp.mean(scaled_second * normed_second, axis=-1, keepdims=True)
    )
    residual_grad = upstream + grad_middle
    branch_grad = residual_grad.astype(BF16)
    grad_mixed = jnp.einsum(
        "td,ed->te", branch_grad, output_full, preferred_element_type=F32
    ).astype(BF16)

    sent_grad = jnp.stack([grad_mixed[:, s : s + LANES] for s in starts])
    row_grad = lax.all_to_all(sent_grad, SEQ, split_axis=0, concat_axis=0, tiled=True).reshape(
        length, LANES
    )
    grad_qkv = attend_back(active, qkv, stat, row_grad, mixed_full, row_count, scaling)
    grad_pieces = to_tokens(grad_qkv)
    grad_projected = jnp.concatenate(
        [
            jnp.einsum(
                "jtc,jcd->td",
                grad_pieces[:, :, k * LANES : (k + 1) * LANES],
                head_places,
                preferred_element_type=F32,
            ).astype(BF16)
            for k in range(3)
        ],
        axis=1,
    )
    grad_attend_in = jnp.einsum(
        "tc,dc->td", grad_projected, projection_full, preferred_element_type=F32
    )
    scaled_first = grad_attend_in * gain_first
    gain_first_part = jnp.sum(grad_attend_in * normed_first, axis=0)
    input_grad = (
        residual_grad
        + scale_first
        * (
            scaled_first
            - normed_first * jnp.mean(scaled_first * normed_first, axis=-1, keepdims=True)
        )
    )[None]

    output_term = jnp.einsum("tc,te->ce", attend_out, branch_grad, preferred_element_type=F32)
    output_grad = lax.psum_scatter(
        output_term.astype(BF16), ALL, scatter_dimension=0, tiled=True
    ).astype(F32)
    column_term = jnp.einsum("tc,te->ce", row_in, grad_qkv, preferred_element_type=F32)
    column_terms = lax.all_to_all(
        column_term.astype(BF16).reshape(count * groups, weight_rows, 3 * LANES),
        ALL,
        split_axis=0,
        concat_axis=0,
        tiled=True,
    ).reshape(count, groups, weight_rows, 3 * LANES)
    column_sums = jnp.sum(column_terms.astype(F32), axis=1)
    head_grads = []
    for k in range(3):
        for head in range(HEADS):
            parts = [
                column_sums[j, :, k * LANES + slot * HALF : k * LANES + (slot + 1) * HALF]
                for j in range(count)
                for slot in range(2)
                if used[j, slot] and first_heads[j] + slot == head
            ]
            head_grads.append(functools.reduce(jnp.add, parts))
    projection_grad = jnp.concatenate(head_grads, axis=1)

    gains_grad = spread_sum(jnp.stack([gain_first_part, gain_second_part]))
    local_square = jnp.sum(projection_grad * projection_grad) + jnp.sum(output_grad * output_grad)
    local_square = local_square + jnp.sum(up_grad * up_grad) + jnp.sum(down_grad * down_grad)
    square_total = spread_sum(jnp.broadcast_to(local_square, (LANES,)))[0]
    grad_norm = jnp.sqrt(square_total + jnp.sum(gains_grad * gains_grad))
    factor = jnp.minimum(1.0, CLIP / (grad_norm + 1e-06))
    projection_moment, projection_square, projection_new = adam_update(
        projection, projection_grad, projection_first, projection_second, factor, RATE_MATRIX, DECAY
    )
    output_moment, output_square, output_new = adam_update(
        output_weight, output_grad, output_first, output_second, factor, RATE_OUTPUT, DECAY
    )
    up_moment, up_square, up_new = adam_update(
        expert_up, up_grad, up_first, up_second, factor, RATE_MATRIX, DECAY
    )
    down_moment, down_square, down_new = adam_update(
        expert_down, down_grad, down_first, down_second, factor, RATE_MATRIX, DECAY
    )
    gains_moment, gains_square, gains_new = adam_update(
        norm_gains, gains_grad, gains_first, gains_second, factor, RATE_GAIN, 0.0
    )
    return (
        block_output,
        input_grad,
        grad_norm,
        projection_grad,
        projection_moment,
        projection_square,
        projection_new,
        output_grad,
        output_moment,
        output_square,
        output_new,
        up_grad,
        up_moment,
        up_square,
        up_new,
        down_grad,
        down_moment,
        down_square,
        down_new,
        gains_grad,
        gains_moment,
        gains_square,
        gains_new,
    )


def solution(mesh):
    token = P("exp", SEQ, None)
    dense = P(ALL, None)
    expert = P("exp", SEQ, None)
    in_specs = (
        (token, token, P("exp", SEQ), token)
        + (dense, dense, expert, expert, P())
        + (dense,) * 4
        + (expert,) * 4
        + (P(), P())
    )
    out_specs = (token, token, P()) + (dense,) * 8 + (expert,) * 8 + (P(),) * 4
    rows, groups = mesh.devices.shape
    fine = Mesh(mesh.devices.reshape(rows // 4, 2, 2, groups), ALL)
    return jax.shard_map(body, mesh=fine, in_specs=in_specs, out_specs=out_specs, check_vma=False)
```

```python
import functools
import math

import jax
import jax.numpy as jnp
import numpy as np
from jax import lax
from jax.experimental import pallas as pl
from jax.experimental.pallas import tpu as pltpu
from jax.sharding import Mesh
from jax.sharding import PartitionSpec as P

HEADS = 12
CAP = 128
STEP = 10


EPSILON = 1e-05
CLIP = 1.0
BETA_ONE = 0.9
BETA_TWO = 0.99
ADAM_FLOOR = 1e-08
DECAY = 0.1
RATE_MATRIX = 0.04
RATE_OUTPUT = 0.1
RATE_GAIN = 0.5

SEQ = ("hi", "lo", "in")
EXP = ("exp",)
ALL = SEQ + EXP
TEAM = ("lo",)
SHARE = ("hi", "in")
LANES = 128
HALF = 64
FAR = -1e30
BF16 = jnp.bfloat16
F32 = jnp.float32
VMEM_LIMIT = 60 * 1024 * 1024


def head_plan(count):
    whole = math.lcm(HEADS, count)
    units, parts = whole // count, whole // HEADS
    first = np.zeros((count,), np.int64)
    active = np.zeros((count, 2, count), np.int32)
    for device in range(count):
        first[device] = min(units * device // parts, HEADS - 2)
        for unit in range(units * device, units * (device + 1)):
            slot = unit // parts - first[device]
            for block in range(count):
                turn = block % (2 * parts)
                if min(turn, 2 * parts - 1 - turn) == unit % parts:
                    active[device, slot, block] = 1
    return first, active


def three_parts(value):
    high = value.astype(BF16).astype(F32)
    middle = (value - high).astype(BF16).astype(F32)
    return high, middle, value - high - middle


def contract(left, right, left_axis, right_axis):
    return lax.dot_general(
        left, right, (((left_axis,), (right_axis,)), ((), ())), preferred_element_type=F32
    )


def attend_kernel(active_ref, qkv_ref, low_ref, full_ref, stat_ref, mixed_ref, *, block, chunk):
    at = pl.program_id(0)
    rows = pl.ds(pl.multiple_of(at * block, block), block)
    lane = lax.broadcasted_iota(jnp.int32, (block, LANES), 1)
    last = lax.div(at * block, chunk)
    for slot in range(2):
        spare = HALF - HALF * slot
        own = (lane < HALF) if slot == 0 else (lane >= HALF)
        columns = slice(slot * LANES, (slot + 1) * LANES)

        @pl.when(active_ref[slot, at] != 0)
        def _():
            query = qkv_ref[rows, columns]

            def step(index, carry, edge):
                top, weighted = carry
                place = pl.ds(pl.multiple_of(index * chunk, chunk), chunk)
                keys = qkv_ref[place, 2 * LANES + slot * LANES : 3 * LANES + slot * LANES]
                values = qkv_ref[place, 4 * LANES + slot * LANES : 5 * LANES + slot * LANES]
                scores = contract(query, keys, 1, 1)
                if edge:
                    key_at = index * chunk + lax.broadcasted_iota(jnp.int32, (block, chunk), 1)
                    query_at = at * block + lax.broadcasted_iota(jnp.int32, (block, chunk), 0)
                    scores = jnp.where(key_at <= query_at, scores, FAR)
                new_top = jnp.maximum(top, jnp.max(scores, axis=1, keepdims=True))
                weights = jnp.exp(scores - new_top).astype(BF16)
                weighted = weighted * jnp.exp(top - new_top) + contract(weights, values, 1, 0)
                return new_top, weighted

            carry = (jnp.full((block, 1), FAR, F32), jnp.zeros((block, LANES), F32))
            carry = lax.fori_loop(0, last, lambda index, state: step(index, state, False), carry)
            top, weighted = step(last, carry, True)
            total = weighted[:, spare : spare + 1]
            mixed_ref[slot] = jnp.where(own, weighted / total, 0.0)
            log_total = top + jnp.log(total)
            high, middle, small = three_parts(log_total)
            extra = jnp.where(lane == spare + 3, -high, 0.0)
            extra = jnp.where(lane == spare + 4, -middle, extra)
            extra = jnp.where(lane == spare + 5, -small, extra)
            stat_ref[:, columns] = (query.astype(F32) + extra).astype(BF16)

        @pl.when(active_ref[slot, at] == 0)
        def _():
            mixed_ref[slot] = jnp.zeros((block, LANES), F32)
            stat_ref[:, columns] = jnp.zeros((block, LANES), BF16)

    mixed = mixed_ref[0] + mixed_ref[1]
    full_ref[...] = mixed
    low_ref[...] = mixed.astype(BF16)


def attend_back_kernel(
    active_ref,
    qkv_ref,
    stat_ref,
    grad_ref,
    mixed_ref,
    out_ref,
    key_sum_ref,
    value_sum_ref,
    query_sum_ref,
    *,
    block,
    chunk,
    scaling,
):
    at = pl.program_id(0)
    rows = pl.ds(pl.multiple_of(at * block, block), block)
    lane = lax.broadcasted_iota(jnp.int32, (block, LANES), 1)
    last = lax.div(at * block, chunk)

    @pl.when(at == 0)
    def _():
        key_sum_ref[...] = jnp.zeros_like(key_sum_ref)
        value_sum_ref[...] = jnp.zeros_like(value_sum_ref)

    for slot in range(2):
        spare = HALF - HALF * slot
        own = (lane < HALF) if slot == 0 else (lane >= HALF)
        columns = slice(slot * LANES, (slot + 1) * LANES)
        query_sum_ref[slot] = jnp.zeros((block, LANES), F32)

        @pl.when(active_ref[slot, at] != 0)
        def _():
            query = stat_ref[:, columns]
            grad = grad_ref[...].astype(F32)
            delta = jnp.sum(jnp.where(own, grad * mixed_ref[...], 0.0), axis=1, keepdims=True)
            high, middle, small = three_parts(delta)
            extra = jnp.where(lane == spare, -high, 0.0)
            extra = jnp.where(lane == spare + 1, -middle, extra)
            extra = jnp.where(lane == spare + 2, -small, extra)
            grad_low = jnp.where(own, grad, extra).astype(BF16)

            def step(index, edge):
                place = pl.ds(pl.multiple_of(index * chunk, chunk), chunk)
                keys = qkv_ref[place, 2 * LANES + slot * LANES : 3 * LANES + slot * LANES]
                values = qkv_ref[place, 4 * LANES + slot * LANES : 5 * LANES + slot * LANES]
                scores = contract(keys, query, 1, 1)
                if edge:
                    key_at = index * chunk + lax.broadcasted_iota(jnp.int32, (chunk, block), 0)
                    query_at = at * block + lax.broadcasted_iota(jnp.int32, (chunk, block), 1)
                    scores = jnp.where(key_at <= query_at, scores, FAR)
                weights = jnp.exp(scores)
                grad_weights = contract(values, grad_low, 1, 1)
                grad_scores = (weights * grad_weights).astype(BF16)
                value_sum_ref[slot, place, :] += contract(weights.astype(BF16), grad_low, 1, 0)
                key_sum_ref[slot, place, :] += contract(grad_scores, query, 1, 0)
                query_sum_ref[slot] += contract(grad_scores, keys, 0, 0)

            @pl.loop(0, last)
            def _(index):
                step(index, False)

            step(last, True)

    first_half = lane < HALF
    query_grad = jnp.where(first_half, query_sum_ref[0], query_sum_ref[1]) * scaling
    out_ref[rows, :LANES] = query_grad.astype(BF16)

    @pl.when(at == pl.num_programs(0) - 1)
    def _():
        @pl.loop(0, pl.num_programs(0))
        def _(index):
            place = pl.ds(pl.multiple_of(index * block, block), block)
            key_grad = jnp.where(first_half, key_sum_ref[0, place, :], key_sum_ref[1, place, :])
            value_grad = jnp.where(
                first_half, value_sum_ref[0, place, :], value_sum_ref[1, place, :]
            )
            out_ref[place, LANES : 2 * LANES] = key_grad.astype(BF16)
            out_ref[place, 2 * LANES :] = value_grad.astype(BF16)


def attend(active, qkv, block):
    length = qkv.shape[0]
    count = length // block
    pairs = length * length * 3 // 4
    return pl.pallas_call(
        functools.partial(attend_kernel, block=block, chunk=2 * block),
        grid_spec=pltpu.PrefetchScalarGridSpec(
            num_scalar_prefetch=1,
            grid=(count,),
            in_specs=[
                pl.BlockSpec(qkv.shape, lambda i, a: (0, 0), pipeline_mode=pl.Buffered(1)),
            ],
            out_specs=[
                pl.BlockSpec((block, LANES), lambda i, a: (i, 0)),
                pl.BlockSpec((block, LANES), lambda i, a: (i, 0)),
                pl.BlockSpec((block, 2 * LANES), lambda i, a: (i, 0)),
            ],
            scratch_shapes=[pltpu.VMEM((2, block, LANES), F32)],
        ),
        out_shape=[
            jax.ShapeDtypeStruct((length, LANES), BF16),
            jax.ShapeDtypeStruct((length, LANES), F32),
            jax.ShapeDtypeStruct((length, 2 * LANES), BF16),
        ],
        compiler_params=pltpu.CompilerParams(vmem_limit_bytes=VMEM_LIMIT),
        cost_estimate=pl.CostEstimate(
            flops=pairs * 4 * LANES, bytes_accessed=length * 2 * 10 * LANES, transcendentals=pairs
        ),
    )(active, qkv)


def attend_back(active, qkv, stat, grad, mixed, block, scaling):
    length = qkv.shape[0]
    count = length // block
    pairs = length * length * 3 // 4
    return pl.pallas_call(
        functools.partial(attend_back_kernel, block=block, chunk=2 * block, scaling=scaling),
        grid_spec=pltpu.PrefetchScalarGridSpec(
            num_scalar_prefetch=1,
            grid=(count,),
            in_specs=[
                pl.BlockSpec(qkv.shape, lambda i, a: (0, 0), pipeline_mode=pl.Buffered(1)),
                pl.BlockSpec((block, 2 * LANES), lambda i, a: (i, 0)),
                pl.BlockSpec((block, LANES), lambda i, a: (i, 0)),
                pl.BlockSpec((block, LANES), lambda i, a: (i, 0)),
            ],
            out_specs=pl.BlockSpec(
                (length, 3 * LANES), lambda i, a: (0, 0), pipeline_mode=pl.Buffered(1)
            ),
            scratch_shapes=[
                pltpu.VMEM((2, length, LANES), F32),
                pltpu.VMEM((2, length, LANES), F32),
                pltpu.VMEM((2, block, LANES), F32),
            ],
        ),
        out_shape=jax.ShapeDtypeStruct((length, 3 * LANES), BF16),
        compiler_params=pltpu.CompilerParams(vmem_limit_bytes=VMEM_LIMIT),
        cost_estimate=pl.CostEstimate(
            flops=pairs * 10 * LANES, bytes_accessed=length * 2 * 15 * LANES, transcendentals=pairs
        ),
    )(active, qkv, stat, grad, mixed)


def adam_update(weight, grad, first, second, factor, rate, decay):
    clipped = grad * factor
    first_new = BETA_ONE * first + (1.0 - BETA_ONE) * clipped
    second_new = BETA_TWO * second + (1.0 - BETA_TWO) * clipped * clipped
    first_hat = first_new / (1.0 - BETA_ONE**STEP)
    second_hat = second_new / (1.0 - BETA_TWO**STEP)
    weight_new = weight - rate * (first_hat / (jnp.sqrt(second_hat) + ADAM_FLOOR) + decay * weight)
    return (first_new, second_new, weight_new)


def adam_kernel(factor_ref, *refs, rates):
    count = len(rates)
    factor = factor_ref[0]
    for index, rate in enumerate(rates):
        weight, grad, first, second = [ref[...] for ref in refs[4 * index : 4 * index + 4]]
        outs = refs[4 * count + 3 * index : 4 * count + 3 * index + 3]
        for out, value in zip(
            outs, adam_update(weight, grad, first, second, factor, rate, DECAY), strict=True
        ):
            out[...] = value


def adam_all(factor, leaves, rates, steps):
    flat = [value.reshape(value.shape[-2:]) for leaf in leaves for value in leaf]

    def spec(value):
        rows, columns = value.shape
        if rows % (8 * steps) == 0:
            return pl.BlockSpec((rows // steps, columns), lambda i: (i, 0))
        lanes = columns // steps
        return pl.BlockSpec((rows, lanes), lambda i: (0, i))

    shapes = [jax.ShapeDtypeStruct(value.shape, F32) for value in flat[::4] for _ in range(3)]
    outs = pl.pallas_call(
        functools.partial(adam_kernel, rates=rates),
        grid=(steps,),
        in_specs=[pl.BlockSpec(memory_space=pltpu.SMEM)] + [spec(value) for value in flat],
        out_specs=[spec(shape) for shape in shapes],
        out_shape=shapes,
        compiler_params=pltpu.CompilerParams(vmem_limit_bytes=VMEM_LIMIT),
        cost_estimate=pl.CostEstimate(
            flops=20 * sum(value.size for value in flat[::4]),
            bytes_accessed=28 * sum(value.size for value in flat[::4]),
            transcendentals=0,
        ),
    )(factor.reshape(1), *flat)
    return [
        [out.reshape(leaf[0].shape) for out in outs[3 * index : 3 * index + 3]]
        for index, leaf in enumerate(leaves)
    ]


def others(value, axis):
    size = lax.axis_size(axis)
    return jnp.concatenate(
        [
            lax.ppermute(value, axis, [((i + step) % size, i) for i in range(size)])
            for step in range(1, size)
        ],
        axis=0,
    )


def sum_own(blocks, axis):
    size = lax.axis_size(axis)
    total = blocks[0].astype(F32)
    for step in range(1, size):
        total = total + lax.ppermute(
            blocks[step].astype(BF16), axis, [(i, (i + step) % size) for i in range(size)]
        ).astype(F32)
    return total


def spread_sum(value):
    count = lax.axis_size(ALL)
    copies = jnp.broadcast_to(value[None], (count, *value.shape))
    return jnp.sum(lax.all_to_all(copies, ALL, split_axis=0, concat_axis=0, tiled=True), axis=0)


def lane_table(kind):
    table = np.zeros((3, 2, LANES), np.float32)
    for slot in range(2):
        spare = HALF - HALF * slot
        for segment in range(3):
            for other in range(3):
                if kind == "query":
                    table[segment, slot, spare + other] = 0.0 if other == segment else FAR
                elif kind == "key":
                    table[segment, slot, spare + other] = 1.0 if other == segment else 0.0
                    table[segment, slot, spare + 3 + other] = 1.0
                else:
                    table[segment, slot, spare + other] = 1.0
    return table.reshape(3, 2 * LANES)


def body(
    tokens,
    cotangent,
    segment_ids,
    expert_ids,
    projection,
    output_weight,
    expert_up,
    expert_down,
    norm_gains,
    projection_first,
    projection_second,
    output_first,
    output_second,
    up_first,
    up_second,
    down_first,
    down_second,
    gains_first,
    gains_second,
):
    inputs = tokens[0].astype(F32)
    upstream = cotangent[0].astype(F32)
    row_count = inputs.shape[0]
    width = inputs.shape[1]
    head_size = width // HEADS
    scaling = head_size ** (-0.5)
    count = lax.axis_size(SEQ)
    groups = lax.axis_size("exp")
    team = lax.axis_size(TEAM)
    position = lax.axis_index(SEQ)
    length = count * row_count
    weight_rows = projection.shape[0]
    first_heads, active_table = head_plan(count)
    starts = [int(head) * head_size for head in first_heads]
    active = lax.dynamic_index_in_dim(jnp.asarray(active_table), position, 0, keepdims=False)
    gain_first = norm_gains[0]
    gain_second = norm_gains[1]
    used = active_table.any(axis=2)

    scale_first = lax.rsqrt(jnp.mean(inputs * inputs, axis=-1, keepdims=True) + EPSILON)
    normed_first = inputs * scale_first
    attend_in = (normed_first * gain_first).astype(BF16)
    row_in = lax.all_gather(attend_in, SEQ, axis=0, tiled=True)
    projection_low = projection.astype(BF16)
    group = lax.axis_index(EXP)
    pieces = [
        jnp.concatenate(
            [projection_low[:, k * width + s : k * width + s + LANES] for k in range(3)], axis=1
        )
        for s in starts
    ]
    sent_rows = weight_rows + 8
    own_documents = jnp.zeros((8, 3 * LANES), BF16)
    own_documents = own_documents.at[0, :row_count].set(segment_ids[0].astype(BF16))
    sent_columns = jnp.stack([jnp.concatenate([piece, own_documents], axis=0) for piece in pieces])
    sent_columns = jnp.broadcast_to(
        sent_columns[:, None], (count, groups, sent_rows, 3 * LANES)
    ).reshape(count * groups, sent_rows, 3 * LANES)
    got_columns = lax.all_to_all(sent_columns, ALL, split_axis=0, concat_axis=0, tiled=True)
    columns = got_columns[:, :weight_rows].reshape(width, 3, 2, head_size)
    segments = lax.dynamic_index_in_dim(
        got_columns[:, weight_rows, :row_count].reshape(count, groups, row_count),
        group,
        1,
        keepdims=False,
    ).reshape(length)
    blank = jnp.zeros((width, 3, 1, head_size), BF16)
    padded = jnp.stack(
        [
            jnp.concatenate([columns[:, :, :1], blank], axis=2),
            jnp.concatenate([blank, columns[:, :, 1:]], axis=2),
        ],
        axis=2,
    ).reshape(width, 6 * LANES)
    output_low = lax.optimization_barrier((output_weight.astype(BF16), got_columns))[0]
    output_full = lax.all_to_all(
        jnp.broadcast_to(output_low[None], (count * groups, weight_rows, width)),
        ALL,
        split_axis=0,
        concat_axis=0,
        tiled=True,
    ).reshape(width, width)

    slots = groups * CAP
    chosen = expert_ids[0, :, 0]
    one_hot = (chosen[:, None] == jnp.arange(groups, dtype=jnp.int32)[None, :]).astype(jnp.int32)
    rank = jnp.sum(jnp.cumsum(one_hot, axis=0) * one_hot, axis=1) - 1
    target = chosen * CAP + rank
    placing = (target[:, None] == jnp.arange(slots, dtype=jnp.int32)[None, :]).astype(BF16)

    def dispatch(values, earlier=None):
        outgoing = jnp.einsum("ts,td->sd", placing, values, preferred_element_type=F32)
        outgoing = outgoing.astype(BF16)
        if earlier is not None:
            outgoing = lax.optimization_barrier((outgoing, earlier))[0]
        outgoing = outgoing.reshape(1, groups, CAP, width)
        outgoing = jnp.broadcast_to(outgoing, (team, groups, CAP, width))
        return lax.all_to_all(
            outgoing.reshape(team * groups, CAP, width),
            TEAM + EXP,
            split_axis=0,
            concat_axis=0,
            tiled=True,
        ).reshape(team * slots, width)

    def combine(values):
        returned = lax.all_to_all(
            values.reshape(team * groups, CAP, width),
            TEAM + EXP,
            split_axis=0,
            concat_axis=0,
            tiled=True,
        ).reshape(team, slots, width)
        return jnp.einsum("ts,jsd->td", placing, returned, preferred_element_type=F32)

    grad_arrived = dispatch(cotangent[0], row_in)

    own_units = jnp.concatenate([expert_up[0], expert_down[0]], axis=1).astype(BF16)
    near_units = jnp.concatenate([own_units, others(own_units, "hi")], axis=0)
    far_units = others(near_units, "in")
    projection_full = lax.all_gather(projection_low, ALL, axis=0, tiled=True)

    tables = [lane_table(kind) for kind in ("query", "key", "value")]
    table = jnp.asarray(np.concatenate(tables, axis=1), BF16)
    documents = segments[:, None]
    extra = jnp.where(documents == 0, table[0], jnp.where(documents == 1, table[1], table[2]))
    scales = np.ones((6 * LANES,), np.float32)
    scales[: 2 * LANES] = scaling
    qkv = jnp.dot(row_in, padded, preferred_element_type=F32).astype(BF16)
    qkv = qkv * jnp.asarray(scales, BF16) + extra
    mixed_low, mixed_full, stat = attend(active, qkv, row_count)

    def place_heads():
        index = np.arange(LANES)
        matrix = np.zeros((count, LANES, width), np.float32)
        for device in range(count):
            for slot in range(2):
                if used[device, slot]:
                    own = index[slot * HALF : (slot + 1) * HALF]
                    matrix[device, own, starts[device] + own] = 1.0
        return jnp.asarray(matrix, BF16)

    head_places = place_heads()

    def to_tokens(values):
        return lax.all_to_all(
            values.reshape(count, row_count, values.shape[1]),
            SEQ,
            split_axis=0,
            concat_axis=0,
            tiled=True,
        )

    attend_out = jnp.einsum(
        "jtc,jcd->td", to_tokens(mixed_low), head_places, preferred_element_type=F32
    ).astype(BF16)
    branch = jnp.dot(attend_out, output_full, preferred_element_type=F32)
    middle = inputs + branch
    scale_second = lax.rsqrt(jnp.mean(middle * middle, axis=-1, keepdims=True) + EPSILON)
    normed_second = middle * scale_second
    expert_in = (normed_second * gain_second).astype(BF16)

    arrived = dispatch(expert_in)
    unit_parts = []
    for units in (near_units, far_units):
        up_matrix = units[:, :width]
        down_matrix = units[:, width:]
        hidden = jnp.einsum("sd,hd->sh", arrived, up_matrix, preferred_element_type=F32)
        active_units = jax.nn.gelu(hidden).astype(BF16)
        grad_active = jnp.einsum("sd,hd->sh", grad_arrived, down_matrix, preferred_element_type=F32)
        unused, gelu_pull = jax.vjp(jax.nn.gelu, hidden)
        grad_hidden = gelu_pull(grad_active)[0].astype(BF16)
        unit_parts.append((up_matrix, down_matrix, active_units, grad_hidden))
    grad_slots = sum(
        jnp.einsum("sh,hd->sd", grad_hidden, up_matrix, preferred_element_type=F32)
        for up_matrix, down_matrix, active_units, grad_hidden in unit_parts
    )
    grad_expert_in = combine(grad_slots.astype(BF16))
    produced = sum(
        jnp.einsum("sh,hd->sd", active_units, down_matrix, preferred_element_type=F32)
        for up_matrix, down_matrix, active_units, grad_hidden in unit_parts
    ).astype(BF16)

    def unit_grads(left, right):
        near, far = [
            jnp.einsum("sh,sd->hd", left[part], right, preferred_element_type=F32)
            for part in range(2)
        ]
        size = lax.axis_size("hi")
        near = sum_own([near, far], "in")
        return sum_own(list(near.reshape(size, -1, width)), "hi")

    up_grad = unit_grads([part[3] for part in unit_parts], arrived)[None]
    down_grad = unit_grads([part[2] for part in unit_parts], grad_arrived)[None]

    scaled_second = grad_expert_in * gain_second
    gain_second_part = jnp.sum(grad_expert_in * normed_second, axis=0)
    grad_middle = scale_second * (
        scaled_second
        - normed_second * jnp.mean(scaled_second * normed_second, axis=-1, keepdims=True)
    )
    residual_grad = upstream + grad_middle
    branch_grad = residual_grad.astype(BF16)
    grad_mixed = jnp.einsum(
        "td,ed->te", branch_grad, output_full, preferred_element_type=F32
    ).astype(BF16)

    sent_grad = jnp.stack([grad_mixed[:, s : s + LANES] for s in starts])
    row_grad = lax.all_to_all(sent_grad, SEQ, split_axis=0, concat_axis=0, tiled=True).reshape(
        length, LANES
    )
    produced, output_low = lax.optimization_barrier(
        (
            produced,
            jnp.einsum("tc,te->ce", attend_out, branch_grad, preferred_element_type=F32).astype(BF16),
            row_grad,
        )
    )[:2]
    expert_part = combine(produced)
    block_output = (middle + expert_part).astype(BF16)[None]
    output_grad = jnp.sum(
        lax.all_to_all(
            output_low.reshape(count * groups, weight_rows, width),
            ALL,
            split_axis=0,
            concat_axis=0,
            tiled=True,
        ).astype(F32),
        axis=0,
    )
    grad_qkv = attend_back(active, qkv, stat, row_grad, mixed_full, row_count, scaling)
    grad_pieces = to_tokens(grad_qkv)
    grad_projected = jnp.concatenate(
        [
            jnp.einsum(
                "jtc,jcd->td",
                grad_pieces[:, :, k * LANES : (k + 1) * LANES],
                head_places,
                preferred_element_type=F32,
            ).astype(BF16)
            for k in range(3)
        ],
        axis=1,
    )
    grad_attend_in = jnp.einsum(
        "tc,dc->td", grad_projected, projection_full, preferred_element_type=F32
    )
    scaled_first = grad_attend_in * gain_first
    gain_first_part = jnp.sum(grad_attend_in * normed_first, axis=0)
    input_grad = (
        residual_grad
        + scale_first
        * (
            scaled_first
            - normed_first * jnp.mean(scaled_first * normed_first, axis=-1, keepdims=True)
        )
    )[None]

    column_term = jnp.einsum("tc,te->ce", row_in, grad_qkv, preferred_element_type=F32)
    column_low = lax.optimization_barrier((column_term.astype(BF16), grad_pieces))[0]
    column_terms = lax.all_to_all(
        column_low.reshape(count * groups, weight_rows, 3 * LANES),
        ALL,
        split_axis=0,
        concat_axis=0,
        tiled=True,
    ).reshape(count, groups, weight_rows, 3 * LANES)
    column_sums = jnp.sum(column_terms.astype(F32), axis=1)
    head_grads = []
    for k in range(3):
        for head in range(HEADS):
            parts = [
                column_sums[j, :, k * LANES + slot * HALF : k * LANES + (slot + 1) * HALF]
                for j in range(count)
                for slot in range(2)
                if used[j, slot] and first_heads[j] + slot == head
            ]
            head_grads.append(functools.reduce(jnp.add, parts))
    projection_grad = jnp.concatenate(head_grads, axis=1)

    gains_grad = spread_sum(jnp.stack([gain_first_part, gain_second_part]))
    local_square = jnp.sum(projection_grad * projection_grad) + jnp.sum(output_grad * output_grad)
    local_square = local_square + jnp.sum(up_grad * up_grad) + jnp.sum(down_grad * down_grad)
    square_total = spread_sum(jnp.broadcast_to(local_square, (LANES,)))[0]
    grad_norm = jnp.sqrt(square_total + jnp.sum(gains_grad * gains_grad))
    factor = jnp.minimum(1.0, CLIP / (grad_norm + 1e-06))
    (
        (projection_moment, projection_square, projection_new),
        (output_moment, output_square, output_new),
        (up_moment, up_square, up_new),
        (down_moment, down_square, down_new),
    ) = adam_all(
        factor,
        [
            (projection, projection_grad, projection_first, projection_second),
            (output_weight, output_grad, output_first, output_second),
            (expert_up, up_grad, up_first, up_second),
            (expert_down, down_grad, down_first, down_second),
        ],
        (RATE_MATRIX, RATE_OUTPUT, RATE_MATRIX, RATE_MATRIX),
        3,
    )
    gains_moment, gains_square, gains_new = adam_update(
        norm_gains, gains_grad, gains_first, gains_second, factor, RATE_GAIN, 0.0
    )
    return (
        block_output,
        input_grad,
        grad_norm,
        projection_grad,
        projection_moment,
        projection_square,
        projection_new,
        output_grad,
        output_moment,
        output_square,
        output_new,
        up_grad,
        up_moment,
        up_square,
        up_new,
        down_grad,
        down_moment,
        down_square,
        down_new,
        gains_grad,
        gains_moment,
        gains_square,
        gains_new,
    )


def solution(mesh):
    token = P("exp", SEQ, None)
    dense = P(ALL, None)
    expert = P("exp", SEQ, None)
    in_specs = (
        (token, token, P("exp", SEQ), token)
        + (dense, dense, expert, expert, P())
        + (dense,) * 4
        + (expert,) * 4
        + (P(), P())
    )
    out_specs = (token, token, P()) + (dense,) * 8 + (expert,) * 8 + (P(),) * 4
    rows, groups = mesh.devices.shape
    fine = Mesh(mesh.devices.reshape(rows // 4, 2, 2, groups), ALL)
    return jax.shard_map(body, mesh=fine, in_specs=in_specs, out_specs=out_specs, check_vma=False)
```

```python
import functools
import math

import jax
import jax.numpy as jnp
import numpy as np
from jax import lax
from jax.experimental import pallas as pl
from jax.experimental.pallas import tpu as pltpu
from jax.sharding import Mesh
from jax.sharding import PartitionSpec as P

HEADS = 12
CAP = 128
STEP = 10


EPSILON = 1e-05
CLIP = 1.0
BETA_ONE = 0.9
BETA_TWO = 0.99
ADAM_FLOOR = 1e-08
DECAY = 0.1
RATE_MATRIX = 0.04
RATE_OUTPUT = 0.1
RATE_GAIN = 0.5

SEQ = ("hi", "lo", "in")
EXP = ("exp",)
ALL = SEQ + EXP
TEAM = ("lo",)
SHARE = ("hi", "in")
LANES = 128
HALF = 64
FAR = -1e30
BF16 = jnp.bfloat16
F32 = jnp.float32
VMEM_LIMIT = 60 * 1024 * 1024


def head_plan(count):
    whole = math.lcm(HEADS, count)
    units, parts = whole // count, whole // HEADS
    first = np.zeros((count,), np.int64)
    active = np.zeros((count, 2, count), np.int32)
    for device in range(count):
        first[device] = min(units * device // parts, HEADS - 2)
        for unit in range(units * device, units * (device + 1)):
            slot = unit // parts - first[device]
            for block in range(count):
                turn = block % (2 * parts)
                if min(turn, 2 * parts - 1 - turn) == unit % parts:
                    active[device, slot, block] = 1
    return first, active


def three_parts(value):
    high = value.astype(BF16).astype(F32)
    middle = (value - high).astype(BF16).astype(F32)
    return high, middle, value - high - middle


def contract(left, right, left_axis, right_axis):
    return lax.dot_general(
        left, right, (((left_axis,), (right_axis,)), ((), ())), preferred_element_type=F32
    )


def attend_kernel(active_ref, qkv_ref, low_ref, full_ref, stat_ref, mixed_ref, *, block, chunk):
    at = pl.program_id(0)
    rows = pl.ds(pl.multiple_of(at * block, block), block)
    lane = lax.broadcasted_iota(jnp.int32, (block, LANES), 1)
    last = lax.div(at * block, chunk)
    for slot in range(2):
        spare = HALF - HALF * slot
        own = (lane < HALF) if slot == 0 else (lane >= HALF)
        columns = slice(slot * LANES, (slot + 1) * LANES)

        @pl.when(active_ref[slot, at] != 0)
        def _():
            query = qkv_ref[rows, columns]

            def step(index, carry, edge):
                top, weighted = carry
                place = pl.ds(pl.multiple_of(index * chunk, chunk), chunk)
                keys = qkv_ref[place, 2 * LANES + slot * LANES : 3 * LANES + slot * LANES]
                values = qkv_ref[place, 4 * LANES + slot * LANES : 5 * LANES + slot * LANES]
                scores = contract(query, keys, 1, 1)
                if edge:
                    key_at = index * chunk + lax.broadcasted_iota(jnp.int32, (block, chunk), 1)
                    query_at = at * block + lax.broadcasted_iota(jnp.int32, (block, chunk), 0)
                    scores = jnp.where(key_at <= query_at, scores, FAR)
                new_top = jnp.maximum(top, jnp.max(scores, axis=1, keepdims=True))
                weights = jnp.exp(scores - new_top).astype(BF16)
                weighted = weighted * jnp.exp(top - new_top) + contract(weights, values, 1, 0)
                return new_top, weighted

            carry = (jnp.full((block, 1), FAR, F32), jnp.zeros((block, LANES), F32))
            carry = lax.fori_loop(0, last, lambda index, state: step(index, state, False), carry)
            top, weighted = step(last, carry, True)
            total = weighted[:, spare : spare + 1]
            mixed_ref[slot] = jnp.where(own, weighted / total, 0.0)
            log_total = top + jnp.log(total)
            high, middle, small = three_parts(log_total)
            extra = jnp.where(lane == spare + 3, -high, 0.0)
            extra = jnp.where(lane == spare + 4, -middle, extra)
            extra = jnp.where(lane == spare + 5, -small, extra)
            stat_ref[:, columns] = (query.astype(F32) + extra).astype(BF16)

        @pl.when(active_ref[slot, at] == 0)
        def _():
            mixed_ref[slot] = jnp.zeros((block, LANES), F32)
            stat_ref[:, columns] = jnp.zeros((block, LANES), BF16)

    mixed = mixed_ref[0] + mixed_ref[1]
    full_ref[...] = mixed
    low_ref[...] = mixed.astype(BF16)


def attend_back_kernel(
    active_ref,
    qkv_ref,
    stat_ref,
    grad_ref,
    mixed_ref,
    out_ref,
    key_sum_ref,
    value_sum_ref,
    query_sum_ref,
    *,
    block,
    chunk,
    scaling,
):
    at = pl.program_id(0)
    rows = pl.ds(pl.multiple_of(at * block, block), block)
    lane = lax.broadcasted_iota(jnp.int32, (block, LANES), 1)
    last = lax.div(at * block, chunk)

    @pl.when(at == 0)
    def _():
        key_sum_ref[...] = jnp.zeros_like(key_sum_ref)
        value_sum_ref[...] = jnp.zeros_like(value_sum_ref)

    for slot in range(2):
        spare = HALF - HALF * slot
        own = (lane < HALF) if slot == 0 else (lane >= HALF)
        columns = slice(slot * LANES, (slot + 1) * LANES)
        query_sum_ref[slot] = jnp.zeros((block, LANES), F32)

        @pl.when(active_ref[slot, at] != 0)
        def _():
            query = stat_ref[:, columns]
            grad = grad_ref[...].astype(F32)
            delta = jnp.sum(jnp.where(own, grad * mixed_ref[...], 0.0), axis=1, keepdims=True)
            high, middle, small = three_parts(delta)
            extra = jnp.where(lane == spare, -high, 0.0)
            extra = jnp.where(lane == spare + 1, -middle, extra)
            extra = jnp.where(lane == spare + 2, -small, extra)
            grad_low = jnp.where(own, grad, extra).astype(BF16)

            def step(index, edge):
                place = pl.ds(pl.multiple_of(index * chunk, chunk), chunk)
                keys = qkv_ref[place, 2 * LANES + slot * LANES : 3 * LANES + slot * LANES]
                values = qkv_ref[place, 4 * LANES + slot * LANES : 5 * LANES + slot * LANES]
                scores = contract(keys, query, 1, 1)
                if edge:
                    key_at = index * chunk + lax.broadcasted_iota(jnp.int32, (chunk, block), 0)
                    query_at = at * block + lax.broadcasted_iota(jnp.int32, (chunk, block), 1)
                    scores = jnp.where(key_at <= query_at, scores, FAR)
                weights = jnp.exp(scores)
                grad_weights = contract(values, grad_low, 1, 1)
                grad_scores = (weights * grad_weights).astype(BF16)
                value_sum_ref[slot, place, :] += contract(weights.astype(BF16), grad_low, 1, 0)
                key_sum_ref[slot, place, :] += contract(grad_scores, query, 1, 0)
                query_sum_ref[slot] += contract(grad_scores, keys, 0, 0)

            @pl.loop(0, last)
            def _(index):
                step(index, False)

            step(last, True)

    first_half = lane < HALF
    query_grad = jnp.where(first_half, query_sum_ref[0], query_sum_ref[1]) * scaling
    out_ref[rows, :LANES] = query_grad.astype(BF16)

    @pl.when(at == pl.num_programs(0) - 1)
    def _():
        @pl.loop(0, pl.num_programs(0))
        def _(index):
            place = pl.ds(pl.multiple_of(index * block, block), block)
            key_grad = jnp.where(first_half, key_sum_ref[0, place, :], key_sum_ref[1, place, :])
            value_grad = jnp.where(
                first_half, value_sum_ref[0, place, :], value_sum_ref[1, place, :]
            )
            out_ref[place, LANES : 2 * LANES] = key_grad.astype(BF16)
            out_ref[place, 2 * LANES :] = value_grad.astype(BF16)


def attend(active, qkv, block):
    length = qkv.shape[0]
    count = length // block
    pairs = length * length * 3 // 4
    return pl.pallas_call(
        functools.partial(attend_kernel, block=block, chunk=2 * block),
        grid_spec=pltpu.PrefetchScalarGridSpec(
            num_scalar_prefetch=1,
            grid=(count,),
            in_specs=[
                pl.BlockSpec(qkv.shape, lambda i, a: (0, 0), pipeline_mode=pl.Buffered(1)),
            ],
            out_specs=[
                pl.BlockSpec((block, LANES), lambda i, a: (i, 0)),
                pl.BlockSpec((block, LANES), lambda i, a: (i, 0)),
                pl.BlockSpec((block, 2 * LANES), lambda i, a: (i, 0)),
            ],
            scratch_shapes=[pltpu.VMEM((2, block, LANES), F32)],
        ),
        out_shape=[
            jax.ShapeDtypeStruct((length, LANES), BF16),
            jax.ShapeDtypeStruct((length, LANES), F32),
            jax.ShapeDtypeStruct((length, 2 * LANES), BF16),
        ],
        compiler_params=pltpu.CompilerParams(vmem_limit_bytes=VMEM_LIMIT),
        cost_estimate=pl.CostEstimate(
            flops=pairs * 4 * LANES, bytes_accessed=length * 2 * 10 * LANES, transcendentals=pairs
        ),
    )(active, qkv)


def attend_back(active, qkv, stat, grad, mixed, block, scaling):
    length = qkv.shape[0]
    count = length // block
    pairs = length * length * 3 // 4
    return pl.pallas_call(
        functools.partial(attend_back_kernel, block=block, chunk=2 * block, scaling=scaling),
        grid_spec=pltpu.PrefetchScalarGridSpec(
            num_scalar_prefetch=1,
            grid=(count,),
            in_specs=[
                pl.BlockSpec(qkv.shape, lambda i, a: (0, 0), pipeline_mode=pl.Buffered(1)),
                pl.BlockSpec((block, 2 * LANES), lambda i, a: (i, 0)),
                pl.BlockSpec((block, LANES), lambda i, a: (i, 0)),
                pl.BlockSpec((block, LANES), lambda i, a: (i, 0)),
            ],
            out_specs=pl.BlockSpec(
                (length, 3 * LANES), lambda i, a: (0, 0), pipeline_mode=pl.Buffered(1)
            ),
            scratch_shapes=[
                pltpu.VMEM((2, length, LANES), F32),
                pltpu.VMEM((2, length, LANES), F32),
                pltpu.VMEM((2, block, LANES), F32),
            ],
        ),
        out_shape=jax.ShapeDtypeStruct((length, 3 * LANES), BF16),
        compiler_params=pltpu.CompilerParams(vmem_limit_bytes=VMEM_LIMIT),
        cost_estimate=pl.CostEstimate(
            flops=pairs * 10 * LANES, bytes_accessed=length * 2 * 15 * LANES, transcendentals=pairs
        ),
    )(active, qkv, stat, grad, mixed)


def adam_update(weight, grad, first, second, factor, rate, decay):
    clipped = grad * factor
    first_new = BETA_ONE * first + (1.0 - BETA_ONE) * clipped
    second_new = BETA_TWO * second + (1.0 - BETA_TWO) * clipped * clipped
    first_hat = first_new / (1.0 - BETA_ONE**STEP)
    second_hat = second_new / (1.0 - BETA_TWO**STEP)
    weight_new = weight - rate * (first_hat / (jnp.sqrt(second_hat) + ADAM_FLOOR) + decay * weight)
    return (first_new, second_new, weight_new)


def after(value, *earlier):
    return lax.optimization_barrier((value, *earlier))[0]


def swap(value, axes):
    return lax.all_to_all(value, axes, split_axis=0, concat_axis=0, tiled=True)


def adam_kernel(factor_ref, *refs, rates):
    count = len(rates)
    factor = factor_ref[0]
    for index, rate in enumerate(rates):
        weight, grad, first, second = [ref[...] for ref in refs[4 * index : 4 * index + 4]]
        outs = refs[4 * count + 3 * index : 4 * count + 3 * index + 3]
        for out, value in zip(
            outs, adam_update(weight, grad, first, second, factor, rate, DECAY), strict=True
        ):
            out[...] = value


def adam_all(factor, leaves, rates, steps):
    flat = [value.reshape(value.shape[-2:]) for leaf in leaves for value in leaf]

    def spec(value):
        rows, columns = value.shape
        if rows % (8 * steps) == 0:
            return pl.BlockSpec((rows // steps, columns), lambda i: (i, 0))
        lanes = columns // steps
        return pl.BlockSpec((rows, lanes), lambda i: (0, i))

    shapes = [jax.ShapeDtypeStruct(value.shape, F32) for value in flat[::4] for _ in range(3)]
    outs = pl.pallas_call(
        functools.partial(adam_kernel, rates=rates),
        grid=(steps,),
        in_specs=[pl.BlockSpec(memory_space=pltpu.SMEM)] + [spec(value) for value in flat],
        out_specs=[spec(shape) for shape in shapes],
        out_shape=shapes,
        compiler_params=pltpu.CompilerParams(vmem_limit_bytes=VMEM_LIMIT),
        cost_estimate=pl.CostEstimate(
            flops=20 * sum(value.size for value in flat[::4]),
            bytes_accessed=28 * sum(value.size for value in flat[::4]),
            transcendentals=0,
        ),
    )(factor.reshape(1), *flat)
    return [
        [out.reshape(leaf[0].shape) for out in outs[3 * index : 3 * index + 3]]
        for index, leaf in enumerate(leaves)
    ]


def others(value, axis):
    size = lax.axis_size(axis)
    return jnp.concatenate(
        [
            lax.ppermute(value, axis, [((i + step) % size, i) for i in range(size)])
            for step in range(1, size)
        ],
        axis=0,
    )


def sum_own(blocks, axis):
    size = lax.axis_size(axis)
    total = blocks[0].astype(F32)
    for step in range(1, size):
        total = total + lax.ppermute(
            blocks[step].astype(BF16), axis, [(i, (i + step) % size) for i in range(size)]
        ).astype(F32)
    return total


def spread_sum(value):
    count = lax.axis_size(ALL)
    return jnp.sum(swap(jnp.broadcast_to(value[None], (count, *value.shape)), ALL), axis=0)


def lane_table(kind):
    table = np.zeros((3, 2, LANES), np.float32)
    for slot in range(2):
        spare = HALF - HALF * slot
        for segment in range(3):
            for other in range(3):
                if kind == "query":
                    table[segment, slot, spare + other] = 0.0 if other == segment else FAR
                elif kind == "key":
                    table[segment, slot, spare + other] = 1.0 if other == segment else 0.0
                    table[segment, slot, spare + 3 + other] = 1.0
                else:
                    table[segment, slot, spare + other] = 1.0
    return table.reshape(3, 2 * LANES)


def body(
    tokens,
    cotangent,
    segment_ids,
    expert_ids,
    projection,
    output_weight,
    expert_up,
    expert_down,
    norm_gains,
    projection_first,
    projection_second,
    output_first,
    output_second,
    up_first,
    up_second,
    down_first,
    down_second,
    gains_first,
    gains_second,
):
    inputs = tokens[0].astype(F32)
    upstream = cotangent[0].astype(F32)
    row_count = inputs.shape[0]
    width = inputs.shape[1]
    head_size = width // HEADS
    scaling = head_size ** (-0.5)
    count = lax.axis_size(SEQ)
    groups = lax.axis_size("exp")
    team = lax.axis_size(TEAM)
    position = lax.axis_index(SEQ)
    length = count * row_count
    weight_rows = projection.shape[0]
    first_heads, active_table = head_plan(count)
    starts = [int(head) * head_size for head in first_heads]
    active = lax.dynamic_index_in_dim(jnp.asarray(active_table), position, 0, keepdims=False)
    gain_first = norm_gains[0]
    gain_second = norm_gains[1]
    used = active_table.any(axis=2)

    scale_first = lax.rsqrt(jnp.mean(inputs * inputs, axis=-1, keepdims=True) + EPSILON)
    normed_first = inputs * scale_first
    attend_in = (normed_first * gain_first).astype(BF16)
    row_in = lax.all_gather(attend_in, SEQ, axis=0, tiled=True)
    projection_low = projection.astype(BF16)
    sent_rows = weight_rows + 8
    own_documents = jnp.zeros((8, 3 * LANES + width), BF16)
    own_documents = own_documents.at[0, :row_count].set(segment_ids[0].astype(BF16))
    output_low = output_weight.astype(BF16)
    pieces = [
        jnp.concatenate(
            [projection_low[:, k * width + s : k * width + s + LANES] for k in range(3)]
            + [output_low],
            axis=1,
        )
        for s in starts
    ]
    got_rows = swap(
        jnp.stack([jnp.concatenate([piece, own_documents], axis=0) for piece in pieces]), SEQ
    )
    segments = got_rows[:, weight_rows, :row_count].reshape(length)

    def all_rows(value, earlier):
        copies = jnp.broadcast_to(after(value, earlier)[None], (groups, *value.shape))
        return jnp.swapaxes(swap(copies, EXP), 0, 1).reshape(width, value.shape[-1])

    columns = all_rows(got_rows[:, :weight_rows, : 3 * LANES], got_rows)
    output_full = all_rows(got_rows[:, :weight_rows, 3 * LANES :], columns)
    columns = columns.reshape(width, 3, 2, head_size)
    blank = jnp.zeros((width, 3, 1, head_size), BF16)
    padded = jnp.stack(
        [
            jnp.concatenate([columns[:, :, :1], blank], axis=2),
            jnp.concatenate([blank, columns[:, :, 1:]], axis=2),
        ],
        axis=2,
    ).reshape(width, 6 * LANES)

    slots = groups * CAP
    chosen = expert_ids[0, :, 0]
    one_hot = (chosen[:, None] == jnp.arange(groups, dtype=jnp.int32)[None, :]).astype(jnp.int32)
    rank = jnp.sum(jnp.cumsum(one_hot, axis=0) * one_hot, axis=1) - 1
    target = chosen * CAP + rank
    placing = (target[:, None] == jnp.arange(slots, dtype=jnp.int32)[None, :]).astype(BF16)

    def dispatch(values, earlier=None):
        outgoing = jnp.einsum("ts,td->sd", placing, values, preferred_element_type=F32)
        outgoing = outgoing.astype(BF16)
        if earlier is not None:
            outgoing = lax.optimization_barrier((outgoing, earlier))[0]
        outgoing = outgoing.reshape(1, groups, CAP, width)
        outgoing = jnp.broadcast_to(outgoing, (team, groups, CAP, width))
        return swap(outgoing.reshape(team * groups, CAP, width), TEAM + EXP).reshape(
            team * slots, width
        )

    def send_back(values):
        return swap(values.reshape(team * groups, CAP, width), TEAM + EXP).reshape(
            team, slots, width
        )

    def collect(returned):
        return jnp.einsum("ts,jsd->td", placing, returned, preferred_element_type=F32)

    grad_arrived = dispatch(cotangent[0], row_in)

    near_units = []
    for matrix in (expert_up, expert_down):
        own_units = matrix[0].astype(BF16)
        near_units.append(jnp.concatenate([own_units, others(own_units, "hi")], axis=0))
    far_units = [others(units, "in") for units in near_units]
    projection_full = lax.all_gather(projection_low, ALL, axis=0, tiled=True)

    tables = [lane_table(kind) for kind in ("query", "key", "value")]
    table = jnp.asarray(np.concatenate(tables, axis=1), BF16)
    documents = segments[:, None]
    extra = jnp.where(documents == 0, table[0], jnp.where(documents == 1, table[1], table[2]))
    scales = np.ones((6 * LANES,), np.float32)
    scales[: 2 * LANES] = scaling
    qkv = jnp.dot(after(row_in, output_full, *near_units), padded, preferred_element_type=F32).astype(BF16)
    qkv = qkv * jnp.asarray(scales, BF16) + extra
    mixed_low, mixed_full, stat = attend(active, qkv, row_count)

    def place_heads():
        index = np.arange(LANES)
        matrix = np.zeros((count, LANES, width), np.float32)
        for device in range(count):
            for slot in range(2):
                if used[device, slot]:
                    own = index[slot * HALF : (slot + 1) * HALF]
                    matrix[device, own, starts[device] + own] = 1.0
        return jnp.asarray(matrix, BF16)

    head_places = place_heads()

    def to_tokens(values):
        return swap(values.reshape(count, row_count, values.shape[1]), SEQ)

    attend_out = jnp.einsum(
        "jtc,jcd->td",
        to_tokens(after(mixed_low, grad_arrived, far_units[0])),
        head_places,
        preferred_element_type=F32,
    ).astype(BF16)
    branch = jnp.dot(attend_out, output_full, preferred_element_type=F32)
    middle = inputs + branch
    scale_second = lax.rsqrt(jnp.mean(middle * middle, axis=-1, keepdims=True) + EPSILON)
    normed_second = middle * scale_second
    expert_in = (normed_second * gain_second).astype(BF16)

    arrived = dispatch(expert_in, far_units[1])
    unit_parts = []
    for up_matrix, down_matrix in (near_units, far_units):
        hidden = jnp.einsum("sd,hd->sh", arrived, up_matrix, preferred_element_type=F32)
        active_units = jax.nn.gelu(hidden).astype(BF16)
        grad_active = jnp.einsum("sd,hd->sh", grad_arrived, down_matrix, preferred_element_type=F32)
        unused, gelu_pull = jax.vjp(jax.nn.gelu, hidden)
        grad_hidden = gelu_pull(grad_active)[0].astype(BF16)
        unit_parts.append((up_matrix, down_matrix, active_units, grad_hidden))
    grad_slots = sum(
        jnp.einsum("sh,hd->sd", grad_hidden, up_matrix, preferred_element_type=F32)
        for up_matrix, down_matrix, active_units, grad_hidden in unit_parts
    )
    returned_grad = send_back(grad_slots.astype(BF16))
    produced = sum(
        jnp.einsum("sh,hd->sd", active_units, down_matrix, preferred_element_type=F32)
        for up_matrix, down_matrix, active_units, grad_hidden in unit_parts
    ).astype(BF16)

    def unit_terms(left, right):
        return jnp.einsum("sh,sd->hd", left, right, preferred_element_type=F32)

    down_far = unit_terms(unit_parts[1][2], grad_arrived).astype(BF16)
    up_far = unit_terms(unit_parts[1][3], arrived).astype(BF16)
    down_near = unit_terms(unit_parts[0][2], grad_arrived)
    up_near = unit_terms(unit_parts[0][3], arrived)
    peers = lax.axis_size("hi")
    grad_expert_in = collect(after(returned_grad, down_far, up_far, produced))

    scaled_second = grad_expert_in * gain_second
    gain_second_part = jnp.sum(grad_expert_in * normed_second, axis=0)
    grad_middle = scale_second * (
        scaled_second
        - normed_second * jnp.mean(scaled_second * normed_second, axis=-1, keepdims=True)
    )
    residual_grad = upstream + grad_middle
    branch_grad = residual_grad.astype(BF16)
    grad_mixed = jnp.einsum(
        "td,ed->te", branch_grad, output_full, preferred_element_type=F32
    ).astype(BF16)

    sent_grad = jnp.stack([grad_mixed[:, s : s + LANES] for s in starts])
    row_grad = swap(sent_grad, SEQ).reshape(length, LANES)
    down_near = sum_own([down_near, down_far], "in")
    expert_part = collect(send_back(after(produced, row_grad)))
    block_output = (middle + expert_part).astype(BF16)[None]

    def group_sum(value, earlier):
        rows = jnp.swapaxes(value.astype(BF16).reshape(count, groups, weight_rows, -1), 0, 1)
        return jnp.sum(swap(after(rows, earlier), EXP).astype(F32), axis=0).astype(BF16)

    output_term = jnp.einsum("tc,te->ce", attend_out, branch_grad, preferred_element_type=F32)
    output_rows = group_sum(output_term, row_grad)
    grad_qkv = attend_back(
        active, qkv, stat, after(row_grad, down_near), mixed_full, row_count, scaling
    )
    up_near = sum_own([up_near, up_far], "in")
    grad_pieces = to_tokens(after(grad_qkv, output_rows, up_near))
    grad_projected = jnp.concatenate(
        [
            jnp.einsum(
                "jtc,jcd->td",
                grad_pieces[:, :, k * LANES : (k + 1) * LANES],
                head_places,
                preferred_element_type=F32,
            ).astype(BF16)
            for k in range(3)
        ],
        axis=1,
    )
    grad_attend_in = jnp.einsum(
        "tc,dc->td", grad_projected, projection_full, preferred_element_type=F32
    )
    scaled_first = grad_attend_in * gain_first
    gain_first_part = jnp.sum(grad_attend_in * normed_first, axis=0)
    input_grad = (
        residual_grad
        + scale_first
        * (
            scaled_first
            - normed_first * jnp.mean(scaled_first * normed_first, axis=-1, keepdims=True)
        )
    )[None]

    column_term = jnp.einsum("tc,te->ce", row_in, grad_qkv, preferred_element_type=F32)
    column_rows = group_sum(column_term, grad_pieces)
    got_terms = swap(jnp.concatenate([column_rows, output_rows], axis=2), SEQ).astype(F32)
    column_sums = got_terms[:, :, : 3 * LANES]
    output_grad = jnp.sum(got_terms[:, :, 3 * LANES :], axis=0)
    head_grads = []
    for k in range(3):
        for head in range(HEADS):
            parts = [
                column_sums[j, :, k * LANES + slot * HALF : k * LANES + (slot + 1) * HALF]
                for j in range(count)
                for slot in range(2)
                if used[j, slot] and first_heads[j] + slot == head
            ]
            head_grads.append(functools.reduce(jnp.add, parts))
    projection_grad = jnp.concatenate(head_grads, axis=1)

    down_grad = sum_own(list(down_near.reshape(peers, -1, width)), "hi")[None]
    up_grad = sum_own(list(up_near.reshape(peers, -1, width)), "hi")[None]
    local_square = jnp.sum(projection_grad * projection_grad) + jnp.sum(output_grad * output_grad)
    local_square = local_square + jnp.sum(up_grad * up_grad) + jnp.sum(down_grad * down_grad)
    summed = spread_sum(
        jnp.concatenate(
            [gain_first_part, gain_second_part, jnp.broadcast_to(local_square, (LANES,))]
        )[None]
    )[0]
    gains_grad = summed[: 2 * width].reshape(2, width)
    grad_norm = jnp.sqrt(summed[2 * width] + jnp.sum(gains_grad * gains_grad))
    factor = jnp.minimum(1.0, CLIP / (grad_norm + 1e-06))
    (
        (projection_moment, projection_square, projection_new),
        (output_moment, output_square, output_new),
        (up_moment, up_square, up_new),
        (down_moment, down_square, down_new),
    ) = adam_all(
        factor,
        [
            (projection, projection_grad, projection_first, projection_second),
            (output_weight, output_grad, output_first, output_second),
            (expert_up, up_grad, up_first, up_second),
            (expert_down, down_grad, down_first, down_second),
        ],
        (RATE_MATRIX, RATE_OUTPUT, RATE_MATRIX, RATE_MATRIX),
        3,
    )
    gains_moment, gains_square, gains_new = adam_update(
        norm_gains, gains_grad, gains_first, gains_second, factor, RATE_GAIN, 0.0
    )
    return (
        block_output,
        input_grad,
        grad_norm,
        projection_grad,
        projection_moment,
        projection_square,
        projection_new,
        output_grad,
        output_moment,
        output_square,
        output_new,
        up_grad,
        up_moment,
        up_square,
        up_new,
        down_grad,
        down_moment,
        down_square,
        down_new,
        gains_grad,
        gains_moment,
        gains_square,
        gains_new,
    )


def solution(mesh):
    token = P("exp", SEQ, None)
    dense = P(ALL, None)
    expert = P("exp", SEQ, None)
    in_specs = (
        (token, token, P("exp", SEQ), token)
        + (dense, dense, expert, expert, P())
        + (dense,) * 4
        + (expert,) * 4
        + (P(), P())
    )
    out_specs = (token, token, P()) + (dense,) * 8 + (expert,) * 8 + (P(),) * 4
    rows, groups = mesh.devices.shape
    fine = Mesh(mesh.devices.reshape(rows // 4, 2, 2, groups), ALL)
    return jax.shard_map(body, mesh=fine, in_specs=in_specs, out_specs=out_specs, check_vma=False)
```

```python
import functools
import math

import jax
import jax.numpy as jnp
import numpy as np
from jax import lax
from jax.experimental import pallas as pl
from jax.experimental.pallas import tpu as pltpu
from jax.sharding import Mesh
from jax.sharding import PartitionSpec as P

HEADS = 12
CAP = 128
STEP = 10


EPSILON = 1e-05
CLIP = 1.0
BETA_ONE = 0.9
BETA_TWO = 0.99
ADAM_FLOOR = 1e-08
DECAY = 0.1
RATE_MATRIX = 0.04
RATE_OUTPUT = 0.1
RATE_GAIN = 0.5

SEQ = ("hi", "lo", "in")
EXP = ("exp",)
ALL = SEQ + EXP
TEAM = ("lo",)
SHARE = ("hi", "in")
LANES = 128
HALF = 64
FAR = -1e30
BF16 = jnp.bfloat16
F32 = jnp.float32
VMEM_LIMIT = 60 * 1024 * 1024


def head_plan(count):
    whole = math.lcm(HEADS, count)
    units, parts = whole // count, whole // HEADS
    first = np.zeros((count,), np.int64)
    active = np.zeros((count, 2, count), np.int32)
    for device in range(count):
        first[device] = min(units * device // parts, HEADS - 2)
        for unit in range(units * device, units * (device + 1)):
            slot = unit // parts - first[device]
            for block in range(count):
                turn = block % (2 * parts)
                if min(turn, 2 * parts - 1 - turn) == unit % parts:
                    active[device, slot, block] = 1
    return first, active


def three_parts(value):
    high = value.astype(BF16).astype(F32)
    middle = (value - high).astype(BF16).astype(F32)
    return high, middle, value - high - middle


def contract(left, right, left_axis, right_axis):
    return lax.dot_general(
        left, right, (((left_axis,), (right_axis,)), ((), ())), preferred_element_type=F32
    )


def slot_arrays(packed, documents, kind, slot):
    spare = HALF - HALF * slot
    lane = lax.broadcasted_iota(jnp.int32, packed.shape, 1)
    own = (lane < HALF) if slot == 0 else (lane >= HALF)
    place = (lane - spare).astype(F32)
    ours = place == documents
    first = (lane >= spare) & (lane < spare + 3)
    if kind == "query":
        extra = jnp.where(first & jnp.logical_not(ours), FAR, 0.0)
    elif kind == "key":
        extra = jnp.where(ours | ((lane >= spare + 3) & (lane < spare + 6)), 1.0, 0.0)
    else:
        extra = jnp.where(first, 1.0, 0.0)
    return jnp.where(own, packed, extra).astype(BF16)


def fill_slots(qkv_ref, documents_ref, wide_ref, kinds, block):
    @pl.loop(0, pl.num_programs(0))
    def _(index):
        place = pl.ds(pl.multiple_of(index * block, block), block)
        documents = documents_ref[place, :].astype(F32)
        for number, kind in enumerate(kinds):
            source = ("query", "key", "value").index(kind)
            packed = qkv_ref[place, source * LANES : (source + 1) * LANES].astype(F32)
            if kind == "query":
                packed = packed * 0.125
            for slot in range(2):
                column = (2 * number + slot) * LANES
                wide_ref[place, column : column + LANES] = slot_arrays(
                    packed, documents, kind, slot
                )


def attend_kernel(
    active_ref, qkv_ref, documents_ref, low_ref, full_ref, stat_ref, mixed_ref, wide_ref, *, block, chunk
):
    at = pl.program_id(0)

    @pl.when(at == 0)
    def _():
        fill_slots(qkv_ref, documents_ref, wide_ref, ("query", "key", "value"), block)

    rows = pl.ds(pl.multiple_of(at * block, block), block)
    lane = lax.broadcasted_iota(jnp.int32, (block, LANES), 1)
    last = lax.div(at * block, chunk)
    for slot in range(2):
        spare = HALF - HALF * slot
        own = (lane < HALF) if slot == 0 else (lane >= HALF)
        columns = slice(slot * LANES, (slot + 1) * LANES)

        @pl.when(active_ref[slot, at] != 0)
        def _():
            query = wide_ref[rows, columns]

            def step(index, carry, edge):
                top, weighted = carry
                place = pl.ds(pl.multiple_of(index * chunk, chunk), chunk)
                keys = wide_ref[place, 2 * LANES + slot * LANES : 3 * LANES + slot * LANES]
                values = wide_ref[place, 4 * LANES + slot * LANES : 5 * LANES + slot * LANES]
                scores = contract(query, keys, 1, 1)
                if edge:
                    key_at = index * chunk + lax.broadcasted_iota(jnp.int32, (block, chunk), 1)
                    query_at = at * block + lax.broadcasted_iota(jnp.int32, (block, chunk), 0)
                    scores = jnp.where(key_at <= query_at, scores, FAR)
                new_top = jnp.maximum(top, jnp.max(scores, axis=1, keepdims=True))
                weights = jnp.exp(scores - new_top).astype(BF16)
                weighted = weighted * jnp.exp(top - new_top) + contract(weights, values, 1, 0)
                return new_top, weighted

            carry = (jnp.full((block, 1), FAR, F32), jnp.zeros((block, LANES), F32))
            carry = lax.fori_loop(0, last, lambda index, state: step(index, state, False), carry)
            top, weighted = step(last, carry, True)
            total = weighted[:, spare : spare + 1]
            mixed_ref[slot] = jnp.where(own, weighted / total, 0.0)
            log_total = top + jnp.log(total)
            high, middle, small = three_parts(log_total)
            extra = jnp.where(lane == spare + 3, -high, 0.0)
            extra = jnp.where(lane == spare + 4, -middle, extra)
            extra = jnp.where(lane == spare + 5, -small, extra)
            stat_ref[:, columns] = (query.astype(F32) + extra).astype(BF16)

        @pl.when(active_ref[slot, at] == 0)
        def _():
            mixed_ref[slot] = jnp.zeros((block, LANES), F32)
            stat_ref[:, columns] = jnp.zeros((block, LANES), BF16)

    mixed = mixed_ref[0] + mixed_ref[1]
    full_ref[...] = mixed
    low_ref[...] = mixed.astype(BF16)


def attend_back_kernel(
    active_ref,
    qkv_ref,
    documents_ref,
    stat_ref,
    grad_ref,
    mixed_ref,
    out_ref,
    key_sum_ref,
    value_sum_ref,
    query_sum_ref,
    wide_ref,
    *,
    block,
    chunk,
    scaling,
):
    at = pl.program_id(0)
    rows = pl.ds(pl.multiple_of(at * block, block), block)
    lane = lax.broadcasted_iota(jnp.int32, (block, LANES), 1)
    last = lax.div(at * block, chunk)

    @pl.when(at == 0)
    def _():
        fill_slots(qkv_ref, documents_ref, wide_ref, ("key", "value"), block)
        key_sum_ref[...] = jnp.zeros_like(key_sum_ref)
        value_sum_ref[...] = jnp.zeros_like(value_sum_ref)

    for slot in range(2):
        spare = HALF - HALF * slot
        own = (lane < HALF) if slot == 0 else (lane >= HALF)
        columns = slice(slot * LANES, (slot + 1) * LANES)
        query_sum_ref[slot] = jnp.zeros((block, LANES), F32)

        @pl.when(active_ref[slot, at] != 0)
        def _():
            query = stat_ref[:, columns]
            grad = grad_ref[...].astype(F32)
            delta = jnp.sum(jnp.where(own, grad * mixed_ref[...], 0.0), axis=1, keepdims=True)
            high, middle, small = three_parts(delta)
            extra = jnp.where(lane == spare, -high, 0.0)
            extra = jnp.where(lane == spare + 1, -middle, extra)
            extra = jnp.where(lane == spare + 2, -small, extra)
            grad_low = jnp.where(own, grad, extra).astype(BF16)

            def step(index, edge):
                place = pl.ds(pl.multiple_of(index * chunk, chunk), chunk)
                keys = wide_ref[place, slot * LANES : (slot + 1) * LANES]
                values = wide_ref[place, (2 + slot) * LANES : (3 + slot) * LANES]
                scores = contract(keys, query, 1, 1)
                if edge:
                    key_at = index * chunk + lax.broadcasted_iota(jnp.int32, (chunk, block), 0)
                    query_at = at * block + lax.broadcasted_iota(jnp.int32, (chunk, block), 1)
                    scores = jnp.where(key_at <= query_at, scores, FAR)
                weights = jnp.exp(scores)
                grad_weights = contract(values, grad_low, 1, 1)
                grad_scores = (weights * grad_weights).astype(BF16)
                value_sum_ref[slot, place, :] += contract(weights.astype(BF16), grad_low, 1, 0)
                key_sum_ref[slot, place, :] += contract(grad_scores, query, 1, 0)
                query_sum_ref[slot] += contract(grad_scores, keys, 0, 0)

            @pl.loop(0, last)
            def _(index):
                step(index, False)

            step(last, True)

    first_half = lane < HALF
    query_grad = jnp.where(first_half, query_sum_ref[0], query_sum_ref[1]) * scaling
    out_ref[rows, :LANES] = query_grad.astype(BF16)

    @pl.when(at == pl.num_programs(0) - 1)
    def _():
        @pl.loop(0, pl.num_programs(0))
        def _(index):
            place = pl.ds(pl.multiple_of(index * block, block), block)
            key_grad = jnp.where(first_half, key_sum_ref[0, place, :], key_sum_ref[1, place, :])
            value_grad = jnp.where(
                first_half, value_sum_ref[0, place, :], value_sum_ref[1, place, :]
            )
            out_ref[place, LANES : 2 * LANES] = key_grad.astype(BF16)
            out_ref[place, 2 * LANES :] = value_grad.astype(BF16)


def attend(active, qkv, documents, block):
    length = qkv.shape[0]
    count = length // block
    pairs = length * length * 3 // 4
    return pl.pallas_call(
        functools.partial(attend_kernel, block=block, chunk=2 * block),
        grid_spec=pltpu.PrefetchScalarGridSpec(
            num_scalar_prefetch=1,
            grid=(count,),
            in_specs=[
                pl.BlockSpec(qkv.shape, lambda i, a: (0, 0), pipeline_mode=pl.Buffered(1)),
                pl.BlockSpec(documents.shape, lambda i, a: (0, 0), pipeline_mode=pl.Buffered(1)),
            ],
            out_specs=[
                pl.BlockSpec((block, LANES), lambda i, a: (i, 0)),
                pl.BlockSpec((block, LANES), lambda i, a: (i, 0)),
                pl.BlockSpec((block, 2 * LANES), lambda i, a: (i, 0)),
            ],
            scratch_shapes=[
                pltpu.VMEM((2, block, LANES), F32),
                pltpu.VMEM((length, 6 * LANES), BF16),
            ],
        ),
        out_shape=[
            jax.ShapeDtypeStruct((length, LANES), BF16),
            jax.ShapeDtypeStruct((length, LANES), F32),
            jax.ShapeDtypeStruct((length, 2 * LANES), BF16),
        ],
        compiler_params=pltpu.CompilerParams(vmem_limit_bytes=VMEM_LIMIT),
        cost_estimate=pl.CostEstimate(
            flops=pairs * 4 * LANES, bytes_accessed=length * 2 * 10 * LANES, transcendentals=pairs
        ),
    )(active, qkv, documents)


def attend_back(active, qkv, documents, stat, grad, mixed, block, scaling):
    length = qkv.shape[0]
    count = length // block
    pairs = length * length * 3 // 4
    return pl.pallas_call(
        functools.partial(attend_back_kernel, block=block, chunk=2 * block, scaling=scaling),
        grid_spec=pltpu.PrefetchScalarGridSpec(
            num_scalar_prefetch=1,
            grid=(count,),
            in_specs=[
                pl.BlockSpec(qkv.shape, lambda i, a: (0, 0), pipeline_mode=pl.Buffered(1)),
                pl.BlockSpec(documents.shape, lambda i, a: (0, 0), pipeline_mode=pl.Buffered(1)),
                pl.BlockSpec((block, 2 * LANES), lambda i, a: (i, 0)),
                pl.BlockSpec((block, LANES), lambda i, a: (i, 0)),
                pl.BlockSpec((block, LANES), lambda i, a: (i, 0)),
            ],
            out_specs=pl.BlockSpec(
                (length, 3 * LANES), lambda i, a: (0, 0), pipeline_mode=pl.Buffered(1)
            ),
            scratch_shapes=[
                pltpu.VMEM((2, length, LANES), F32),
                pltpu.VMEM((2, length, LANES), F32),
                pltpu.VMEM((2, block, LANES), F32),
                pltpu.VMEM((length, 4 * LANES), BF16),
            ],
        ),
        out_shape=jax.ShapeDtypeStruct((length, 3 * LANES), BF16),
        compiler_params=pltpu.CompilerParams(vmem_limit_bytes=VMEM_LIMIT),
        cost_estimate=pl.CostEstimate(
            flops=pairs * 10 * LANES, bytes_accessed=length * 2 * 15 * LANES, transcendentals=pairs
        ),
    )(active, qkv, documents, stat, grad, mixed)


def adam_update(weight, grad, first, second, factor, rate, decay):
    clipped = grad * factor
    first_new = BETA_ONE * first + (1.0 - BETA_ONE) * clipped
    second_new = BETA_TWO * second + (1.0 - BETA_TWO) * clipped * clipped
    first_hat = first_new / (1.0 - BETA_ONE**STEP)
    second_hat = second_new / (1.0 - BETA_TWO**STEP)
    weight_new = weight - rate * (first_hat / (jnp.sqrt(second_hat) + ADAM_FLOOR) + decay * weight)
    return (first_new, second_new, weight_new)


def after(value, *earlier):
    return lax.optimization_barrier((value, *earlier))[0]


def swap(value, axes):
    return lax.all_to_all(value, axes, split_axis=0, concat_axis=0, tiled=True)


def adam_kernel(factor_ref, *refs, rates):
    count = len(rates)
    factor = factor_ref[0]
    for index, rate in enumerate(rates):
        weight, grad, first, second = [ref[...] for ref in refs[4 * index : 4 * index + 4]]
        outs = refs[4 * count + 3 * index : 4 * count + 3 * index + 3]
        for out, value in zip(
            outs, adam_update(weight, grad, first, second, factor, rate, DECAY), strict=True
        ):
            out[...] = value


def adam_all(factor, leaves, rates, steps):
    flat = [value.reshape(value.shape[-2:]) for leaf in leaves for value in leaf]

    def spec(value):
        rows, columns = value.shape
        if rows % (8 * steps) == 0:
            return pl.BlockSpec((rows // steps, columns), lambda i: (i, 0))
        lanes = columns // steps
        return pl.BlockSpec((rows, lanes), lambda i: (0, i))

    shapes = [jax.ShapeDtypeStruct(value.shape, F32) for value in flat[::4] for _ in range(3)]
    outs = pl.pallas_call(
        functools.partial(adam_kernel, rates=rates),
        grid=(steps,),
        in_specs=[pl.BlockSpec(memory_space=pltpu.SMEM)] + [spec(value) for value in flat],
        out_specs=[spec(shape) for shape in shapes],
        out_shape=shapes,
        compiler_params=pltpu.CompilerParams(vmem_limit_bytes=VMEM_LIMIT),
        cost_estimate=pl.CostEstimate(
            flops=20 * sum(value.size for value in flat[::4]),
            bytes_accessed=28 * sum(value.size for value in flat[::4]),
            transcendentals=0,
        ),
    )(factor.reshape(1), *flat)
    return [
        [out.reshape(leaf[0].shape) for out in outs[3 * index : 3 * index + 3]]
        for index, leaf in enumerate(leaves)
    ]


def others(value, axis):
    size = lax.axis_size(axis)
    return jnp.concatenate(
        [
            lax.ppermute(value, axis, [((i + step) % size, i) for i in range(size)])
            for step in range(1, size)
        ],
        axis=0,
    )


def sum_own(blocks, axis):
    size = lax.axis_size(axis)
    total = blocks[0].astype(F32)
    for step in range(1, size):
        total = total + lax.ppermute(
            blocks[step].astype(BF16), axis, [(i, (i + step) % size) for i in range(size)]
        ).astype(F32)
    return total


def spread_sum(value):
    count = lax.axis_size(ALL)
    return jnp.sum(swap(jnp.broadcast_to(value[None], (count, *value.shape)), ALL), axis=0)


def body(
    tokens,
    cotangent,
    segment_ids,
    expert_ids,
    projection,
    output_weight,
    expert_up,
    expert_down,
    norm_gains,
    projection_first,
    projection_second,
    output_first,
    output_second,
    up_first,
    up_second,
    down_first,
    down_second,
    gains_first,
    gains_second,
):
    inputs = tokens[0].astype(F32)
    upstream = cotangent[0].astype(F32)
    row_count = inputs.shape[0]
    width = inputs.shape[1]
    head_size = width // HEADS
    scaling = head_size ** (-0.5)
    count = lax.axis_size(SEQ)
    groups = lax.axis_size("exp")
    team = lax.axis_size(TEAM)
    position = lax.axis_index(SEQ)
    length = count * row_count
    weight_rows = projection.shape[0]
    first_heads, active_table = head_plan(count)
    starts = [int(head) * head_size for head in first_heads]
    active = lax.dynamic_index_in_dim(jnp.asarray(active_table), position, 0, keepdims=False)
    gain_first = norm_gains[0]
    gain_second = norm_gains[1]
    used = active_table.any(axis=2)

    scale_first = lax.rsqrt(jnp.mean(inputs * inputs, axis=-1, keepdims=True) + EPSILON)
    normed_first = inputs * scale_first
    attend_in = (normed_first * gain_first).astype(BF16)
    row_in = lax.all_gather(attend_in, SEQ, axis=0, tiled=True)
    projection_low = projection.astype(BF16)
    sent_rows = weight_rows + 8
    own_documents = jnp.zeros((8, 3 * LANES + width), BF16)
    own_documents = own_documents.at[0, :row_count].set(segment_ids[0].astype(BF16))
    output_low = output_weight.astype(BF16)
    pieces = [
        jnp.concatenate(
            [projection_low[:, k * width + s : k * width + s + LANES] for k in range(3)]
            + [output_low],
            axis=1,
        )
        for s in starts
    ]
    got_rows = swap(
        jnp.stack([jnp.concatenate([piece, own_documents], axis=0) for piece in pieces]), SEQ
    )
    documents = jnp.broadcast_to(
        got_rows[:, weight_rows, :row_count].reshape(length, 1), (length, LANES)
    )

    def all_rows(value, earlier):
        copies = jnp.broadcast_to(after(value, earlier)[None], (groups, *value.shape))
        return jnp.swapaxes(swap(copies, EXP), 0, 1).reshape(width, value.shape[-1])

    columns = all_rows(got_rows[:, :weight_rows, : 3 * LANES], got_rows)
    output_full = all_rows(got_rows[:, :weight_rows, 3 * LANES :], columns)
    slots = groups * CAP
    chosen = expert_ids[0, :, 0]
    one_hot = (chosen[:, None] == jnp.arange(groups, dtype=jnp.int32)[None, :]).astype(jnp.int32)
    rank = jnp.sum(jnp.cumsum(one_hot, axis=0) * one_hot, axis=1) - 1
    target = chosen * CAP + rank
    placing = (target[:, None] == jnp.arange(slots, dtype=jnp.int32)[None, :]).astype(BF16)

    def dispatch(values, *earlier):
        outgoing = jnp.einsum("ts,td->sd", placing, values, preferred_element_type=F32)
        outgoing = after(outgoing.astype(BF16), *earlier).reshape(1, groups, CAP, width)
        outgoing = jnp.broadcast_to(outgoing, (team, groups, CAP, width))
        return swap(outgoing.reshape(team * groups, CAP, width), TEAM + EXP).reshape(
            team * slots, width
        )

    def send_back(values):
        return swap(values.reshape(team * groups, CAP, width), TEAM + EXP).reshape(
            team, slots, width
        )

    def collect(returned):
        return jnp.einsum("ts,jsd->td", placing, returned, preferred_element_type=F32)

    grad_arrived = dispatch(cotangent[0], row_in, output_full)

    def gather_near(matrix, earlier):
        own_units = matrix[0].astype(BF16)
        return jnp.concatenate([own_units, others(after(own_units, earlier), "hi")], axis=0)

    near_up = gather_near(expert_up, row_in)
    projection_full = lax.all_gather(projection_low, ALL, axis=0, tiled=True)

    qkv = jnp.dot(row_in, columns, preferred_element_type=F32).astype(BF16)
    mixed_low, mixed_full, stat = attend(active, qkv, documents, row_count)
    near_down = gather_near(expert_down, mixed_low)

    def place_heads():
        index = np.arange(LANES)
        matrix = np.zeros((count, LANES, width), np.float32)
        for device in range(count):
            for slot in range(2):
                if used[device, slot]:
                    own = index[slot * HALF : (slot + 1) * HALF]
                    matrix[device, own, starts[device] + own] = 1.0
        return jnp.asarray(matrix, BF16)

    head_places = place_heads()

    def to_tokens(values):
        return swap(values.reshape(count, row_count, values.shape[1]), SEQ)

    attend_out = jnp.einsum(
        "jtc,jcd->td",
        to_tokens(after(mixed_low, grad_arrived, near_up)),
        head_places,
        preferred_element_type=F32,
    ).astype(BF16)
    branch = jnp.dot(attend_out, output_full, preferred_element_type=F32)
    middle = inputs + branch
    scale_second = lax.rsqrt(jnp.mean(middle * middle, axis=-1, keepdims=True) + EPSILON)
    normed_second = middle * scale_second
    expert_in = (normed_second * gain_second).astype(BF16)

    arrived = dispatch(expert_in, near_down)
    far_up, far_down = others(near_up, "in"), others(near_down, "in")
    unit_parts = []
    for up_matrix, down_matrix in ((near_up, near_down), (far_up, far_down)):
        hidden = jnp.einsum("sd,hd->sh", arrived, up_matrix, preferred_element_type=F32)
        active_units = jax.nn.gelu(hidden).astype(BF16)
        grad_active = jnp.einsum("sd,hd->sh", grad_arrived, down_matrix, preferred_element_type=F32)
        unused, gelu_pull = jax.vjp(jax.nn.gelu, hidden)
        grad_hidden = gelu_pull(grad_active)[0].astype(BF16)
        unit_parts.append((up_matrix, down_matrix, active_units, grad_hidden))
    grad_slots = sum(
        jnp.einsum("sh,hd->sd", grad_hidden, up_matrix, preferred_element_type=F32)
        for up_matrix, down_matrix, active_units, grad_hidden in unit_parts
    )
    returned_grad = send_back(grad_slots.astype(BF16))
    produced = sum(
        jnp.einsum("sh,hd->sd", active_units, down_matrix, preferred_element_type=F32)
        for up_matrix, down_matrix, active_units, grad_hidden in unit_parts
    ).astype(BF16)

    def unit_terms(left, right):
        return jnp.einsum("sh,sd->hd", left, right, preferred_element_type=F32)

    down_far = unit_terms(unit_parts[1][2], grad_arrived).astype(BF16)
    up_far = unit_terms(unit_parts[1][3], arrived).astype(BF16)
    down_near = unit_terms(unit_parts[0][2], grad_arrived)
    up_near = unit_terms(unit_parts[0][3], arrived)
    peers = lax.axis_size("hi")
    grad_expert_in = collect(after(returned_grad, down_far, up_far, produced))

    scaled_second = grad_expert_in * gain_second
    gain_second_part = jnp.sum(grad_expert_in * normed_second, axis=0)
    grad_middle = scale_second * (
        scaled_second
        - normed_second * jnp.mean(scaled_second * normed_second, axis=-1, keepdims=True)
    )
    residual_grad = upstream + grad_middle
    branch_grad = residual_grad.astype(BF16)
    grad_mixed = jnp.einsum(
        "td,ed->te", branch_grad, output_full, preferred_element_type=F32
    ).astype(BF16)

    down_near = sum_own([down_near, down_far], "in")
    down_parts = list(down_near.astype(BF16).reshape(peers, -1, width))
    sent_grad = jnp.stack([grad_mixed[:, s : s + LANES] for s in starts])
    row_grad = swap(after(sent_grad, down_near), SEQ).reshape(length, LANES)
    up_near = sum_own([up_near, up_far], "in")
    expert_part = collect(send_back(after(produced, row_grad)))
    block_output = (middle + expert_part).astype(BF16)[None]

    def group_rows(value):
        return jnp.swapaxes(value.astype(BF16).reshape(count, groups, weight_rows, -1), 0, 1)

    output_term = jnp.einsum("tc,te->ce", attend_out, branch_grad, preferred_element_type=F32)
    output_parts = group_rows(output_term)
    group = lax.axis_index(EXP)
    output_rows = sum_own(
        [
            lax.dynamic_index_in_dim(
                output_parts, lax.rem(group + step, groups), 0, keepdims=False
            )
            for step in range(groups)
        ],
        "exp",
    ).astype(BF16)
    grad_qkv = attend_back(
        active,
        qkv,
        documents,
        stat,
        after(row_grad, up_near),
        mixed_full,
        row_count,
        scaling,
    )
    down_grad = sum_own([down_near[: down_near.shape[0] // peers]] + down_parts[1:], "hi")[None]
    grad_pieces = to_tokens(after(grad_qkv, output_rows, down_grad))
    grad_projected = jnp.concatenate(
        [
            jnp.einsum(
                "jtc,jcd->td",
                grad_pieces[:, :, k * LANES : (k + 1) * LANES],
                head_places,
                preferred_element_type=F32,
            ).astype(BF16)
            for k in range(3)
        ],
        axis=1,
    )
    grad_attend_in = jnp.einsum(
        "tc,dc->td", grad_projected, projection_full, preferred_element_type=F32
    )
    scaled_first = grad_attend_in * gain_first
    gain_first_part = jnp.sum(grad_attend_in * normed_first, axis=0)
    input_grad = (
        residual_grad
        + scale_first
        * (
            scaled_first
            - normed_first * jnp.mean(scaled_first * normed_first, axis=-1, keepdims=True)
        )
    )[None]

    column_term = jnp.einsum("tc,te->ce", row_in, grad_qkv, preferred_element_type=F32)
    column_rows = swap(after(group_rows(column_term), grad_pieces), EXP).astype(F32)
    column_rows = jnp.sum(column_rows, axis=0).astype(BF16)
    got_terms = swap(jnp.concatenate([column_rows, output_rows], axis=2), SEQ).astype(F32)
    column_sums = got_terms[:, :, : 3 * LANES]
    output_grad = jnp.sum(got_terms[:, :, 3 * LANES :], axis=0)
    head_grads = []
    for k in range(3):
        for head in range(HEADS):
            parts = [
                column_sums[j, :, k * LANES + slot * HALF : k * LANES + (slot + 1) * HALF]
                for j in range(count)
                for slot in range(2)
                if used[j, slot] and first_heads[j] + slot == head
            ]
            head_grads.append(functools.reduce(jnp.add, parts))
    projection_grad = jnp.concatenate(head_grads, axis=1)

    up_grad = sum_own(list(up_near.reshape(peers, -1, width)), "hi")[None]
    local_square = jnp.sum(projection_grad * projection_grad) + jnp.sum(output_grad * output_grad)
    local_square = local_square + jnp.sum(up_grad * up_grad) + jnp.sum(down_grad * down_grad)
    summed = spread_sum(
        jnp.concatenate(
            [gain_first_part, gain_second_part, jnp.broadcast_to(local_square, (LANES,))]
        )[None]
    )[0]
    gains_grad = summed[: 2 * width].reshape(2, width)
    grad_norm = jnp.sqrt(summed[2 * width] + jnp.sum(gains_grad * gains_grad))
    factor = jnp.minimum(1.0, CLIP / (grad_norm + 1e-06))
    (
        (projection_moment, projection_square, projection_new),
        (output_moment, output_square, output_new),
        (up_moment, up_square, up_new),
        (down_moment, down_square, down_new),
    ) = adam_all(
        factor,
        [
            (projection, projection_grad, projection_first, projection_second),
            (output_weight, output_grad, output_first, output_second),
            (expert_up, up_grad, up_first, up_second),
            (expert_down, down_grad, down_first, down_second),
        ],
        (RATE_MATRIX, RATE_OUTPUT, RATE_MATRIX, RATE_MATRIX),
        3,
    )
    gains_moment, gains_square, gains_new = adam_update(
        norm_gains, gains_grad, gains_first, gains_second, factor, RATE_GAIN, 0.0
    )
    return (
        block_output,
        input_grad,
        grad_norm,
        projection_grad,
        projection_moment,
        projection_square,
        projection_new,
        output_grad,
        output_moment,
        output_square,
        output_new,
        up_grad,
        up_moment,
        up_square,
        up_new,
        down_grad,
        down_moment,
        down_square,
        down_new,
        gains_grad,
        gains_moment,
        gains_square,
        gains_new,
    )


def solution(mesh):
    token = P("exp", SEQ, None)
    dense = P(ALL, None)
    expert = P("exp", SEQ, None)
    in_specs = (
        (token, token, P("exp", SEQ), token)
        + (dense, dense, expert, expert, P())
        + (dense,) * 4
        + (expert,) * 4
        + (P(), P())
    )
    out_specs = (token, token, P()) + (dense,) * 8 + (expert,) * 8 + (P(),) * 4
    rows, groups = mesh.devices.shape
    fine = Mesh(mesh.devices.reshape(rows // 4, 2, 2, groups), ALL)
    return jax.shard_map(body, mesh=fine, in_specs=in_specs, out_specs=out_specs, check_vma=False)
```

```python
import functools
import math

import jax
import jax.numpy as jnp
import numpy as np
from jax import lax
from jax.experimental import pallas as pl
from jax.experimental.pallas import tpu as pltpu
from jax.sharding import Mesh
from jax.sharding import PartitionSpec as P

HEADS = 12
CAP = 128
STEP = 10


EPSILON = 1e-05
CLIP = 1.0
BETA_ONE = 0.9
BETA_TWO = 0.99
ADAM_FLOOR = 1e-08
DECAY = 0.1
RATE_MATRIX = 0.04
RATE_OUTPUT = 0.1
RATE_GAIN = 0.5

SEQ = ("hi", "lo", "in")
EXP = ("exp",)
ALL = SEQ + EXP
TEAM = ("lo",)
SHARE = ("hi", "in")
LANES = 128
HALF = 64
FAR = -1e30
BF16 = jnp.bfloat16
F32 = jnp.float32
VMEM_LIMIT = 60 * 1024 * 1024


def head_plan(count):
    whole = math.lcm(HEADS, count)
    units, parts = whole // count, whole // HEADS
    first = np.zeros((count,), np.int64)
    active = np.zeros((count, 2, count), np.int32)
    for device in range(count):
        first[device] = min(units * device // parts, HEADS - 2)
        for unit in range(units * device, units * (device + 1)):
            slot = unit // parts - first[device]
            for block in range(count):
                turn = block % (2 * parts)
                if min(turn, 2 * parts - 1 - turn) == unit % parts:
                    active[device, slot, block] = 1
    return first, active


def three_parts(value):
    high = value.astype(BF16).astype(F32)
    middle = (value - high).astype(BF16).astype(F32)
    return high, middle, value - high - middle


def contract(left, right, left_axis, right_axis):
    return lax.dot_general(
        left, right, (((left_axis,), (right_axis,)), ((), ())), preferred_element_type=F32
    )


def slot_arrays(packed, documents, kind, slot):
    spare = HALF - HALF * slot
    lane = lax.broadcasted_iota(jnp.int32, packed.shape, 1)
    own = (lane < HALF) if slot == 0 else (lane >= HALF)
    place = (lane - spare).astype(F32)
    ours = place == documents
    first = (lane >= spare) & (lane < spare + 3)
    if kind == "query":
        extra = jnp.where(first & jnp.logical_not(ours), FAR, 0.0)
    elif kind == "key":
        extra = jnp.where(ours | ((lane >= spare + 3) & (lane < spare + 6)), 1.0, 0.0)
    else:
        extra = jnp.where(first, 1.0, 0.0)
    return jnp.where(own, packed, extra).astype(BF16)


def fill_slots(qkv_ref, documents_ref, wide_ref, kinds, block):
    @pl.loop(0, pl.num_programs(0))
    def _(index):
        place = pl.ds(pl.multiple_of(index * block, block), block)
        documents = documents_ref[place, :].astype(F32)
        for number, kind in enumerate(kinds):
            source = ("query", "key", "value").index(kind)
            packed = qkv_ref[place, source * LANES : (source + 1) * LANES].astype(F32)
            if kind == "query":
                packed = packed * 0.125
            for slot in range(2):
                column = (2 * number + slot) * LANES
                wide_ref[place, column : column + LANES] = slot_arrays(
                    packed, documents, kind, slot
                )


def attend_kernel(
    active_ref, qkv_ref, documents_ref, low_ref, full_ref, stat_ref, mixed_ref, wide_ref, *, block, chunk
):
    at = pl.program_id(0)

    @pl.when(at == 0)
    def _():
        fill_slots(qkv_ref, documents_ref, wide_ref, ("query", "key", "value"), block)

    rows = pl.ds(pl.multiple_of(at * block, block), block)
    lane = lax.broadcasted_iota(jnp.int32, (block, LANES), 1)
    last = lax.div(at * block, chunk)
    for slot in range(2):
        spare = HALF - HALF * slot
        own = (lane < HALF) if slot == 0 else (lane >= HALF)
        columns = slice(slot * LANES, (slot + 1) * LANES)

        @pl.when(active_ref[slot, at] != 0)
        def _():
            query = wide_ref[rows, columns]

            def step(index, carry, edge):
                top, weighted = carry
                place = pl.ds(pl.multiple_of(index * chunk, chunk), chunk)
                keys = wide_ref[place, 2 * LANES + slot * LANES : 3 * LANES + slot * LANES]
                values = wide_ref[place, 4 * LANES + slot * LANES : 5 * LANES + slot * LANES]
                scores = contract(query, keys, 1, 1)
                if edge:
                    key_at = index * chunk + lax.broadcasted_iota(jnp.int32, (block, chunk), 1)
                    query_at = at * block + lax.broadcasted_iota(jnp.int32, (block, chunk), 0)
                    scores = jnp.where(key_at <= query_at, scores, FAR)
                new_top = jnp.maximum(top, jnp.max(scores, axis=1, keepdims=True))
                weights = jnp.exp(scores - new_top).astype(BF16)
                weighted = weighted * jnp.exp(top - new_top) + contract(weights, values, 1, 0)
                return new_top, weighted

            carry = (jnp.full((block, 1), FAR, F32), jnp.zeros((block, LANES), F32))
            carry = lax.fori_loop(0, last, lambda index, state: step(index, state, False), carry)
            top, weighted = step(last, carry, True)
            total = weighted[:, spare : spare + 1]
            mixed_ref[slot] = jnp.where(own, weighted / total, 0.0)
            log_total = top + jnp.log(total)
            high, middle, small = three_parts(log_total)
            extra = jnp.where(lane == spare + 3, -high, 0.0)
            extra = jnp.where(lane == spare + 4, -middle, extra)
            extra = jnp.where(lane == spare + 5, -small, extra)
            stat_ref[:, columns] = (query.astype(F32) + extra).astype(BF16)

        @pl.when(active_ref[slot, at] == 0)
        def _():
            mixed_ref[slot] = jnp.zeros((block, LANES), F32)
            stat_ref[:, columns] = jnp.zeros((block, LANES), BF16)

    mixed = mixed_ref[0] + mixed_ref[1]
    full_ref[...] = mixed
    low_ref[...] = mixed.astype(BF16)


def attend_back_kernel(
    active_ref,
    qkv_ref,
    documents_ref,
    stat_ref,
    grad_ref,
    mixed_ref,
    out_ref,
    key_sum_ref,
    value_sum_ref,
    query_sum_ref,
    wide_ref,
    *,
    block,
    chunk,
    scaling,
):
    at = pl.program_id(0)
    rows = pl.ds(pl.multiple_of(at * block, block), block)
    lane = lax.broadcasted_iota(jnp.int32, (block, LANES), 1)
    last = lax.div(at * block, chunk)

    @pl.when(at == 0)
    def _():
        fill_slots(qkv_ref, documents_ref, wide_ref, ("key", "value"), block)
        key_sum_ref[...] = jnp.zeros_like(key_sum_ref)
        value_sum_ref[...] = jnp.zeros_like(value_sum_ref)

    for slot in range(2):
        spare = HALF - HALF * slot
        own = (lane < HALF) if slot == 0 else (lane >= HALF)
        columns = slice(slot * LANES, (slot + 1) * LANES)
        query_sum_ref[slot] = jnp.zeros((block, LANES), F32)

        @pl.when(active_ref[slot, at] != 0)
        def _():
            query = stat_ref[:, columns]
            grad = grad_ref[...].astype(F32)
            delta = jnp.sum(jnp.where(own, grad * mixed_ref[...], 0.0), axis=1, keepdims=True)
            high, middle, small = three_parts(delta)
            extra = jnp.where(lane == spare, -high, 0.0)
            extra = jnp.where(lane == spare + 1, -middle, extra)
            extra = jnp.where(lane == spare + 2, -small, extra)
            grad_low = jnp.where(own, grad, extra).astype(BF16)

            def step(index, edge):
                place = pl.ds(pl.multiple_of(index * chunk, chunk), chunk)
                keys = wide_ref[place, slot * LANES : (slot + 1) * LANES]
                values = wide_ref[place, (2 + slot) * LANES : (3 + slot) * LANES]
                scores = contract(keys, query, 1, 1)
                if edge:
                    key_at = index * chunk + lax.broadcasted_iota(jnp.int32, (chunk, block), 0)
                    query_at = at * block + lax.broadcasted_iota(jnp.int32, (chunk, block), 1)
                    scores = jnp.where(key_at <= query_at, scores, FAR)
                weights = jnp.exp(scores)
                grad_weights = contract(values, grad_low, 1, 1)
                grad_scores = (weights * grad_weights).astype(BF16)
                value_sum_ref[slot, place, :] += contract(weights.astype(BF16), grad_low, 1, 0)
                key_sum_ref[slot, place, :] += contract(grad_scores, query, 1, 0)
                query_sum_ref[slot] += contract(grad_scores, keys, 0, 0)

            @pl.loop(0, last)
            def _(index):
                step(index, False)

            step(last, True)

    first_half = lane < HALF
    query_grad = jnp.where(first_half, query_sum_ref[0], query_sum_ref[1]) * scaling
    out_ref[rows, :LANES] = query_grad.astype(BF16)

    @pl.when(at == pl.num_programs(0) - 1)
    def _():
        @pl.loop(0, pl.num_programs(0))
        def _(index):
            place = pl.ds(pl.multiple_of(index * block, block), block)
            key_grad = jnp.where(first_half, key_sum_ref[0, place, :], key_sum_ref[1, place, :])
            value_grad = jnp.where(
                first_half, value_sum_ref[0, place, :], value_sum_ref[1, place, :]
            )
            out_ref[place, LANES : 2 * LANES] = key_grad.astype(BF16)
            out_ref[place, 2 * LANES :] = value_grad.astype(BF16)


def attend(active, qkv, documents, block):
    length = qkv.shape[0]
    count = length // block
    pairs = length * length * 3 // 4
    return pl.pallas_call(
        functools.partial(attend_kernel, block=block, chunk=2 * block),
        grid_spec=pltpu.PrefetchScalarGridSpec(
            num_scalar_prefetch=1,
            grid=(count,),
            in_specs=[
                pl.BlockSpec(qkv.shape, lambda i, a: (0, 0), pipeline_mode=pl.Buffered(1)),
                pl.BlockSpec(documents.shape, lambda i, a: (0, 0), pipeline_mode=pl.Buffered(1)),
            ],
            out_specs=[
                pl.BlockSpec((block, LANES), lambda i, a: (i, 0)),
                pl.BlockSpec((block, LANES), lambda i, a: (i, 0)),
                pl.BlockSpec((block, 2 * LANES), lambda i, a: (i, 0)),
            ],
            scratch_shapes=[
                pltpu.VMEM((2, block, LANES), F32),
                pltpu.VMEM((length, 6 * LANES), BF16),
            ],
        ),
        out_shape=[
            jax.ShapeDtypeStruct((length, LANES), BF16),
            jax.ShapeDtypeStruct((length, LANES), F32),
            jax.ShapeDtypeStruct((length, 2 * LANES), BF16),
        ],
        compiler_params=pltpu.CompilerParams(vmem_limit_bytes=VMEM_LIMIT),
        cost_estimate=pl.CostEstimate(
            flops=pairs * 4 * LANES, bytes_accessed=length * 2 * 10 * LANES, transcendentals=pairs
        ),
    )(active, qkv, documents)


def attend_back(active, qkv, documents, stat, grad, mixed, block, scaling):
    length = qkv.shape[0]
    count = length // block
    pairs = length * length * 3 // 4
    return pl.pallas_call(
        functools.partial(attend_back_kernel, block=block, chunk=2 * block, scaling=scaling),
        grid_spec=pltpu.PrefetchScalarGridSpec(
            num_scalar_prefetch=1,
            grid=(count,),
            in_specs=[
                pl.BlockSpec(qkv.shape, lambda i, a: (0, 0), pipeline_mode=pl.Buffered(1)),
                pl.BlockSpec(documents.shape, lambda i, a: (0, 0), pipeline_mode=pl.Buffered(1)),
                pl.BlockSpec((block, 2 * LANES), lambda i, a: (i, 0)),
                pl.BlockSpec((block, LANES), lambda i, a: (i, 0)),
                pl.BlockSpec((block, LANES), lambda i, a: (i, 0)),
            ],
            out_specs=pl.BlockSpec(
                (length, 3 * LANES), lambda i, a: (0, 0), pipeline_mode=pl.Buffered(1)
            ),
            scratch_shapes=[
                pltpu.VMEM((2, length, LANES), F32),
                pltpu.VMEM((2, length, LANES), F32),
                pltpu.VMEM((2, block, LANES), F32),
                pltpu.VMEM((length, 4 * LANES), BF16),
            ],
        ),
        out_shape=jax.ShapeDtypeStruct((length, 3 * LANES), BF16),
        compiler_params=pltpu.CompilerParams(vmem_limit_bytes=VMEM_LIMIT),
        cost_estimate=pl.CostEstimate(
            flops=pairs * 10 * LANES, bytes_accessed=length * 2 * 15 * LANES, transcendentals=pairs
        ),
    )(active, qkv, documents, stat, grad, mixed)


def adam_update(weight, grad, first, second, factor, rate, decay):
    clipped = grad * factor
    first_new = BETA_ONE * first + (1.0 - BETA_ONE) * clipped
    second_new = BETA_TWO * second + (1.0 - BETA_TWO) * clipped * clipped
    first_hat = first_new / (1.0 - BETA_ONE**STEP)
    second_hat = second_new / (1.0 - BETA_TWO**STEP)
    weight_new = weight - rate * (first_hat / (jnp.sqrt(second_hat) + ADAM_FLOOR) + decay * weight)
    return (first_new, second_new, weight_new)


def after(value, *earlier):
    return lax.optimization_barrier((value, *earlier))[0]


def swap(value, axes):
    return lax.all_to_all(value, axes, split_axis=0, concat_axis=0, tiled=True)


def adam_kernel(factor_ref, *refs, rates):
    count = len(rates)
    factor = factor_ref[0]
    for index, rate in enumerate(rates):
        weight, grad, first, second = [ref[...] for ref in refs[4 * index : 4 * index + 4]]
        outs = refs[4 * count + 3 * index : 4 * count + 3 * index + 3]
        for out, value in zip(
            outs, adam_update(weight, grad, first, second, factor, rate, DECAY), strict=True
        ):
            out[...] = value


def adam_all(factor, leaves, rates, steps):
    flat = [value.reshape(value.shape[-2:]) for leaf in leaves for value in leaf]

    def spec(value):
        rows, columns = value.shape
        if rows % (8 * steps) == 0:
            return pl.BlockSpec((rows // steps, columns), lambda i: (i, 0))
        lanes = columns // steps
        return pl.BlockSpec((rows, lanes), lambda i: (0, i))

    shapes = [jax.ShapeDtypeStruct(value.shape, F32) for value in flat[::4] for _ in range(3)]
    outs = pl.pallas_call(
        functools.partial(adam_kernel, rates=rates),
        grid=(steps,),
        in_specs=[pl.BlockSpec(memory_space=pltpu.SMEM)] + [spec(value) for value in flat],
        out_specs=[spec(shape) for shape in shapes],
        out_shape=shapes,
        compiler_params=pltpu.CompilerParams(vmem_limit_bytes=VMEM_LIMIT),
        cost_estimate=pl.CostEstimate(
            flops=20 * sum(value.size for value in flat[::4]),
            bytes_accessed=28 * sum(value.size for value in flat[::4]),
            transcendentals=0,
        ),
    )(factor.reshape(1), *flat)
    return [
        [out.reshape(leaf[0].shape) for out in outs[3 * index : 3 * index + 3]]
        for index, leaf in enumerate(leaves)
    ]


def others(value, axis):
    size = lax.axis_size(axis)
    return jnp.concatenate(
        [
            lax.ppermute(value, axis, [((i + step) % size, i) for i in range(size)])
            for step in range(1, size)
        ],
        axis=0,
    )


def sum_own(blocks, axis):
    size = lax.axis_size(axis)
    total = blocks[0].astype(F32)
    for step in range(1, size):
        total = total + lax.ppermute(
            blocks[step].astype(BF16), axis, [(i, (i + step) % size) for i in range(size)]
        ).astype(F32)
    return total


def spread_sum(value):
    count = lax.axis_size(ALL)
    return jnp.sum(swap(jnp.broadcast_to(value[None], (count, *value.shape)), ALL), axis=0)


def body(
    tokens,
    cotangent,
    segment_ids,
    expert_ids,
    projection,
    output_weight,
    expert_up,
    expert_down,
    norm_gains,
    projection_first,
    projection_second,
    output_first,
    output_second,
    up_first,
    up_second,
    down_first,
    down_second,
    gains_first,
    gains_second,
):
    inputs = tokens[0].astype(F32)
    upstream = cotangent[0].astype(F32)
    row_count = inputs.shape[0]
    width = inputs.shape[1]
    head_size = width // HEADS
    scaling = head_size ** (-0.5)
    count = lax.axis_size(SEQ)
    groups = lax.axis_size("exp")
    team = lax.axis_size(TEAM)
    position = lax.axis_index(SEQ)
    length = count * row_count
    weight_rows = projection.shape[0]
    first_heads, active_table = head_plan(count)
    starts = [int(head) * head_size for head in first_heads]
    active = lax.dynamic_index_in_dim(jnp.asarray(active_table), position, 0, keepdims=False)
    gain_first = norm_gains[0]
    gain_second = norm_gains[1]
    used = active_table.any(axis=2)

    scale_first = lax.rsqrt(jnp.mean(inputs * inputs, axis=-1, keepdims=True) + EPSILON)
    normed_first = inputs * scale_first
    attend_in = (normed_first * gain_first).astype(BF16)
    row_in = lax.all_gather(attend_in, SEQ, axis=0, tiled=True)
    projection_low = projection.astype(BF16)
    sent_rows = weight_rows + 8
    own_documents = jnp.zeros((8, 3 * LANES + width), BF16)
    own_documents = own_documents.at[0, :row_count].set(segment_ids[0].astype(BF16))
    output_low = output_weight.astype(BF16)
    pieces = [
        jnp.concatenate(
            [projection_low[:, k * width + s : k * width + s + LANES] for k in range(3)]
            + [output_low],
            axis=1,
        )
        for s in starts
    ]
    got_rows = swap(
        jnp.stack([jnp.concatenate([piece, own_documents], axis=0) for piece in pieces]), SEQ
    )
    documents = jnp.broadcast_to(
        got_rows[:, weight_rows, :row_count].reshape(length, 1), (length, LANES)
    )

    def all_rows(value, earlier):
        copies = jnp.broadcast_to(after(value, earlier)[None], (groups, *value.shape))
        return jnp.swapaxes(swap(copies, EXP), 0, 1).reshape(width, value.shape[-1])

    columns = all_rows(got_rows[:, :weight_rows, : 3 * LANES], got_rows)
    output_full = all_rows(got_rows[:, :weight_rows, 3 * LANES :], columns)
    slots = groups * CAP
    chosen = expert_ids[0, :, 0]
    one_hot = (chosen[:, None] == jnp.arange(groups, dtype=jnp.int32)[None, :]).astype(jnp.int32)
    rank = jnp.sum(jnp.cumsum(one_hot, axis=0) * one_hot, axis=1) - 1
    target = chosen * CAP + rank
    placing = (target[:, None] == jnp.arange(slots, dtype=jnp.int32)[None, :]).astype(BF16)

    def dispatch(values, *earlier):
        outgoing = jnp.einsum("ts,td->sd", placing, values, preferred_element_type=F32)
        outgoing = after(outgoing.astype(BF16), *earlier).reshape(1, groups, CAP, width)
        outgoing = jnp.broadcast_to(outgoing, (team, groups, CAP, width))
        return swap(outgoing.reshape(team * groups, CAP, width), TEAM + EXP).reshape(
            team * slots, width
        )

    def send_back(values):
        return swap(values.reshape(team * groups, CAP, width), TEAM + EXP).reshape(
            team, slots, width
        )

    def collect(returned):
        return jnp.einsum("ts,jsd->td", placing, returned, preferred_element_type=F32)

    grad_arrived = dispatch(cotangent[0], row_in, output_full)

    def gather_near(matrix, earlier):
        own_units = matrix[0].astype(BF16)
        return jnp.concatenate([own_units, others(after(own_units, earlier), "hi")], axis=0)

    near_up = gather_near(expert_up, row_in)
    near_down = gather_near(expert_down, row_in)
    projection_full = lax.all_gather(projection_low, ALL, axis=0, tiled=True)

    qkv = jnp.dot(row_in, columns, preferred_element_type=F32).astype(BF16)
    mixed_low, mixed_full, stat = attend(active, qkv, documents, row_count)

    def place_heads():
        index = np.arange(LANES)
        matrix = np.zeros((count, LANES, width), np.float32)
        for device in range(count):
            for slot in range(2):
                if used[device, slot]:
                    own = index[slot * HALF : (slot + 1) * HALF]
                    matrix[device, own, starts[device] + own] = 1.0
        return jnp.asarray(matrix, BF16)

    head_places = place_heads()

    def to_tokens(values):
        return swap(values.reshape(count, row_count, values.shape[1]), SEQ)

    attend_out = jnp.einsum(
        "jtc,jcd->td",
        after(to_tokens(after(mixed_low, grad_arrived, near_up)), near_down),
        head_places,
        preferred_element_type=F32,
    ).astype(BF16)
    branch = jnp.dot(attend_out, output_full, preferred_element_type=F32)
    middle = inputs + branch
    scale_second = lax.rsqrt(jnp.mean(middle * middle, axis=-1, keepdims=True) + EPSILON)
    normed_second = middle * scale_second
    expert_in = (normed_second * gain_second).astype(BF16)

    arrived = dispatch(expert_in)
    far_up, far_down = others(near_up, "in"), others(near_down, "in")
    unit_parts = []
    for up_matrix, down_matrix in ((near_up, near_down), (far_up, far_down)):
        hidden = jnp.einsum("sd,hd->sh", arrived, up_matrix, preferred_element_type=F32)
        active_units = jax.nn.gelu(hidden).astype(BF16)
        grad_active = jnp.einsum("sd,hd->sh", grad_arrived, down_matrix, preferred_element_type=F32)
        unused, gelu_pull = jax.vjp(jax.nn.gelu, hidden)
        grad_hidden = gelu_pull(grad_active)[0].astype(BF16)
        unit_parts.append((up_matrix, down_matrix, active_units, grad_hidden))
    grad_slots = sum(
        jnp.einsum("sh,hd->sd", grad_hidden, up_matrix, preferred_element_type=F32)
        for up_matrix, down_matrix, active_units, grad_hidden in unit_parts
    )
    returned_grad = send_back(grad_slots.astype(BF16))
    produced = sum(
        jnp.einsum("sh,hd->sd", active_units, down_matrix, preferred_element_type=F32)
        for up_matrix, down_matrix, active_units, grad_hidden in unit_parts
    ).astype(BF16)

    def unit_terms(left, right):
        return jnp.einsum("sh,sd->hd", left, right, preferred_element_type=F32)

    down_far = unit_terms(unit_parts[1][2], grad_arrived).astype(BF16)
    up_far = unit_terms(unit_parts[1][3], arrived).astype(BF16)
    down_near = unit_terms(unit_parts[0][2], grad_arrived)
    up_near = unit_terms(unit_parts[0][3], arrived)
    peers = lax.axis_size("hi")
    grad_expert_in = collect(after(returned_grad, down_far, up_far, produced))

    scaled_second = grad_expert_in * gain_second
    gain_second_part = jnp.sum(grad_expert_in * normed_second, axis=0)
    grad_middle = scale_second * (
        scaled_second
        - normed_second * jnp.mean(scaled_second * normed_second, axis=-1, keepdims=True)
    )
    residual_grad = upstream + grad_middle
    branch_grad = residual_grad.astype(BF16)
    grad_mixed = jnp.einsum(
        "td,ed->te", branch_grad, output_full, preferred_element_type=F32
    ).astype(BF16)

    down_near = sum_own([down_near, down_far], "in")
    down_parts = list(down_near.astype(BF16).reshape(peers, -1, width))
    sent_grad = jnp.stack([grad_mixed[:, s : s + LANES] for s in starts])
    row_grad = swap(sent_grad, SEQ).reshape(length, LANES)
    up_near = sum_own([up_near, up_far], "in")
    returned = send_back(after(produced, row_grad))
    expert_part = collect(returned)
    block_output = (middle + expert_part).astype(BF16)[None]

    def group_rows(value):
        return jnp.swapaxes(value.astype(BF16).reshape(count, groups, weight_rows, -1), 0, 1)

    output_term = jnp.einsum("tc,te->ce", attend_out, branch_grad, preferred_element_type=F32)
    output_parts = group_rows(output_term)
    group = lax.axis_index(EXP)
    output_rows = sum_own(
        [
            lax.dynamic_index_in_dim(
                output_parts, lax.rem(group + step, groups), 0, keepdims=False
            )
            for step in range(groups)
        ],
        "exp",
    ).astype(BF16)
    grad_qkv = attend_back(
        active,
        qkv,
        documents,
        stat,
        after(row_grad, down_near),
        mixed_full,
        row_count,
        scaling,
    )
    down_grad = sum_own([down_near[: down_near.shape[0] // peers]] + down_parts[1:], "hi")[None]
    up_parts = list(up_near.astype(BF16).reshape(peers, -1, width))
    up_grad = sum_own([up_near[: up_near.shape[0] // peers]] + up_parts[1:], "hi")[None]
    grad_pieces = to_tokens(after(grad_qkv, returned, up_near, down_grad))
    grad_projected = jnp.concatenate(
        [
            jnp.einsum(
                "jtc,jcd->td",
                grad_pieces[:, :, k * LANES : (k + 1) * LANES],
                head_places,
                preferred_element_type=F32,
            ).astype(BF16)
            for k in range(3)
        ],
        axis=1,
    )
    grad_attend_in = jnp.einsum(
        "tc,dc->td", grad_projected, projection_full, preferred_element_type=F32
    )
    scaled_first = grad_attend_in * gain_first
    gain_first_part = jnp.sum(grad_attend_in * normed_first, axis=0)
    input_grad = (
        residual_grad
        + scale_first
        * (
            scaled_first
            - normed_first * jnp.mean(scaled_first * normed_first, axis=-1, keepdims=True)
        )
    )[None]

    column_term = jnp.einsum("tc,te->ce", row_in, grad_qkv, preferred_element_type=F32)
    column_rows = swap(after(group_rows(column_term), grad_pieces, up_grad), EXP).astype(F32)
    column_rows = jnp.sum(column_rows, axis=0).astype(BF16)
    got_terms = swap(jnp.concatenate([column_rows, output_rows], axis=2), SEQ).astype(F32)
    column_sums = got_terms[:, :, : 3 * LANES]
    output_grad = jnp.sum(got_terms[:, :, 3 * LANES :], axis=0)
    head_grads = []
    for k in range(3):
        for head in range(HEADS):
            parts = [
                column_sums[j, :, k * LANES + slot * HALF : k * LANES + (slot + 1) * HALF]
                for j in range(count)
                for slot in range(2)
                if used[j, slot] and first_heads[j] + slot == head
            ]
            head_grads.append(functools.reduce(jnp.add, parts))
    projection_grad = jnp.concatenate(head_grads, axis=1)

    local_square = jnp.sum(projection_grad * projection_grad) + jnp.sum(output_grad * output_grad)
    local_square = local_square + jnp.sum(up_grad * up_grad) + jnp.sum(down_grad * down_grad)
    summed = spread_sum(
        jnp.concatenate(
            [gain_first_part, gain_second_part, jnp.broadcast_to(local_square, (LANES,))]
        )[None]
    )[0]
    gains_grad = summed[: 2 * width].reshape(2, width)
    grad_norm = jnp.sqrt(summed[2 * width] + jnp.sum(gains_grad * gains_grad))
    factor = jnp.minimum(1.0, CLIP / (grad_norm + 1e-06))
    (
        (projection_moment, projection_square, projection_new),
        (output_moment, output_square, output_new),
        (up_moment, up_square, up_new),
        (down_moment, down_square, down_new),
    ) = adam_all(
        factor,
        [
            (projection, projection_grad, projection_first, projection_second),
            (output_weight, output_grad, output_first, output_second),
            (expert_up, up_grad, up_first, up_second),
            (expert_down, down_grad, down_first, down_second),
        ],
        (RATE_MATRIX, RATE_OUTPUT, RATE_MATRIX, RATE_MATRIX),
        3,
    )
    gains_moment, gains_square, gains_new = adam_update(
        norm_gains, gains_grad, gains_first, gains_second, factor, RATE_GAIN, 0.0
    )
    return (
        block_output,
        input_grad,
        grad_norm,
        projection_grad,
        projection_moment,
        projection_square,
        projection_new,
        output_grad,
        output_moment,
        output_square,
        output_new,
        up_grad,
        up_moment,
        up_square,
        up_new,
        down_grad,
        down_moment,
        down_square,
        down_new,
        gains_grad,
        gains_moment,
        gains_square,
        gains_new,
    )


def solution(mesh):
    token = P("exp", SEQ, None)
    dense = P(ALL, None)
    expert = P("exp", SEQ, None)
    in_specs = (
        (token, token, P("exp", SEQ), token)
        + (dense, dense, expert, expert, P())
        + (dense,) * 4
        + (expert,) * 4
        + (P(), P())
    )
    out_specs = (token, token, P()) + (dense,) * 8 + (expert,) * 8 + (P(),) * 4
    rows, groups = mesh.devices.shape
    fine = Mesh(mesh.devices.reshape(rows // 4, 2, 2, groups), ALL)
    return jax.shard_map(body, mesh=fine, in_specs=in_specs, out_specs=out_specs, check_vma=False)
```

```python
import functools
import math

import jax
import jax.numpy as jnp
import numpy as np
from jax import lax
from jax.experimental import pallas as pl
from jax.experimental.pallas import tpu as pltpu
from jax.sharding import Mesh
from jax.sharding import PartitionSpec as P

HEADS = 12
CAP = 128
STEP = 10


EPSILON = 1e-05
CLIP = 1.0
BETA_ONE = 0.9
BETA_TWO = 0.99
ADAM_FLOOR = 1e-08
DECAY = 0.1
RATE_MATRIX = 0.04
RATE_OUTPUT = 0.1
RATE_GAIN = 0.5

SEQ = ("hi", "lo", "in")
EXP = ("exp",)
ALL = SEQ + EXP
TEAM = ("lo",)
SHARE = ("hi", "in")
LANES = 128
HALF = 64
FAR = -1e30
BF16 = jnp.bfloat16
F32 = jnp.float32
VMEM_LIMIT = 60 * 1024 * 1024


def head_plan(count):
    whole = math.lcm(HEADS, count)
    units, parts = whole // count, whole // HEADS
    first = np.zeros((count,), np.int64)
    active = np.zeros((count, 2, count), np.int32)
    for device in range(count):
        first[device] = min(units * device // parts, HEADS - 2)
        for unit in range(units * device, units * (device + 1)):
            slot = unit // parts - first[device]
            for block in range(count):
                turn = block % (2 * parts)
                if min(turn, 2 * parts - 1 - turn) == unit % parts:
                    active[device, slot, block] = 1
    return first, active


def three_parts(value):
    high = value.astype(BF16).astype(F32)
    middle = (value - high).astype(BF16).astype(F32)
    return high, middle, value - high - middle


def contract(left, right, left_axis, right_axis):
    return lax.dot_general(
        left, right, (((left_axis,), (right_axis,)), ((), ())), preferred_element_type=F32
    )


def slot_arrays(packed, documents, kind, slot):
    spare = HALF - HALF * slot
    lane = lax.broadcasted_iota(jnp.int32, packed.shape, 1)
    own = (lane < HALF) if slot == 0 else (lane >= HALF)
    place = (lane - spare).astype(F32)
    ours = place == documents
    first = (lane >= spare) & (lane < spare + 3)
    if kind == "query":
        extra = jnp.where(first & jnp.logical_not(ours), FAR, 0.0)
    elif kind == "key":
        extra = jnp.where(ours | ((lane >= spare + 3) & (lane < spare + 6)), 1.0, 0.0)
    else:
        extra = jnp.where(first, 1.0, 0.0)
    return jnp.where(own, packed, extra).astype(BF16)


def fill_slots(qkv_ref, documents_ref, wide_ref, kinds, block):
    @pl.loop(0, pl.num_programs(0))
    def _(index):
        place = pl.ds(pl.multiple_of(index * block, block), block)
        documents = documents_ref[place, :].astype(F32)
        for number, kind in enumerate(kinds):
            source = ("query", "key", "value").index(kind)
            packed = qkv_ref[place, source * LANES : (source + 1) * LANES].astype(F32)
            if kind == "query":
                packed = packed * 0.125
            for slot in range(2):
                column = (2 * number + slot) * LANES
                wide_ref[place, column : column + LANES] = slot_arrays(
                    packed, documents, kind, slot
                )


def attend_kernel(
    active_ref, qkv_ref, documents_ref, low_ref, full_ref, stat_ref, mixed_ref, wide_ref, *, block, chunk
):
    at = pl.program_id(0)

    @pl.when(at == 0)
    def _():
        fill_slots(qkv_ref, documents_ref, wide_ref, ("query", "key", "value"), block)

    rows = pl.ds(pl.multiple_of(at * block, block), block)
    lane = lax.broadcasted_iota(jnp.int32, (block, LANES), 1)
    last = lax.div(at * block, chunk)
    for slot in range(2):
        spare = HALF - HALF * slot
        own = (lane < HALF) if slot == 0 else (lane >= HALF)
        columns = slice(slot * LANES, (slot + 1) * LANES)

        @pl.when(active_ref[slot, at] != 0)
        def _():
            query = wide_ref[rows, columns]

            def step(index, carry, edge):
                top, weighted = carry
                place = pl.ds(pl.multiple_of(index * chunk, chunk), chunk)
                keys = wide_ref[place, 2 * LANES + slot * LANES : 3 * LANES + slot * LANES]
                values = wide_ref[place, 4 * LANES + slot * LANES : 5 * LANES + slot * LANES]
                scores = contract(query, keys, 1, 1)
                if edge:
                    key_at = index * chunk + lax.broadcasted_iota(jnp.int32, (block, chunk), 1)
                    query_at = at * block + lax.broadcasted_iota(jnp.int32, (block, chunk), 0)
                    scores = jnp.where(key_at <= query_at, scores, FAR)
                new_top = jnp.maximum(top, jnp.max(scores, axis=1, keepdims=True))
                weights = jnp.exp(scores - new_top).astype(BF16)
                weighted = weighted * jnp.exp(top - new_top) + contract(weights, values, 1, 0)
                return new_top, weighted

            carry = (jnp.full((block, 1), FAR, F32), jnp.zeros((block, LANES), F32))
            carry = lax.fori_loop(0, last, lambda index, state: step(index, state, False), carry)
            top, weighted = step(last, carry, True)
            total = weighted[:, spare : spare + 1]
            mixed_ref[slot] = jnp.where(own, weighted / total, 0.0)
            log_total = top + jnp.log(total)
            high, middle, small = three_parts(log_total)
            extra = jnp.where(lane == spare + 3, -high, 0.0)
            extra = jnp.where(lane == spare + 4, -middle, extra)
            extra = jnp.where(lane == spare + 5, -small, extra)
            stat_ref[:, columns] = (query.astype(F32) + extra).astype(BF16)

        @pl.when(active_ref[slot, at] == 0)
        def _():
            mixed_ref[slot] = jnp.zeros((block, LANES), F32)
            stat_ref[:, columns] = jnp.zeros((block, LANES), BF16)

    mixed = mixed_ref[0] + mixed_ref[1]
    full_ref[...] = mixed
    low_ref[...] = mixed.astype(BF16)


def attend_back_kernel(
    active_ref,
    qkv_ref,
    documents_ref,
    stat_ref,
    grad_ref,
    mixed_ref,
    out_ref,
    key_sum_ref,
    value_sum_ref,
    query_sum_ref,
    wide_ref,
    *,
    block,
    chunk,
    scaling,
):
    at = pl.program_id(0)
    rows = pl.ds(pl.multiple_of(at * block, block), block)
    lane = lax.broadcasted_iota(jnp.int32, (block, LANES), 1)
    last = lax.div(at * block, chunk)

    @pl.when(at == 0)
    def _():
        fill_slots(qkv_ref, documents_ref, wide_ref, ("key", "value"), block)
        key_sum_ref[...] = jnp.zeros_like(key_sum_ref)
        value_sum_ref[...] = jnp.zeros_like(value_sum_ref)

    for slot in range(2):
        spare = HALF - HALF * slot
        own = (lane < HALF) if slot == 0 else (lane >= HALF)
        columns = slice(slot * LANES, (slot + 1) * LANES)
        query_sum_ref[slot] = jnp.zeros((block, LANES), F32)

        @pl.when(active_ref[slot, at] != 0)
        def _():
            query = stat_ref[:, columns]
            grad = grad_ref[...].astype(F32)
            delta = jnp.sum(jnp.where(own, grad * mixed_ref[...], 0.0), axis=1, keepdims=True)
            high, middle, small = three_parts(delta)
            extra = jnp.where(lane == spare, -high, 0.0)
            extra = jnp.where(lane == spare + 1, -middle, extra)
            extra = jnp.where(lane == spare + 2, -small, extra)
            grad_low = jnp.where(own, grad, extra).astype(BF16)

            def step(index, edge):
                place = pl.ds(pl.multiple_of(index * chunk, chunk), chunk)
                keys = wide_ref[place, slot * LANES : (slot + 1) * LANES]
                values = wide_ref[place, (2 + slot) * LANES : (3 + slot) * LANES]
                scores = contract(keys, query, 1, 1)
                if edge:
                    key_at = index * chunk + lax.broadcasted_iota(jnp.int32, (chunk, block), 0)
                    query_at = at * block + lax.broadcasted_iota(jnp.int32, (chunk, block), 1)
                    scores = jnp.where(key_at <= query_at, scores, FAR)
                weights = jnp.exp(scores)
                grad_weights = contract(values, grad_low, 1, 1)
                grad_scores = (weights * grad_weights).astype(BF16)
                value_sum_ref[slot, place, :] += contract(weights.astype(BF16), grad_low, 1, 0)
                key_sum_ref[slot, place, :] += contract(grad_scores, query, 1, 0)
                query_sum_ref[slot] += contract(grad_scores, keys, 0, 0)

            @pl.loop(0, last)
            def _(index):
                step(index, False)

            step(last, True)

    first_half = lane < HALF
    query_grad = jnp.where(first_half, query_sum_ref[0], query_sum_ref[1]) * scaling
    out_ref[rows, :LANES] = query_grad.astype(BF16)

    @pl.when(at == pl.num_programs(0) - 1)
    def _():
        @pl.loop(0, pl.num_programs(0))
        def _(index):
            place = pl.ds(pl.multiple_of(index * block, block), block)
            key_grad = jnp.where(first_half, key_sum_ref[0, place, :], key_sum_ref[1, place, :])
            value_grad = jnp.where(
                first_half, value_sum_ref[0, place, :], value_sum_ref[1, place, :]
            )
            out_ref[place, LANES : 2 * LANES] = key_grad.astype(BF16)
            out_ref[place, 2 * LANES :] = value_grad.astype(BF16)


def attend(active, qkv, documents, block):
    length = qkv.shape[0]
    count = length // block
    pairs = length * length * 3 // 4
    return pl.pallas_call(
        functools.partial(attend_kernel, block=block, chunk=2 * block),
        grid_spec=pltpu.PrefetchScalarGridSpec(
            num_scalar_prefetch=1,
            grid=(count,),
            in_specs=[
                pl.BlockSpec(qkv.shape, lambda i, a: (0, 0), pipeline_mode=pl.Buffered(1)),
                pl.BlockSpec(documents.shape, lambda i, a: (0, 0), pipeline_mode=pl.Buffered(1)),
            ],
            out_specs=[
                pl.BlockSpec((block, LANES), lambda i, a: (i, 0)),
                pl.BlockSpec((block, LANES), lambda i, a: (i, 0)),
                pl.BlockSpec((block, 2 * LANES), lambda i, a: (i, 0)),
            ],
            scratch_shapes=[
                pltpu.VMEM((2, block, LANES), F32),
                pltpu.VMEM((length, 6 * LANES), BF16),
            ],
        ),
        out_shape=[
            jax.ShapeDtypeStruct((length, LANES), BF16),
            jax.ShapeDtypeStruct((length, LANES), F32),
            jax.ShapeDtypeStruct((length, 2 * LANES), BF16),
        ],
        compiler_params=pltpu.CompilerParams(vmem_limit_bytes=VMEM_LIMIT),
        cost_estimate=pl.CostEstimate(
            flops=pairs * 4 * LANES, bytes_accessed=length * 2 * 10 * LANES, transcendentals=pairs
        ),
    )(active, qkv, documents)


def attend_back(active, qkv, documents, stat, grad, mixed, block, scaling):
    length = qkv.shape[0]
    count = length // block
    pairs = length * length * 3 // 4
    return pl.pallas_call(
        functools.partial(attend_back_kernel, block=block, chunk=2 * block, scaling=scaling),
        grid_spec=pltpu.PrefetchScalarGridSpec(
            num_scalar_prefetch=1,
            grid=(count,),
            in_specs=[
                pl.BlockSpec(qkv.shape, lambda i, a: (0, 0), pipeline_mode=pl.Buffered(1)),
                pl.BlockSpec(documents.shape, lambda i, a: (0, 0), pipeline_mode=pl.Buffered(1)),
                pl.BlockSpec((block, 2 * LANES), lambda i, a: (i, 0)),
                pl.BlockSpec((block, LANES), lambda i, a: (i, 0)),
                pl.BlockSpec((block, LANES), lambda i, a: (i, 0)),
            ],
            out_specs=pl.BlockSpec(
                (length, 3 * LANES), lambda i, a: (0, 0), pipeline_mode=pl.Buffered(1)
            ),
            scratch_shapes=[
                pltpu.VMEM((2, length, LANES), F32),
                pltpu.VMEM((2, length, LANES), F32),
                pltpu.VMEM((2, block, LANES), F32),
                pltpu.VMEM((length, 4 * LANES), BF16),
            ],
        ),
        out_shape=jax.ShapeDtypeStruct((length, 3 * LANES), BF16),
        compiler_params=pltpu.CompilerParams(vmem_limit_bytes=VMEM_LIMIT),
        cost_estimate=pl.CostEstimate(
            flops=pairs * 10 * LANES, bytes_accessed=length * 2 * 15 * LANES, transcendentals=pairs
        ),
    )(active, qkv, documents, stat, grad, mixed)


def adam_update(weight, grad, first, second, factor, rate, decay):
    clipped = grad * factor
    first_new = BETA_ONE * first + (1.0 - BETA_ONE) * clipped
    second_new = BETA_TWO * second + (1.0 - BETA_TWO) * clipped * clipped
    first_hat = first_new / (1.0 - BETA_ONE**STEP)
    second_hat = second_new / (1.0 - BETA_TWO**STEP)
    weight_new = weight - rate * (first_hat / (jnp.sqrt(second_hat) + ADAM_FLOOR) + decay * weight)
    return (first_new, second_new, weight_new)


def together(*values):
    return lax.optimization_barrier(values)


def swap(value, axes):
    return lax.all_to_all(value, axes, split_axis=0, concat_axis=0, tiled=True)


def adam_kernel(factor_ref, *refs, rates):
    count = len(rates)
    factor = factor_ref[0]
    for index, rate in enumerate(rates):
        weight, grad, first, second = [ref[...] for ref in refs[4 * index : 4 * index + 4]]
        outs = refs[4 * count + 3 * index : 4 * count + 3 * index + 3]
        for out, value in zip(
            outs, adam_update(weight, grad, first, second, factor, rate, DECAY), strict=True
        ):
            out[...] = value


def adam_all(factor, leaves, rates, steps):
    flat = [value.reshape(value.shape[-2:]) for leaf in leaves for value in leaf]

    def spec(value):
        rows, columns = value.shape
        if rows % (8 * steps) == 0:
            return pl.BlockSpec((rows // steps, columns), lambda i: (i, 0))
        lanes = columns // steps
        return pl.BlockSpec((rows, lanes), lambda i: (0, i))

    shapes = [jax.ShapeDtypeStruct(value.shape, F32) for value in flat[::4] for _ in range(3)]
    outs = pl.pallas_call(
        functools.partial(adam_kernel, rates=rates),
        grid=(steps,),
        in_specs=[pl.BlockSpec(memory_space=pltpu.SMEM)] + [spec(value) for value in flat],
        out_specs=[spec(shape) for shape in shapes],
        out_shape=shapes,
        compiler_params=pltpu.CompilerParams(vmem_limit_bytes=VMEM_LIMIT),
        cost_estimate=pl.CostEstimate(
            flops=20 * sum(value.size for value in flat[::4]),
            bytes_accessed=28 * sum(value.size for value in flat[::4]),
            transcendentals=0,
        ),
    )(factor.reshape(1), *flat)
    return [
        [out.reshape(leaf[0].shape) for out in outs[3 * index : 3 * index + 3]]
        for index, leaf in enumerate(leaves)
    ]


def others(value, axis):
    size = lax.axis_size(axis)
    return jnp.concatenate(
        [
            lax.ppermute(value, axis, [((i + step) % size, i) for i in range(size)])
            for step in range(1, size)
        ],
        axis=0,
    )


def sum_own(blocks, axis):
    size = lax.axis_size(axis)
    total = blocks[0].astype(F32)
    for step in range(1, size):
        total = total + lax.ppermute(
            blocks[step].astype(BF16), axis, [(i, (i + step) % size) for i in range(size)]
        ).astype(F32)
    return total


def spread_sum(value):
    count = lax.axis_size(ALL)
    return jnp.sum(swap(jnp.broadcast_to(value[None], (count, *value.shape)), ALL), axis=0)


def body(
    tokens,
    cotangent,
    segment_ids,
    expert_ids,
    projection,
    output_weight,
    expert_up,
    expert_down,
    norm_gains,
    projection_first,
    projection_second,
    output_first,
    output_second,
    up_first,
    up_second,
    down_first,
    down_second,
    gains_first,
    gains_second,
):
    inputs = tokens[0].astype(F32)
    upstream = cotangent[0].astype(F32)
    row_count = inputs.shape[0]
    width = inputs.shape[1]
    head_size = width // HEADS
    scaling = head_size ** (-0.5)
    count = lax.axis_size(SEQ)
    groups = lax.axis_size("exp")
    team = lax.axis_size(TEAM)
    position = lax.axis_index(SEQ)
    length = count * row_count
    weight_rows = projection.shape[0]
    first_heads, active_table = head_plan(count)
    starts = [int(head) * head_size for head in first_heads]
    active = lax.dynamic_index_in_dim(jnp.asarray(active_table), position, 0, keepdims=False)
    gain_first = norm_gains[0]
    gain_second = norm_gains[1]
    used = active_table.any(axis=2)

    scale_first = lax.rsqrt(jnp.mean(inputs * inputs, axis=-1, keepdims=True) + EPSILON)
    normed_first = inputs * scale_first
    attend_in = (normed_first * gain_first).astype(BF16)
    row_in = lax.all_gather(attend_in, SEQ, axis=0, tiled=True)
    projection_low = projection.astype(BF16)
    sent_rows = weight_rows + 8
    own_documents = jnp.zeros((8, 3 * LANES + width), BF16)
    own_documents = own_documents.at[0, :row_count].set(segment_ids[0].astype(BF16))
    output_low = output_weight.astype(BF16)
    pieces = [
        jnp.concatenate(
            [projection_low[:, k * width + s : k * width + s + LANES] for k in range(3)]
            + [output_low],
            axis=1,
        )
        for s in starts
    ]
    got_rows = swap(
        jnp.stack([jnp.concatenate([piece, own_documents], axis=0) for piece in pieces]), SEQ
    )
    documents = jnp.broadcast_to(
        got_rows[:, weight_rows, :row_count].reshape(length, 1), (length, LANES)
    )

    def all_rows(value):
        copies = jnp.broadcast_to(value[None], (groups, *value.shape))
        return jnp.swapaxes(swap(copies, EXP), 0, 1).reshape(width, value.shape[-1])

    columns = all_rows(got_rows[:, :weight_rows, : 3 * LANES])
    columns, output_rows = together(columns, got_rows[:, :weight_rows, 3 * LANES :])
    output_full = all_rows(output_rows)
    slots = groups * CAP
    chosen = expert_ids[0, :, 0]
    one_hot = (chosen[:, None] == jnp.arange(groups, dtype=jnp.int32)[None, :]).astype(jnp.int32)
    rank = jnp.sum(jnp.cumsum(one_hot, axis=0) * one_hot, axis=1) - 1
    target = chosen * CAP + rank
    placing = (target[:, None] == jnp.arange(slots, dtype=jnp.int32)[None, :]).astype(BF16)

    def to_slots(values):
        outgoing = jnp.einsum("ts,td->sd", placing, values, preferred_element_type=F32)
        return outgoing.astype(BF16)

    def dispatch(outgoing):
        outgoing = jnp.broadcast_to(
            outgoing.reshape(1, groups, CAP, width), (team, groups, CAP, width)
        )
        return swap(outgoing.reshape(team * groups, CAP, width), TEAM + EXP).reshape(
            team * slots, width
        )

    def send_back(values):
        return swap(values.reshape(team * groups, CAP, width), TEAM + EXP).reshape(
            team, slots, width
        )

    def collect(returned):
        return jnp.einsum("ts,jsd->td", placing, returned, preferred_element_type=F32)

    own_up = expert_up[0].astype(BF16)
    own_down = expert_down[0].astype(BF16)
    row_in, output_full, grad_slots_out, own_up, own_down = together(
        row_in, output_full, to_slots(cotangent[0]), own_up, own_down
    )
    grad_arrived = dispatch(grad_slots_out)

    near_up = jnp.concatenate([own_up, others(own_up, "hi")], axis=0)
    near_down = jnp.concatenate([own_down, others(own_down, "hi")], axis=0)
    projection_full = lax.all_gather(projection_low, ALL, axis=0, tiled=True)

    qkv = jnp.dot(row_in, columns, preferred_element_type=F32).astype(BF16)
    mixed_low, mixed_full, stat = attend(active, qkv, documents, row_count)

    def place_heads():
        index = np.arange(LANES)
        matrix = np.zeros((count, LANES, width), np.float32)
        for device in range(count):
            for slot in range(2):
                if used[device, slot]:
                    own = index[slot * HALF : (slot + 1) * HALF]
                    matrix[device, own, starts[device] + own] = 1.0
        return jnp.asarray(matrix, BF16)

    head_places = place_heads()

    def to_tokens(values):
        return swap(values.reshape(count, row_count, values.shape[1]), SEQ)

    mixed_low, grad_arrived, near_up, near_down = together(
        mixed_low, grad_arrived, near_up, near_down
    )
    far_up = others(near_up, "in")
    far_down = others(near_down, "in")
    attend_out = jnp.einsum(
        "jtc,jcd->td",
        to_tokens(mixed_low),
        head_places,
        preferred_element_type=F32,
    ).astype(BF16)
    branch = jnp.dot(attend_out, output_full, preferred_element_type=F32)
    middle = inputs + branch
    scale_second = lax.rsqrt(jnp.mean(middle * middle, axis=-1, keepdims=True) + EPSILON)
    normed_second = middle * scale_second
    expert_in = (normed_second * gain_second).astype(BF16)

    expert_slots, far_up = together(to_slots(expert_in), far_up)
    arrived = dispatch(expert_slots)
    unit_parts = []
    for up_matrix, down_matrix in ((near_up, near_down), (far_up, far_down)):
        hidden = jnp.einsum("sd,hd->sh", arrived, up_matrix, preferred_element_type=F32)
        active_units = jax.nn.gelu(hidden).astype(BF16)
        grad_active = jnp.einsum("sd,hd->sh", grad_arrived, down_matrix, preferred_element_type=F32)
        unused, gelu_pull = jax.vjp(jax.nn.gelu, hidden)
        grad_hidden = gelu_pull(grad_active)[0].astype(BF16)
        unit_parts.append((up_matrix, down_matrix, active_units, grad_hidden))
    grad_slots = sum(
        jnp.einsum("sh,hd->sd", grad_hidden, up_matrix, preferred_element_type=F32)
        for up_matrix, down_matrix, active_units, grad_hidden in unit_parts
    )
    returned_grad = send_back(grad_slots.astype(BF16))
    produced = sum(
        jnp.einsum("sh,hd->sd", active_units, down_matrix, preferred_element_type=F32)
        for up_matrix, down_matrix, active_units, grad_hidden in unit_parts
    ).astype(BF16)

    def unit_terms(left, right):
        return jnp.einsum("sh,sd->hd", left, right, preferred_element_type=F32)

    down_far = unit_terms(unit_parts[1][2], grad_arrived).astype(BF16)
    up_far = unit_terms(unit_parts[1][3], arrived).astype(BF16)
    down_near = unit_terms(unit_parts[0][2], grad_arrived)
    up_near = unit_terms(unit_parts[0][3], arrived)
    peers = lax.axis_size("hi")
    returned_grad, down_far, up_far, produced = together(
        returned_grad, down_far, up_far, produced
    )
    grad_expert_in = collect(returned_grad)

    scaled_second = grad_expert_in * gain_second
    gain_second_part = jnp.sum(grad_expert_in * normed_second, axis=0)
    grad_middle = scale_second * (
        scaled_second
        - normed_second * jnp.mean(scaled_second * normed_second, axis=-1, keepdims=True)
    )
    residual_grad = upstream + grad_middle
    branch_grad = residual_grad.astype(BF16)
    grad_mixed = jnp.einsum(
        "td,ed->te", branch_grad, output_full, preferred_element_type=F32
    ).astype(BF16)

    down_near = sum_own([down_near, down_far], "in")
    sent_grad = jnp.stack([grad_mixed[:, s : s + LANES] for s in starts])
    row_grad = swap(sent_grad, SEQ).reshape(length, LANES)
    row_grad, down_near, projection_full, produced = together(
        row_grad, down_near, projection_full, produced
    )
    down_parts = list(down_near.astype(BF16).reshape(peers, -1, width))
    up_near = sum_own([up_near, up_far], "in")
    returned = send_back(produced)

    def group_rows(value):
        return jnp.swapaxes(value.astype(BF16).reshape(count, groups, weight_rows, -1), 0, 1)

    output_term = jnp.einsum("tc,te->ce", attend_out, branch_grad, preferred_element_type=F32)
    output_parts = group_rows(output_term)
    group = lax.axis_index(EXP)
    output_rows = sum_own(
        [
            lax.dynamic_index_in_dim(
                output_parts, lax.rem(group + step, groups), 0, keepdims=False
            )
            for step in range(groups)
        ],
        "exp",
    ).astype(BF16)
    grad_qkv = attend_back(
        active,
        qkv,
        documents,
        stat,
        row_grad,
        mixed_full,
        row_count,
        scaling,
    )
    down_grad = sum_own([down_near[: down_near.shape[0] // peers]] + down_parts[1:], "hi")[None]
    grad_qkv, returned, up_near, down_grad, output_rows = together(
        grad_qkv, returned, up_near, down_grad, output_rows
    )
    expert_part = collect(returned)
    block_output = (middle + expert_part).astype(BF16)[None]
    up_own = up_near[: up_near.shape[0] // peers]
    grad_pieces, *up_parts = together(
        to_tokens(grad_qkv), *list(up_near.astype(BF16).reshape(peers, -1, width))[1:]
    )
    up_grad = sum_own([up_own, *up_parts], "hi")[None]
    column_term = jnp.einsum("tc,te->ce", row_in, grad_qkv, preferred_element_type=F32)
    grad_pieces, column_parts = together(grad_pieces, group_rows(column_term))
    grad_projected = jnp.concatenate(
        [
            jnp.einsum(
                "jtc,jcd->td",
                grad_pieces[:, :, k * LANES : (k + 1) * LANES],
                head_places,
                preferred_element_type=F32,
            ).astype(BF16)
            for k in range(3)
        ],
        axis=1,
    )
    grad_attend_in = jnp.einsum(
        "tc,dc->td", grad_projected, projection_full, preferred_element_type=F32
    )
    scaled_first = grad_attend_in * gain_first
    gain_first_part = jnp.sum(grad_attend_in * normed_first, axis=0)
    input_grad = (
        residual_grad
        + scale_first
        * (
            scaled_first
            - normed_first * jnp.mean(scaled_first * normed_first, axis=-1, keepdims=True)
        )
    )[None]

    column_rows = swap(column_parts, EXP).astype(F32)
    column_rows = jnp.sum(column_rows, axis=0).astype(BF16)
    got_terms = swap(jnp.concatenate([column_rows, output_rows], axis=2), SEQ).astype(F32)
    column_sums = got_terms[:, :, : 3 * LANES]
    output_grad = jnp.sum(got_terms[:, :, 3 * LANES :], axis=0)
    head_grads = []
    for k in range(3):
        for head in range(HEADS):
            parts = [
                column_sums[j, :, k * LANES + slot * HALF : k * LANES + (slot + 1) * HALF]
                for j in range(count)
                for slot in range(2)
                if used[j, slot] and first_heads[j] + slot == head
            ]
            head_grads.append(functools.reduce(jnp.add, parts))
    projection_grad = jnp.concatenate(head_grads, axis=1)

    local_square = jnp.sum(projection_grad * projection_grad) + jnp.sum(output_grad * output_grad)
    local_square = local_square + jnp.sum(up_grad * up_grad) + jnp.sum(down_grad * down_grad)
    summed = spread_sum(
        jnp.concatenate(
            [gain_first_part, gain_second_part, jnp.broadcast_to(local_square, (LANES,))]
        )[None]
    )[0]
    gains_grad = summed[: 2 * width].reshape(2, width)
    grad_norm = jnp.sqrt(summed[2 * width] + jnp.sum(gains_grad * gains_grad))
    factor = jnp.minimum(1.0, CLIP / (grad_norm + 1e-06))
    (
        (projection_moment, projection_square, projection_new),
        (output_moment, output_square, output_new),
        (up_moment, up_square, up_new),
        (down_moment, down_square, down_new),
    ) = adam_all(
        factor,
        [
            (projection, projection_grad, projection_first, projection_second),
            (output_weight, output_grad, output_first, output_second),
            (expert_up, up_grad, up_first, up_second),
            (expert_down, down_grad, down_first, down_second),
        ],
        (RATE_MATRIX, RATE_OUTPUT, RATE_MATRIX, RATE_MATRIX),
        3,
    )
    gains_moment, gains_square, gains_new = adam_update(
        norm_gains, gains_grad, gains_first, gains_second, factor, RATE_GAIN, 0.0
    )
    return (
        block_output,
        input_grad,
        grad_norm,
        projection_grad,
        projection_moment,
        projection_square,
        projection_new,
        output_grad,
        output_moment,
        output_square,
        output_new,
        up_grad,
        up_moment,
        up_square,
        up_new,
        down_grad,
        down_moment,
        down_square,
        down_new,
        gains_grad,
        gains_moment,
        gains_square,
        gains_new,
    )


def solution(mesh):
    token = P("exp", SEQ, None)
    dense = P(ALL, None)
    expert = P("exp", SEQ, None)
    in_specs = (
        (token, token, P("exp", SEQ), token)
        + (dense, dense, expert, expert, P())
        + (dense,) * 4
        + (expert,) * 4
        + (P(), P())
    )
    out_specs = (token, token, P()) + (dense,) * 8 + (expert,) * 8 + (P(),) * 4
    rows, groups = mesh.devices.shape
    fine = Mesh(mesh.devices.reshape(rows // 4, 2, 2, groups), ALL)
    return jax.shard_map(body, mesh=fine, in_specs=in_specs, out_specs=out_specs, check_vma=False)
```

```python
import functools
import math

import jax
import jax.numpy as jnp
import numpy as np
from jax import lax
from jax.experimental import pallas as pl
from jax.experimental.pallas import tpu as pltpu
from jax.sharding import Mesh
from jax.sharding import PartitionSpec as P

HEADS = 12
CAP = 128
STEP = 10


EPSILON = 1e-05
CLIP = 1.0
BETA_ONE = 0.9
BETA_TWO = 0.99
ADAM_FLOOR = 1e-08
DECAY = 0.1
RATE_MATRIX = 0.04
RATE_OUTPUT = 0.1
RATE_GAIN = 0.5

SEQ = ("hi", "lo", "in")
EXP = ("exp",)
ALL = SEQ + EXP
TEAM = ("lo",)
SHARE = ("hi", "in")
LANES = 128
HALF = 64
FAR = -1e30
BF16 = jnp.bfloat16
F32 = jnp.float32
VMEM_LIMIT = 60 * 1024 * 1024


def head_plan(count):
    whole = math.lcm(HEADS, count)
    units, parts = whole // count, whole // HEADS
    first = np.zeros((count,), np.int64)
    active = np.zeros((count, 2, count), np.int32)
    for device in range(count):
        first[device] = min(units * device // parts, HEADS - 2)
        for unit in range(units * device, units * (device + 1)):
            slot = unit // parts - first[device]
            for block in range(count):
                turn = block % (2 * parts)
                if min(turn, 2 * parts - 1 - turn) == unit % parts:
                    active[device, slot, block] = 1
    return first, active


def three_parts(value):
    high = value.astype(BF16).astype(F32)
    middle = (value - high).astype(BF16).astype(F32)
    return high, middle, value - high - middle


def contract(left, right, left_axis, right_axis):
    return lax.dot_general(
        left, right, (((left_axis,), (right_axis,)), ((), ())), preferred_element_type=F32
    )


def slot_arrays(packed, documents, kind, slot):
    spare = HALF - HALF * slot
    lane = lax.broadcasted_iota(jnp.int32, packed.shape, 1)
    own = (lane < HALF) if slot == 0 else (lane >= HALF)
    place = (lane - spare).astype(F32)
    ours = place == documents
    first = (lane >= spare) & (lane < spare + 3)
    if kind == "query":
        extra = jnp.where(first & jnp.logical_not(ours), FAR, 0.0)
    elif kind == "key":
        extra = jnp.where(ours | ((lane >= spare + 3) & (lane < spare + 6)), 1.0, 0.0)
    else:
        extra = jnp.where(first, 1.0, 0.0)
    return jnp.where(own, packed, extra).astype(BF16)


def fill_slots(order_ref, qkv_ref, documents_ref, wide_ref, kinds, block):
    @pl.loop(0, pl.num_programs(0))
    def _(index):
        place = pl.ds(pl.multiple_of(index * block, block), block)
        lying = pl.ds(pl.multiple_of(order_ref[index] * block, block), block)
        documents = documents_ref[place, :].astype(F32)
        for number, kind in enumerate(kinds):
            source = ("query", "key", "value").index(kind)
            packed = qkv_ref[lying, source * LANES : (source + 1) * LANES].astype(F32)
            if kind == "query":
                packed = packed * 0.125
            for slot in range(2):
                column = (2 * number + slot) * LANES
                wide_ref[place, column : column + LANES] = slot_arrays(
                    packed, documents, kind, slot
                )


def attend_kernel(
    active_ref,
    order_ref,
    qkv_ref,
    documents_ref,
    low_ref,
    full_ref,
    stat_ref,
    mixed_ref,
    wide_ref,
    *,
    block,
    chunk,
):
    at = pl.program_id(0)

    @pl.when(at == 0)
    def _():
        fill_slots(
            order_ref, qkv_ref, documents_ref, wide_ref, ("query", "key", "value"), block
        )

    rows = pl.ds(pl.multiple_of(at * block, block), block)
    lane = lax.broadcasted_iota(jnp.int32, (block, LANES), 1)
    last = lax.div(at * block, chunk)
    for slot in range(2):
        spare = HALF - HALF * slot
        own = (lane < HALF) if slot == 0 else (lane >= HALF)
        columns = slice(slot * LANES, (slot + 1) * LANES)

        @pl.when(active_ref[slot, at] != 0)
        def _():
            query = wide_ref[rows, columns]

            def step(index, carry, edge):
                top, weighted = carry
                place = pl.ds(pl.multiple_of(index * chunk, chunk), chunk)
                keys = wide_ref[place, 2 * LANES + slot * LANES : 3 * LANES + slot * LANES]
                values = wide_ref[place, 4 * LANES + slot * LANES : 5 * LANES + slot * LANES]
                scores = contract(query, keys, 1, 1)
                if edge:
                    key_at = index * chunk + lax.broadcasted_iota(jnp.int32, (block, chunk), 1)
                    query_at = at * block + lax.broadcasted_iota(jnp.int32, (block, chunk), 0)
                    scores = jnp.where(key_at <= query_at, scores, FAR)
                new_top = jnp.maximum(top, jnp.max(scores, axis=1, keepdims=True))
                weights = jnp.exp(scores - new_top).astype(BF16)
                weighted = weighted * jnp.exp(top - new_top) + contract(weights, values, 1, 0)
                return new_top, weighted

            carry = (jnp.full((block, 1), FAR, F32), jnp.zeros((block, LANES), F32))
            carry = lax.fori_loop(0, last, lambda index, state: step(index, state, False), carry)
            top, weighted = step(last, carry, True)
            total = weighted[:, spare : spare + 1]
            mixed_ref[slot] = jnp.where(own, weighted / total, 0.0)
            log_total = top + jnp.log(total)
            high, middle, small = three_parts(log_total)
            extra = jnp.where(lane == spare + 3, -high, 0.0)
            extra = jnp.where(lane == spare + 4, -middle, extra)
            extra = jnp.where(lane == spare + 5, -small, extra)
            stat_ref[:, columns] = (query.astype(F32) + extra).astype(BF16)

        @pl.when(active_ref[slot, at] == 0)
        def _():
            mixed_ref[slot] = jnp.zeros((block, LANES), F32)
            stat_ref[:, columns] = jnp.zeros((block, LANES), BF16)

    mixed = mixed_ref[0] + mixed_ref[1]
    full_ref[...] = mixed
    low_ref[...] = mixed.astype(BF16)


def attend_back_kernel(
    active_ref,
    order_ref,
    qkv_ref,
    documents_ref,
    stat_ref,
    grad_ref,
    mixed_ref,
    out_ref,
    lying_ref,
    key_sum_ref,
    value_sum_ref,
    query_sum_ref,
    wide_ref,
    *,
    block,
    chunk,
    scaling,
):
    at = pl.program_id(0)
    rows = pl.ds(pl.multiple_of(at * block, block), block)
    lane = lax.broadcasted_iota(jnp.int32, (block, LANES), 1)
    last = lax.div(at * block, chunk)

    @pl.when(at == 0)
    def _():
        fill_slots(order_ref, qkv_ref, documents_ref, wide_ref, ("key", "value"), block)
        key_sum_ref[...] = jnp.zeros_like(key_sum_ref)
        value_sum_ref[...] = jnp.zeros_like(value_sum_ref)

    for slot in range(2):
        spare = HALF - HALF * slot
        own = (lane < HALF) if slot == 0 else (lane >= HALF)
        columns = slice(slot * LANES, (slot + 1) * LANES)
        query_sum_ref[slot] = jnp.zeros((block, LANES), F32)

        @pl.when(active_ref[slot, at] != 0)
        def _():
            query = stat_ref[:, columns]
            grad = grad_ref[...].astype(F32)
            delta = jnp.sum(jnp.where(own, grad * mixed_ref[...], 0.0), axis=1, keepdims=True)
            high, middle, small = three_parts(delta)
            extra = jnp.where(lane == spare, -high, 0.0)
            extra = jnp.where(lane == spare + 1, -middle, extra)
            extra = jnp.where(lane == spare + 2, -small, extra)
            grad_low = jnp.where(own, grad, extra).astype(BF16)

            def step(index, edge):
                place = pl.ds(pl.multiple_of(index * chunk, chunk), chunk)
                keys = wide_ref[place, slot * LANES : (slot + 1) * LANES]
                values = wide_ref[place, (2 + slot) * LANES : (3 + slot) * LANES]
                scores = contract(keys, query, 1, 1)
                if edge:
                    key_at = index * chunk + lax.broadcasted_iota(jnp.int32, (chunk, block), 0)
                    query_at = at * block + lax.broadcasted_iota(jnp.int32, (chunk, block), 1)
                    scores = jnp.where(key_at <= query_at, scores, FAR)
                weights = jnp.exp(scores)
                grad_weights = contract(values, grad_low, 1, 1)
                grad_scores = (weights * grad_weights).astype(BF16)
                value_sum_ref[slot, place, :] += contract(weights.astype(BF16), grad_low, 1, 0)
                key_sum_ref[slot, place, :] += contract(grad_scores, query, 1, 0)
                query_sum_ref[slot] += contract(grad_scores, keys, 0, 0)

            @pl.loop(0, last)
            def _(index):
                step(index, False)

            step(last, True)

    first_half = lane < HALF
    query_grad = jnp.where(first_half, query_sum_ref[0], query_sum_ref[1]) * scaling
    out_ref[rows, :LANES] = query_grad.astype(BF16)
    lying = pl.ds(pl.multiple_of(order_ref[at] * block, block), block)
    lying_ref[lying, :LANES] = query_grad.astype(BF16)

    @pl.when(at == pl.num_programs(0) - 1)
    def _():
        @pl.loop(0, pl.num_programs(0))
        def _(index):
            place = pl.ds(pl.multiple_of(index * block, block), block)
            key_grad = jnp.where(first_half, key_sum_ref[0, place, :], key_sum_ref[1, place, :])
            value_grad = jnp.where(
                first_half, value_sum_ref[0, place, :], value_sum_ref[1, place, :]
            )
            out_ref[place, LANES : 2 * LANES] = key_grad.astype(BF16)
            out_ref[place, 2 * LANES :] = value_grad.astype(BF16)
            lying = pl.ds(pl.multiple_of(order_ref[index] * block, block), block)
            lying_ref[lying, LANES : 2 * LANES] = key_grad.astype(BF16)
            lying_ref[lying, 2 * LANES :] = value_grad.astype(BF16)


def attend(active, order, qkv, documents, block):
    length = qkv.shape[0]
    count = length // block
    pairs = length * length * 3 // 4
    return pl.pallas_call(
        functools.partial(attend_kernel, block=block, chunk=2 * block),
        grid_spec=pltpu.PrefetchScalarGridSpec(
            num_scalar_prefetch=2,
            grid=(count,),
            in_specs=[
                pl.BlockSpec(qkv.shape, lambda i, a, o: (0, 0), pipeline_mode=pl.Buffered(1)),
                pl.BlockSpec(documents.shape, lambda i, a, o: (0, 0), pipeline_mode=pl.Buffered(1)),
            ],
            out_specs=[
                pl.BlockSpec((block, LANES), lambda i, a, o: (i, 0)),
                pl.BlockSpec((block, LANES), lambda i, a, o: (i, 0)),
                pl.BlockSpec((block, 2 * LANES), lambda i, a, o: (i, 0)),
            ],
            scratch_shapes=[
                pltpu.VMEM((2, block, LANES), F32),
                pltpu.VMEM((length, 6 * LANES), BF16),
            ],
        ),
        out_shape=[
            jax.ShapeDtypeStruct((length, LANES), BF16),
            jax.ShapeDtypeStruct((length, LANES), F32),
            jax.ShapeDtypeStruct((length, 2 * LANES), BF16),
        ],
        compiler_params=pltpu.CompilerParams(vmem_limit_bytes=VMEM_LIMIT),
        cost_estimate=pl.CostEstimate(
            flops=pairs * 4 * LANES, bytes_accessed=length * 2 * 10 * LANES, transcendentals=pairs
        ),
    )(active, order, qkv, documents)


def attend_back(active, order, qkv, documents, stat, grad, mixed, block, scaling):
    length = qkv.shape[0]
    count = length // block
    pairs = length * length * 3 // 4
    return pl.pallas_call(
        functools.partial(attend_back_kernel, block=block, chunk=2 * block, scaling=scaling),
        grid_spec=pltpu.PrefetchScalarGridSpec(
            num_scalar_prefetch=2,
            grid=(count,),
            in_specs=[
                pl.BlockSpec(qkv.shape, lambda i, a, o: (0, 0), pipeline_mode=pl.Buffered(1)),
                pl.BlockSpec(documents.shape, lambda i, a, o: (0, 0), pipeline_mode=pl.Buffered(1)),
                pl.BlockSpec((block, 2 * LANES), lambda i, a, o: (i, 0)),
                pl.BlockSpec((block, LANES), lambda i, a, o: (i, 0)),
                pl.BlockSpec((block, LANES), lambda i, a, o: (i, 0)),
            ],
            out_specs=[
                pl.BlockSpec(
                    (length, 3 * LANES), lambda i, a, o: (0, 0), pipeline_mode=pl.Buffered(1)
                )
            ]
            * 2,
            scratch_shapes=[
                pltpu.VMEM((2, length, LANES), F32),
                pltpu.VMEM((2, length, LANES), F32),
                pltpu.VMEM((2, block, LANES), F32),
                pltpu.VMEM((length, 4 * LANES), BF16),
            ],
        ),
        out_shape=[jax.ShapeDtypeStruct((length, 3 * LANES), BF16)] * 2,
        compiler_params=pltpu.CompilerParams(vmem_limit_bytes=VMEM_LIMIT),
        cost_estimate=pl.CostEstimate(
            flops=pairs * 10 * LANES, bytes_accessed=length * 2 * 15 * LANES, transcendentals=pairs
        ),
    )(active, order, qkv, documents, stat, grad, mixed)


def adam_update(weight, grad, first, second, factor, rate, decay):
    clipped = grad * factor
    first_new = BETA_ONE * first + (1.0 - BETA_ONE) * clipped
    second_new = BETA_TWO * second + (1.0 - BETA_TWO) * clipped * clipped
    first_hat = first_new / (1.0 - BETA_ONE**STEP)
    second_hat = second_new / (1.0 - BETA_TWO**STEP)
    weight_new = weight - rate * (first_hat / (jnp.sqrt(second_hat) + ADAM_FLOOR) + decay * weight)
    return (first_new, second_new, weight_new)


def together(*values):
    return lax.optimization_barrier(values)


def swap(value, axes):
    return lax.all_to_all(value, axes, split_axis=0, concat_axis=0, tiled=True)


def adam_kernel(factor_ref, *refs, rates):
    count = len(rates)
    factor = factor_ref[0]
    for index, rate in enumerate(rates):
        weight, grad, first, second = [ref[...] for ref in refs[4 * index : 4 * index + 4]]
        outs = refs[4 * count + 3 * index : 4 * count + 3 * index + 3]
        for out, value in zip(
            outs, adam_update(weight, grad, first, second, factor, rate, DECAY), strict=True
        ):
            out[...] = value


def adam_all(factor, leaves, rates, steps):
    flat = [value.reshape(value.shape[-2:]) for leaf in leaves for value in leaf]

    def spec(value):
        rows, columns = value.shape
        if rows % (8 * steps) == 0:
            return pl.BlockSpec((rows // steps, columns), lambda i: (i, 0))
        lanes = columns // steps
        return pl.BlockSpec((rows, lanes), lambda i: (0, i))

    shapes = [jax.ShapeDtypeStruct(value.shape, F32) for value in flat[::4] for _ in range(3)]
    outs = pl.pallas_call(
        functools.partial(adam_kernel, rates=rates),
        grid=(steps,),
        in_specs=[pl.BlockSpec(memory_space=pltpu.SMEM)] + [spec(value) for value in flat],
        out_specs=[spec(shape) for shape in shapes],
        out_shape=shapes,
        compiler_params=pltpu.CompilerParams(vmem_limit_bytes=VMEM_LIMIT),
        cost_estimate=pl.CostEstimate(
            flops=20 * sum(value.size for value in flat[::4]),
            bytes_accessed=28 * sum(value.size for value in flat[::4]),
            transcendentals=0,
        ),
    )(factor.reshape(1), *flat)
    return [
        [out.reshape(leaf[0].shape) for out in outs[3 * index : 3 * index + 3]]
        for index, leaf in enumerate(leaves)
    ]


def gather_row(value):
    position, count = lax.axis_index(SEQ), lax.axis_size(SEQ)
    if count != 8:
        blocks = [lax.all_gather(value, SEQ, axis=0, tiled=True)]
        return blocks, jnp.arange(count, dtype=jnp.int32)
    blocks = [value, others(value, "lo")]
    blocks += [others(block, "hi") for block in blocks]
    blocks = [held for block in blocks for held in (block, others(block, "in"))]
    return blocks, jnp.arange(count, dtype=jnp.int32) ^ position


def others(value, axis):
    size = lax.axis_size(axis)
    return jnp.concatenate(
        [
            lax.ppermute(value, axis, [((i + step) % size, i) for i in range(size)])
            for step in range(1, size)
        ],
        axis=0,
    )


def sum_own(blocks, axis):
    size = lax.axis_size(axis)
    total = blocks[0].astype(F32)
    for step in range(1, size):
        total = total + lax.ppermute(
            blocks[step].astype(BF16), axis, [(i, (i + step) % size) for i in range(size)]
        ).astype(F32)
    return total


def spread_sum(value):
    count = lax.axis_size(ALL)
    return jnp.sum(swap(jnp.broadcast_to(value[None], (count, *value.shape)), ALL), axis=0)


def body(
    tokens,
    cotangent,
    segment_ids,
    expert_ids,
    projection,
    output_weight,
    expert_up,
    expert_down,
    norm_gains,
    projection_first,
    projection_second,
    output_first,
    output_second,
    up_first,
    up_second,
    down_first,
    down_second,
    gains_first,
    gains_second,
):
    inputs = tokens[0].astype(F32)
    upstream = cotangent[0].astype(F32)
    row_count = inputs.shape[0]
    width = inputs.shape[1]
    head_size = width // HEADS
    scaling = head_size ** (-0.5)
    count = lax.axis_size(SEQ)
    groups = lax.axis_size("exp")
    team = lax.axis_size(TEAM)
    position = lax.axis_index(SEQ)
    length = count * row_count
    weight_rows = projection.shape[0]
    first_heads, active_table = head_plan(count)
    starts = [int(head) * head_size for head in first_heads]
    active = lax.dynamic_index_in_dim(jnp.asarray(active_table), position, 0, keepdims=False)
    gain_first = norm_gains[0]
    gain_second = norm_gains[1]
    used = active_table.any(axis=2)

    scale_first = lax.rsqrt(jnp.mean(inputs * inputs, axis=-1, keepdims=True) + EPSILON)
    normed_first = inputs * scale_first
    attend_in = (normed_first * gain_first).astype(BF16)
    row_blocks, order = gather_row(attend_in)
    projection_low = projection.astype(BF16)
    sent_rows = weight_rows + 8
    own_documents = jnp.zeros((8, 3 * LANES + width), BF16)
    own_documents = own_documents.at[0, :row_count].set(segment_ids[0].astype(BF16))
    output_low = output_weight.astype(BF16)
    pieces = [
        jnp.concatenate(
            [projection_low[:, k * width + s : k * width + s + LANES] for k in range(3)]
            + [output_low],
            axis=1,
        )
        for s in starts
    ]
    got_rows = swap(
        jnp.stack([jnp.concatenate([piece, own_documents], axis=0) for piece in pieces]), SEQ
    )
    documents = jnp.broadcast_to(
        got_rows[:, weight_rows, :row_count].reshape(length, 1), (length, LANES)
    )

    def all_rows(value):
        copies = jnp.broadcast_to(value[None], (groups, *value.shape))
        return jnp.swapaxes(swap(copies, EXP), 0, 1).reshape(width, value.shape[-1])

    columns = all_rows(got_rows[:, :weight_rows, : 3 * LANES])
    columns, output_rows = together(columns, got_rows[:, :weight_rows, 3 * LANES :])
    output_full = all_rows(output_rows)
    slots = groups * CAP
    chosen = expert_ids[0, :, 0]
    one_hot = (chosen[:, None] == jnp.arange(groups, dtype=jnp.int32)[None, :]).astype(jnp.int32)
    rank = jnp.sum(jnp.cumsum(one_hot, axis=0) * one_hot, axis=1) - 1
    target = chosen * CAP + rank
    placing = (target[:, None] == jnp.arange(slots, dtype=jnp.int32)[None, :]).astype(BF16)

    def to_slots(values):
        outgoing = jnp.einsum("ts,td->sd", placing, values, preferred_element_type=F32)
        return outgoing.astype(BF16)

    def dispatch(outgoing):
        outgoing = jnp.broadcast_to(
            outgoing.reshape(1, groups, CAP, width), (team, groups, CAP, width)
        )
        return swap(outgoing.reshape(team * groups, CAP, width), TEAM + EXP).reshape(
            team * slots, width
        )

    def send_back(values):
        return swap(values.reshape(team * groups, CAP, width), TEAM + EXP).reshape(
            team, slots, width
        )

    def collect(returned):
        return jnp.einsum("ts,jsd->td", placing, returned, preferred_element_type=F32)

    own_up = expert_up[0].astype(BF16)
    own_down = expert_down[0].astype(BF16)
    last_far = max(len(row_blocks) - 2, 0)
    row_blocks[last_far], own_up, own_down = together(row_blocks[last_far], own_up, own_down)
    row_in, output_full, grad_slots_out = together(
        jnp.concatenate(row_blocks, axis=0), output_full, to_slots(cotangent[0])
    )
    grad_arrived = dispatch(grad_slots_out)

    near_up = jnp.concatenate([own_up, others(own_up, "hi")], axis=0)
    near_down = jnp.concatenate([own_down, others(own_down, "hi")], axis=0)
    projection_full = lax.all_gather(projection_low, ALL, axis=0, tiled=True)

    qkv = jnp.dot(row_in, columns, preferred_element_type=F32).astype(BF16)
    mixed_low, mixed_full, stat = attend(active, order, qkv, documents, row_count)

    def place_heads():
        index = np.arange(LANES)
        matrix = np.zeros((count, LANES, width), np.float32)
        for device in range(count):
            for slot in range(2):
                if used[device, slot]:
                    own = index[slot * HALF : (slot + 1) * HALF]
                    matrix[device, own, starts[device] + own] = 1.0
        return jnp.asarray(matrix, BF16)

    head_places = place_heads()

    def to_tokens(values):
        return swap(values.reshape(count, row_count, values.shape[1]), SEQ)

    mixed_low, grad_arrived, near_up, near_down = together(
        mixed_low, grad_arrived, near_up, near_down
    )
    far_up = others(near_up, "in")
    far_down = others(near_down, "in")
    attend_out = jnp.einsum(
        "jtc,jcd->td",
        to_tokens(mixed_low),
        head_places,
        preferred_element_type=F32,
    ).astype(BF16)
    branch = jnp.dot(attend_out, output_full, preferred_element_type=F32)
    middle = inputs + branch
    scale_second = lax.rsqrt(jnp.mean(middle * middle, axis=-1, keepdims=True) + EPSILON)
    normed_second = middle * scale_second
    expert_in = (normed_second * gain_second).astype(BF16)

    expert_slots, far_up = together(to_slots(expert_in), far_up)
    arrived = dispatch(expert_slots)
    unit_parts = []
    for up_matrix, down_matrix in ((near_up, near_down), (far_up, far_down)):
        hidden = jnp.einsum("sd,hd->sh", arrived, up_matrix, preferred_element_type=F32)
        active_units = jax.nn.gelu(hidden).astype(BF16)
        grad_active = jnp.einsum("sd,hd->sh", grad_arrived, down_matrix, preferred_element_type=F32)
        unused, gelu_pull = jax.vjp(jax.nn.gelu, hidden)
        grad_hidden = gelu_pull(grad_active)[0].astype(BF16)
        unit_parts.append((up_matrix, down_matrix, active_units, grad_hidden))
    grad_slots = sum(
        jnp.einsum("sh,hd->sd", grad_hidden, up_matrix, preferred_element_type=F32)
        for up_matrix, down_matrix, active_units, grad_hidden in unit_parts
    )
    returned_grad = send_back(grad_slots.astype(BF16))
    produced = sum(
        jnp.einsum("sh,hd->sd", active_units, down_matrix, preferred_element_type=F32)
        for up_matrix, down_matrix, active_units, grad_hidden in unit_parts
    ).astype(BF16)

    def unit_terms(left, right):
        return jnp.einsum("sh,sd->hd", left, right, preferred_element_type=F32)

    down_far = unit_terms(unit_parts[1][2], grad_arrived).astype(BF16)
    up_far = unit_terms(unit_parts[1][3], arrived).astype(BF16)
    down_near = unit_terms(unit_parts[0][2], grad_arrived)
    up_near = unit_terms(unit_parts[0][3], arrived)
    peers = lax.axis_size("hi")
    returned_grad, down_far, up_far, produced = together(
        returned_grad, down_far, up_far, produced
    )
    grad_expert_in = collect(returned_grad)

    scaled_second = grad_expert_in * gain_second
    gain_second_part = jnp.sum(grad_expert_in * normed_second, axis=0)
    grad_middle = scale_second * (
        scaled_second
        - normed_second * jnp.mean(scaled_second * normed_second, axis=-1, keepdims=True)
    )
    residual_grad = upstream + grad_middle
    branch_grad = residual_grad.astype(BF16)
    grad_mixed = jnp.einsum(
        "td,ed->te", branch_grad, output_full, preferred_element_type=F32
    ).astype(BF16)

    down_near = sum_own([down_near, down_far], "in")
    sent_grad = jnp.stack([grad_mixed[:, s : s + LANES] for s in starts])
    sent_grad, down_near = together(sent_grad, down_near)
    row_grad = swap(sent_grad, SEQ).reshape(length, LANES)
    def sum_hi(near):
        parts = list(near.astype(BF16).reshape(peers, -1, width))
        return sum_own([near[: near.shape[0] // peers], *parts[1:]], "hi")[None]

    down_grad = sum_hi(down_near)
    up_near = sum_own([up_near, up_far], "in")
    row_grad, projection_full, produced, down_grad, up_near = together(
        row_grad, projection_full, produced, down_grad, up_near
    )
    returned = send_back(produced)
    up_grad = sum_hi(up_near)
    grad_qkv, grad_lying = attend_back(
        active, order, qkv, documents, stat, row_grad, mixed_full, row_count, scaling
    )
    grad_qkv, grad_lying, returned, up_grad = together(grad_qkv, grad_lying, returned, up_grad)
    expert_part = collect(returned)
    block_output = (middle + expert_part).astype(BF16)[None]

    column_term = jnp.einsum("tc,te->ce", row_in, grad_lying, preferred_element_type=F32)
    output_term = jnp.einsum("tc,te->ce", attend_out, branch_grad, preferred_element_type=F32)
    dense_parts = jnp.concatenate([column_term.astype(BF16), output_term.astype(BF16)], axis=1)
    dense_parts = jnp.swapaxes(dense_parts.reshape(count, groups, weight_rows, -1), 0, 1)
    group = lax.axis_index(EXP)
    dense_rows = sum_own(
        [
            lax.dynamic_index_in_dim(dense_parts, lax.rem(group + step, groups), 0, keepdims=False)
            for step in range(groups)
        ],
        "exp",
    ).astype(BF16)
    grad_pieces, dense_rows = together(to_tokens(grad_qkv), dense_rows)
    grad_projected = jnp.concatenate(
        [
            jnp.einsum(
                "jtc,jcd->td",
                grad_pieces[:, :, k * LANES : (k + 1) * LANES],
                head_places,
                preferred_element_type=F32,
            ).astype(BF16)
            for k in range(3)
        ],
        axis=1,
    )
    grad_attend_in = jnp.einsum(
        "tc,dc->td", grad_projected, projection_full, preferred_element_type=F32
    )
    scaled_first = grad_attend_in * gain_first
    gain_first_part = jnp.sum(grad_attend_in * normed_first, axis=0)
    input_grad = (
        residual_grad
        + scale_first
        * (
            scaled_first
            - normed_first * jnp.mean(scaled_first * normed_first, axis=-1, keepdims=True)
        )
    )[None]

    got_terms = swap(dense_rows, SEQ).astype(F32)
    column_sums = got_terms[:, :, : 3 * LANES]
    output_grad = jnp.sum(got_terms[:, :, 3 * LANES :], axis=0)
    head_grads = []
    for k in range(3):
        for head in range(HEADS):
            parts = [
                column_sums[j, :, k * LANES + slot * HALF : k * LANES + (slot + 1) * HALF]
                for j in range(count)
                for slot in range(2)
                if used[j, slot] and first_heads[j] + slot == head
            ]
            head_grads.append(functools.reduce(jnp.add, parts))
    projection_grad = jnp.concatenate(head_grads, axis=1)

    local_square = jnp.sum(projection_grad * projection_grad) + jnp.sum(output_grad * output_grad)
    local_square = local_square + jnp.sum(up_grad * up_grad) + jnp.sum(down_grad * down_grad)
    summed = spread_sum(
        jnp.concatenate(
            [gain_first_part, gain_second_part, jnp.broadcast_to(local_square, (LANES,))]
        )[None]
    )[0]
    gains_grad = summed[: 2 * width].reshape(2, width)
    grad_norm = jnp.sqrt(summed[2 * width] + jnp.sum(gains_grad * gains_grad))
    factor = jnp.minimum(1.0, CLIP / (grad_norm + 1e-06))
    (
        (projection_moment, projection_square, projection_new),
        (output_moment, output_square, output_new),
        (up_moment, up_square, up_new),
        (down_moment, down_square, down_new),
    ) = adam_all(
        factor,
        [
            (projection, projection_grad, projection_first, projection_second),
            (output_weight, output_grad, output_first, output_second),
            (expert_up, up_grad, up_first, up_second),
            (expert_down, down_grad, down_first, down_second),
        ],
        (RATE_MATRIX, RATE_OUTPUT, RATE_MATRIX, RATE_MATRIX),
        3,
    )
    gains_moment, gains_square, gains_new = adam_update(
        norm_gains, gains_grad, gains_first, gains_second, factor, RATE_GAIN, 0.0
    )
    return (
        block_output,
        input_grad,
        grad_norm,
        projection_grad,
        projection_moment,
        projection_square,
        projection_new,
        output_grad,
        output_moment,
        output_square,
        output_new,
        up_grad,
        up_moment,
        up_square,
        up_new,
        down_grad,
        down_moment,
        down_square,
        down_new,
        gains_grad,
        gains_moment,
        gains_square,
        gains_new,
    )


def solution(mesh):
    token = P("exp", SEQ, None)
    dense = P(ALL, None)
    expert = P("exp", SEQ, None)
    in_specs = (
        (token, token, P("exp", SEQ), token)
        + (dense, dense, expert, expert, P())
        + (dense,) * 4
        + (expert,) * 4
        + (P(), P())
    )
    out_specs = (token, token, P()) + (dense,) * 8 + (expert,) * 8 + (P(),) * 4
    rows, groups = mesh.devices.shape
    fine = Mesh(mesh.devices.reshape(rows // 4, 2, 2, groups), ALL)
    return jax.shard_map(body, mesh=fine, in_specs=in_specs, out_specs=out_specs, check_vma=False)
```

```python
import functools
import math

import jax
import jax.numpy as jnp
import numpy as np
from jax import lax
from jax.experimental import pallas as pl
from jax.experimental.pallas import tpu as pltpu
from jax.sharding import Mesh
from jax.sharding import PartitionSpec as P

HEADS = 12
CAP = 128
STEP = 10


EPSILON = 1e-05
CLIP = 1.0
BETA_ONE = 0.9
BETA_TWO = 0.99
ADAM_FLOOR = 1e-08
DECAY = 0.1
RATE_MATRIX = 0.04
RATE_OUTPUT = 0.1
RATE_GAIN = 0.5

SEQ = ("hi", "lo", "in")
EXP = ("exp",)
ALL = SEQ + EXP
TEAM = ("lo",)
SHARE = ("hi", "in")
LANES = 128
HALF = 64
FAR = -1e30
BF16 = jnp.bfloat16
F32 = jnp.float32
VMEM_LIMIT = 60 * 1024 * 1024


def head_plan(count):
    whole = math.lcm(HEADS, count)
    units, parts = whole // count, whole // HEADS
    first = np.zeros((count,), np.int64)
    active = np.zeros((count, 2, count), np.int32)
    for device in range(count):
        first[device] = min(units * device // parts, HEADS - 2)
        for unit in range(units * device, units * (device + 1)):
            slot = unit // parts - first[device]
            for block in range(count):
                turn = block % (2 * parts)
                if min(turn, 2 * parts - 1 - turn) == unit % parts:
                    active[device, slot, block] = 1
    return first, active


def three_parts(value):
    high = value.astype(BF16).astype(F32)
    middle = (value - high).astype(BF16).astype(F32)
    return high, middle, value - high - middle


def contract(left, right, left_axis, right_axis):
    return lax.dot_general(
        left, right, (((left_axis,), (right_axis,)), ((), ())), preferred_element_type=F32
    )


def slot_arrays(packed, documents, kind, slot):
    spare = HALF - HALF * slot
    lane = lax.broadcasted_iota(jnp.int32, packed.shape, 1)
    own = (lane < HALF) if slot == 0 else (lane >= HALF)
    place = (lane - spare).astype(F32)
    ours = place == documents
    first = (lane >= spare) & (lane < spare + 3)
    if kind == "query":
        extra = jnp.where(first & jnp.logical_not(ours), FAR, 0.0)
    elif kind == "key":
        extra = jnp.where(ours | ((lane >= spare + 3) & (lane < spare + 6)), 1.0, 0.0)
    else:
        extra = jnp.where(first, 1.0, 0.0)
    return jnp.where(own, packed, extra).astype(BF16)


def fill_slots(packed_of, documents_ref, wide_ref, kinds, place):
    documents = documents_ref[place, :].astype(F32)
    for number, kind in enumerate(kinds):
        packed = packed_of(kind).astype(F32)
        if kind == "query":
            packed = packed * 0.125
        for slot in range(2):
            column = (2 * number + slot) * LANES
            wide_ref[place, column : column + LANES] = slot_arrays(packed, documents, kind, slot)


def attend_kernel(active_ref, order_ref, *refs, block, chunk, held):
    row_refs = refs[:held]
    columns_ref, documents_ref = refs[held : held + 2]
    low_ref, full_ref, stat_ref, pair_ref, mixed_ref, wide_ref = refs[held + 2 :]
    at = pl.program_id(0)

    @pl.when(at == 0)
    def _():
        def fill(tokens, index):
            place = pl.ds(pl.multiple_of(order_ref[index] * block, block), block)
            packed = contract(tokens, columns_ref[...], 1, 0).astype(BF16)
            pair_ref[place, :] = packed[:, LANES:]
            parts = {
                kind: packed[:, part * LANES : (part + 1) * LANES]
                for part, kind in enumerate(("query", "key", "value"))
            }
            fill_slots(parts.get, documents_ref, wide_ref, tuple(parts), place)

        if held > 1:
            for index, row_ref in enumerate(row_refs):
                fill(row_ref[...], index)
        else:

            @pl.loop(0, pl.num_programs(0))
            def _(index):
                fill(row_refs[0][pl.ds(pl.multiple_of(index * block, block), block), :], index)

    rows = pl.ds(pl.multiple_of(at * block, block), block)
    lane = lax.broadcasted_iota(jnp.int32, (block, LANES), 1)
    last = lax.div(at * block, chunk)
    for slot in range(2):
        spare = HALF - HALF * slot
        own = (lane < HALF) if slot == 0 else (lane >= HALF)
        columns = slice(slot * LANES, (slot + 1) * LANES)

        @pl.when(active_ref[slot, at] != 0)
        def _():
            query = wide_ref[rows, columns]

            def step(index, carry, edge):
                top, weighted = carry
                place = pl.ds(pl.multiple_of(index * chunk, chunk), chunk)
                keys = wide_ref[place, 2 * LANES + slot * LANES : 3 * LANES + slot * LANES]
                values = wide_ref[place, 4 * LANES + slot * LANES : 5 * LANES + slot * LANES]
                scores = contract(query, keys, 1, 1)
                if edge:
                    key_at = index * chunk + lax.broadcasted_iota(jnp.int32, (block, chunk), 1)
                    query_at = at * block + lax.broadcasted_iota(jnp.int32, (block, chunk), 0)
                    scores = jnp.where(key_at <= query_at, scores, FAR)
                new_top = jnp.maximum(top, jnp.max(scores, axis=1, keepdims=True))
                weights = jnp.exp(scores - new_top).astype(BF16)
                weighted = weighted * jnp.exp(top - new_top) + contract(weights, values, 1, 0)
                return new_top, weighted

            carry = (jnp.full((block, 1), FAR, F32), jnp.zeros((block, LANES), F32))
            carry = lax.fori_loop(0, last, lambda index, state: step(index, state, False), carry)
            top, weighted = step(last, carry, True)
            total = weighted[:, spare : spare + 1]
            mixed_ref[slot] = jnp.where(own, weighted / total, 0.0)
            log_total = top + jnp.log(total)
            high, middle, small = three_parts(log_total)
            extra = jnp.where(lane == spare + 3, -high, 0.0)
            extra = jnp.where(lane == spare + 4, -middle, extra)
            extra = jnp.where(lane == spare + 5, -small, extra)
            stat_ref[:, columns] = (query.astype(F32) + extra).astype(BF16)

        @pl.when(active_ref[slot, at] == 0)
        def _():
            mixed_ref[slot] = jnp.zeros((block, LANES), F32)
            stat_ref[:, columns] = jnp.zeros((block, LANES), BF16)

    mixed = mixed_ref[0] + mixed_ref[1]
    full_ref[...] = mixed
    low_ref[...] = mixed.astype(BF16)


def attend_back_kernel(
    active_ref,
    order_ref,
    pair_ref,
    documents_ref,
    stat_ref,
    grad_ref,
    mixed_ref,
    out_ref,
    lying_ref,
    key_sum_ref,
    value_sum_ref,
    query_sum_ref,
    wide_ref,
    *,
    block,
    chunk,
    scaling,
):
    at = pl.program_id(0)
    rows = pl.ds(pl.multiple_of(at * block, block), block)
    lane = lax.broadcasted_iota(jnp.int32, (block, LANES), 1)
    last = lax.div(at * block, chunk)

    @pl.when(at == 0)
    def _():
        @pl.loop(0, pl.num_programs(0))
        def _(index):
            place = pl.ds(pl.multiple_of(index * block, block), block)
            parts = {"key": pair_ref[place, :LANES], "value": pair_ref[place, LANES:]}
            fill_slots(parts.get, documents_ref, wide_ref, tuple(parts), place)

        key_sum_ref[...] = jnp.zeros_like(key_sum_ref)
        value_sum_ref[...] = jnp.zeros_like(value_sum_ref)

    for slot in range(2):
        spare = HALF - HALF * slot
        own = (lane < HALF) if slot == 0 else (lane >= HALF)
        columns = slice(slot * LANES, (slot + 1) * LANES)
        query_sum_ref[slot] = jnp.zeros((block, LANES), F32)

        @pl.when(active_ref[slot, at] != 0)
        def _():
            query = stat_ref[:, columns]
            grad = grad_ref[...].astype(F32)
            delta = jnp.sum(jnp.where(own, grad * mixed_ref[...], 0.0), axis=1, keepdims=True)
            high, middle, small = three_parts(delta)
            extra = jnp.where(lane == spare, -high, 0.0)
            extra = jnp.where(lane == spare + 1, -middle, extra)
            extra = jnp.where(lane == spare + 2, -small, extra)
            grad_low = jnp.where(own, grad, extra).astype(BF16)

            def step(index, edge):
                place = pl.ds(pl.multiple_of(index * chunk, chunk), chunk)
                keys = wide_ref[place, slot * LANES : (slot + 1) * LANES]
                values = wide_ref[place, (2 + slot) * LANES : (3 + slot) * LANES]
                scores = contract(keys, query, 1, 1)
                if edge:
                    key_at = index * chunk + lax.broadcasted_iota(jnp.int32, (chunk, block), 0)
                    query_at = at * block + lax.broadcasted_iota(jnp.int32, (chunk, block), 1)
                    scores = jnp.where(key_at <= query_at, scores, FAR)
                weights = jnp.exp(scores)
                grad_weights = contract(values, grad_low, 1, 1)
                grad_scores = (weights * grad_weights).astype(BF16)
                value_sum_ref[slot, place, :] += contract(weights.astype(BF16), grad_low, 1, 0)
                key_sum_ref[slot, place, :] += contract(grad_scores, query, 1, 0)
                query_sum_ref[slot] += contract(grad_scores, keys, 0, 0)

            @pl.loop(0, last)
            def _(index):
                step(index, False)

            step(last, True)

    first_half = lane < HALF
    query_grad = jnp.where(first_half, query_sum_ref[0], query_sum_ref[1]) * scaling
    out_ref[rows, :LANES] = query_grad.astype(BF16)
    lying = pl.ds(pl.multiple_of(order_ref[at] * block, block), block)
    lying_ref[lying, :LANES] = query_grad.astype(BF16)

    @pl.when(at == pl.num_programs(0) - 1)
    def _():
        @pl.loop(0, pl.num_programs(0))
        def _(index):
            place = pl.ds(pl.multiple_of(index * block, block), block)
            key_grad = jnp.where(first_half, key_sum_ref[0, place, :], key_sum_ref[1, place, :])
            value_grad = jnp.where(
                first_half, value_sum_ref[0, place, :], value_sum_ref[1, place, :]
            )
            out_ref[place, LANES : 2 * LANES] = key_grad.astype(BF16)
            out_ref[place, 2 * LANES :] = value_grad.astype(BF16)
            lying = pl.ds(pl.multiple_of(order_ref[index] * block, block), block)
            lying_ref[lying, LANES : 2 * LANES] = key_grad.astype(BF16)
            lying_ref[lying, 2 * LANES :] = value_grad.astype(BF16)


def whole(value):
    return pl.BlockSpec(value.shape, lambda i, *unused: (0, 0), pipeline_mode=pl.Buffered(1))


SMALL = pl.CostEstimate(flops=1, bytes_accessed=1, transcendentals=0)


def attend(active, order, row_blocks, columns, documents, block):
    length = documents.shape[0]
    pair = jax.ShapeDtypeStruct((length, 2 * LANES), BF16)
    return pl.pallas_call(
        functools.partial(attend_kernel, block=block, chunk=2 * block, held=len(row_blocks)),
        grid_spec=pltpu.PrefetchScalarGridSpec(
            num_scalar_prefetch=2,
            grid=(length // block,),
            in_specs=[whole(value) for value in (*row_blocks, columns, documents)],
            out_specs=[
                pl.BlockSpec((block, LANES), lambda i, a, o: (i, 0)),
                pl.BlockSpec((block, LANES), lambda i, a, o: (i, 0)),
                pl.BlockSpec((block, 2 * LANES), lambda i, a, o: (i, 0)),
                whole(pair),
            ],
            scratch_shapes=[
                pltpu.VMEM((2, block, LANES), F32),
                pltpu.VMEM((length, 6 * LANES), BF16),
            ],
        ),
        out_shape=[
            jax.ShapeDtypeStruct((length, LANES), BF16),
            jax.ShapeDtypeStruct((length, LANES), F32),
            jax.ShapeDtypeStruct((length, 2 * LANES), BF16),
            pair,
        ],
        compiler_params=pltpu.CompilerParams(vmem_limit_bytes=VMEM_LIMIT),
        cost_estimate=SMALL,
    )(active, order, *row_blocks, columns, documents)


def attend_back(active, order, pair, documents, stat, grad, mixed, block, scaling):
    length = pair.shape[0]
    count = length // block
    return pl.pallas_call(
        functools.partial(attend_back_kernel, block=block, chunk=2 * block, scaling=scaling),
        grid_spec=pltpu.PrefetchScalarGridSpec(
            num_scalar_prefetch=2,
            grid=(count,),
            in_specs=[
                whole(pair),
                whole(documents),
                pl.BlockSpec((block, 2 * LANES), lambda i, a, o: (i, 0)),
                pl.BlockSpec((block, LANES), lambda i, a, o: (i, 0)),
                pl.BlockSpec((block, LANES), lambda i, a, o: (i, 0)),
            ],
            out_specs=[
                pl.BlockSpec(
                    (length, 3 * LANES), lambda i, a, o: (0, 0), pipeline_mode=pl.Buffered(1)
                )
            ]
            * 2,
            scratch_shapes=[
                pltpu.VMEM((2, length, LANES), F32),
                pltpu.VMEM((2, length, LANES), F32),
                pltpu.VMEM((2, block, LANES), F32),
                pltpu.VMEM((length, 4 * LANES), BF16),
            ],
        ),
        out_shape=[jax.ShapeDtypeStruct((length, 3 * LANES), BF16)] * 2,
        compiler_params=pltpu.CompilerParams(vmem_limit_bytes=VMEM_LIMIT),
        cost_estimate=SMALL,
    )(active, order, pair, documents, stat, grad, mixed)


def expert_kernel(arrived_ref, grad_ref, up_ref, down_ref, *refs, first):
    active_ref, hidden_ref, total_ref = refs[-3:]
    up = up_ref[...]
    hidden = contract(arrived_ref[...], up, 1, 1)
    squared = hidden * hidden
    scale = math.sqrt(2.0 / math.pi)
    bend = jnp.tanh(scale * hidden * (1.0 + 0.044715 * squared))
    half = 0.5 + 0.5 * bend
    active_ref[...] = (hidden * half).astype(BF16)
    slope = half + (0.5 * scale) * hidden * (1.0 - bend * bend) * (1.0 + 3 * 0.044715 * squared)
    grad_hidden = (slope * contract(grad_ref[...], down_ref[...], 1, 1)).astype(BF16)
    hidden_ref[...] = grad_hidden
    total = contract(grad_hidden, up, 1, 0)
    if not first:
        total = total + refs[0][...]
    total_ref[...] = total.astype(total_ref.dtype)


def expert_part(arrived, grad_arrived, up, down, total):
    slots, width = arrived.shape
    units = up.shape[0]
    block = 256
    inputs = (arrived, grad_arrived, up, down) + (() if total is None else (total,))

    def rows(value):
        return pl.BlockSpec((block, value.shape[1]), lambda i: (i, 0))

    outs = [
        jax.ShapeDtypeStruct((slots, units), BF16),
        jax.ShapeDtypeStruct((slots, units), BF16),
        jax.ShapeDtypeStruct((slots, width), F32 if total is None else BF16),
    ]
    return pl.pallas_call(
        functools.partial(expert_kernel, first=total is None),
        grid=(slots // block,),
        in_specs=[rows(arrived), rows(grad_arrived), whole(up), whole(down)]
        + [rows(value) for value in inputs[4:]],
        out_specs=[rows(out) for out in outs],
        out_shape=outs,
        compiler_params=pltpu.CompilerParams(vmem_limit_bytes=VMEM_LIMIT),
        cost_estimate=SMALL,
    )(*inputs)


def unit_kernel(active_ref, grad_ref, hidden_ref, arrived_ref, down_ref, up_ref):
    down_ref[...] = contract(active_ref[...], grad_ref[...], 0, 0).astype(down_ref.dtype)
    up_ref[...] = contract(hidden_ref[...], arrived_ref[...], 0, 0).astype(up_ref.dtype)


def unit_grads(active, grad_arrived, grad_hidden, arrived, kind):
    slots, units = active.shape
    width = arrived.shape[1]
    block = 256
    left = pl.BlockSpec((slots, block), lambda i: (0, i))
    out = pl.BlockSpec((block, width), lambda i: (i, 0))
    return pl.pallas_call(
        unit_kernel,
        grid=(units // block,),
        in_specs=[left, whole(grad_arrived), left, whole(arrived)],
        out_specs=[out, out],
        out_shape=[jax.ShapeDtypeStruct((units, width), kind)] * 2,
        compiler_params=pltpu.CompilerParams(vmem_limit_bytes=VMEM_LIMIT),
        cost_estimate=SMALL,
    )(active, grad_arrived, grad_hidden, arrived)


def adam_update(weight, grad, first, second, factor, rate, decay):
    clipped = grad * factor
    first_new = BETA_ONE * first + (1.0 - BETA_ONE) * clipped
    second_new = BETA_TWO * second + (1.0 - BETA_TWO) * clipped * clipped
    first_hat = first_new / (1.0 - BETA_ONE**STEP)
    second_hat = second_new / (1.0 - BETA_TWO**STEP)
    weight_new = weight - rate * (first_hat / (jnp.sqrt(second_hat) + ADAM_FLOOR) + decay * weight)
    return (first_new, second_new, weight_new)


def together(*values):
    return lax.optimization_barrier(values)


def swap(value, axes):
    return lax.all_to_all(value, axes, split_axis=0, concat_axis=0, tiled=True)


def adam_kernel(factor_ref, *refs, rates):
    count = len(rates)
    factor = factor_ref[0]
    for index, rate in enumerate(rates):
        weight, grad, first, second = [ref[...] for ref in refs[4 * index : 4 * index + 4]]
        outs = refs[4 * count + 3 * index : 4 * count + 3 * index + 3]
        for out, value in zip(
            outs, adam_update(weight, grad, first, second, factor, rate, DECAY), strict=True
        ):
            out[...] = value


def adam_all(factor, leaves, rates, steps):
    flat = [value.reshape(value.shape[-2:]) for leaf in leaves for value in leaf]

    def spec(value):
        rows, columns = value.shape
        if rows % (8 * steps) == 0:
            return pl.BlockSpec((rows // steps, columns), lambda i: (i, 0))
        lanes = columns // steps
        return pl.BlockSpec((rows, lanes), lambda i: (0, i))

    shapes = [jax.ShapeDtypeStruct(value.shape, F32) for value in flat[::4] for _ in range(3)]
    outs = pl.pallas_call(
        functools.partial(adam_kernel, rates=rates),
        grid=(steps,),
        in_specs=[pl.BlockSpec(memory_space=pltpu.SMEM)] + [spec(value) for value in flat],
        out_specs=[spec(shape) for shape in shapes],
        out_shape=shapes,
        compiler_params=pltpu.CompilerParams(vmem_limit_bytes=VMEM_LIMIT),
        cost_estimate=pl.CostEstimate(
            flops=20 * sum(value.size for value in flat[::4]),
            bytes_accessed=28 * sum(value.size for value in flat[::4]),
            transcendentals=0,
        ),
    )(factor.reshape(1), *flat)
    return [
        [out.reshape(leaf[0].shape) for out in outs[3 * index : 3 * index + 3]]
        for index, leaf in enumerate(leaves)
    ]


def gather_row(value):
    position, count = lax.axis_index(SEQ), lax.axis_size(SEQ)
    if count != 8:
        blocks = [lax.all_gather(value, SEQ, axis=0, tiled=True)]
        return blocks, jnp.arange(count, dtype=jnp.int32)
    blocks = [value, others(value, "lo")]
    blocks += [others(block, "hi") for block in blocks]
    blocks = [held for block in blocks for held in (block, others(block, "in"))]
    return blocks, jnp.arange(count, dtype=jnp.int32) ^ position


def others(value, axis):
    size = lax.axis_size(axis)
    parts = [
        lax.ppermute(value, axis, [((i + step) % size, i) for i in range(size)])
        for step in range(1, size)
    ]
    return parts[0] if size == 2 else jnp.concatenate(parts, axis=0)


def to_owners(blocks, axis):
    size = lax.axis_size(axis)
    return [
        lax.ppermute(block, axis, [(i, (i + step) % size) for i in range(size)])
        for step, block in enumerate(blocks, 1)
    ]


def add_all(own, parts):
    return functools.reduce(lambda total, part: total + part.astype(F32), parts, own.astype(F32))


def spread_sum(value):
    count = lax.axis_size(ALL)
    return jnp.sum(swap(jnp.broadcast_to(value[None], (count, *value.shape)), ALL), axis=0)


def body(
    tokens,
    cotangent,
    segment_ids,
    expert_ids,
    projection,
    output_weight,
    expert_up,
    expert_down,
    norm_gains,
    projection_first,
    projection_second,
    output_first,
    output_second,
    up_first,
    up_second,
    down_first,
    down_second,
    gains_first,
    gains_second,
):
    inputs = tokens[0].astype(F32)
    upstream = cotangent[0].astype(F32)
    row_count = inputs.shape[0]
    width = inputs.shape[1]
    head_size = width // HEADS
    scaling = head_size ** (-0.5)
    count = lax.axis_size(SEQ)
    groups = lax.axis_size("exp")
    team = lax.axis_size(TEAM)
    position = lax.axis_index(SEQ)
    length = count * row_count
    weight_rows = projection.shape[0]
    first_heads, active_table = head_plan(count)
    starts = [int(head) * head_size for head in first_heads]
    active = lax.dynamic_index_in_dim(jnp.asarray(active_table), position, 0, keepdims=False)
    gain_first = norm_gains[0]
    gain_second = norm_gains[1]
    used = active_table.any(axis=2)

    scale_first = lax.rsqrt(jnp.mean(inputs * inputs, axis=-1, keepdims=True) + EPSILON)
    normed_first = inputs * scale_first
    attend_in = (normed_first * gain_first).astype(BF16)
    row_blocks, order = gather_row(attend_in)
    projection_low = projection.astype(BF16)
    sent_rows = weight_rows + 8
    own_documents = jnp.zeros((8, 3 * LANES + width), BF16)
    own_documents = own_documents.at[0, :row_count].set(segment_ids[0].astype(BF16))
    output_low = output_weight.astype(BF16)
    pieces = [
        jnp.concatenate(
            [projection_low[:, k * width + s : k * width + s + LANES] for k in range(3)]
            + [output_low],
            axis=1,
        )
        for s in starts
    ]
    got_rows = swap(
        jnp.stack([jnp.concatenate([piece, own_documents], axis=0) for piece in pieces]), SEQ
    )
    documents = jnp.broadcast_to(
        got_rows[:, weight_rows, :row_count].reshape(length, 1), (length, LANES)
    )

    def all_rows(value):
        copies = jnp.broadcast_to(value[None], (groups, *value.shape))
        return jnp.swapaxes(swap(copies, EXP), 0, 1).reshape(width, value.shape[-1])

    columns = all_rows(got_rows[:, :weight_rows, : 3 * LANES])
    columns, output_rows = together(columns, got_rows[:, :weight_rows, 3 * LANES :])
    output_full = all_rows(output_rows)
    slots = groups * CAP
    chosen = expert_ids[0, :, 0]
    one_hot = (chosen[:, None] == jnp.arange(groups, dtype=jnp.int32)[None, :]).astype(jnp.int32)
    rank = jnp.sum(jnp.cumsum(one_hot, axis=0) * one_hot, axis=1) - 1
    target = chosen * CAP + rank
    placing = (target[:, None] == jnp.arange(slots, dtype=jnp.int32)[None, :]).astype(BF16)

    def to_slots(values):
        outgoing = jnp.einsum("ts,td->sd", placing, values, preferred_element_type=F32)
        return outgoing.astype(BF16)

    def dispatch(outgoing):
        outgoing = jnp.broadcast_to(
            outgoing.reshape(1, groups, CAP, width), (team, groups, CAP, width)
        )
        return swap(outgoing.reshape(team * groups, CAP, width), TEAM + EXP).reshape(
            team * slots, width
        )

    def send_back(values):
        return swap(values.reshape(team * groups, CAP, width), TEAM + EXP).reshape(
            team, slots, width
        )

    def collect(returned):
        return jnp.einsum("ts,jsd->td", placing, returned, preferred_element_type=F32)

    own_up = expert_up[0].astype(BF16)
    own_down = expert_down[0].astype(BF16)
    last_far = max(len(row_blocks) - 2, 0)
    row_blocks[last_far], own_up, own_down = together(row_blocks[last_far], own_up, own_down)
    *row_blocks, output_full, grad_slots_out = together(
        *row_blocks, output_full, to_slots(cotangent[0])
    )
    grad_arrived = dispatch(grad_slots_out)

    peer_up = others(own_up, "hi")
    peer_down = others(own_down, "hi")
    projection_full = lax.all_gather(projection_low, ALL, axis=0, tiled=True)

    mixed_low, mixed_full, stat, pair = attend(
        active, order, row_blocks, columns, documents, row_count
    )

    def place_heads():
        index = np.arange(LANES)
        matrix = np.zeros((count, LANES, width), np.float32)
        for device in range(count):
            for slot in range(2):
                if used[device, slot]:
                    own = index[slot * HALF : (slot + 1) * HALF]
                    matrix[device, own, starts[device] + own] = 1.0
        return jnp.asarray(matrix, BF16)

    head_places = place_heads()

    def to_tokens(values):
        return swap(values.reshape(count, row_count, values.shape[1]), SEQ)

    mixed_low, grad_arrived, peer_up, peer_down = together(
        mixed_low, grad_arrived, peer_up, peer_down
    )
    near_up = jnp.concatenate([own_up, peer_up], axis=0)
    near_down = jnp.concatenate([own_down, peer_down], axis=0)
    far_up = others(near_up, "in")
    far_down = others(near_down, "in")
    attend_out = jnp.einsum(
        "jtc,jcd->td",
        to_tokens(mixed_low),
        head_places,
        preferred_element_type=F32,
    ).astype(BF16)
    branch = jnp.dot(attend_out, output_full, preferred_element_type=F32)
    middle = inputs + branch
    scale_second = lax.rsqrt(jnp.mean(middle * middle, axis=-1, keepdims=True) + EPSILON)
    normed_second = middle * scale_second
    expert_in = (normed_second * gain_second).astype(BF16)

    expert_slots, far_up = together(to_slots(expert_in), far_up)
    arrived, projection_full = together(dispatch(expert_slots), projection_full)
    active_near, hidden_near, total_near = expert_part(
        arrived, grad_arrived, near_up, near_down, None
    )
    active_far, hidden_far, grad_slots = expert_part(
        arrived, grad_arrived, far_up, far_down, total_near
    )
    returned_grad = send_back(grad_slots)
    down_far, up_far = unit_grads(active_far, grad_arrived, hidden_far, arrived, BF16)
    (down_part,) = to_owners([down_far], "in")
    down_near, up_near = unit_grads(active_near, grad_arrived, hidden_near, arrived, F32)
    produced = sum(
        jnp.einsum("sh,hd->sd", active_units, matrix, preferred_element_type=F32)
        for active_units, matrix in ((active_near, near_down), (active_far, far_down))
    ).astype(BF16)
    peers = lax.axis_size("hi")
    returned_grad, down_part, up_far, produced = together(
        returned_grad, down_part, up_far, produced
    )
    (up_part,) = to_owners([up_far], "in")
    grad_expert_in = collect(returned_grad)

    def hi_parts(near):
        return to_owners(list(near.astype(BF16).reshape(peers, -1, width))[1:], "hi")

    def hi_sum(near, parts):
        return add_all(near[: near.shape[0] // peers], parts)[None]

    down_near = add_all(down_near, [down_part])
    down_parts = hi_parts(down_near)

    scaled_second = grad_expert_in * gain_second
    gain_second_part = jnp.sum(grad_expert_in * normed_second, axis=0)
    grad_middle = scale_second * (
        scaled_second
        - normed_second * jnp.mean(scaled_second * normed_second, axis=-1, keepdims=True)
    )
    residual_grad = upstream + grad_middle
    branch_grad = residual_grad.astype(BF16)
    grad_mixed = jnp.einsum(
        "td,ed->te", branch_grad, output_full, preferred_element_type=F32
    ).astype(BF16)

    sent_grad = jnp.stack([grad_mixed[:, s : s + LANES] for s in starts])
    row_grad = swap(sent_grad, SEQ).reshape(length, LANES)
    row_grad, produced, up_part, *down_parts = together(row_grad, produced, up_part, *down_parts)
    down_grad = hi_sum(down_near, down_parts)
    up_near = add_all(up_near, [up_part])
    up_parts = hi_parts(up_near)
    returned = send_back(produced)
    grad_qkv, grad_lying = attend_back(
        active, order, pair, documents, stat, row_grad, mixed_full, row_count, scaling
    )
    grad_qkv, grad_lying, returned, *up_parts = together(
        grad_qkv, grad_lying, returned, *up_parts
    )
    up_grad = hi_sum(up_near, up_parts)
    block_output = (middle + collect(returned)).astype(BF16)[None]

    row_in = jnp.concatenate(row_blocks, axis=0)
    column_term = jnp.einsum("tc,te->ce", row_in, grad_lying, preferred_element_type=F32)
    output_term = jnp.einsum("tc,te->ce", attend_out, branch_grad, preferred_element_type=F32)
    dense_parts = jnp.concatenate([column_term.astype(BF16), output_term.astype(BF16)], axis=1)
    dense_parts = jnp.swapaxes(dense_parts.reshape(count, groups, weight_rows, -1), 0, 1)
    group = lax.axis_index(EXP)
    own_rows, *other_rows = [
        lax.dynamic_index_in_dim(dense_parts, lax.rem(group + step, groups), 0, keepdims=False)
        for step in range(groups)
    ]
    other_rows = to_owners(other_rows, "exp")
    grad_pieces, *other_rows = together(to_tokens(grad_qkv), *other_rows)
    dense_rows = add_all(own_rows, other_rows).astype(BF16)
    grad_projected = jnp.concatenate(
        [
            jnp.einsum(
                "jtc,jcd->td",
                grad_pieces[:, :, k * LANES : (k + 1) * LANES],
                head_places,
                preferred_element_type=F32,
            ).astype(BF16)
            for k in range(3)
        ],
        axis=1,
    )
    grad_attend_in = jnp.einsum(
        "tc,dc->td", grad_projected, projection_full, preferred_element_type=F32
    )
    scaled_first = grad_attend_in * gain_first
    gain_first_part = jnp.sum(grad_attend_in * normed_first, axis=0)
    input_grad = (
        residual_grad
        + scale_first
        * (
            scaled_first
            - normed_first * jnp.mean(scaled_first * normed_first, axis=-1, keepdims=True)
        )
    )[None]

    got_terms = swap(dense_rows, SEQ).astype(F32)
    column_sums = got_terms[:, :, : 3 * LANES]
    output_grad = jnp.sum(got_terms[:, :, 3 * LANES :], axis=0)
    head_grads = []
    for k in range(3):
        for head in range(HEADS):
            parts = [
                column_sums[j, :, k * LANES + slot * HALF : k * LANES + (slot + 1) * HALF]
                for j in range(count)
                for slot in range(2)
                if used[j, slot] and first_heads[j] + slot == head
            ]
            head_grads.append(functools.reduce(jnp.add, parts))
    projection_grad = jnp.concatenate(head_grads, axis=1)

    local_square = jnp.sum(projection_grad * projection_grad) + jnp.sum(output_grad * output_grad)
    local_square = local_square + jnp.sum(up_grad * up_grad) + jnp.sum(down_grad * down_grad)
    summed = spread_sum(
        jnp.concatenate(
            [gain_first_part, gain_second_part, jnp.broadcast_to(local_square, (LANES,))]
        )[None]
    )[0]
    gains_grad = summed[: 2 * width].reshape(2, width)
    grad_norm = jnp.sqrt(summed[2 * width] + jnp.sum(gains_grad * gains_grad))
    factor = jnp.minimum(1.0, CLIP / (grad_norm + 1e-06))
    (
        (projection_moment, projection_square, projection_new),
        (output_moment, output_square, output_new),
        (up_moment, up_square, up_new),
        (down_moment, down_square, down_new),
    ) = adam_all(
        factor,
        [
            (projection, projection_grad, projection_first, projection_second),
            (output_weight, output_grad, output_first, output_second),
            (expert_up, up_grad, up_first, up_second),
            (expert_down, down_grad, down_first, down_second),
        ],
        (RATE_MATRIX, RATE_OUTPUT, RATE_MATRIX, RATE_MATRIX),
        3,
    )
    gains_moment, gains_square, gains_new = adam_update(
        norm_gains, gains_grad, gains_first, gains_second, factor, RATE_GAIN, 0.0
    )
    return (
        block_output,
        input_grad,
        grad_norm,
        projection_grad,
        projection_moment,
        projection_square,
        projection_new,
        output_grad,
        output_moment,
        output_square,
        output_new,
        up_grad,
        up_moment,
        up_square,
        up_new,
        down_grad,
        down_moment,
        down_square,
        down_new,
        gains_grad,
        gains_moment,
        gains_square,
        gains_new,
    )


def solution(mesh):
    token = P("exp", SEQ, None)
    dense = P(ALL, None)
    expert = P("exp", SEQ, None)
    in_specs = (
        (token, token, P("exp", SEQ), token)
        + (dense, dense, expert, expert, P())
        + (dense,) * 4
        + (expert,) * 4
        + (P(), P())
    )
    out_specs = (token, token, P()) + (dense,) * 8 + (expert,) * 8 + (P(),) * 4
    rows, groups = mesh.devices.shape
    fine = Mesh(mesh.devices.reshape(rows // 4, 2, 2, groups), ALL)
    return jax.shard_map(body, mesh=fine, in_specs=in_specs, out_specs=out_specs, check_vma=False)
```

```python
import functools
import math

import jax
import jax.numpy as jnp
import numpy as np
from jax import lax
from jax.experimental import pallas as pl
from jax.experimental.pallas import tpu as pltpu
from jax.sharding import Mesh
from jax.sharding import PartitionSpec as P

HEADS = 12
CAP = 128
STEP = 10


EPSILON = 1e-05
CLIP = 1.0
BETA_ONE = 0.9
BETA_TWO = 0.99
ADAM_FLOOR = 1e-08
DECAY = 0.1
RATE_MATRIX = 0.04
RATE_OUTPUT = 0.1
RATE_GAIN = 0.5

SEQ = ("hi", "lo", "in")
EXP = ("exp",)
ALL = SEQ + EXP
TEAM = ("lo",)
SHARE = ("hi", "in")
LANES = 128
HALF = 64
FAR = -1e30
BF16 = jnp.bfloat16
F32 = jnp.float32
VMEM_LIMIT = 60 * 1024 * 1024


def head_plan(count):
    whole = math.lcm(HEADS, count)
    units, parts = whole // count, whole // HEADS
    first = np.zeros((count,), np.int64)
    active = np.zeros((count, 2, count), np.int32)
    for device in range(count):
        first[device] = min(units * device // parts, HEADS - 2)
        for unit in range(units * device, units * (device + 1)):
            slot = unit // parts - first[device]
            for block in range(count):
                turn = block % (2 * parts)
                if min(turn, 2 * parts - 1 - turn) == unit % parts:
                    active[device, slot, block] = 1
    return first, active


def three_parts(value):
    high = value.astype(BF16).astype(F32)
    middle = (value - high).astype(BF16).astype(F32)
    return high, middle, value - high - middle


def contract(left, right, left_axis, right_axis):
    return lax.dot_general(
        left, right, (((left_axis,), (right_axis,)), ((), ())), preferred_element_type=F32
    )


def slot_arrays(packed, documents, kind, slot):
    spare = HALF - HALF * slot
    lane = lax.broadcasted_iota(jnp.int32, packed.shape, 1)
    own = (lane < HALF) if slot == 0 else (lane >= HALF)
    place = (lane - spare).astype(F32)
    ours = place == documents
    first = (lane >= spare) & (lane < spare + 3)
    if kind == "query":
        extra = jnp.where(first & jnp.logical_not(ours), FAR, 0.0)
    elif kind == "key":
        extra = jnp.where(ours | ((lane >= spare + 3) & (lane < spare + 6)), 1.0, 0.0)
    else:
        extra = jnp.where(first, 1.0, 0.0)
    return jnp.where(own, packed, extra).astype(BF16)


def fill_slots(packed_of, documents_ref, wide_ref, kinds, place):
    documents = documents_ref[place, :].astype(F32)
    for number, kind in enumerate(kinds):
        packed = packed_of(kind).astype(F32)
        if kind == "query":
            packed = packed * 0.125
        for slot in range(2):
            column = (2 * number + slot) * LANES
            wide_ref[place, column : column + LANES] = slot_arrays(packed, documents, kind, slot)


def attend_kernel(active_ref, order_ref, *refs, block, chunk, held):
    row_refs = refs[:held]
    columns_ref, documents_ref = refs[held : held + 2]
    low_ref, full_ref, stat_ref, pair_ref, mixed_ref, wide_ref = refs[held + 2 :]
    at = pl.program_id(0)

    @pl.when(at == 0)
    def _():
        def fill(tokens, index):
            place = pl.ds(pl.multiple_of(order_ref[index] * block, block), block)
            packed = contract(tokens, columns_ref[...], 1, 0).astype(BF16)
            pair_ref[place, :] = packed[:, LANES:]
            parts = {
                kind: packed[:, part * LANES : (part + 1) * LANES]
                for part, kind in enumerate(("query", "key", "value"))
            }
            fill_slots(parts.get, documents_ref, wide_ref, tuple(parts), place)

        if held > 1:
            for index, row_ref in enumerate(row_refs):
                fill(row_ref[...], index)
        else:

            @pl.loop(0, pl.num_programs(0))
            def _(index):
                fill(row_refs[0][pl.ds(pl.multiple_of(index * block, block), block), :], index)

    rows = pl.ds(pl.multiple_of(at * block, block), block)
    lane = lax.broadcasted_iota(jnp.int32, (block, LANES), 1)
    last = lax.div(at * block, chunk)
    for slot in range(2):
        spare = HALF - HALF * slot
        own = (lane < HALF) if slot == 0 else (lane >= HALF)
        columns = slice(slot * LANES, (slot + 1) * LANES)

        @pl.when(active_ref[slot, at] != 0)
        def _():
            query = wide_ref[rows, columns]

            def step(index, carry, edge):
                top, weighted = carry
                place = pl.ds(pl.multiple_of(index * chunk, chunk), chunk)
                keys = wide_ref[place, 2 * LANES + slot * LANES : 3 * LANES + slot * LANES]
                values = wide_ref[place, 4 * LANES + slot * LANES : 5 * LANES + slot * LANES]
                scores = contract(query, keys, 1, 1)
                if edge:
                    key_at = index * chunk + lax.broadcasted_iota(jnp.int32, (block, chunk), 1)
                    query_at = at * block + lax.broadcasted_iota(jnp.int32, (block, chunk), 0)
                    scores = jnp.where(key_at <= query_at, scores, FAR)
                new_top = jnp.maximum(top, jnp.max(scores, axis=1, keepdims=True))
                weights = jnp.exp(scores - new_top).astype(BF16)
                weighted = weighted * jnp.exp(top - new_top) + contract(weights, values, 1, 0)
                return new_top, weighted

            carry = (jnp.full((block, 1), FAR, F32), jnp.zeros((block, LANES), F32))
            carry = lax.fori_loop(0, last, lambda index, state: step(index, state, False), carry)
            top, weighted = step(last, carry, True)
            total = weighted[:, spare : spare + 1]
            mixed_ref[slot] = jnp.where(own, weighted / total, 0.0)
            log_total = top + jnp.log(total)
            high, middle, small = three_parts(log_total)
            extra = jnp.where(lane == spare + 3, -high, 0.0)
            extra = jnp.where(lane == spare + 4, -middle, extra)
            extra = jnp.where(lane == spare + 5, -small, extra)
            stat_ref[:, columns] = (query.astype(F32) + extra).astype(BF16)

        @pl.when(active_ref[slot, at] == 0)
        def _():
            mixed_ref[slot] = jnp.zeros((block, LANES), F32)
            stat_ref[:, columns] = jnp.zeros((block, LANES), BF16)

    mixed = mixed_ref[0] + mixed_ref[1]
    full_ref[...] = mixed
    low_ref[...] = mixed.astype(BF16)


def attend_back_kernel(
    active_ref,
    order_ref,
    pair_ref,
    documents_ref,
    stat_ref,
    grad_ref,
    mixed_ref,
    out_ref,
    lying_ref,
    key_sum_ref,
    value_sum_ref,
    query_sum_ref,
    wide_ref,
    *,
    block,
    chunk,
    scaling,
):
    at = pl.program_id(0)
    rows = pl.ds(pl.multiple_of(at * block, block), block)
    lane = lax.broadcasted_iota(jnp.int32, (block, LANES), 1)
    last = lax.div(at * block, chunk)

    @pl.when(at == 0)
    def _():
        @pl.loop(0, pl.num_programs(0))
        def _(index):
            place = pl.ds(pl.multiple_of(index * block, block), block)
            parts = {"key": pair_ref[place, :LANES], "value": pair_ref[place, LANES:]}
            fill_slots(parts.get, documents_ref, wide_ref, tuple(parts), place)

        key_sum_ref[...] = jnp.zeros_like(key_sum_ref)
        value_sum_ref[...] = jnp.zeros_like(value_sum_ref)

    for slot in range(2):
        spare = HALF - HALF * slot
        own = (lane < HALF) if slot == 0 else (lane >= HALF)
        columns = slice(slot * LANES, (slot + 1) * LANES)
        query_sum_ref[slot] = jnp.zeros((block, LANES), F32)

        @pl.when(active_ref[slot, at] != 0)
        def _():
            query = stat_ref[:, columns]
            grad = grad_ref[...].astype(F32)
            delta = jnp.sum(jnp.where(own, grad * mixed_ref[...], 0.0), axis=1, keepdims=True)
            high, middle, small = three_parts(delta)
            extra = jnp.where(lane == spare, -high, 0.0)
            extra = jnp.where(lane == spare + 1, -middle, extra)
            extra = jnp.where(lane == spare + 2, -small, extra)
            grad_low = jnp.where(own, grad, extra).astype(BF16)

            def step(index, edge):
                place = pl.ds(pl.multiple_of(index * chunk, chunk), chunk)
                keys = wide_ref[place, slot * LANES : (slot + 1) * LANES]
                values = wide_ref[place, (2 + slot) * LANES : (3 + slot) * LANES]
                scores = contract(keys, query, 1, 1)
                if edge:
                    key_at = index * chunk + lax.broadcasted_iota(jnp.int32, (chunk, block), 0)
                    query_at = at * block + lax.broadcasted_iota(jnp.int32, (chunk, block), 1)
                    scores = jnp.where(key_at <= query_at, scores, FAR)
                weights = jnp.exp(scores)
                grad_weights = contract(values, grad_low, 1, 1)
                grad_scores = (weights * grad_weights).astype(BF16)
                value_sum_ref[slot, place, :] += contract(weights.astype(BF16), grad_low, 1, 0)
                key_sum_ref[slot, place, :] += contract(grad_scores, query, 1, 0)
                query_sum_ref[slot] += contract(grad_scores, keys, 0, 0)

            @pl.loop(0, last)
            def _(index):
                step(index, False)

            step(last, True)

    first_half = lane < HALF
    query_grad = jnp.where(first_half, query_sum_ref[0], query_sum_ref[1]) * scaling
    out_ref[rows, :LANES] = query_grad.astype(BF16)
    lying = pl.ds(pl.multiple_of(order_ref[at] * block, block), block)
    lying_ref[lying, :LANES] = query_grad.astype(BF16)

    @pl.when(at == pl.num_programs(0) - 1)
    def _():
        @pl.loop(0, pl.num_programs(0))
        def _(index):
            place = pl.ds(pl.multiple_of(index * block, block), block)
            key_grad = jnp.where(first_half, key_sum_ref[0, place, :], key_sum_ref[1, place, :])
            value_grad = jnp.where(
                first_half, value_sum_ref[0, place, :], value_sum_ref[1, place, :]
            )
            out_ref[place, LANES : 2 * LANES] = key_grad.astype(BF16)
            out_ref[place, 2 * LANES :] = value_grad.astype(BF16)
            lying = pl.ds(pl.multiple_of(order_ref[index] * block, block), block)
            lying_ref[lying, LANES : 2 * LANES] = key_grad.astype(BF16)
            lying_ref[lying, 2 * LANES :] = value_grad.astype(BF16)


def whole(value):
    return pl.BlockSpec(value.shape, lambda i, *unused: (0, 0), pipeline_mode=pl.Buffered(1))


SMALL = pl.CostEstimate(flops=1, bytes_accessed=1, transcendentals=0)


def attend(active, order, row_blocks, columns, documents, block):
    length = documents.shape[0]
    pair = jax.ShapeDtypeStruct((length, 2 * LANES), BF16)
    return pl.pallas_call(
        functools.partial(attend_kernel, block=block, chunk=2 * block, held=len(row_blocks)),
        grid_spec=pltpu.PrefetchScalarGridSpec(
            num_scalar_prefetch=2,
            grid=(length // block,),
            in_specs=[whole(value) for value in (*row_blocks, columns, documents)],
            out_specs=[
                pl.BlockSpec((block, LANES), lambda i, a, o: (i, 0)),
                pl.BlockSpec((block, LANES), lambda i, a, o: (i, 0)),
                pl.BlockSpec((block, 2 * LANES), lambda i, a, o: (i, 0)),
                whole(pair),
            ],
            scratch_shapes=[
                pltpu.VMEM((2, block, LANES), F32),
                pltpu.VMEM((length, 6 * LANES), BF16),
            ],
        ),
        out_shape=[
            jax.ShapeDtypeStruct((length, LANES), BF16),
            jax.ShapeDtypeStruct((length, LANES), F32),
            jax.ShapeDtypeStruct((length, 2 * LANES), BF16),
            pair,
        ],
        compiler_params=pltpu.CompilerParams(vmem_limit_bytes=VMEM_LIMIT),
        cost_estimate=SMALL,
    )(active, order, *row_blocks, columns, documents)


def attend_back(active, order, pair, documents, stat, grad, mixed, block, scaling):
    length = pair.shape[0]
    count = length // block
    return pl.pallas_call(
        functools.partial(attend_back_kernel, block=block, chunk=2 * block, scaling=scaling),
        grid_spec=pltpu.PrefetchScalarGridSpec(
            num_scalar_prefetch=2,
            grid=(count,),
            in_specs=[
                whole(pair),
                whole(documents),
                pl.BlockSpec((block, 2 * LANES), lambda i, a, o: (i, 0)),
                pl.BlockSpec((block, LANES), lambda i, a, o: (i, 0)),
                pl.BlockSpec((block, LANES), lambda i, a, o: (i, 0)),
            ],
            out_specs=[
                pl.BlockSpec(
                    (length, 3 * LANES), lambda i, a, o: (0, 0), pipeline_mode=pl.Buffered(1)
                )
            ]
            * 2,
            scratch_shapes=[
                pltpu.VMEM((2, length, LANES), F32),
                pltpu.VMEM((2, length, LANES), F32),
                pltpu.VMEM((2, block, LANES), F32),
                pltpu.VMEM((length, 4 * LANES), BF16),
            ],
        ),
        out_shape=[jax.ShapeDtypeStruct((length, 3 * LANES), BF16)] * 2,
        compiler_params=pltpu.CompilerParams(vmem_limit_bytes=VMEM_LIMIT),
        cost_estimate=SMALL,
    )(active, order, pair, documents, stat, grad, mixed)


def expert_kernel(arrived_ref, grad_ref, *refs, count):
    up_refs, down_refs = refs[:count], refs[count : 2 * count]
    total_ref = refs[2 * count]
    active_refs, hidden_refs = refs[2 * count + 1 : 3 * count + 1], refs[3 * count + 1 :]
    arrived, grad_arrived = arrived_ref[...], grad_ref[...]
    scale = math.sqrt(2.0 / math.pi)
    total = jnp.zeros(total_ref.shape, F32)
    for up_ref, down_ref, active_ref, hidden_ref in zip(
        up_refs, down_refs, active_refs, hidden_refs, strict=True
    ):
        up = up_ref[...]
        hidden = contract(arrived, up, 1, 1)
        squared = hidden * hidden
        bend = jnp.tanh(scale * hidden * (1.0 + 0.044715 * squared))
        half = 0.5 + 0.5 * bend
        active_ref[...] = (hidden * half).astype(BF16)
        slope = half + (0.5 * scale) * hidden * (1.0 - bend * bend) * (1.0 + 3 * 0.044715 * squared)
        grad_hidden = (slope * contract(grad_arrived, down_ref[...], 1, 1)).astype(BF16)
        hidden_ref[...] = grad_hidden
        total = total + contract(grad_hidden, up, 1, 0)
    total_ref[...] = total.astype(BF16)


def rows_spec(value, block):
    return pl.BlockSpec((block, value.shape[1]), lambda i: (i, 0))


def expert_part(arrived, grad_arrived, ups, downs):
    slots, width = arrived.shape
    block = 256
    units = [jax.ShapeDtypeStruct((slots, up.shape[0]), BF16) for up in ups]
    outs = [jax.ShapeDtypeStruct((slots, width), BF16), *units, *units]
    total, *parts = pl.pallas_call(
        functools.partial(expert_kernel, count=len(ups)),
        grid=(slots // block,),
        in_specs=[rows_spec(arrived, block), rows_spec(grad_arrived, block)]
        + [whole(value) for value in (*ups, *downs)],
        out_specs=[rows_spec(out, block) for out in outs],
        out_shape=outs,
        compiler_params=pltpu.CompilerParams(vmem_limit_bytes=VMEM_LIMIT),
        cost_estimate=SMALL,
    )(arrived, grad_arrived, *ups, *downs)
    return total, parts[: len(ups)], parts[len(ups) :]


def produced_kernel(*refs, count):
    total = contract(refs[0][...], refs[count][...], 1, 0)
    for index in range(1, count):
        total = total + contract(refs[index][...], refs[count + index][...], 1, 0)
    refs[-1][...] = total.astype(BF16)


def produced_part(actives, downs):
    slots, width = actives[0].shape[0], downs[0].shape[1]
    block = 256
    out = jax.ShapeDtypeStruct((slots, width), BF16)
    return pl.pallas_call(
        functools.partial(produced_kernel, count=len(actives)),
        grid=(slots // block,),
        in_specs=[rows_spec(value, block) for value in actives] + [whole(down) for down in downs],
        out_specs=rows_spec(out, block),
        out_shape=out,
        compiler_params=pltpu.CompilerParams(vmem_limit_bytes=VMEM_LIMIT),
        cost_estimate=SMALL,
    )(*actives, *downs)


def unit_kernel(active_ref, grad_ref, hidden_ref, arrived_ref, down_ref, up_ref):
    down_ref[...] = contract(active_ref[...], grad_ref[...], 0, 0).astype(down_ref.dtype)
    up_ref[...] = contract(hidden_ref[...], arrived_ref[...], 0, 0).astype(up_ref.dtype)


def unit_grads(active, grad_arrived, grad_hidden, arrived, kind):
    slots, units = active.shape
    width = arrived.shape[1]
    block = LANES if units % LANES == 0 else units
    left = pl.BlockSpec((slots, block), lambda i: (0, i))
    out = pl.BlockSpec((block, width), lambda i: (i, 0))
    return pl.pallas_call(
        unit_kernel,
        grid=(units // block,),
        in_specs=[left, whole(grad_arrived), left, whole(arrived)],
        out_specs=[out, out],
        out_shape=[jax.ShapeDtypeStruct((units, width), kind)] * 2,
        compiler_params=pltpu.CompilerParams(vmem_limit_bytes=VMEM_LIMIT),
        cost_estimate=SMALL,
    )(active, grad_arrived, grad_hidden, arrived)


def dense_kernel(*refs, held):
    row_refs = refs[:held]
    lying_ref, attend_ref, branch_ref, out_ref = refs[held:]
    start, total = 0, None
    for row_ref in row_refs:
        rows = row_ref.shape[0]
        part = contract(row_ref[...], lying_ref[start : start + rows, :], 0, 0)
        total = part if total is None else total + part
        start += rows
    out_ref[:, : 3 * LANES] = total.astype(BF16)
    out_ref[:, 3 * LANES :] = contract(attend_ref[...], branch_ref[...], 0, 0).astype(BF16)


def dense_terms(row_blocks, grad_lying, attend_out, branch_grad):
    width = attend_out.shape[1]
    block = 256

    def columns(value):
        return pl.BlockSpec((value.shape[0], block), lambda i: (0, i))

    out = jax.ShapeDtypeStruct((width, 3 * LANES + width), BF16)
    return pl.pallas_call(
        functools.partial(dense_kernel, held=len(row_blocks)),
        grid=(width // block,),
        in_specs=[columns(value) for value in row_blocks]
        + [whole(grad_lying), columns(attend_out), whole(branch_grad)],
        out_specs=rows_spec(out, block),
        out_shape=out,
        compiler_params=pltpu.CompilerParams(vmem_limit_bytes=VMEM_LIMIT),
        cost_estimate=SMALL,
    )(*row_blocks, grad_lying, attend_out, branch_grad)


def adam_update(weight, grad, first, second, factor, rate, decay):
    clipped = grad * factor
    first_new = BETA_ONE * first + (1.0 - BETA_ONE) * clipped
    second_new = BETA_TWO * second + (1.0 - BETA_TWO) * clipped * clipped
    first_hat = first_new / (1.0 - BETA_ONE**STEP)
    second_hat = second_new / (1.0 - BETA_TWO**STEP)
    weight_new = weight - rate * (first_hat / (jnp.sqrt(second_hat) + ADAM_FLOOR) + decay * weight)
    return (first_new, second_new, weight_new)


def together(*values):
    return lax.optimization_barrier(values)


def swap(value, axes):
    return lax.all_to_all(value, axes, split_axis=0, concat_axis=0, tiled=True)


def adam_kernel(factor_ref, *refs, rates):
    count = len(rates)
    factor = factor_ref[0]
    for index, rate in enumerate(rates):
        weight, grad, first, second = [ref[...] for ref in refs[4 * index : 4 * index + 4]]
        outs = refs[4 * count + 3 * index : 4 * count + 3 * index + 3]
        for out, value in zip(
            outs, adam_update(weight, grad, first, second, factor, rate, DECAY), strict=True
        ):
            out[...] = value


def adam_all(factor, leaves, rates, steps):
    flat = [value.reshape(value.shape[-2:]) for leaf in leaves for value in leaf]

    def spec(value):
        rows, columns = value.shape
        if rows % (8 * steps) == 0:
            return pl.BlockSpec((rows // steps, columns), lambda i: (i, 0))
        lanes = columns // steps
        return pl.BlockSpec((rows, lanes), lambda i: (0, i))

    shapes = [jax.ShapeDtypeStruct(value.shape, F32) for value in flat[::4] for _ in range(3)]
    outs = pl.pallas_call(
        functools.partial(adam_kernel, rates=rates),
        grid=(steps,),
        in_specs=[pl.BlockSpec(memory_space=pltpu.SMEM)] + [spec(value) for value in flat],
        out_specs=[spec(shape) for shape in shapes],
        out_shape=shapes,
        compiler_params=pltpu.CompilerParams(vmem_limit_bytes=VMEM_LIMIT),
        cost_estimate=pl.CostEstimate(
            flops=20 * sum(value.size for value in flat[::4]),
            bytes_accessed=28 * sum(value.size for value in flat[::4]),
            transcendentals=0,
        ),
    )(factor.reshape(1), *flat)
    return [
        [out.reshape(leaf[0].shape) for out in outs[3 * index : 3 * index + 3]]
        for index, leaf in enumerate(leaves)
    ]


def flip(value, bits):
    count = lax.axis_size(SEQ)
    return lax.ppermute(value, SEQ, [(index, index ^ bits) for index in range(count)])


def others(value, axis):
    size = lax.axis_size(axis)
    parts = [
        lax.ppermute(value, axis, [((i + step) % size, i) for i in range(size)])
        for step in range(1, size)
    ]
    return parts[0] if size == 2 else jnp.concatenate(parts, axis=0)


def to_owners(blocks, axis):
    size = lax.axis_size(axis)
    return [
        lax.ppermute(block, axis, [(i, (i + step) % size) for i in range(size)])
        for step, block in enumerate(blocks, 1)
    ]


def add_all(own, parts):
    return functools.reduce(lambda total, part: total + part.astype(F32), parts, own.astype(F32))


def spread_sum(value):
    count = lax.axis_size(ALL)
    return jnp.sum(swap(jnp.broadcast_to(value[None], (count, *value.shape)), ALL), axis=0)


def body(
    tokens,
    cotangent,
    segment_ids,
    expert_ids,
    projection,
    output_weight,
    expert_up,
    expert_down,
    norm_gains,
    projection_first,
    projection_second,
    output_first,
    output_second,
    up_first,
    up_second,
    down_first,
    down_second,
    gains_first,
    gains_second,
):
    inputs = tokens[0].astype(F32)
    upstream = cotangent[0].astype(F32)
    row_count = inputs.shape[0]
    width = inputs.shape[1]
    head_size = width // HEADS
    scaling = head_size ** (-0.5)
    count = lax.axis_size(SEQ)
    groups = lax.axis_size("exp")
    team = lax.axis_size(TEAM)
    position = lax.axis_index(SEQ)
    length = count * row_count
    weight_rows = projection.shape[0]
    first_heads, active_table = head_plan(count)
    starts = [int(head) * head_size for head in first_heads]
    active = lax.dynamic_index_in_dim(jnp.asarray(active_table), position, 0, keepdims=False)
    gain_first = norm_gains[0]
    gain_second = norm_gains[1]
    used = active_table.any(axis=2)

    scale_first = lax.rsqrt(jnp.mean(inputs * inputs, axis=-1, keepdims=True) + EPSILON)
    normed_first = inputs * scale_first
    attend_in = (normed_first * gain_first).astype(BF16)
    projection_low = projection.astype(BF16)
    sent_rows = weight_rows + 8
    own_documents = jnp.zeros((8, 3 * LANES + width), BF16)
    own_documents = own_documents.at[0, :row_count].set(segment_ids[0].astype(BF16))
    output_low = output_weight.astype(BF16)
    pieces = [
        jnp.concatenate(
            [projection_low[:, k * width + s : k * width + s + LANES] for k in range(3)]
            + [output_low],
            axis=1,
        )
        for s in starts
    ]
    pieces = jnp.stack([jnp.concatenate([piece, own_documents], axis=0) for piece in pieces])
    pairwise = count == 8
    if pairwise:
        order = jnp.arange(count, dtype=jnp.int32) ^ position
        held = [attend_in, flip(attend_in, 2), flip(attend_in, 4), flip(attend_in, 6)]
        pieces, held[1] = together(pieces, held[1])
        got_rows = swap(pieces, SEQ)
        got_rows, held[2] = together(got_rows, held[2])
    else:
        order = jnp.arange(count, dtype=jnp.int32)
        held = [lax.all_gather(attend_in, SEQ, axis=0, tiled=True)]
        got_rows = swap(pieces, SEQ)
    documents = jnp.broadcast_to(
        got_rows[:, weight_rows, :row_count].reshape(length, 1), (length, LANES)
    )

    def all_rows(value):
        copies = jnp.broadcast_to(value[None], (groups, *value.shape))
        return jnp.swapaxes(swap(copies, EXP), 0, 1).reshape(width, value.shape[-1])

    columns = all_rows(got_rows[:, :weight_rows, : 3 * LANES])
    own_up = expert_up[0].astype(BF16)
    own_down = expert_down[0].astype(BF16)
    columns, output_rows, held[-1], own_up, own_down = together(
        columns, got_rows[:, :weight_rows, 3 * LANES :], held[-1], own_up, own_down
    )
    output_full = all_rows(output_rows)
    row_blocks = [part for block in held for part in (block, flip(block, 1))] if pairwise else held

    slots = groups * CAP
    chosen = expert_ids[0, :, 0]
    one_hot = (chosen[:, None] == jnp.arange(groups, dtype=jnp.int32)[None, :]).astype(jnp.int32)
    rank = jnp.sum(jnp.cumsum(one_hot, axis=0) * one_hot, axis=1) - 1
    target = chosen * CAP + rank
    placing = (target[:, None] == jnp.arange(slots, dtype=jnp.int32)[None, :]).astype(BF16)

    def to_slots(values):
        outgoing = jnp.einsum("ts,td->sd", placing, values, preferred_element_type=F32)
        return outgoing.astype(BF16)

    def dispatch(outgoing):
        outgoing = jnp.broadcast_to(
            outgoing.reshape(1, groups, CAP, width), (team, groups, CAP, width)
        )
        return swap(outgoing.reshape(team * groups, CAP, width), TEAM + EXP).reshape(
            team * slots, width
        )

    def send_back(values):
        return swap(values.reshape(team * groups, CAP, width), TEAM + EXP).reshape(
            team, slots, width
        )

    def collect(returned):
        return jnp.einsum("ts,jsd->td", placing, returned, preferred_element_type=F32)

    peer_up = others(own_up, "hi")
    peer_down = others(own_down, "hi")
    *row_blocks, output_full, grad_slots_out, early_up, early_down = together(
        *row_blocks, output_full, to_slots(cotangent[0]), own_up, own_down
    )
    grad_arrived = dispatch(grad_slots_out)
    side_up = others(early_up, "in")
    side_down = others(early_down, "in")
    row_blocks[0], peer_up = together(row_blocks[0], peer_up)

    mixed_low, mixed_full, stat, pair = attend(
        active, order, row_blocks, columns, documents, row_count
    )

    def place_heads():
        index = np.arange(LANES)
        matrix = np.zeros((count, LANES, width), np.float32)
        for device in range(count):
            for slot in range(2):
                if used[device, slot]:
                    own = index[slot * HALF : (slot + 1) * HALF]
                    matrix[device, own, starts[device] + own] = 1.0
        return jnp.asarray(matrix, BF16)

    head_places = place_heads()

    def to_tokens(values):
        return swap(values.reshape(count, row_count, values.shape[1]), SEQ)

    mixed_low, grad_arrived, peer_down, side_up, side_down = together(
        mixed_low, grad_arrived, peer_down, side_up, side_down
    )
    far_up = others(peer_up, "in")
    far_down = others(peer_down, "in")
    mixed_pieces, projection_low = together(to_tokens(mixed_low), projection_low)
    projection_full = lax.all_gather(projection_low, ALL, axis=0, tiled=True)
    attend_out = jnp.einsum(
        "jtc,jcd->td", mixed_pieces, head_places, preferred_element_type=F32
    ).astype(BF16)
    branch = jnp.dot(attend_out, output_full, preferred_element_type=F32)
    middle = inputs + branch
    scale_second = lax.rsqrt(jnp.mean(middle * middle, axis=-1, keepdims=True) + EPSILON)
    normed_second = middle * scale_second
    expert_in = (normed_second * gain_second).astype(BF16)

    expert_slots, far_up = together(to_slots(expert_in), far_up)
    arrived, far_down = together(dispatch(expert_slots), far_down)
    ups, downs = (own_up, peer_up, side_up, far_up), (own_down, peer_down, side_down, far_down)
    grad_slots, actives, hiddens = expert_part(arrived, grad_arrived, ups, downs)
    returned_grad = send_back(grad_slots)

    def unit_pair(block, kind):
        return unit_grads(actives[block], grad_arrived, hiddens[block], arrived, kind)

    down_far, up_far = unit_pair(3, BF16)
    (down_part,) = to_owners([down_far], "in")
    down_peer, up_peer = unit_pair(1, F32)
    down_side, up_side = unit_pair(2, BF16)
    down_own, up_own = unit_pair(0, F32)
    produced = produced_part(actives, downs)
    (
        returned_grad,
        down_part,
        up_far,
        down_peer,
        up_peer,
        down_side,
        up_side,
        down_own,
        up_own,
        produced,
    ) = together(
        returned_grad,
        down_part,
        up_far,
        down_peer,
        up_peer,
        down_side,
        up_side,
        down_own,
        up_own,
        produced,
    )
    grad_expert_in = collect(returned_grad)
    (up_part,) = to_owners([up_far], "in")
    peers = lax.axis_size("hi")

    def hi_parts(value):
        return to_owners(list(value.astype(BF16).reshape(peers - 1, -1, width)), "hi")

    down_hi = hi_parts(add_all(down_peer, [down_part]))

    scaled_second = grad_expert_in * gain_second
    gain_second_part = jnp.sum(grad_expert_in * normed_second, axis=0)
    grad_middle = scale_second * (
        scaled_second
        - normed_second * jnp.mean(scaled_second * normed_second, axis=-1, keepdims=True)
    )
    residual_grad = upstream + grad_middle
    branch_grad = residual_grad.astype(BF16)
    grad_mixed = jnp.einsum(
        "td,ed->te", branch_grad, output_full, preferred_element_type=F32
    ).astype(BF16)

    sent_grad = jnp.stack([grad_mixed[:, s : s + LANES] for s in starts])
    sent_grad, up_part = together(sent_grad, up_part)
    up_hi = hi_parts(add_all(up_peer, [up_part]))
    (down_early,) = to_owners([down_side], "in")
    (up_early,) = to_owners([up_side], "in")
    row_grad = swap(sent_grad, SEQ).reshape(length, LANES)
    row_grad, produced, *down_hi = together(row_grad, produced, *down_hi)
    returned = send_back(produced)
    grad_qkv, grad_lying = attend_back(
        active, order, pair, documents, stat, row_grad, mixed_full, row_count, scaling
    )
    grad_qkv, grad_lying, returned, down_early, up_early, *up_hi = together(
        grad_qkv, grad_lying, returned, down_early, up_early, *up_hi
    )
    down_grad = add_all(down_own, [down_early, *down_hi])[None]
    up_grad = add_all(up_own, [up_early, *up_hi])[None]
    block_output = (middle + collect(returned)).astype(BF16)[None]

    dense = dense_terms(row_blocks, grad_lying, attend_out, branch_grad)
    dense = dense.reshape(count, groups, weight_rows, -1)
    group = lax.axis_index(EXP)
    own_rows, *other_rows = [
        lax.dynamic_index_in_dim(dense, lax.rem(group + step, groups), 1, keepdims=False)
        for step in range(groups)
    ]
    dense_rows = add_all(own_rows, to_owners(other_rows, "exp")).astype(BF16)
    if pairwise:
        lying_terms = [
            lax.dynamic_index_in_dim(dense_rows, position ^ bits, 0, keepdims=False)
            for bits in range(count)
        ]
        lying_terms[1:] = [flip(lying_terms[bits], bits) for bits in range(1, count)]
        grad_pieces, *lying_terms = together(to_tokens(grad_qkv), *lying_terms)
        lying_terms = jnp.stack(lying_terms)
        got_terms = [
            lax.dynamic_index_in_dim(lying_terms, position ^ j, 0, keepdims=False)
            for j in range(count)
        ]
    else:
        grad_pieces, dense_rows = together(to_tokens(grad_qkv), dense_rows)
        got_terms = list(swap(dense_rows, SEQ))
    got_terms = [term.astype(F32) for term in got_terms]
    grad_projected = jnp.concatenate(
        [
            jnp.einsum(
                "jtc,jcd->td",
                grad_pieces[:, :, k * LANES : (k + 1) * LANES],
                head_places,
                preferred_element_type=F32,
            ).astype(BF16)
            for k in range(3)
        ],
        axis=1,
    )
    grad_attend_in = jnp.einsum(
        "tc,dc->td", grad_projected, projection_full, preferred_element_type=F32
    )
    scaled_first = grad_attend_in * gain_first
    gain_first_part = jnp.sum(grad_attend_in * normed_first, axis=0)
    input_grad = (
        residual_grad
        + scale_first
        * (
            scaled_first
            - normed_first * jnp.mean(scaled_first * normed_first, axis=-1, keepdims=True)
        )
    )[None]
    output_grad = functools.reduce(jnp.add, [term[:, 3 * LANES :] for term in got_terms])
    head_grads = []
    for k in range(3):
        for head in range(HEADS):
            parts = [
                got_terms[j][:, k * LANES + slot * HALF : k * LANES + (slot + 1) * HALF]
                for j in range(count)
                for slot in range(2)
                if used[j, slot] and first_heads[j] + slot == head
            ]
            head_grads.append(functools.reduce(jnp.add, parts))
    projection_grad = jnp.concatenate(head_grads, axis=1)

    local_square = jnp.sum(projection_grad * projection_grad) + jnp.sum(output_grad * output_grad)
    local_square = local_square + jnp.sum(up_grad * up_grad) + jnp.sum(down_grad * down_grad)
    summed = spread_sum(
        jnp.concatenate(
            [gain_first_part, gain_second_part, jnp.broadcast_to(local_square, (LANES,))]
        )[None]
    )[0]
    gains_grad = summed[: 2 * width].reshape(2, width)
    grad_norm = jnp.sqrt(summed[2 * width] + jnp.sum(gains_grad * gains_grad))
    factor = jnp.minimum(1.0, CLIP / (grad_norm + 1e-06))
    (
        (projection_moment, projection_square, projection_new),
        (output_moment, output_square, output_new),
        (up_moment, up_square, up_new),
        (down_moment, down_square, down_new),
    ) = adam_all(
        factor,
        [
            (projection, projection_grad, projection_first, projection_second),
            (output_weight, output_grad, output_first, output_second),
            (expert_up, up_grad, up_first, up_second),
            (expert_down, down_grad, down_first, down_second),
        ],
        (RATE_MATRIX, RATE_OUTPUT, RATE_MATRIX, RATE_MATRIX),
        3,
    )
    gains_moment, gains_square, gains_new = adam_update(
        norm_gains, gains_grad, gains_first, gains_second, factor, RATE_GAIN, 0.0
    )
    return (
        block_output,
        input_grad,
        grad_norm,
        projection_grad,
        projection_moment,
        projection_square,
        projection_new,
        output_grad,
        output_moment,
        output_square,
        output_new,
        up_grad,
        up_moment,
        up_square,
        up_new,
        down_grad,
        down_moment,
        down_square,
        down_new,
        gains_grad,
        gains_moment,
        gains_square,
        gains_new,
    )


def solution(mesh):
    token = P("exp", SEQ, None)
    dense = P(ALL, None)
    expert = P("exp", SEQ, None)
    in_specs = (
        (token, token, P("exp", SEQ), token)
        + (dense, dense, expert, expert, P())
        + (dense,) * 4
        + (expert,) * 4
        + (P(), P())
    )
    out_specs = (token, token, P()) + (dense,) * 8 + (expert,) * 8 + (P(),) * 4
    rows, groups = mesh.devices.shape
    fine = Mesh(mesh.devices.reshape(rows // 4, 2, 2, groups), ALL)
    return jax.shard_map(body, mesh=fine, in_specs=in_specs, out_specs=out_specs, check_vma=False)
```

```python
import functools
import math

import jax
import jax.numpy as jnp
import numpy as np
from jax import lax
from jax.experimental import pallas as pl
from jax.experimental.pallas import tpu as pltpu
from jax.sharding import Mesh
from jax.sharding import PartitionSpec as P

HEADS = 12
CAP = 128
STEP = 10


EPSILON = 1e-05
CLIP = 1.0
BETA_ONE = 0.9
BETA_TWO = 0.99
ADAM_FLOOR = 1e-08
DECAY = 0.1
RATE_MATRIX = 0.04
RATE_OUTPUT = 0.1
RATE_GAIN = 0.5

SEQ = ("hi", "lo", "in")
EXP = ("exp",)
ALL = SEQ + EXP
TEAM = ("lo",)
SHARE = ("hi", "in")
LANES = 128
HALF = 64
FAR = -1e30
BF16 = jnp.bfloat16
F32 = jnp.float32
VMEM_LIMIT = 60 * 1024 * 1024


def head_plan(count):
    whole = math.lcm(HEADS, count)
    units, parts = whole // count, whole // HEADS
    first = np.zeros((count,), np.int64)
    active = np.zeros((count, 2, count), np.int32)
    for device in range(count):
        first[device] = min(units * device // parts, HEADS - 2)
        for unit in range(units * device, units * (device + 1)):
            slot = unit // parts - first[device]
            for block in range(count):
                turn = block % (2 * parts)
                if min(turn, 2 * parts - 1 - turn) == unit % parts:
                    active[device, slot, block] = 1
    return first, active


def three_parts(value):
    high = value.astype(BF16).astype(F32)
    middle = (value - high).astype(BF16).astype(F32)
    return high, middle, value - high - middle


def contract(left, right, left_axis, right_axis):
    return lax.dot_general(
        left, right, (((left_axis,), (right_axis,)), ((), ())), preferred_element_type=F32
    )


def slot_arrays(packed, documents, kind, slot):
    spare = HALF - HALF * slot
    lane = lax.broadcasted_iota(jnp.int32, packed.shape, 1)
    own = (lane < HALF) if slot == 0 else (lane >= HALF)
    place = (lane - spare).astype(F32)
    ours = place == documents
    first = (lane >= spare) & (lane < spare + 3)
    if kind == "query":
        extra = jnp.where(first & jnp.logical_not(ours), FAR, 0.0)
    elif kind == "key":
        extra = jnp.where(ours | ((lane >= spare + 3) & (lane < spare + 6)), 1.0, 0.0)
    else:
        extra = jnp.where(first, 1.0, 0.0)
    return jnp.where(own, packed, extra).astype(BF16)


def fill_slots(packed_of, documents_ref, wide_ref, kinds, place):
    documents = documents_ref[place, :].astype(F32)
    for number, kind in enumerate(kinds):
        packed = packed_of(kind).astype(F32)
        if kind == "query":
            packed = packed * 0.125
        for slot in range(2):
            column = (2 * number + slot) * LANES
            wide_ref[place, column : column + LANES] = slot_arrays(packed, documents, kind, slot)


def attend_kernel(active_ref, order_ref, *refs, block, chunk, held):
    row_refs = refs[:held]
    columns_ref, documents_ref = refs[held : held + 2]
    low_ref, full_ref, stat_ref, pair_ref, mixed_ref, wide_ref = refs[held + 2 :]
    at = pl.program_id(0)

    @pl.when(at == 0)
    def _():
        def fill(tokens, index):
            place = pl.ds(pl.multiple_of(order_ref[index] * block, block), block)
            packed = contract(tokens, columns_ref[...], 1, 0).astype(BF16)
            pair_ref[place, :] = packed[:, LANES:]
            parts = {
                kind: packed[:, part * LANES : (part + 1) * LANES]
                for part, kind in enumerate(("query", "key", "value"))
            }
            fill_slots(parts.get, documents_ref, wide_ref, tuple(parts), place)

        if held > 1:
            for index, row_ref in enumerate(row_refs):
                fill(row_ref[...], index)
        else:

            @pl.loop(0, pl.num_programs(0))
            def _(index):
                fill(row_refs[0][pl.ds(pl.multiple_of(index * block, block), block), :], index)

    rows = pl.ds(pl.multiple_of(at * block, block), block)
    lane = lax.broadcasted_iota(jnp.int32, (block, LANES), 1)
    last = lax.div(at * block, chunk)
    for slot in range(2):
        spare = HALF - HALF * slot
        own = (lane < HALF) if slot == 0 else (lane >= HALF)
        columns = slice(slot * LANES, (slot + 1) * LANES)

        @pl.when(active_ref[slot, at] != 0)
        def _():
            query = wide_ref[rows, columns]

            def step(index, carry, edge):
                top, weighted = carry
                place = pl.ds(pl.multiple_of(index * chunk, chunk), chunk)
                keys = wide_ref[place, 2 * LANES + slot * LANES : 3 * LANES + slot * LANES]
                values = wide_ref[place, 4 * LANES + slot * LANES : 5 * LANES + slot * LANES]
                scores = contract(query, keys, 1, 1)
                if edge:
                    key_at = index * chunk + lax.broadcasted_iota(jnp.int32, (block, chunk), 1)
                    query_at = at * block + lax.broadcasted_iota(jnp.int32, (block, chunk), 0)
                    scores = jnp.where(key_at <= query_at, scores, FAR)
                new_top = jnp.maximum(top, jnp.max(scores, axis=1, keepdims=True))
                weights = jnp.exp(scores - new_top).astype(BF16)
                weighted = weighted * jnp.exp(top - new_top) + contract(weights, values, 1, 0)
                return new_top, weighted

            carry = (jnp.full((block, 1), FAR, F32), jnp.zeros((block, LANES), F32))
            carry = lax.fori_loop(0, last, lambda index, state: step(index, state, False), carry)
            top, weighted = step(last, carry, True)
            total = weighted[:, spare : spare + 1]
            mixed_ref[slot] = jnp.where(own, weighted / total, 0.0)
            log_total = top + jnp.log(total)
            high, middle, small = three_parts(log_total)
            extra = jnp.where(lane == spare + 3, -high, 0.0)
            extra = jnp.where(lane == spare + 4, -middle, extra)
            extra = jnp.where(lane == spare + 5, -small, extra)
            stat_ref[:, columns] = (query.astype(F32) + extra).astype(BF16)

        @pl.when(active_ref[slot, at] == 0)
        def _():
            mixed_ref[slot] = jnp.zeros((block, LANES), F32)
            stat_ref[:, columns] = jnp.zeros((block, LANES), BF16)

    mixed = mixed_ref[0] + mixed_ref[1]
    full_ref[...] = mixed
    low_ref[...] = mixed.astype(BF16)


def attend_back_kernel(
    active_ref,
    order_ref,
    pair_ref,
    documents_ref,
    stat_ref,
    grad_ref,
    mixed_ref,
    out_ref,
    lying_ref,
    key_sum_ref,
    value_sum_ref,
    query_sum_ref,
    wide_ref,
    *,
    block,
    chunk,
    scaling,
):
    at = pl.program_id(0)
    rows = pl.ds(pl.multiple_of(at * block, block), block)
    lane = lax.broadcasted_iota(jnp.int32, (block, LANES), 1)
    last = lax.div(at * block, chunk)

    @pl.when(at == 0)
    def _():
        @pl.loop(0, pl.num_programs(0))
        def _(index):
            place = pl.ds(pl.multiple_of(index * block, block), block)
            parts = {"key": pair_ref[place, :LANES], "value": pair_ref[place, LANES:]}
            fill_slots(parts.get, documents_ref, wide_ref, tuple(parts), place)

        key_sum_ref[...] = jnp.zeros_like(key_sum_ref)
        value_sum_ref[...] = jnp.zeros_like(value_sum_ref)

    for slot in range(2):
        spare = HALF - HALF * slot
        own = (lane < HALF) if slot == 0 else (lane >= HALF)
        columns = slice(slot * LANES, (slot + 1) * LANES)
        query_sum_ref[slot] = jnp.zeros((block, LANES), F32)

        @pl.when(active_ref[slot, at] != 0)
        def _():
            query = stat_ref[:, columns]
            grad = grad_ref[...].astype(F32)
            delta = jnp.sum(jnp.where(own, grad * mixed_ref[...], 0.0), axis=1, keepdims=True)
            high, middle, small = three_parts(delta)
            extra = jnp.where(lane == spare, -high, 0.0)
            extra = jnp.where(lane == spare + 1, -middle, extra)
            extra = jnp.where(lane == spare + 2, -small, extra)
            grad_low = jnp.where(own, grad, extra).astype(BF16)

            def step(index, edge):
                place = pl.ds(pl.multiple_of(index * chunk, chunk), chunk)
                keys = wide_ref[place, slot * LANES : (slot + 1) * LANES]
                values = wide_ref[place, (2 + slot) * LANES : (3 + slot) * LANES]
                scores = contract(keys, query, 1, 1)
                if edge:
                    key_at = index * chunk + lax.broadcasted_iota(jnp.int32, (chunk, block), 0)
                    query_at = at * block + lax.broadcasted_iota(jnp.int32, (chunk, block), 1)
                    scores = jnp.where(key_at <= query_at, scores, FAR)
                weights = jnp.exp(scores)
                grad_weights = contract(values, grad_low, 1, 1)
                grad_scores = (weights * grad_weights).astype(BF16)
                value_sum_ref[slot, place, :] += contract(weights.astype(BF16), grad_low, 1, 0)
                key_sum_ref[slot, place, :] += contract(grad_scores, query, 1, 0)
                query_sum_ref[slot] += contract(grad_scores, keys, 0, 0)

            @pl.loop(0, last)
            def _(index):
                step(index, False)

            step(last, True)

    first_half = lane < HALF
    query_grad = jnp.where(first_half, query_sum_ref[0], query_sum_ref[1]) * scaling
    out_ref[rows, :LANES] = query_grad.astype(BF16)
    lying = pl.ds(pl.multiple_of(order_ref[at] * block, block), block)
    lying_ref[lying, :LANES] = query_grad.astype(BF16)

    @pl.when(at == pl.num_programs(0) - 1)
    def _():
        @pl.loop(0, pl.num_programs(0))
        def _(index):
            place = pl.ds(pl.multiple_of(index * block, block), block)
            key_grad = jnp.where(first_half, key_sum_ref[0, place, :], key_sum_ref[1, place, :])
            value_grad = jnp.where(
                first_half, value_sum_ref[0, place, :], value_sum_ref[1, place, :]
            )
            out_ref[place, LANES : 2 * LANES] = key_grad.astype(BF16)
            out_ref[place, 2 * LANES :] = value_grad.astype(BF16)
            lying = pl.ds(pl.multiple_of(order_ref[index] * block, block), block)
            lying_ref[lying, LANES : 2 * LANES] = key_grad.astype(BF16)
            lying_ref[lying, 2 * LANES :] = value_grad.astype(BF16)


def whole(value):
    return pl.BlockSpec(value.shape, lambda i, *unused: (0, 0), pipeline_mode=pl.Buffered(1))


SMALL = pl.CostEstimate(flops=1, bytes_accessed=1, transcendentals=0)


def attend(active, order, row_blocks, columns, documents, block):
    length = documents.shape[0]
    pair = jax.ShapeDtypeStruct((length, 2 * LANES), BF16)
    return pl.pallas_call(
        functools.partial(attend_kernel, block=block, chunk=2 * block, held=len(row_blocks)),
        grid_spec=pltpu.PrefetchScalarGridSpec(
            num_scalar_prefetch=2,
            grid=(length // block,),
            in_specs=[whole(value) for value in (*row_blocks, columns, documents)],
            out_specs=[
                pl.BlockSpec((block, LANES), lambda i, a, o: (i, 0)),
                pl.BlockSpec((block, LANES), lambda i, a, o: (i, 0)),
                pl.BlockSpec((block, 2 * LANES), lambda i, a, o: (i, 0)),
                whole(pair),
            ],
            scratch_shapes=[
                pltpu.VMEM((2, block, LANES), F32),
                pltpu.VMEM((length, 6 * LANES), BF16),
            ],
        ),
        out_shape=[
            jax.ShapeDtypeStruct((length, LANES), BF16),
            jax.ShapeDtypeStruct((length, LANES), F32),
            jax.ShapeDtypeStruct((length, 2 * LANES), BF16),
            pair,
        ],
        compiler_params=pltpu.CompilerParams(vmem_limit_bytes=VMEM_LIMIT),
        cost_estimate=SMALL,
    )(active, order, *row_blocks, columns, documents)


def attend_back(active, order, pair, documents, stat, grad, mixed, block, scaling):
    length = pair.shape[0]
    count = length // block
    return pl.pallas_call(
        functools.partial(attend_back_kernel, block=block, chunk=2 * block, scaling=scaling),
        grid_spec=pltpu.PrefetchScalarGridSpec(
            num_scalar_prefetch=2,
            grid=(count,),
            in_specs=[
                whole(pair),
                whole(documents),
                pl.BlockSpec((block, 2 * LANES), lambda i, a, o: (i, 0)),
                pl.BlockSpec((block, LANES), lambda i, a, o: (i, 0)),
                pl.BlockSpec((block, LANES), lambda i, a, o: (i, 0)),
            ],
            out_specs=[
                pl.BlockSpec(
                    (length, 3 * LANES), lambda i, a, o: (0, 0), pipeline_mode=pl.Buffered(1)
                )
            ]
            * 2,
            scratch_shapes=[
                pltpu.VMEM((2, length, LANES), F32),
                pltpu.VMEM((2, length, LANES), F32),
                pltpu.VMEM((2, block, LANES), F32),
                pltpu.VMEM((length, 4 * LANES), BF16),
            ],
        ),
        out_shape=[jax.ShapeDtypeStruct((length, 3 * LANES), BF16)] * 2,
        compiler_params=pltpu.CompilerParams(vmem_limit_bytes=VMEM_LIMIT),
        cost_estimate=SMALL,
    )(active, order, pair, documents, stat, grad, mixed)


def expert_kernel(arrived_ref, grad_ref, *refs, count):
    up_refs, down_refs = refs[:count], refs[count : 2 * count]
    total_ref = refs[2 * count]
    active_refs, hidden_refs = refs[2 * count + 1 : 3 * count + 1], refs[3 * count + 1 :]
    arrived, grad_arrived = arrived_ref[...], grad_ref[...]
    scale = math.sqrt(2.0 / math.pi)
    total = jnp.zeros(total_ref.shape, F32)
    for up_ref, down_ref, active_ref, hidden_ref in zip(
        up_refs, down_refs, active_refs, hidden_refs, strict=True
    ):
        up = up_ref[...]
        hidden = contract(arrived, up, 1, 1)
        squared = hidden * hidden
        bend = jnp.tanh(scale * hidden * (1.0 + 0.044715 * squared))
        half = 0.5 + 0.5 * bend
        active_ref[...] = (hidden * half).astype(BF16)
        slope = half + (0.5 * scale) * hidden * (1.0 - bend * bend) * (1.0 + 3 * 0.044715 * squared)
        grad_hidden = (slope * contract(grad_arrived, down_ref[...], 1, 1)).astype(BF16)
        hidden_ref[...] = grad_hidden
        total = total + contract(grad_hidden, up, 1, 0)
    total_ref[...] = total.astype(BF16)


def rows_spec(value, block):
    return pl.BlockSpec((block, value.shape[1]), lambda i: (i, 0))


def expert_part(arrived, grad_arrived, ups, downs):
    slots, width = arrived.shape
    block = 256
    units = [jax.ShapeDtypeStruct((slots, up.shape[0]), BF16) for up in ups]
    outs = [jax.ShapeDtypeStruct((slots, width), BF16), *units, *units]
    total, *parts = pl.pallas_call(
        functools.partial(expert_kernel, count=len(ups)),
        grid=(slots // block,),
        in_specs=[rows_spec(arrived, block), rows_spec(grad_arrived, block)]
        + [whole(value) for value in (*ups, *downs)],
        out_specs=[rows_spec(out, block) for out in outs],
        out_shape=outs,
        compiler_params=pltpu.CompilerParams(vmem_limit_bytes=VMEM_LIMIT),
        cost_estimate=SMALL,
    )(arrived, grad_arrived, *ups, *downs)
    return total, parts[: len(ups)], parts[len(ups) :]


def produced_kernel(*refs, count):
    total = contract(refs[0][...], refs[count][...], 1, 0)
    for index in range(1, count):
        total = total + contract(refs[index][...], refs[count + index][...], 1, 0)
    refs[-1][...] = total.astype(BF16)


def produced_part(actives, downs):
    slots, width = actives[0].shape[0], downs[0].shape[1]
    block = 256
    out = jax.ShapeDtypeStruct((slots, width), BF16)
    return pl.pallas_call(
        functools.partial(produced_kernel, count=len(actives)),
        grid=(slots // block,),
        in_specs=[rows_spec(value, block) for value in actives] + [whole(down) for down in downs],
        out_specs=rows_spec(out, block),
        out_shape=out,
        compiler_params=pltpu.CompilerParams(vmem_limit_bytes=VMEM_LIMIT),
        cost_estimate=SMALL,
    )(*actives, *downs)


def unit_kernel(grad_ref, arrived_ref, *refs, count):
    for index in range(count):
        active_ref, hidden_ref = refs[2 * index : 2 * index + 2]
        down_ref, up_ref = refs[2 * count + 2 * index : 2 * count + 2 * index + 2]
        down_ref[...] = contract(active_ref[...], grad_ref[...], 0, 0).astype(down_ref.dtype)
        up_ref[...] = contract(hidden_ref[...], arrived_ref[...], 0, 0).astype(up_ref.dtype)


def unit_grads(grad_arrived, arrived, blocks, kinds):
    slots, width = arrived.shape
    block = 256
    right = pl.BlockSpec((slots, block), lambda i: (0, i))
    outs = [
        jax.ShapeDtypeStruct((active.shape[1], width), kind)
        for (active, unused), kind in zip(blocks, kinds, strict=True)
        for part in range(2)
    ]
    flat = [value for pair in blocks for value in pair]
    return pl.pallas_call(
        functools.partial(unit_kernel, count=len(blocks)),
        grid=(width // block,),
        in_specs=[right, right] + [whole(value) for value in flat],
        out_specs=[pl.BlockSpec((out.shape[0], block), lambda i: (0, i)) for out in outs],
        out_shape=outs,
        compiler_params=pltpu.CompilerParams(vmem_limit_bytes=VMEM_LIMIT),
        cost_estimate=SMALL,
    )(grad_arrived, arrived, *flat)


def dense_kernel(*refs, held):
    row_refs = refs[:held]
    lying_ref, attend_ref, branch_ref, out_ref = refs[held:]
    start, total = 0, None
    for row_ref in row_refs:
        rows = row_ref.shape[0]
        part = contract(row_ref[...], lying_ref[start : start + rows, :], 0, 0)
        total = part if total is None else total + part
        start += rows
    out_ref[:, : 3 * LANES] = total.astype(BF16)
    out_ref[:, 3 * LANES :] = contract(attend_ref[...], branch_ref[...], 0, 0).astype(BF16)


def dense_terms(row_blocks, grad_lying, attend_out, branch_grad):
    width = attend_out.shape[1]
    block = 256

    def columns(value):
        return pl.BlockSpec((value.shape[0], block), lambda i: (0, i))

    out = jax.ShapeDtypeStruct((width, 3 * LANES + width), BF16)
    return pl.pallas_call(
        functools.partial(dense_kernel, held=len(row_blocks)),
        grid=(width // block,),
        in_specs=[columns(value) for value in row_blocks]
        + [whole(grad_lying), columns(attend_out), whole(branch_grad)],
        out_specs=rows_spec(out, block),
        out_shape=out,
        compiler_params=pltpu.CompilerParams(vmem_limit_bytes=VMEM_LIMIT),
        cost_estimate=SMALL,
    )(*row_blocks, grad_lying, attend_out, branch_grad)


def adam_update(weight, grad, first, second, factor, rate, decay):
    clipped = grad * factor
    first_new = BETA_ONE * first + (1.0 - BETA_ONE) * clipped
    second_new = BETA_TWO * second + (1.0 - BETA_TWO) * clipped * clipped
    first_hat = first_new / (1.0 - BETA_ONE**STEP)
    second_hat = second_new / (1.0 - BETA_TWO**STEP)
    weight_new = weight - rate * (first_hat / (jnp.sqrt(second_hat) + ADAM_FLOOR) + decay * weight)
    return (first_new, second_new, weight_new)


def together(*values):
    return lax.optimization_barrier(values)


def swap(value, axes):
    return lax.all_to_all(value, axes, split_axis=0, concat_axis=0, tiled=True)


def adam_kernel(factor_ref, *refs, rates):
    count = len(rates)
    factor = factor_ref[0]
    for index, rate in enumerate(rates):
        weight, grad, first, second = [ref[...] for ref in refs[4 * index : 4 * index + 4]]
        outs = refs[4 * count + 3 * index : 4 * count + 3 * index + 3]
        for out, value in zip(
            outs, adam_update(weight, grad, first, second, factor, rate, DECAY), strict=True
        ):
            out[...] = value


def adam_all(factor, leaves, rates, steps):
    flat = [value.reshape(value.shape[-2:]) for leaf in leaves for value in leaf]

    def spec(value):
        rows, columns = value.shape
        if rows % (8 * steps) == 0:
            return pl.BlockSpec((rows // steps, columns), lambda i: (i, 0))
        lanes = columns // steps
        return pl.BlockSpec((rows, lanes), lambda i: (0, i))

    shapes = [jax.ShapeDtypeStruct(value.shape, F32) for value in flat[::4] for _ in range(3)]
    outs = pl.pallas_call(
        functools.partial(adam_kernel, rates=rates),
        grid=(steps,),
        in_specs=[pl.BlockSpec(memory_space=pltpu.SMEM)] + [spec(value) for value in flat],
        out_specs=[spec(shape) for shape in shapes],
        out_shape=shapes,
        compiler_params=pltpu.CompilerParams(vmem_limit_bytes=VMEM_LIMIT),
        cost_estimate=pl.CostEstimate(
            flops=20 * sum(value.size for value in flat[::4]),
            bytes_accessed=28 * sum(value.size for value in flat[::4]),
            transcendentals=0,
        ),
    )(factor.reshape(1), *flat)
    return [
        [out.reshape(leaf[0].shape) for out in outs[3 * index : 3 * index + 3]]
        for index, leaf in enumerate(leaves)
    ]


def flip(value, bits):
    count = lax.axis_size(SEQ)
    return lax.ppermute(value, SEQ, [(index, index ^ bits) for index in range(count)])


def others(value, axis):
    size = lax.axis_size(axis)
    parts = [
        lax.ppermute(value, axis, [((i + step) % size, i) for i in range(size)])
        for step in range(1, size)
    ]
    return parts[0] if size == 2 else jnp.concatenate(parts, axis=0)


def to_owners(blocks, axis):
    size = lax.axis_size(axis)
    return [
        lax.ppermute(block, axis, [(i, (i + step) % size) for i in range(size)])
        for step, block in enumerate(blocks, 1)
    ]


def add_all(own, parts):
    return functools.reduce(lambda total, part: total + part.astype(F32), parts, own.astype(F32))


def spread_sum(value):
    count = lax.axis_size(ALL)
    return jnp.sum(swap(jnp.broadcast_to(value[None], (count, *value.shape)), ALL), axis=0)


def body(
    tokens,
    cotangent,
    segment_ids,
    expert_ids,
    projection,
    output_weight,
    expert_up,
    expert_down,
    norm_gains,
    projection_first,
    projection_second,
    output_first,
    output_second,
    up_first,
    up_second,
    down_first,
    down_second,
    gains_first,
    gains_second,
):
    inputs = tokens[0].astype(F32)
    upstream = cotangent[0].astype(F32)
    row_count = inputs.shape[0]
    width = inputs.shape[1]
    head_size = width // HEADS
    scaling = head_size ** (-0.5)
    count = lax.axis_size(SEQ)
    groups = lax.axis_size("exp")
    team = lax.axis_size(TEAM)
    position = lax.axis_index(SEQ)
    length = count * row_count
    weight_rows = projection.shape[0]
    first_heads, active_table = head_plan(count)
    starts = [int(head) * head_size for head in first_heads]
    active = lax.dynamic_index_in_dim(jnp.asarray(active_table), position, 0, keepdims=False)
    gain_first = norm_gains[0]
    gain_second = norm_gains[1]
    used = active_table.any(axis=2)

    scale_first = lax.rsqrt(jnp.mean(inputs * inputs, axis=-1, keepdims=True) + EPSILON)
    normed_first = inputs * scale_first
    attend_in = (normed_first * gain_first).astype(BF16)
    slots = groups * CAP
    chosen = expert_ids[0, :, 0]
    one_hot = (chosen[:, None] == jnp.arange(groups, dtype=jnp.int32)[None, :]).astype(jnp.int32)
    rank = jnp.sum(jnp.cumsum(one_hot, axis=0) * one_hot, axis=1) - 1
    target = chosen * CAP + rank
    placing = (target[:, None] == jnp.arange(slots, dtype=jnp.int32)[None, :]).astype(BF16)

    def to_slots(values):
        outgoing = jnp.einsum("ts,td->sd", placing, values, preferred_element_type=F32)
        return outgoing.astype(BF16)

    def dispatch(outgoing):
        outgoing = jnp.broadcast_to(
            outgoing.reshape(1, groups, CAP, width), (team, groups, CAP, width)
        )
        return swap(outgoing.reshape(team * groups, CAP, width), TEAM + EXP).reshape(
            team * slots, width
        )

    def send_back(values):
        return swap(values.reshape(team * groups, CAP, width), TEAM + EXP).reshape(
            team, slots, width
        )

    def collect(returned):
        return jnp.einsum("ts,jsd->td", placing, returned, preferred_element_type=F32)

    projection_low = projection.astype(BF16)
    sent_rows = weight_rows + 8
    own_documents = jnp.zeros((8, 3 * LANES + width), BF16)
    own_documents = own_documents.at[0, :row_count].set(segment_ids[0].astype(BF16))
    output_low = output_weight.astype(BF16)
    pieces = [
        jnp.concatenate(
            [projection_low[:, k * width + s : k * width + s + LANES] for k in range(3)]
            + [output_low],
            axis=1,
        )
        for s in starts
    ]
    pieces = jnp.stack([jnp.concatenate([piece, own_documents], axis=0) for piece in pieces])
    pairwise = count == 8
    if pairwise:
        order = jnp.arange(count, dtype=jnp.int32) ^ position
        held = [attend_in, flip(attend_in, 2), flip(attend_in, 4), flip(attend_in, 6)]
        beside = flip(attend_in, 1)
        grad_arrived = dispatch(to_slots(cotangent[0]))
        pieces, beside, grad_arrived, *held[1:] = together(
            pieces, beside, grad_arrived, *held[1:]
        )
        got_rows = swap(pieces, SEQ)
    else:
        order = jnp.arange(count, dtype=jnp.int32)
        held = [lax.all_gather(attend_in, SEQ, axis=0, tiled=True)]
        grad_arrived = dispatch(to_slots(cotangent[0]))
        got_rows = swap(pieces, SEQ)
    documents = jnp.broadcast_to(
        got_rows[:, weight_rows, :row_count].reshape(length, 1), (length, LANES)
    )

    def all_rows(value):
        copies = jnp.broadcast_to(value[None], (groups, *value.shape))
        return jnp.swapaxes(swap(copies, EXP), 0, 1).reshape(width, value.shape[-1])

    columns = all_rows(got_rows[:, :weight_rows, : 3 * LANES])
    own_up = expert_up[0].astype(BF16)
    own_down = expert_down[0].astype(BF16)
    held[-1], own_up, own_down = together(held[-1], own_up, own_down)
    row_blocks = held
    if pairwise:
        row_blocks = [attend_in, beside]
        row_blocks += [part for block in held[1:] for part in (block, flip(block, 1))]

    peer_up = others(own_up, "hi")
    peer_down = others(own_down, "hi")
    columns, output_rows, peer_up = together(
        columns, got_rows[:, :weight_rows, 3 * LANES :], peer_up
    )
    output_full = all_rows(output_rows)
    *row_blocks, early_up, early_down = together(*row_blocks, own_up, own_down)
    side_up = others(early_up, "in")
    side_down = others(early_down, "in")

    mixed_low, mixed_full, stat, pair = attend(
        active, order, row_blocks, columns, documents, row_count
    )

    def place_heads():
        index = np.arange(LANES)
        matrix = np.zeros((count, LANES, width), np.float32)
        for device in range(count):
            for slot in range(2):
                if used[device, slot]:
                    own = index[slot * HALF : (slot + 1) * HALF]
                    matrix[device, own, starts[device] + own] = 1.0
        return jnp.asarray(matrix, BF16)

    head_places = place_heads()

    def to_tokens(values):
        return swap(values.reshape(count, row_count, values.shape[1]), SEQ)

    mixed_low, output_full, peer_down, side_up, side_down = together(
        mixed_low, output_full, peer_down, side_up, side_down
    )
    far_up = others(peer_up, "in")
    far_down = others(peer_down, "in")
    mixed_pieces, projection_low = together(to_tokens(mixed_low), projection_low)
    projection_full = lax.all_gather(projection_low, ALL, axis=0, tiled=True)
    attend_out = jnp.einsum(
        "jtc,jcd->td", mixed_pieces, head_places, preferred_element_type=F32
    ).astype(BF16)
    branch = jnp.dot(attend_out, output_full, preferred_element_type=F32)
    middle = inputs + branch
    scale_second = lax.rsqrt(jnp.mean(middle * middle, axis=-1, keepdims=True) + EPSILON)
    normed_second = middle * scale_second
    expert_in = (normed_second * gain_second).astype(BF16)

    expert_slots, far_up = together(to_slots(expert_in), far_up)
    arrived, far_down = together(dispatch(expert_slots), far_down)
    ups, downs = (own_up, peer_up, side_up, far_up), (own_down, peer_down, side_down, far_down)
    grad_slots, actives, hiddens = expert_part(arrived, grad_arrived, ups, downs)
    returned_grad = send_back(grad_slots)

    blocks = list(zip(actives, hiddens, strict=True))
    down_far, up_far, down_peer, up_peer = unit_grads(
        grad_arrived, arrived, (blocks[3], blocks[1]), (BF16, F32)
    )
    (down_part,) = to_owners([down_far], "in")
    returned_grad, down_part, up_far, up_peer, projection_full = together(
        returned_grad, down_part, up_far, up_peer, projection_full
    )
    grad_expert_in = collect(returned_grad)
    (up_part,) = to_owners([up_far], "in")
    peers = lax.axis_size("hi")

    def hi_parts(value):
        return to_owners(list(value.astype(BF16).reshape(peers - 1, -1, width)), "hi")

    down_hi = hi_parts(add_all(down_peer, [down_part]))

    scaled_second = grad_expert_in * gain_second
    gain_second_part = jnp.sum(grad_expert_in * normed_second, axis=0)
    grad_middle = scale_second * (
        scaled_second
        - normed_second * jnp.mean(scaled_second * normed_second, axis=-1, keepdims=True)
    )
    residual_grad = upstream + grad_middle
    branch_grad = residual_grad.astype(BF16)
    grad_mixed = jnp.einsum(
        "td,ed->te", branch_grad, output_full, preferred_element_type=F32
    ).astype(BF16)

    sent_grad = jnp.stack([grad_mixed[:, s : s + LANES] for s in starts])
    down_side, up_side, down_own, up_own = unit_grads(
        grad_arrived, arrived, (blocks[2], blocks[0]), (BF16, F32)
    )
    (down_early,) = to_owners([down_side], "in")
    (up_early,) = to_owners([up_side], "in")
    produced = produced_part(actives, downs)
    row_grad = swap(sent_grad, SEQ).reshape(length, LANES)
    row_grad, produced, up_part, up_own = together(row_grad, produced, up_part, up_own)
    up_hi = hi_parts(add_all(up_peer, [up_part]))
    returned = send_back(produced)
    grad_qkv, grad_lying = attend_back(
        active, order, pair, documents, stat, row_grad, mixed_full, row_count, scaling
    )
    grad_qkv, grad_lying, returned, down_early, up_early, *down_hi = together(
        grad_qkv, grad_lying, returned, down_early, up_early, *down_hi
    )
    down_grad = add_all(down_own, [down_early, *down_hi])[None]
    block_output = (middle + collect(returned)).astype(BF16)[None]

    dense = dense_terms(row_blocks, grad_lying, attend_out, branch_grad)
    dense = dense.reshape(count, groups, weight_rows, -1)
    group = lax.axis_index(EXP)
    own_rows, *other_rows = [
        lax.dynamic_index_in_dim(dense, lax.rem(group + step, groups), 1, keepdims=False)
        for step in range(groups)
    ]
    dense_rows = add_all(own_rows, to_owners(other_rows, "exp")).astype(BF16)
    if pairwise:
        lying_terms = [
            lax.dynamic_index_in_dim(dense_rows, position ^ bits, 0, keepdims=False)
            for bits in range(count)
        ]
        lying_terms[1:] = [flip(lying_terms[bits], bits) for bits in range(1, count)]
        grad_pieces, *lying_terms = together(to_tokens(grad_qkv), *lying_terms)
        lying_terms = jnp.stack(lying_terms)
        got_terms = [
            lax.dynamic_index_in_dim(lying_terms, position ^ j, 0, keepdims=False)
            for j in range(count)
        ]
    else:
        grad_pieces, dense_rows = together(to_tokens(grad_qkv), dense_rows)
        got_terms = list(swap(dense_rows, SEQ))
    got_terms = [term.astype(F32) for term in got_terms]
    grad_pieces, *up_hi = together(grad_pieces, *up_hi)
    up_grad = add_all(up_own, [up_early, *up_hi])[None]
    grad_projected = jnp.concatenate(
        [
            jnp.einsum(
                "jtc,jcd->td",
                grad_pieces[:, :, k * LANES : (k + 1) * LANES],
                head_places,
                preferred_element_type=F32,
            ).astype(BF16)
            for k in range(3)
        ],
        axis=1,
    )
    grad_attend_in = jnp.einsum(
        "tc,dc->td", grad_projected, projection_full, preferred_element_type=F32
    )
    scaled_first = grad_attend_in * gain_first
    gain_first_part = jnp.sum(grad_attend_in * normed_first, axis=0)
    input_grad = (
        residual_grad
        + scale_first
        * (
            scaled_first
            - normed_first * jnp.mean(scaled_first * normed_first, axis=-1, keepdims=True)
        )
    )[None]
    output_grad = functools.reduce(jnp.add, [term[:, 3 * LANES :] for term in got_terms])
    head_grads = []
    for k in range(3):
        for head in range(HEADS):
            parts = [
                got_terms[j][:, k * LANES + slot * HALF : k * LANES + (slot + 1) * HALF]
                for j in range(count)
                for slot in range(2)
                if used[j, slot] and first_heads[j] + slot == head
            ]
            head_grads.append(functools.reduce(jnp.add, parts))
    projection_grad = jnp.concatenate(head_grads, axis=1)

    local_square = jnp.sum(projection_grad * projection_grad) + jnp.sum(output_grad * output_grad)
    local_square = local_square + jnp.sum(up_grad * up_grad) + jnp.sum(down_grad * down_grad)
    summed = spread_sum(
        jnp.concatenate(
            [gain_first_part, gain_second_part, jnp.broadcast_to(local_square, (LANES,))]
        )[None]
    )[0]
    gains_grad = summed[: 2 * width].reshape(2, width)
    grad_norm = jnp.sqrt(summed[2 * width] + jnp.sum(gains_grad * gains_grad))
    factor = jnp.minimum(1.0, CLIP / (grad_norm + 1e-06))
    (
        (projection_moment, projection_square, projection_new),
        (output_moment, output_square, output_new),
        (up_moment, up_square, up_new),
        (down_moment, down_square, down_new),
    ) = adam_all(
        factor,
        [
            (projection, projection_grad, projection_first, projection_second),
            (output_weight, output_grad, output_first, output_second),
            (expert_up, up_grad, up_first, up_second),
            (expert_down, down_grad, down_first, down_second),
        ],
        (RATE_MATRIX, RATE_OUTPUT, RATE_MATRIX, RATE_MATRIX),
        3,
    )
    gains_moment, gains_square, gains_new = adam_update(
        norm_gains, gains_grad, gains_first, gains_second, factor, RATE_GAIN, 0.0
    )
    return (
        block_output,
        input_grad,
        grad_norm,
        projection_grad,
        projection_moment,
        projection_square,
        projection_new,
        output_grad,
        output_moment,
        output_square,
        output_new,
        up_grad,
        up_moment,
        up_square,
        up_new,
        down_grad,
        down_moment,
        down_square,
        down_new,
        gains_grad,
        gains_moment,
        gains_square,
        gains_new,
    )


def solution(mesh):
    token = P("exp", SEQ, None)
    dense = P(ALL, None)
    expert = P("exp", SEQ, None)
    in_specs = (
        (token, token, P("exp", SEQ), token)
        + (dense, dense, expert, expert, P())
        + (dense,) * 4
        + (expert,) * 4
        + (P(), P())
    )
    out_specs = (token, token, P()) + (dense,) * 8 + (expert,) * 8 + (P(),) * 4
    rows, groups = mesh.devices.shape
    fine = Mesh(mesh.devices.reshape(rows // 4, 2, 2, groups), ALL)
    return jax.shard_map(body, mesh=fine, in_specs=in_specs, out_specs=out_specs, check_vma=False)
```

```python
import functools
import math

import jax
import jax.numpy as jnp
import numpy as np
from jax import lax
from jax.experimental import pallas as pl
from jax.experimental.pallas import tpu as pltpu
from jax.sharding import Mesh
from jax.sharding import PartitionSpec as P

HEADS = 12
CAP = 128
STEP = 10


EPSILON = 1e-05
CLIP = 1.0
BETA_ONE = 0.9
BETA_TWO = 0.99
ADAM_FLOOR = 1e-08
DECAY = 0.1
RATE_MATRIX = 0.04
RATE_OUTPUT = 0.1
RATE_GAIN = 0.5

SEQ = ("hi", "lo", "in")
EXP = ("exp",)
ALL = SEQ + EXP
TEAM = ("lo",)
SHARE = ("hi", "in")
LANES = 128
HALF = 64
FAR = -1e30
BF16 = jnp.bfloat16
F32 = jnp.float32
VMEM_LIMIT = 60 * 1024 * 1024


def head_plan(count):
    whole = math.lcm(HEADS, count)
    units, parts = whole // count, whole // HEADS
    first = np.zeros((count,), np.int64)
    active = np.zeros((count, 2, count), np.int32)
    for device in range(count):
        first[device] = min(units * device // parts, HEADS - 2)
        for unit in range(units * device, units * (device + 1)):
            slot = unit // parts - first[device]
            for block in range(count):
                turn = block % (2 * parts)
                if min(turn, 2 * parts - 1 - turn) == unit % parts:
                    active[device, slot, block] = 1
    return first, active


def three_parts(value):
    high = value.astype(BF16).astype(F32)
    middle = (value - high).astype(BF16).astype(F32)
    return high, middle, value - high - middle


def contract(left, right, left_axis, right_axis):
    return lax.dot_general(
        left, right, (((left_axis,), (right_axis,)), ((), ())), preferred_element_type=F32
    )


def slot_arrays(packed, documents, kind, slot):
    spare = HALF - HALF * slot
    lane = lax.broadcasted_iota(jnp.int32, packed.shape, 1)
    own = (lane < HALF) if slot == 0 else (lane >= HALF)
    place = (lane - spare).astype(F32)
    ours = place == documents
    first = (lane >= spare) & (lane < spare + 3)
    if kind == "query":
        extra = jnp.where(first & jnp.logical_not(ours), FAR, 0.0)
    elif kind == "key":
        extra = jnp.where(ours | ((lane >= spare + 3) & (lane < spare + 6)), 1.0, 0.0)
    else:
        extra = jnp.where(first, 1.0, 0.0)
    return jnp.where(own, packed, extra).astype(BF16)


def fill_slots(packed_of, documents_ref, wide_ref, kinds, place):
    documents = documents_ref[place, :].astype(F32)
    for number, kind in enumerate(kinds):
        packed = packed_of(kind).astype(F32)
        if kind == "query":
            packed = packed * 0.125
        for slot in range(2):
            column = (2 * number + slot) * LANES
            wide_ref[place, column : column + LANES] = slot_arrays(packed, documents, kind, slot)


def attend_kernel(active_ref, order_ref, *refs, block, chunk, held):
    row_refs = refs[:held]
    columns_ref, documents_ref = refs[held : held + 2]
    low_ref, full_ref, stat_ref, pair_ref, mixed_ref, wide_ref = refs[held + 2 :]
    at = pl.program_id(0)

    @pl.when(at == 0)
    def _():
        def fill(tokens, index):
            place = pl.ds(pl.multiple_of(order_ref[index] * block, block), block)
            packed = contract(tokens, columns_ref[...], 1, 0).astype(BF16)
            pair_ref[place, :] = packed[:, LANES:]
            parts = {
                kind: packed[:, part * LANES : (part + 1) * LANES]
                for part, kind in enumerate(("query", "key", "value"))
            }
            fill_slots(parts.get, documents_ref, wide_ref, tuple(parts), place)

        if held > 1:
            for index, row_ref in enumerate(row_refs):
                fill(row_ref[...], index)
        else:

            @pl.loop(0, pl.num_programs(0))
            def _(index):
                fill(row_refs[0][pl.ds(pl.multiple_of(index * block, block), block), :], index)

    rows = pl.ds(pl.multiple_of(at * block, block), block)
    lane = lax.broadcasted_iota(jnp.int32, (block, LANES), 1)
    last = lax.div(at * block, chunk)
    for slot in range(2):
        spare = HALF - HALF * slot
        own = (lane < HALF) if slot == 0 else (lane >= HALF)
        columns = slice(slot * LANES, (slot + 1) * LANES)

        @pl.when(active_ref[slot, at] != 0)
        def _():
            query = wide_ref[rows, columns]

            def step(index, carry, edge):
                top, weighted = carry
                place = pl.ds(pl.multiple_of(index * chunk, chunk), chunk)
                keys = wide_ref[place, 2 * LANES + slot * LANES : 3 * LANES + slot * LANES]
                values = wide_ref[place, 4 * LANES + slot * LANES : 5 * LANES + slot * LANES]
                scores = contract(query, keys, 1, 1)
                if edge:
                    key_at = index * chunk + lax.broadcasted_iota(jnp.int32, (block, chunk), 1)
                    query_at = at * block + lax.broadcasted_iota(jnp.int32, (block, chunk), 0)
                    scores = jnp.where(key_at <= query_at, scores, FAR)
                new_top = jnp.maximum(top, jnp.max(scores, axis=1, keepdims=True))
                weights = jnp.exp(scores - new_top).astype(BF16)
                weighted = weighted * jnp.exp(top - new_top) + contract(weights, values, 1, 0)
                return new_top, weighted

            carry = (jnp.full((block, 1), FAR, F32), jnp.zeros((block, LANES), F32))
            carry = lax.fori_loop(0, last, lambda index, state: step(index, state, False), carry)
            top, weighted = step(last, carry, True)
            total = weighted[:, spare : spare + 1]
            mixed_ref[slot] = jnp.where(own, weighted / total, 0.0)
            log_total = top + jnp.log(total)
            high, middle, small = three_parts(log_total)
            extra = jnp.where(lane == spare + 3, -high, 0.0)
            extra = jnp.where(lane == spare + 4, -middle, extra)
            extra = jnp.where(lane == spare + 5, -small, extra)
            stat_ref[:, columns] = (query.astype(F32) + extra).astype(BF16)

        @pl.when(active_ref[slot, at] == 0)
        def _():
            mixed_ref[slot] = jnp.zeros((block, LANES), F32)
            stat_ref[:, columns] = jnp.zeros((block, LANES), BF16)

    mixed = mixed_ref[0] + mixed_ref[1]
    full_ref[...] = mixed
    low_ref[...] = mixed.astype(BF16)


def attend_back_kernel(
    active_ref,
    order_ref,
    pair_ref,
    documents_ref,
    stat_ref,
    grad_ref,
    mixed_ref,
    out_ref,
    lying_ref,
    key_sum_ref,
    value_sum_ref,
    query_sum_ref,
    wide_ref,
    *,
    block,
    chunk,
    scaling,
):
    at = pl.program_id(0)
    rows = pl.ds(pl.multiple_of(at * block, block), block)
    lane = lax.broadcasted_iota(jnp.int32, (block, LANES), 1)
    last = lax.div(at * block, chunk)

    @pl.when(at == 0)
    def _():
        @pl.loop(0, pl.num_programs(0))
        def _(index):
            place = pl.ds(pl.multiple_of(index * block, block), block)
            parts = {"key": pair_ref[place, :LANES], "value": pair_ref[place, LANES:]}
            fill_slots(parts.get, documents_ref, wide_ref, tuple(parts), place)

        key_sum_ref[...] = jnp.zeros_like(key_sum_ref)
        value_sum_ref[...] = jnp.zeros_like(value_sum_ref)

    for slot in range(2):
        spare = HALF - HALF * slot
        own = (lane < HALF) if slot == 0 else (lane >= HALF)
        columns = slice(slot * LANES, (slot + 1) * LANES)
        query_sum_ref[slot] = jnp.zeros((block, LANES), F32)

        @pl.when(active_ref[slot, at] != 0)
        def _():
            query = stat_ref[:, columns]
            grad = grad_ref[...].astype(F32)
            delta = jnp.sum(jnp.where(own, grad * mixed_ref[...], 0.0), axis=1, keepdims=True)
            high, middle, small = three_parts(delta)
            extra = jnp.where(lane == spare, -high, 0.0)
            extra = jnp.where(lane == spare + 1, -middle, extra)
            extra = jnp.where(lane == spare + 2, -small, extra)
            grad_low = jnp.where(own, grad, extra).astype(BF16)

            def step(index, edge):
                place = pl.ds(pl.multiple_of(index * chunk, chunk), chunk)
                keys = wide_ref[place, slot * LANES : (slot + 1) * LANES]
                values = wide_ref[place, (2 + slot) * LANES : (3 + slot) * LANES]
                scores = contract(keys, query, 1, 1)
                if edge:
                    key_at = index * chunk + lax.broadcasted_iota(jnp.int32, (chunk, block), 0)
                    query_at = at * block + lax.broadcasted_iota(jnp.int32, (chunk, block), 1)
                    scores = jnp.where(key_at <= query_at, scores, FAR)
                weights = jnp.exp(scores)
                grad_weights = contract(values, grad_low, 1, 1)
                grad_scores = (weights * grad_weights).astype(BF16)
                value_sum_ref[slot, place, :] += contract(weights.astype(BF16), grad_low, 1, 0)
                key_sum_ref[slot, place, :] += contract(grad_scores, query, 1, 0)
                query_sum_ref[slot] += contract(grad_scores, keys, 0, 0)

            @pl.loop(0, last)
            def _(index):
                step(index, False)

            step(last, True)

    first_half = lane < HALF
    query_grad = jnp.where(first_half, query_sum_ref[0], query_sum_ref[1]) * scaling
    out_ref[rows, :LANES] = query_grad.astype(BF16)
    lying = pl.ds(pl.multiple_of(order_ref[at] * block, block), block)
    lying_ref[lying, :LANES] = query_grad.astype(BF16)

    @pl.when(at == pl.num_programs(0) - 1)
    def _():
        @pl.loop(0, pl.num_programs(0))
        def _(index):
            place = pl.ds(pl.multiple_of(index * block, block), block)
            key_grad = jnp.where(first_half, key_sum_ref[0, place, :], key_sum_ref[1, place, :])
            value_grad = jnp.where(
                first_half, value_sum_ref[0, place, :], value_sum_ref[1, place, :]
            )
            out_ref[place, LANES : 2 * LANES] = key_grad.astype(BF16)
            out_ref[place, 2 * LANES :] = value_grad.astype(BF16)
            lying = pl.ds(pl.multiple_of(order_ref[index] * block, block), block)
            lying_ref[lying, LANES : 2 * LANES] = key_grad.astype(BF16)
            lying_ref[lying, 2 * LANES :] = value_grad.astype(BF16)


def whole(value):
    return pl.BlockSpec(value.shape, lambda i, *unused: (0, 0), pipeline_mode=pl.Buffered(1))


SMALL = pl.CostEstimate(flops=1, bytes_accessed=1, transcendentals=0)


def attend(active, order, row_blocks, columns, documents, block):
    length = documents.shape[0]
    pair = jax.ShapeDtypeStruct((length, 2 * LANES), BF16)
    return pl.pallas_call(
        functools.partial(attend_kernel, block=block, chunk=2 * block, held=len(row_blocks)),
        grid_spec=pltpu.PrefetchScalarGridSpec(
            num_scalar_prefetch=2,
            grid=(length // block,),
            in_specs=[whole(value) for value in (*row_blocks, columns, documents)],
            out_specs=[
                pl.BlockSpec((block, LANES), lambda i, a, o: (i, 0)),
                pl.BlockSpec((block, LANES), lambda i, a, o: (i, 0)),
                pl.BlockSpec((block, 2 * LANES), lambda i, a, o: (i, 0)),
                whole(pair),
            ],
            scratch_shapes=[
                pltpu.VMEM((2, block, LANES), F32),
                pltpu.VMEM((length, 6 * LANES), BF16),
            ],
        ),
        out_shape=[
            jax.ShapeDtypeStruct((length, LANES), BF16),
            jax.ShapeDtypeStruct((length, LANES), F32),
            jax.ShapeDtypeStruct((length, 2 * LANES), BF16),
            pair,
        ],
        compiler_params=pltpu.CompilerParams(vmem_limit_bytes=VMEM_LIMIT),
        cost_estimate=SMALL,
    )(active, order, *row_blocks, columns, documents)


def attend_back(active, order, pair, documents, stat, grad, mixed, block, scaling):
    length = pair.shape[0]
    count = length // block
    return pl.pallas_call(
        functools.partial(attend_back_kernel, block=block, chunk=2 * block, scaling=scaling),
        grid_spec=pltpu.PrefetchScalarGridSpec(
            num_scalar_prefetch=2,
            grid=(count,),
            in_specs=[
                whole(pair),
                whole(documents),
                pl.BlockSpec((block, 2 * LANES), lambda i, a, o: (i, 0)),
                pl.BlockSpec((block, LANES), lambda i, a, o: (i, 0)),
                pl.BlockSpec((block, LANES), lambda i, a, o: (i, 0)),
            ],
            out_specs=[
                pl.BlockSpec(
                    (length, 3 * LANES), lambda i, a, o: (0, 0), pipeline_mode=pl.Buffered(1)
                )
            ]
            * 2,
            scratch_shapes=[
                pltpu.VMEM((2, length, LANES), F32),
                pltpu.VMEM((2, length, LANES), F32),
                pltpu.VMEM((2, block, LANES), F32),
                pltpu.VMEM((length, 4 * LANES), BF16),
            ],
        ),
        out_shape=[jax.ShapeDtypeStruct((length, 3 * LANES), BF16)] * 2,
        compiler_params=pltpu.CompilerParams(vmem_limit_bytes=VMEM_LIMIT),
        cost_estimate=SMALL,
    )(active, order, pair, documents, stat, grad, mixed)


def expert_kernel(arrived_ref, grad_ref, *refs, count):
    up_refs, down_refs = refs[:count], refs[count : 2 * count]
    total_ref = refs[2 * count]
    active_refs, hidden_refs = refs[2 * count + 1 : 3 * count + 1], refs[3 * count + 1 :]
    arrived, grad_arrived = arrived_ref[...], grad_ref[...]
    scale = math.sqrt(2.0 / math.pi)
    total = jnp.zeros(total_ref.shape, F32)
    for up_ref, down_ref, active_ref, hidden_ref in zip(
        up_refs, down_refs, active_refs, hidden_refs, strict=True
    ):
        up = up_ref[...]
        hidden = contract(arrived, up, 1, 1)
        squared = hidden * hidden
        bend = jnp.tanh(scale * hidden * (1.0 + 0.044715 * squared))
        half = 0.5 + 0.5 * bend
        active_ref[...] = (hidden * half).astype(BF16)
        slope = half + (0.5 * scale) * hidden * (1.0 - bend * bend) * (1.0 + 3 * 0.044715 * squared)
        grad_hidden = (slope * contract(grad_arrived, down_ref[...], 1, 1)).astype(BF16)
        hidden_ref[...] = grad_hidden
        total = total + contract(grad_hidden, up, 1, 0)
    total_ref[...] = total.astype(BF16)


def rows_spec(value, block):
    return pl.BlockSpec((block, value.shape[1]), lambda i: (i, 0))


def expert_part(arrived, grad_arrived, ups, downs):
    slots, width = arrived.shape
    block = 256
    units = [jax.ShapeDtypeStruct((slots, up.shape[0]), BF16) for up in ups]
    outs = [jax.ShapeDtypeStruct((slots, width), BF16), *units, *units]
    total, *parts = pl.pallas_call(
        functools.partial(expert_kernel, count=len(ups)),
        grid=(slots // block,),
        in_specs=[rows_spec(arrived, block), rows_spec(grad_arrived, block)]
        + [whole(value) for value in (*ups, *downs)],
        out_specs=[rows_spec(out, block) for out in outs],
        out_shape=outs,
        compiler_params=pltpu.CompilerParams(vmem_limit_bytes=VMEM_LIMIT),
        cost_estimate=SMALL,
    )(arrived, grad_arrived, *ups, *downs)
    return total, parts[: len(ups)], parts[len(ups) :]


def produced_kernel(*refs, count):
    total = contract(refs[0][...], refs[count][...], 1, 0)
    for index in range(1, count):
        total = total + contract(refs[index][...], refs[count + index][...], 1, 0)
    refs[-1][...] = total.astype(BF16)


def produced_part(actives, downs):
    slots, width = actives[0].shape[0], downs[0].shape[1]
    block = 256
    out = jax.ShapeDtypeStruct((slots, width), BF16)
    return pl.pallas_call(
        functools.partial(produced_kernel, count=len(actives)),
        grid=(slots // block,),
        in_specs=[rows_spec(value, block) for value in actives] + [whole(down) for down in downs],
        out_specs=rows_spec(out, block),
        out_shape=out,
        compiler_params=pltpu.CompilerParams(vmem_limit_bytes=VMEM_LIMIT),
        cost_estimate=SMALL,
    )(*actives, *downs)


def unit_kernel(grad_ref, arrived_ref, *refs, count):
    for index in range(count):
        active_ref, hidden_ref = refs[2 * index : 2 * index + 2]
        down_ref, up_ref = refs[2 * count + 2 * index : 2 * count + 2 * index + 2]
        down_ref[...] = contract(active_ref[...], grad_ref[...], 0, 0).astype(down_ref.dtype)
        up_ref[...] = contract(hidden_ref[...], arrived_ref[...], 0, 0).astype(up_ref.dtype)


def unit_grads(grad_arrived, arrived, blocks, kinds):
    slots, width = arrived.shape
    block = 256
    right = pl.BlockSpec((slots, block), lambda i: (0, i))
    outs = [
        jax.ShapeDtypeStruct((active.shape[1], width), kind)
        for (active, unused), kind in zip(blocks, kinds, strict=True)
        for part in range(2)
    ]
    flat = [value for pair in blocks for value in pair]
    return pl.pallas_call(
        functools.partial(unit_kernel, count=len(blocks)),
        grid=(width // block,),
        in_specs=[right, right] + [whole(value) for value in flat],
        out_specs=[pl.BlockSpec((out.shape[0], block), lambda i: (0, i)) for out in outs],
        out_shape=outs,
        compiler_params=pltpu.CompilerParams(vmem_limit_bytes=VMEM_LIMIT),
        cost_estimate=SMALL,
    )(grad_arrived, arrived, *flat)


def dense_kernel(*refs, held):
    row_refs = refs[:held]
    lying_ref, attend_ref, branch_ref, out_ref = refs[held:]
    start, total = 0, None
    for row_ref in row_refs:
        rows = row_ref.shape[0]
        part = contract(row_ref[...], lying_ref[start : start + rows, :], 0, 0)
        total = part if total is None else total + part
        start += rows
    out_ref[:, : 3 * LANES] = total.astype(BF16)
    out_ref[:, 3 * LANES :] = contract(attend_ref[...], branch_ref[...], 0, 0).astype(BF16)


def dense_terms(row_blocks, grad_lying, attend_out, branch_grad):
    width = attend_out.shape[1]
    block = 256

    def columns(value):
        return pl.BlockSpec((value.shape[0], block), lambda i: (0, i))

    out = jax.ShapeDtypeStruct((width, 3 * LANES + width), BF16)
    return pl.pallas_call(
        functools.partial(dense_kernel, held=len(row_blocks)),
        grid=(width // block,),
        in_specs=[columns(value) for value in row_blocks]
        + [whole(grad_lying), columns(attend_out), whole(branch_grad)],
        out_specs=rows_spec(out, block),
        out_shape=out,
        compiler_params=pltpu.CompilerParams(vmem_limit_bytes=VMEM_LIMIT),
        cost_estimate=SMALL,
    )(*row_blocks, grad_lying, attend_out, branch_grad)


def adam_update(weight, grad, first, second, factor, rate, decay):
    clipped = grad * factor
    first_new = BETA_ONE * first + (1.0 - BETA_ONE) * clipped
    second_new = BETA_TWO * second + (1.0 - BETA_TWO) * clipped * clipped
    first_hat = first_new / (1.0 - BETA_ONE**STEP)
    second_hat = second_new / (1.0 - BETA_TWO**STEP)
    weight_new = weight - rate * (first_hat / (jnp.sqrt(second_hat) + ADAM_FLOOR) + decay * weight)
    return (first_new, second_new, weight_new)


def together(*values):
    return lax.optimization_barrier(values)


def swap(value, axes):
    return lax.all_to_all(value, axes, split_axis=0, concat_axis=0, tiled=True)


def adam_kernel(factor_ref, *refs, rates):
    count = len(rates)
    factor = factor_ref[0]
    for index, rate in enumerate(rates):
        weight, grad, first, second = [ref[...] for ref in refs[4 * index : 4 * index + 4]]
        outs = refs[4 * count + 3 * index : 4 * count + 3 * index + 3]
        for out, value in zip(
            outs, adam_update(weight, grad, first, second, factor, rate, DECAY), strict=True
        ):
            out[...] = value


def adam_all(factor, leaves, rates, steps):
    flat = [value.reshape(value.shape[-2:]) for leaf in leaves for value in leaf]

    def spec(value):
        rows, columns = value.shape
        if rows % (8 * steps) == 0:
            return pl.BlockSpec((rows // steps, columns), lambda i: (i, 0))
        lanes = columns // steps
        return pl.BlockSpec((rows, lanes), lambda i: (0, i))

    shapes = [jax.ShapeDtypeStruct(value.shape, F32) for value in flat[::4] for _ in range(3)]
    outs = pl.pallas_call(
        functools.partial(adam_kernel, rates=rates),
        grid=(steps,),
        in_specs=[pl.BlockSpec(memory_space=pltpu.SMEM)] + [spec(value) for value in flat],
        out_specs=[spec(shape) for shape in shapes],
        out_shape=shapes,
        compiler_params=pltpu.CompilerParams(vmem_limit_bytes=VMEM_LIMIT),
        cost_estimate=pl.CostEstimate(
            flops=20 * sum(value.size for value in flat[::4]),
            bytes_accessed=28 * sum(value.size for value in flat[::4]),
            transcendentals=0,
        ),
    )(factor.reshape(1), *flat)
    return [
        [out.reshape(leaf[0].shape) for out in outs[3 * index : 3 * index + 3]]
        for index, leaf in enumerate(leaves)
    ]


def flip(value, bits):
    count = lax.axis_size(SEQ)
    return lax.ppermute(value, SEQ, [(index, index ^ bits) for index in range(count)])


def others(value, axis):
    size = lax.axis_size(axis)
    parts = [
        lax.ppermute(value, axis, [((i + step) % size, i) for i in range(size)])
        for step in range(1, size)
    ]
    return parts[0] if size == 2 else jnp.concatenate(parts, axis=0)


def to_owners(blocks, axis):
    size = lax.axis_size(axis)
    return [
        lax.ppermute(block, axis, [(i, (i + step) % size) for i in range(size)])
        for step, block in enumerate(blocks, 1)
    ]


def add_all(own, parts):
    return functools.reduce(lambda total, part: total + part.astype(F32), parts, own.astype(F32))


def spread_sum(value):
    count = lax.axis_size(ALL)
    return jnp.sum(swap(jnp.broadcast_to(value[None], (count, *value.shape)), ALL), axis=0)


def body(
    tokens,
    cotangent,
    segment_ids,
    expert_ids,
    projection,
    output_weight,
    expert_up,
    expert_down,
    norm_gains,
    projection_first,
    projection_second,
    output_first,
    output_second,
    up_first,
    up_second,
    down_first,
    down_second,
    gains_first,
    gains_second,
):
    inputs = tokens[0].astype(F32)
    upstream = cotangent[0].astype(F32)
    row_count = inputs.shape[0]
    width = inputs.shape[1]
    head_size = width // HEADS
    scaling = head_size ** (-0.5)
    count = lax.axis_size(SEQ)
    groups = lax.axis_size("exp")
    team = lax.axis_size(TEAM)
    position = lax.axis_index(SEQ)
    length = count * row_count
    weight_rows = projection.shape[0]
    first_heads, active_table = head_plan(count)
    starts = [int(head) * head_size for head in first_heads]
    active = lax.dynamic_index_in_dim(jnp.asarray(active_table), position, 0, keepdims=False)
    gain_first = norm_gains[0]
    gain_second = norm_gains[1]
    used = active_table.any(axis=2)

    scale_first = lax.rsqrt(jnp.mean(inputs * inputs, axis=-1, keepdims=True) + EPSILON)
    normed_first = inputs * scale_first
    attend_in = (normed_first * gain_first).astype(BF16)
    slots = groups * CAP
    chosen = expert_ids[0, :, 0]
    one_hot = (chosen[:, None] == jnp.arange(groups, dtype=jnp.int32)[None, :]).astype(jnp.int32)
    rank = jnp.sum(jnp.cumsum(one_hot, axis=0) * one_hot, axis=1) - 1
    target = chosen * CAP + rank
    placing = (target[:, None] == jnp.arange(slots, dtype=jnp.int32)[None, :]).astype(BF16)

    def to_slots(values):
        outgoing = jnp.einsum("ts,td->sd", placing, values, preferred_element_type=F32)
        return outgoing.astype(BF16)

    def dispatch(outgoing):
        outgoing = jnp.broadcast_to(
            outgoing.reshape(1, groups, CAP, width), (team, groups, CAP, width)
        )
        return swap(outgoing.reshape(team * groups, CAP, width), TEAM + EXP).reshape(
            team * slots, width
        )

    def send_back(values):
        return swap(values.reshape(team * groups, CAP, width), TEAM + EXP).reshape(
            team, slots, width
        )

    def collect(returned):
        return jnp.einsum("ts,jsd->td", placing, returned, preferred_element_type=F32)

    projection_low = projection.astype(BF16)
    sent_rows = weight_rows + 8
    own_documents = jnp.zeros((8, 3 * LANES + width), BF16)
    own_documents = own_documents.at[0, :row_count].set(segment_ids[0].astype(BF16))
    output_low = output_weight.astype(BF16)
    pieces = [
        jnp.concatenate(
            [projection_low[:, k * width + s : k * width + s + LANES] for k in range(3)]
            + [output_low],
            axis=1,
        )
        for s in starts
    ]
    pieces = jnp.stack([jnp.concatenate([piece, own_documents], axis=0) for piece in pieces])
    own_up = expert_up[0].astype(BF16)
    own_down = expert_down[0].astype(BF16)
    pairwise = count == 8
    if pairwise:
        order = jnp.arange(count, dtype=jnp.int32) ^ position
        beside, below, across = flip(attend_in, 1), flip(attend_in, 2), flip(attend_in, 4)
        got_rows, beside, below, across, own_up = together(
            swap(pieces, SEQ), beside, below, across, own_up
        )
        corner = flip(across, 2)
        row_blocks = [attend_in, beside]
        row_blocks += [part for block in (below, across, corner) for part in (block, flip(block, 1))]
    else:
        order = jnp.arange(count, dtype=jnp.int32)
        row_blocks = [lax.all_gather(attend_in, SEQ, axis=0, tiled=True)]
        got_rows = swap(pieces, SEQ)
    documents = jnp.broadcast_to(
        got_rows[:, weight_rows, :row_count].reshape(length, 1), (length, LANES)
    )
    own_copies = jnp.broadcast_to(
        got_rows[None, :, :weight_rows], (groups, count, weight_rows, 3 * LANES + width)
    )
    all_copies = swap(own_copies, EXP)

    peer_up = others(own_up, "hi")
    *row_blocks, all_copies, peer_up, own_up, own_down, grad_slots_out = together(
        *row_blocks, all_copies, peer_up, own_up, own_down, to_slots(cotangent[0])
    )
    all_copies = jnp.swapaxes(all_copies, 0, 1)
    columns = all_copies[..., : 3 * LANES].reshape(width, 3 * LANES)
    output_full = all_copies[..., 3 * LANES :].reshape(width, width)
    grad_arrived = dispatch(grad_slots_out)
    peer_down = others(own_down, "hi")
    side_up = others(own_up, "in")
    far_up = others(peer_up, "in")

    mixed_low, mixed_full, stat, pair = attend(
        active, order, row_blocks, columns, documents, row_count
    )

    def place_heads():
        index = np.arange(LANES)
        matrix = np.zeros((count, LANES, width), np.float32)
        for device in range(count):
            for slot in range(2):
                if used[device, slot]:
                    own = index[slot * HALF : (slot + 1) * HALF]
                    matrix[device, own, starts[device] + own] = 1.0
        return jnp.asarray(matrix, BF16)

    head_places = place_heads()

    def to_tokens(values):
        return swap(values.reshape(count, row_count, values.shape[1]), SEQ)

    mixed_low, grad_arrived, peer_down, side_up, far_up, own_down = together(
        mixed_low, grad_arrived, peer_down, side_up, far_up, own_down
    )
    side_down = others(own_down, "in")
    far_down = others(peer_down, "in")
    mixed_pieces, projection_low = together(to_tokens(mixed_low), projection_low)
    projection_full = lax.all_gather(projection_low, ALL, axis=0, tiled=True)
    attend_out = jnp.einsum(
        "jtc,jcd->td", mixed_pieces, head_places, preferred_element_type=F32
    ).astype(BF16)
    branch = jnp.dot(attend_out, output_full, preferred_element_type=F32)
    middle = inputs + branch
    scale_second = lax.rsqrt(jnp.mean(middle * middle, axis=-1, keepdims=True) + EPSILON)
    normed_second = middle * scale_second
    expert_in = (normed_second * gain_second).astype(BF16)

    expert_slots, side_down = together(to_slots(expert_in), side_down)
    arrived, far_down = together(dispatch(expert_slots), far_down)
    ups, downs = (own_up, peer_up, side_up, far_up), (own_down, peer_down, side_down, far_down)
    grad_slots, actives, hiddens = expert_part(arrived, grad_arrived, ups, downs)
    returned_grad = send_back(grad_slots)

    blocks = list(zip(actives, hiddens, strict=True))
    down_far, up_far, down_peer, up_peer = unit_grads(
        grad_arrived, arrived, (blocks[3], blocks[1]), (BF16, F32)
    )
    (down_part,) = to_owners([down_far], "in")
    down_side, up_side, down_own, up_own = unit_grads(
        grad_arrived, arrived, (blocks[2], blocks[0]), (BF16, F32)
    )
    produced = produced_part(actives, downs)
    returned_grad, down_part, up_far, up_peer, projection_full, produced, down_side, up_own = (
        together(
            returned_grad, down_part, up_far, up_peer, projection_full, produced, down_side, up_own
        )
    )
    grad_expert_in = collect(returned_grad)
    (up_part,) = to_owners([up_far], "in")
    peers = lax.axis_size("hi")

    def hi_parts(value):
        return to_owners(list(value.astype(BF16).reshape(peers - 1, -1, width)), "hi")

    down_hi = hi_parts(add_all(down_peer, [down_part]))

    scaled_second = grad_expert_in * gain_second
    gain_second_part = jnp.sum(grad_expert_in * normed_second, axis=0)
    grad_middle = scale_second * (
        scaled_second
        - normed_second * jnp.mean(scaled_second * normed_second, axis=-1, keepdims=True)
    )
    residual_grad = upstream + grad_middle
    branch_grad = residual_grad.astype(BF16)
    grad_mixed = jnp.einsum(
        "td,ed->te", branch_grad, output_full, preferred_element_type=F32
    ).astype(BF16)

    sent_grad = jnp.stack([grad_mixed[:, s : s + LANES] for s in starts])
    sent_grad, up_part = together(sent_grad, up_part)
    row_grad = swap(sent_grad, SEQ).reshape(length, LANES)
    row_grad, down_side, up_side, *down_hi = together(row_grad, down_side, up_side, *down_hi)
    (down_early,) = to_owners([down_side], "in")
    (up_early,) = to_owners([up_side], "in")
    up_hi = hi_parts(add_all(up_peer, [up_part]))
    returned = send_back(produced)
    grad_qkv, grad_lying = attend_back(
        active, order, pair, documents, stat, row_grad, mixed_full, row_count, scaling
    )
    grad_qkv, grad_lying, returned, down_early, up_early, *up_hi = together(
        grad_qkv, grad_lying, returned, down_early, up_early, *up_hi
    )
    up_grad = add_all(up_own, [up_early, *up_hi])[None]
    down_grad = add_all(down_own, [down_early, *down_hi])[None]
    block_output = (middle + collect(returned)).astype(BF16)[None]

    dense = dense_terms(row_blocks, grad_lying, attend_out, branch_grad)
    dense = dense.reshape(count, groups, weight_rows, -1)
    group = lax.axis_index(EXP)
    own_rows, *other_rows = [
        lax.dynamic_index_in_dim(dense, lax.rem(group + step, groups), 1, keepdims=False)
        for step in range(groups)
    ]
    dense_rows = add_all(own_rows, to_owners(other_rows, "exp")).astype(BF16)
    if pairwise:
        lying_terms = [
            lax.dynamic_index_in_dim(dense_rows, position ^ bits, 0, keepdims=False)
            for bits in range(count)
        ]
        lying_terms[1:] = [flip(lying_terms[bits], bits) for bits in range(1, count)]
        grad_pieces, *lying_terms = together(to_tokens(grad_qkv), *lying_terms)
        lying_terms = jnp.stack(lying_terms)
        got_terms = [
            lax.dynamic_index_in_dim(lying_terms, position ^ j, 0, keepdims=False)
            for j in range(count)
        ]
    else:
        grad_pieces, dense_rows = together(to_tokens(grad_qkv), dense_rows)
        got_terms = list(swap(dense_rows, SEQ))
    got_terms = [term.astype(F32) for term in got_terms]
    grad_projected = jnp.concatenate(
        [
            jnp.einsum(
                "jtc,jcd->td",
                grad_pieces[:, :, k * LANES : (k + 1) * LANES],
                head_places,
                preferred_element_type=F32,
            ).astype(BF16)
            for k in range(3)
        ],
        axis=1,
    )
    grad_attend_in = jnp.einsum(
        "tc,dc->td", grad_projected, projection_full, preferred_element_type=F32
    )
    scaled_first = grad_attend_in * gain_first
    gain_first_part = jnp.sum(grad_attend_in * normed_first, axis=0)
    input_grad = (
        residual_grad
        + scale_first
        * (
            scaled_first
            - normed_first * jnp.mean(scaled_first * normed_first, axis=-1, keepdims=True)
        )
    )[None]
    output_grad = functools.reduce(jnp.add, [term[:, 3 * LANES :] for term in got_terms])
    head_grads = []
    for k in range(3):
        for head in range(HEADS):
            parts = [
                got_terms[j][:, k * LANES + slot * HALF : k * LANES + (slot + 1) * HALF]
                for j in range(count)
                for slot in range(2)
                if used[j, slot] and first_heads[j] + slot == head
            ]
            head_grads.append(functools.reduce(jnp.add, parts))
    projection_grad = jnp.concatenate(head_grads, axis=1)

    local_square = jnp.sum(projection_grad * projection_grad) + jnp.sum(output_grad * output_grad)
    local_square = local_square + jnp.sum(up_grad * up_grad) + jnp.sum(down_grad * down_grad)
    summed = spread_sum(
        jnp.concatenate(
            [gain_first_part, gain_second_part, jnp.broadcast_to(local_square, (LANES,))]
        )[None]
    )[0]
    gains_grad = summed[: 2 * width].reshape(2, width)
    grad_norm = jnp.sqrt(summed[2 * width] + jnp.sum(gains_grad * gains_grad))
    factor = jnp.minimum(1.0, CLIP / (grad_norm + 1e-06))
    (
        (projection_moment, projection_square, projection_new),
        (output_moment, output_square, output_new),
        (up_moment, up_square, up_new),
        (down_moment, down_square, down_new),
    ) = adam_all(
        factor,
        [
            (projection, projection_grad, projection_first, projection_second),
            (output_weight, output_grad, output_first, output_second),
            (expert_up, up_grad, up_first, up_second),
            (expert_down, down_grad, down_first, down_second),
        ],
        (RATE_MATRIX, RATE_OUTPUT, RATE_MATRIX, RATE_MATRIX),
        3,
    )
    gains_moment, gains_square, gains_new = adam_update(
        norm_gains, gains_grad, gains_first, gains_second, factor, RATE_GAIN, 0.0
    )
    return (
        block_output,
        input_grad,
        grad_norm,
        projection_grad,
        projection_moment,
        projection_square,
        projection_new,
        output_grad,
        output_moment,
        output_square,
        output_new,
        up_grad,
        up_moment,
        up_square,
        up_new,
        down_grad,
        down_moment,
        down_square,
        down_new,
        gains_grad,
        gains_moment,
        gains_square,
        gains_new,
    )


def solution(mesh):
    token = P("exp", SEQ, None)
    dense = P(ALL, None)
    expert = P("exp", SEQ, None)
    in_specs = (
        (token, token, P("exp", SEQ), token)
        + (dense, dense, expert, expert, P())
        + (dense,) * 4
        + (expert,) * 4
        + (P(), P())
    )
    out_specs = (token, token, P()) + (dense,) * 8 + (expert,) * 8 + (P(),) * 4
    rows, groups = mesh.devices.shape
    fine = Mesh(mesh.devices.reshape(rows // 4, 2, 2, groups), ALL)
    return jax.shard_map(body, mesh=fine, in_specs=in_specs, out_specs=out_specs, check_vma=False)
```

```python
import functools
import math

import jax
import jax.numpy as jnp
import numpy as np
from jax import lax
from jax.experimental import pallas as pl
from jax.experimental.pallas import tpu as pltpu
from jax.sharding import Mesh
from jax.sharding import PartitionSpec as P

HEADS = 12
CAP = 128
STEP = 10


EPSILON = 1e-05
CLIP = 1.0
BETA_ONE = 0.9
BETA_TWO = 0.99
ADAM_FLOOR = 1e-08
DECAY = 0.1
RATE_MATRIX = 0.04
RATE_OUTPUT = 0.1
RATE_GAIN = 0.5

SEQ = ("hi", "lo", "in")
EXP = ("exp",)
ALL = SEQ + EXP
TEAM = ("lo",)
SHARE = ("hi", "in")
LANES = 128
HALF = 64
FAR = -1e30
BF16 = jnp.bfloat16
F32 = jnp.float32
VMEM_LIMIT = 60 * 1024 * 1024


def head_plan(count):
    whole = math.lcm(HEADS, count)
    units, parts = whole // count, whole // HEADS
    first = np.zeros((count,), np.int64)
    active = np.zeros((count, 2, count), np.int32)
    for device in range(count):
        first[device] = min(units * device // parts, HEADS - 2)
        for unit in range(units * device, units * (device + 1)):
            slot = unit // parts - first[device]
            for block in range(count):
                turn = block % (2 * parts)
                if min(turn, 2 * parts - 1 - turn) == unit % parts:
                    active[device, slot, block] = 1
    return first, active


def three_parts(value):
    high = value.astype(BF16).astype(F32)
    middle = (value - high).astype(BF16).astype(F32)
    return high, middle, value - high - middle


def contract(left, right, left_axis, right_axis):
    return lax.dot_general(
        left, right, (((left_axis,), (right_axis,)), ((), ())), preferred_element_type=F32
    )


def slot_arrays(packed, documents, kind, slot):
    spare = HALF - HALF * slot
    lane = lax.broadcasted_iota(jnp.int32, packed.shape, 1)
    own = (lane < HALF) if slot == 0 else (lane >= HALF)
    place = (lane - spare).astype(F32)
    ours = place == documents
    first = (lane >= spare) & (lane < spare + 3)
    if kind == "query":
        extra = jnp.where(first & jnp.logical_not(ours), FAR, 0.0)
    elif kind == "key":
        extra = jnp.where(ours | ((lane >= spare + 3) & (lane < spare + 6)), 1.0, 0.0)
    else:
        extra = jnp.where(first, 1.0, 0.0)
    return jnp.where(own, packed, extra).astype(BF16)


def fill_slots(packed_of, documents_ref, wide_ref, kinds, place):
    documents = documents_ref[place, :].astype(F32)
    for number, kind in enumerate(kinds):
        packed = packed_of(kind).astype(F32)
        if kind == "query":
            packed = packed * 0.125
        for slot in range(2):
            column = (2 * number + slot) * LANES
            wide_ref[place, column : column + LANES] = slot_arrays(packed, documents, kind, slot)


def attend_kernel(active_ref, order_ref, *refs, block, chunk, held):
    row_refs = refs[:held]
    columns_ref, documents_ref = refs[held : held + 2]
    low_ref, full_ref, stat_ref, pair_ref, mixed_ref, wide_ref = refs[held + 2 :]
    at = pl.program_id(0)

    @pl.when(at == 0)
    def _():
        def fill(tokens, index):
            place = pl.ds(pl.multiple_of(order_ref[index] * block, block), block)
            packed = contract(tokens, columns_ref[...], 1, 0).astype(BF16)
            pair_ref[place, :] = packed[:, LANES:]
            parts = {
                kind: packed[:, part * LANES : (part + 1) * LANES]
                for part, kind in enumerate(("query", "key", "value"))
            }
            fill_slots(parts.get, documents_ref, wide_ref, tuple(parts), place)

        if held > 1:
            for index, row_ref in enumerate(row_refs):
                fill(row_ref[...], index)
        else:

            @pl.loop(0, pl.num_programs(0))
            def _(index):
                fill(row_refs[0][pl.ds(pl.multiple_of(index * block, block), block), :], index)

    rows = pl.ds(pl.multiple_of(at * block, block), block)
    lane = lax.broadcasted_iota(jnp.int32, (block, LANES), 1)
    last = lax.div(at * block, chunk)
    for slot in range(2):
        spare = HALF - HALF * slot
        own = (lane < HALF) if slot == 0 else (lane >= HALF)
        columns = slice(slot * LANES, (slot + 1) * LANES)

        @pl.when(active_ref[slot, at] != 0)
        def _():
            query = wide_ref[rows, columns]

            def step(index, carry, edge):
                top, weighted = carry
                place = pl.ds(pl.multiple_of(index * chunk, chunk), chunk)
                keys = wide_ref[place, 2 * LANES + slot * LANES : 3 * LANES + slot * LANES]
                values = wide_ref[place, 4 * LANES + slot * LANES : 5 * LANES + slot * LANES]
                scores = contract(query, keys, 1, 1)
                if edge:
                    key_at = index * chunk + lax.broadcasted_iota(jnp.int32, (block, chunk), 1)
                    query_at = at * block + lax.broadcasted_iota(jnp.int32, (block, chunk), 0)
                    scores = jnp.where(key_at <= query_at, scores, FAR)
                new_top = jnp.maximum(top, jnp.max(scores, axis=1, keepdims=True))
                weights = jnp.exp(scores - new_top).astype(BF16)
                weighted = weighted * jnp.exp(top - new_top) + contract(weights, values, 1, 0)
                return new_top, weighted

            carry = (jnp.full((block, 1), FAR, F32), jnp.zeros((block, LANES), F32))
            carry = lax.fori_loop(0, last, lambda index, state: step(index, state, False), carry)
            top, weighted = step(last, carry, True)
            total = weighted[:, spare : spare + 1]
            mixed_ref[slot] = jnp.where(own, weighted / total, 0.0)
            log_total = top + jnp.log(total)
            high, middle, small = three_parts(log_total)
            extra = jnp.where(lane == spare + 3, -high, 0.0)
            extra = jnp.where(lane == spare + 4, -middle, extra)
            extra = jnp.where(lane == spare + 5, -small, extra)
            stat_ref[:, columns] = (query.astype(F32) + extra).astype(BF16)

        @pl.when(active_ref[slot, at] == 0)
        def _():
            mixed_ref[slot] = jnp.zeros((block, LANES), F32)
            stat_ref[:, columns] = jnp.zeros((block, LANES), BF16)

    mixed = mixed_ref[0] + mixed_ref[1]
    full_ref[...] = mixed
    low_ref[...] = mixed.astype(BF16)


def attend_back_kernel(
    active_ref,
    order_ref,
    pair_ref,
    documents_ref,
    stat_ref,
    grad_ref,
    mixed_ref,
    out_ref,
    lying_ref,
    key_sum_ref,
    value_sum_ref,
    query_sum_ref,
    wide_ref,
    *,
    block,
    chunk,
    scaling,
):
    at = pl.program_id(0)
    rows = pl.ds(pl.multiple_of(at * block, block), block)
    lane = lax.broadcasted_iota(jnp.int32, (block, LANES), 1)
    last = lax.div(at * block, chunk)

    @pl.when(at == 0)
    def _():
        @pl.loop(0, pl.num_programs(0))
        def _(index):
            place = pl.ds(pl.multiple_of(index * block, block), block)
            parts = {"key": pair_ref[place, :LANES], "value": pair_ref[place, LANES:]}
            fill_slots(parts.get, documents_ref, wide_ref, tuple(parts), place)

        key_sum_ref[...] = jnp.zeros_like(key_sum_ref)
        value_sum_ref[...] = jnp.zeros_like(value_sum_ref)

    for slot in range(2):
        spare = HALF - HALF * slot
        own = (lane < HALF) if slot == 0 else (lane >= HALF)
        columns = slice(slot * LANES, (slot + 1) * LANES)
        query_sum_ref[slot] = jnp.zeros((block, LANES), F32)

        @pl.when(active_ref[slot, at] != 0)
        def _():
            query = stat_ref[:, columns]
            grad = grad_ref[...].astype(F32)
            delta = jnp.sum(jnp.where(own, grad * mixed_ref[...], 0.0), axis=1, keepdims=True)
            high, middle, small = three_parts(delta)
            extra = jnp.where(lane == spare, -high, 0.0)
            extra = jnp.where(lane == spare + 1, -middle, extra)
            extra = jnp.where(lane == spare + 2, -small, extra)
            grad_low = jnp.where(own, grad, extra).astype(BF16)

            def step(index, edge):
                place = pl.ds(pl.multiple_of(index * chunk, chunk), chunk)
                keys = wide_ref[place, slot * LANES : (slot + 1) * LANES]
                values = wide_ref[place, (2 + slot) * LANES : (3 + slot) * LANES]
                scores = contract(keys, query, 1, 1)
                if edge:
                    key_at = index * chunk + lax.broadcasted_iota(jnp.int32, (chunk, block), 0)
                    query_at = at * block + lax.broadcasted_iota(jnp.int32, (chunk, block), 1)
                    scores = jnp.where(key_at <= query_at, scores, FAR)
                weights = jnp.exp(scores)
                grad_weights = contract(values, grad_low, 1, 1)
                grad_scores = (weights * grad_weights).astype(BF16)
                value_sum_ref[slot, place, :] += contract(weights.astype(BF16), grad_low, 1, 0)
                key_sum_ref[slot, place, :] += contract(grad_scores, query, 1, 0)
                query_sum_ref[slot] += contract(grad_scores, keys, 0, 0)

            @pl.loop(0, last)
            def _(index):
                step(index, False)

            step(last, True)

    first_half = lane < HALF
    query_grad = jnp.where(first_half, query_sum_ref[0], query_sum_ref[1]) * scaling
    out_ref[rows, :LANES] = query_grad.astype(BF16)
    lying = pl.ds(pl.multiple_of(order_ref[at] * block, block), block)
    lying_ref[lying, :LANES] = query_grad.astype(BF16)

    @pl.when(at == pl.num_programs(0) - 1)
    def _():
        @pl.loop(0, pl.num_programs(0))
        def _(index):
            place = pl.ds(pl.multiple_of(index * block, block), block)
            key_grad = jnp.where(first_half, key_sum_ref[0, place, :], key_sum_ref[1, place, :])
            value_grad = jnp.where(
                first_half, value_sum_ref[0, place, :], value_sum_ref[1, place, :]
            )
            out_ref[place, LANES : 2 * LANES] = key_grad.astype(BF16)
            out_ref[place, 2 * LANES :] = value_grad.astype(BF16)
            lying = pl.ds(pl.multiple_of(order_ref[index] * block, block), block)
            lying_ref[lying, LANES : 2 * LANES] = key_grad.astype(BF16)
            lying_ref[lying, 2 * LANES :] = value_grad.astype(BF16)


def whole(value):
    return pl.BlockSpec(value.shape, lambda i, *unused: (0, 0), pipeline_mode=pl.Buffered(1))


SMALL = pl.CostEstimate(flops=1, bytes_accessed=1, transcendentals=0)


def attend(active, order, row_blocks, columns, documents, block):
    length = documents.shape[0]
    pair = jax.ShapeDtypeStruct((length, 2 * LANES), BF16)
    return pl.pallas_call(
        functools.partial(attend_kernel, block=block, chunk=2 * block, held=len(row_blocks)),
        grid_spec=pltpu.PrefetchScalarGridSpec(
            num_scalar_prefetch=2,
            grid=(length // block,),
            in_specs=[whole(value) for value in (*row_blocks, columns, documents)],
            out_specs=[
                pl.BlockSpec((block, LANES), lambda i, a, o: (i, 0)),
                pl.BlockSpec((block, LANES), lambda i, a, o: (i, 0)),
                pl.BlockSpec((block, 2 * LANES), lambda i, a, o: (i, 0)),
                whole(pair),
            ],
            scratch_shapes=[
                pltpu.VMEM((2, block, LANES), F32),
                pltpu.VMEM((length, 6 * LANES), BF16),
            ],
        ),
        out_shape=[
            jax.ShapeDtypeStruct((length, LANES), BF16),
            jax.ShapeDtypeStruct((length, LANES), F32),
            jax.ShapeDtypeStruct((length, 2 * LANES), BF16),
            pair,
        ],
        compiler_params=pltpu.CompilerParams(vmem_limit_bytes=VMEM_LIMIT),
        cost_estimate=SMALL,
    )(active, order, *row_blocks, columns, documents)


def attend_back(active, order, pair, documents, stat, grad, mixed, block, scaling):
    length = pair.shape[0]
    count = length // block
    return pl.pallas_call(
        functools.partial(attend_back_kernel, block=block, chunk=2 * block, scaling=scaling),
        grid_spec=pltpu.PrefetchScalarGridSpec(
            num_scalar_prefetch=2,
            grid=(count,),
            in_specs=[
                whole(pair),
                whole(documents),
                pl.BlockSpec((block, 2 * LANES), lambda i, a, o: (i, 0)),
                pl.BlockSpec((block, LANES), lambda i, a, o: (i, 0)),
                pl.BlockSpec((block, LANES), lambda i, a, o: (i, 0)),
            ],
            out_specs=[
                pl.BlockSpec(
                    (length, 3 * LANES), lambda i, a, o: (0, 0), pipeline_mode=pl.Buffered(1)
                )
            ]
            * 2,
            scratch_shapes=[
                pltpu.VMEM((2, length, LANES), F32),
                pltpu.VMEM((2, length, LANES), F32),
                pltpu.VMEM((2, block, LANES), F32),
                pltpu.VMEM((length, 4 * LANES), BF16),
            ],
        ),
        out_shape=[jax.ShapeDtypeStruct((length, 3 * LANES), BF16)] * 2,
        compiler_params=pltpu.CompilerParams(vmem_limit_bytes=VMEM_LIMIT),
        cost_estimate=SMALL,
    )(active, order, pair, documents, stat, grad, mixed)


def expert_kernel(arrived_ref, grad_ref, *refs, count):
    up_refs, down_refs = refs[:count], refs[count : 2 * count]
    total_ref = refs[2 * count]
    active_refs, hidden_refs = refs[2 * count + 1 : 3 * count + 1], refs[3 * count + 1 :]
    arrived, grad_arrived = arrived_ref[...], grad_ref[...]
    scale = math.sqrt(2.0 / math.pi)
    total = jnp.zeros(total_ref.shape, F32)
    for up_ref, down_ref, active_ref, hidden_ref in zip(
        up_refs, down_refs, active_refs, hidden_refs, strict=True
    ):
        up = up_ref[...]
        hidden = contract(arrived, up, 1, 1)
        squared = hidden * hidden
        bend = jnp.tanh(scale * hidden * (1.0 + 0.044715 * squared))
        half = 0.5 + 0.5 * bend
        active_ref[...] = (hidden * half).astype(BF16)
        slope = half + (0.5 * scale) * hidden * (1.0 - bend * bend) * (1.0 + 3 * 0.044715 * squared)
        grad_hidden = (slope * contract(grad_arrived, down_ref[...], 1, 1)).astype(BF16)
        hidden_ref[...] = grad_hidden
        total = total + contract(grad_hidden, up, 1, 0)
    total_ref[...] = total.astype(BF16)


def rows_spec(value, block):
    return pl.BlockSpec((block, value.shape[1]), lambda i: (i, 0))


def expert_part(arrived, grad_arrived, ups, downs):
    slots, width = arrived.shape
    block = 256
    units = [jax.ShapeDtypeStruct((slots, up.shape[0]), BF16) for up in ups]
    outs = [jax.ShapeDtypeStruct((slots, width), BF16), *units, *units]
    total, *parts = pl.pallas_call(
        functools.partial(expert_kernel, count=len(ups)),
        grid=(slots // block,),
        in_specs=[rows_spec(arrived, block), rows_spec(grad_arrived, block)]
        + [whole(value) for value in (*ups, *downs)],
        out_specs=[rows_spec(out, block) for out in outs],
        out_shape=outs,
        compiler_params=pltpu.CompilerParams(vmem_limit_bytes=VMEM_LIMIT),
        cost_estimate=SMALL,
    )(arrived, grad_arrived, *ups, *downs)
    return total, parts[: len(ups)], parts[len(ups) :]


def produced_kernel(*refs, count):
    total = contract(refs[0][...], refs[count][...], 1, 0)
    for index in range(1, count):
        total = total + contract(refs[index][...], refs[count + index][...], 1, 0)
    refs[-1][...] = total.astype(BF16)


def produced_part(actives, downs):
    slots, width = actives[0].shape[0], downs[0].shape[1]
    block = 256
    out = jax.ShapeDtypeStruct((slots, width), BF16)
    return pl.pallas_call(
        functools.partial(produced_kernel, count=len(actives)),
        grid=(slots // block,),
        in_specs=[rows_spec(value, block) for value in actives] + [whole(down) for down in downs],
        out_specs=rows_spec(out, block),
        out_shape=out,
        compiler_params=pltpu.CompilerParams(vmem_limit_bytes=VMEM_LIMIT),
        cost_estimate=SMALL,
    )(*actives, *downs)


def unit_kernel(grad_ref, arrived_ref, *refs, count):
    for index in range(count):
        active_ref, hidden_ref = refs[2 * index : 2 * index + 2]
        down_ref, up_ref = refs[2 * count + 2 * index : 2 * count + 2 * index + 2]
        down_ref[...] = contract(active_ref[...], grad_ref[...], 0, 0).astype(down_ref.dtype)
        up_ref[...] = contract(hidden_ref[...], arrived_ref[...], 0, 0).astype(up_ref.dtype)


def unit_grads(grad_arrived, arrived, blocks, kinds):
    slots, width = arrived.shape
    block = 256
    right = pl.BlockSpec((slots, block), lambda i: (0, i))
    outs = [
        jax.ShapeDtypeStruct((active.shape[1], width), kind)
        for (active, unused), kind in zip(blocks, kinds, strict=True)
        for part in range(2)
    ]
    flat = [value for pair in blocks for value in pair]
    return pl.pallas_call(
        functools.partial(unit_kernel, count=len(blocks)),
        grid=(width // block,),
        in_specs=[right, right] + [whole(value) for value in flat],
        out_specs=[pl.BlockSpec((out.shape[0], block), lambda i: (0, i)) for out in outs],
        out_shape=outs,
        compiler_params=pltpu.CompilerParams(vmem_limit_bytes=VMEM_LIMIT),
        cost_estimate=SMALL,
    )(grad_arrived, arrived, *flat)


def column_kernel(*refs, held):
    row_refs = refs[:held]
    lying_ref, out_ref = refs[held:]
    start, total = 0, None
    for row_ref in row_refs:
        rows = row_ref.shape[0]
        part = contract(row_ref[...], lying_ref[start : start + rows, :], 0, 0)
        total = part if total is None else total + part
        start += rows
    out_ref[...] = total.astype(BF16)


def column_terms(row_blocks, grad_lying):
    width = row_blocks[0].shape[1]
    block = 256
    out = jax.ShapeDtypeStruct((width, 3 * LANES), BF16)
    return pl.pallas_call(
        functools.partial(column_kernel, held=len(row_blocks)),
        grid=(width // block,),
        in_specs=[
            pl.BlockSpec((value.shape[0], block), lambda i: (0, i)) for value in row_blocks
        ]
        + [whole(grad_lying)],
        out_specs=rows_spec(out, block),
        out_shape=out,
        compiler_params=pltpu.CompilerParams(vmem_limit_bytes=VMEM_LIMIT),
        cost_estimate=SMALL,
    )(*row_blocks, grad_lying)


def close_kernel(pieces_ref, columns_ref, tokens_ref, gain_ref, residual_ref, out_ref, part_ref, sum_ref):
    at = pl.program_id(0)

    @pl.when(at == 0)
    def _():
        sum_ref[...] = jnp.zeros_like(sum_ref)

    sum_ref[...] += contract(pieces_ref[0], columns_ref[...], 1, 1)

    @pl.when(at == pl.num_programs(0) - 1)
    def _():
        inputs = tokens_ref[...].astype(F32)
        scale = lax.rsqrt(jnp.mean(inputs * inputs, axis=-1, keepdims=True) + EPSILON)
        normed = inputs * scale
        grad = sum_ref[...]
        scaled = grad * gain_ref[...]
        mean = jnp.mean(scaled * normed, axis=-1, keepdims=True)
        out_ref[...] = residual_ref[...] + scale * (scaled - normed * mean)
        part_ref[...] = jnp.sum(grad * normed, axis=0, keepdims=True)


def close_norm(pieces, columns, tokens, gain, residual):
    count, rows, lanes = pieces.shape
    width = tokens.shape[1]
    outs = [
        jax.ShapeDtypeStruct((rows, width), F32),
        jax.ShapeDtypeStruct((1, width), F32),
    ]
    return pl.pallas_call(
        close_kernel,
        grid=(count,),
        in_specs=[
            pl.BlockSpec((1, rows, lanes), lambda i: (i, 0, 0)),
            pl.BlockSpec((width, lanes), lambda i: (0, i)),
            whole(tokens),
            whole(gain),
            whole(residual),
        ],
        out_specs=[whole(out) for out in outs],
        out_shape=outs,
        scratch_shapes=[pltpu.VMEM((rows, width), F32)],
        compiler_params=pltpu.CompilerParams(vmem_limit_bytes=VMEM_LIMIT),
        cost_estimate=SMALL,
    )(pieces, columns, tokens, gain, residual)


def adam_update(weight, grad, first, second, factor, rate, decay):
    clipped = grad * factor
    first_new = BETA_ONE * first + (1.0 - BETA_ONE) * clipped
    second_new = BETA_TWO * second + (1.0 - BETA_TWO) * clipped * clipped
    first_hat = first_new / (1.0 - BETA_ONE**STEP)
    second_hat = second_new / (1.0 - BETA_TWO**STEP)
    weight_new = weight - rate * (first_hat / (jnp.sqrt(second_hat) + ADAM_FLOOR) + decay * weight)
    return (first_new, second_new, weight_new)


def together(*values):
    return lax.optimization_barrier(values)


def swap(value, axes):
    return lax.all_to_all(value, axes, split_axis=0, concat_axis=0, tiled=True)


def adam_kernel(factor_ref, *refs, rates):
    count = len(rates)
    factor = factor_ref[0]
    for index, rate in enumerate(rates):
        weight, grad, first, second = [ref[...] for ref in refs[4 * index : 4 * index + 4]]
        outs = refs[4 * count + 3 * index : 4 * count + 3 * index + 3]
        for out, value in zip(
            outs, adam_update(weight, grad, first, second, factor, rate, DECAY), strict=True
        ):
            out[...] = value


def adam_all(factor, leaves, rates, steps):
    flat = [value.reshape(value.shape[-2:]) for leaf in leaves for value in leaf]

    def spec(value):
        rows, columns = value.shape
        if rows % (8 * steps) == 0:
            return pl.BlockSpec((rows // steps, columns), lambda i: (i, 0))
        lanes = columns // steps
        return pl.BlockSpec((rows, lanes), lambda i: (0, i))

    shapes = [jax.ShapeDtypeStruct(value.shape, F32) for value in flat[::4] for _ in range(3)]
    outs = pl.pallas_call(
        functools.partial(adam_kernel, rates=rates),
        grid=(steps,),
        in_specs=[pl.BlockSpec(memory_space=pltpu.SMEM)] + [spec(value) for value in flat],
        out_specs=[spec(shape) for shape in shapes],
        out_shape=shapes,
        compiler_params=pltpu.CompilerParams(vmem_limit_bytes=VMEM_LIMIT),
        cost_estimate=pl.CostEstimate(
            flops=20 * sum(value.size for value in flat[::4]),
            bytes_accessed=28 * sum(value.size for value in flat[::4]),
            transcendentals=0,
        ),
    )(factor.reshape(1), *flat)
    return [
        [out.reshape(leaf[0].shape) for out in outs[3 * index : 3 * index + 3]]
        for index, leaf in enumerate(leaves)
    ]


def flip(value, bits):
    count = lax.axis_size(SEQ)
    return lax.ppermute(value, SEQ, [(index, index ^ bits) for index in range(count)])


def others(value, axis):
    size = lax.axis_size(axis)
    parts = [
        lax.ppermute(value, axis, [((i + step) % size, i) for i in range(size)])
        for step in range(1, size)
    ]
    return parts[0] if size == 2 else jnp.concatenate(parts, axis=0)


def to_owners(blocks, axis):
    size = lax.axis_size(axis)
    return [
        lax.ppermute(block, axis, [(i, (i + step) % size) for i in range(size)])
        for step, block in enumerate(blocks, 1)
    ]


def add_all(own, parts):
    return functools.reduce(lambda total, part: total + part.astype(F32), parts, own.astype(F32))


def spread_sum(value):
    count = lax.axis_size(ALL)
    return jnp.sum(swap(jnp.broadcast_to(value[None], (count, *value.shape)), ALL), axis=0)


def body(
    tokens,
    cotangent,
    segment_ids,
    expert_ids,
    projection,
    output_weight,
    expert_up,
    expert_down,
    norm_gains,
    projection_first,
    projection_second,
    output_first,
    output_second,
    up_first,
    up_second,
    down_first,
    down_second,
    gains_first,
    gains_second,
):
    inputs = tokens[0].astype(F32)
    upstream = cotangent[0].astype(F32)
    row_count = inputs.shape[0]
    width = inputs.shape[1]
    head_size = width // HEADS
    scaling = head_size ** (-0.5)
    count = lax.axis_size(SEQ)
    groups = lax.axis_size("exp")
    team = lax.axis_size(TEAM)
    position = lax.axis_index(SEQ)
    length = count * row_count
    weight_rows = projection.shape[0]
    first_heads, active_table = head_plan(count)
    starts = [int(head) * head_size for head in first_heads]
    active = lax.dynamic_index_in_dim(jnp.asarray(active_table), position, 0, keepdims=False)
    gain_first = norm_gains[0]
    gain_second = norm_gains[1]
    used = active_table.any(axis=2)

    scale_first = lax.rsqrt(jnp.mean(inputs * inputs, axis=-1, keepdims=True) + EPSILON)
    normed_first = inputs * scale_first
    attend_in = (normed_first * gain_first).astype(BF16)
    slots = groups * CAP
    chosen = expert_ids[0, :, 0]
    one_hot = (chosen[:, None] == jnp.arange(groups, dtype=jnp.int32)[None, :]).astype(jnp.int32)
    rank = jnp.sum(jnp.cumsum(one_hot, axis=0) * one_hot, axis=1) - 1
    target = chosen * CAP + rank
    placing = (target[:, None] == jnp.arange(slots, dtype=jnp.int32)[None, :]).astype(BF16)

    def to_slots(values):
        outgoing = jnp.einsum("ts,td->sd", placing, values, preferred_element_type=F32)
        return outgoing.astype(BF16)

    def dispatch(outgoing):
        outgoing = jnp.broadcast_to(
            outgoing.reshape(1, groups, CAP, width), (team, groups, CAP, width)
        )
        return swap(outgoing.reshape(team * groups, CAP, width), TEAM + EXP).reshape(
            team * slots, width
        )

    def send_back(values):
        return swap(values.reshape(team * groups, CAP, width), TEAM + EXP).reshape(
            team, slots, width
        )

    def collect(returned):
        return jnp.einsum("ts,jsd->td", placing, returned, preferred_element_type=F32)

    projection_low = projection.astype(BF16)
    sent_rows = weight_rows + 8
    own_documents = jnp.zeros((8, 3 * LANES + width), BF16)
    own_documents = own_documents.at[0, :row_count].set(segment_ids[0].astype(BF16))
    output_low = output_weight.astype(BF16)
    pieces = [
        jnp.concatenate(
            [projection_low[:, k * width + s : k * width + s + LANES] for k in range(3)]
            + [output_low],
            axis=1,
        )
        for s in starts
    ]
    pieces = jnp.stack([jnp.concatenate([piece, own_documents], axis=0) for piece in pieces])
    own_up = expert_up[0].astype(BF16)
    own_down = expert_down[0].astype(BF16)
    pairwise = count == 8
    if pairwise:
        order = jnp.arange(count, dtype=jnp.int32) ^ position
        beside, below, across = flip(attend_in, 1), flip(attend_in, 2), flip(attend_in, 4)
        got_rows, beside, below, across, own_up = together(
            swap(pieces, SEQ), beside, below, across, own_up
        )
        corner = flip(across, 2)
        row_blocks = [attend_in, beside]
        row_blocks += [part for block in (below, across, corner) for part in (block, flip(block, 1))]
    else:
        order = jnp.arange(count, dtype=jnp.int32)
        row_blocks = [lax.all_gather(attend_in, SEQ, axis=0, tiled=True)]
        got_rows = swap(pieces, SEQ)
    documents = jnp.broadcast_to(
        got_rows[:, weight_rows, :row_count].reshape(length, 1), (length, LANES)
    )
    own_copies = jnp.broadcast_to(
        got_rows[None, :, :weight_rows], (groups, count, weight_rows, 3 * LANES + width)
    )
    all_copies = swap(own_copies, EXP)

    peer_up = others(own_up, "hi")
    *row_blocks, all_copies, peer_up, own_up, own_down, grad_slots_out = together(
        *row_blocks, all_copies, peer_up, own_up, own_down, to_slots(cotangent[0])
    )
    all_copies = jnp.swapaxes(all_copies, 0, 1)
    columns = all_copies[..., : 3 * LANES].reshape(width, 3 * LANES)
    output_full = all_copies[..., 3 * LANES :].reshape(width, width)
    grad_arrived = dispatch(grad_slots_out)
    peer_down = others(own_down, "hi")
    side_up = others(own_up, "in")
    side_down = others(own_down, "in")
    far_up = others(peer_up, "in")

    mixed_low, mixed_full, stat, pair = attend(
        active, order, row_blocks, columns, documents, row_count
    )

    def place_heads():
        index = np.arange(LANES)
        matrix = np.zeros((count, LANES, width), np.float32)
        for device in range(count):
            for slot in range(2):
                if used[device, slot]:
                    own = index[slot * HALF : (slot + 1) * HALF]
                    matrix[device, own, starts[device] + own] = 1.0
        return jnp.asarray(matrix, BF16)

    head_places = place_heads()

    def to_tokens(values):
        return swap(values.reshape(count, row_count, values.shape[1]), SEQ)

    mixed_low, grad_arrived, peer_down, side_up, side_down, far_up = together(
        mixed_low, grad_arrived, peer_down, side_up, side_down, far_up
    )
    far_down = others(peer_down, "in")
    mixed_pieces, projection_low = together(to_tokens(mixed_low), projection_low)
    projection_full = lax.all_gather(projection_low, ALL, axis=0, tiled=True)
    attend_out = jnp.einsum(
        "jtc,jcd->td", mixed_pieces, head_places, preferred_element_type=F32
    ).astype(BF16)
    branch = jnp.dot(attend_out, output_full, preferred_element_type=F32)
    middle = inputs + branch
    scale_second = lax.rsqrt(jnp.mean(middle * middle, axis=-1, keepdims=True) + EPSILON)
    normed_second = middle * scale_second
    expert_in = (normed_second * gain_second).astype(BF16)

    expert_slots, far_down = together(to_slots(expert_in), far_down)
    arrived = dispatch(expert_slots)
    ups, downs = (own_up, peer_up, side_up, far_up), (own_down, peer_down, side_down, far_down)
    grad_slots, actives, hiddens = expert_part(arrived, grad_arrived, ups, downs)
    returned_grad = send_back(grad_slots)

    blocks = list(zip(actives, hiddens, strict=True))
    down_far, up_far, down_peer, up_peer = unit_grads(
        grad_arrived, arrived, (blocks[3], blocks[1]), (BF16, F32)
    )
    (down_part,) = to_owners([down_far], "in")
    down_side, up_side, down_own, up_own = unit_grads(
        grad_arrived, arrived, (blocks[2], blocks[0]), (BF16, F32)
    )
    produced = produced_part(actives, downs)
    returned_grad, down_part, up_far, up_peer, projection_full, produced, down_side, up_own = (
        together(
            returned_grad, down_part, up_far, up_peer, projection_full, produced, down_side, up_own
        )
    )
    grad_expert_in = collect(returned_grad)
    (up_part,) = to_owners([up_far], "in")
    peers = lax.axis_size("hi")

    def hi_parts(value):
        return to_owners(list(value.astype(BF16).reshape(peers - 1, -1, width)), "hi")

    down_hi = hi_parts(add_all(down_peer, [down_part]))

    scaled_second = grad_expert_in * gain_second
    gain_second_part = jnp.sum(grad_expert_in * normed_second, axis=0)
    grad_middle = scale_second * (
        scaled_second
        - normed_second * jnp.mean(scaled_second * normed_second, axis=-1, keepdims=True)
    )
    residual_grad = upstream + grad_middle
    branch_grad = residual_grad.astype(BF16)
    grad_mixed = jnp.einsum(
        "td,ed->te", branch_grad, output_full, preferred_element_type=F32
    ).astype(BF16)

    sent_grad = jnp.stack([grad_mixed[:, s : s + LANES] for s in starts])
    sent_grad, *down_hi = together(sent_grad, *down_hi)
    row_grad = swap(sent_grad, SEQ).reshape(length, LANES)

    group = lax.axis_index(EXP)

    def group_rows(value):
        rows = value.reshape(count, groups, weight_rows, -1)
        own, *away = [
            lax.dynamic_index_in_dim(rows, lax.rem(group + step, groups), 1, keepdims=False)
            for step in range(groups)
        ]
        return own, away

    output_term = jnp.einsum("tc,te->ce", attend_out, branch_grad, preferred_element_type=F32)
    output_own, output_away = group_rows(output_term.astype(BF16))
    row_grad, produced, down_side, up_side, up_part, *output_away = together(
        row_grad, produced, down_side, up_side, up_part, *output_away
    )
    output_away = to_owners(output_away, "exp")
    (down_early,) = to_owners([down_side], "in")
    (up_early,) = to_owners([up_side], "in")
    up_hi = hi_parts(add_all(up_peer, [up_part]))
    returned = send_back(produced)
    grad_qkv, grad_lying = attend_back(
        active, order, pair, documents, stat, row_grad, mixed_full, row_count, scaling
    )
    grad_qkv, grad_lying, returned, down_early, up_early, *held = together(
        grad_qkv, grad_lying, returned, down_early, up_early, *up_hi, *output_away
    )
    up_hi, output_away = held[: len(up_hi)], held[len(up_hi) :]
    up_grad = add_all(up_own, [up_early, *up_hi])[None]
    down_grad = add_all(down_own, [down_early, *down_hi])[None]
    block_output = (middle + collect(returned)).astype(BF16)[None]

    column_own, column_away = group_rows(column_terms(row_blocks, grad_lying))
    dense_rows = jnp.concatenate(
        [
            add_all(column_own, to_owners(column_away, "exp")).astype(BF16),
            add_all(output_own, output_away).astype(BF16),
        ],
        axis=2,
    )
    wide_columns = jnp.concatenate(
        [projection_full[:, k * width + s : k * width + s + LANES] for s in starts for k in range(3)],
        axis=1,
    )
    if pairwise:
        lying_terms = [
            lax.dynamic_index_in_dim(dense_rows, position ^ bits, 0, keepdims=False)
            for bits in range(count)
        ]
        lying_terms[1:] = [flip(lying_terms[bits], bits) for bits in range(1, count)]
        grad_pieces, wide_columns, *lying_terms = together(
            to_tokens(grad_qkv), wide_columns, *lying_terms
        )
        lying_terms = jnp.stack(lying_terms)
        got_terms = [
            lax.dynamic_index_in_dim(lying_terms, position ^ j, 0, keepdims=False)
            for j in range(count)
        ]
    else:
        grad_pieces, dense_rows = together(to_tokens(grad_qkv), dense_rows)
        got_terms = list(swap(dense_rows, SEQ))
    got_terms = [term.astype(F32) for term in got_terms]
    input_grad, gain_first_part = close_norm(
        grad_pieces, wide_columns, tokens[0], gain_first[None], residual_grad
    )
    input_grad, gain_first_part = input_grad[None], gain_first_part[0]
    output_grad = functools.reduce(jnp.add, [term[:, 3 * LANES :] for term in got_terms])
    head_grads = []
    for k in range(3):
        for head in range(HEADS):
            parts = [
                got_terms[j][:, k * LANES + slot * HALF : k * LANES + (slot + 1) * HALF]
                for j in range(count)
                for slot in range(2)
                if used[j, slot] and first_heads[j] + slot == head
            ]
            head_grads.append(functools.reduce(jnp.add, parts))
    projection_grad = jnp.concatenate(head_grads, axis=1)

    local_square = jnp.sum(projection_grad * projection_grad) + jnp.sum(output_grad * output_grad)
    local_square = local_square + jnp.sum(up_grad * up_grad) + jnp.sum(down_grad * down_grad)
    summed = spread_sum(
        jnp.concatenate(
            [gain_first_part, gain_second_part, jnp.broadcast_to(local_square, (LANES,))]
        )[None]
    )[0]
    gains_grad = summed[: 2 * width].reshape(2, width)
    grad_norm = jnp.sqrt(summed[2 * width] + jnp.sum(gains_grad * gains_grad))
    factor = jnp.minimum(1.0, CLIP / (grad_norm + 1e-06))
    (
        (projection_moment, projection_square, projection_new),
        (output_moment, output_square, output_new),
        (up_moment, up_square, up_new),
        (down_moment, down_square, down_new),
    ) = adam_all(
        factor,
        [
            (projection, projection_grad, projection_first, projection_second),
            (output_weight, output_grad, output_first, output_second),
            (expert_up, up_grad, up_first, up_second),
            (expert_down, down_grad, down_first, down_second),
        ],
        (RATE_MATRIX, RATE_OUTPUT, RATE_MATRIX, RATE_MATRIX),
        6,
    )
    gains_moment, gains_square, gains_new = adam_update(
        norm_gains, gains_grad, gains_first, gains_second, factor, RATE_GAIN, 0.0
    )
    return (
        block_output,
        input_grad,
        grad_norm,
        projection_grad,
        projection_moment,
        projection_square,
        projection_new,
        output_grad,
        output_moment,
        output_square,
        output_new,
        up_grad,
        up_moment,
        up_square,
        up_new,
        down_grad,
        down_moment,
        down_square,
        down_new,
        gains_grad,
        gains_moment,
        gains_square,
        gains_new,
    )


def solution(mesh):
    token = P("exp", SEQ, None)
    dense = P(ALL, None)
    expert = P("exp", SEQ, None)
    in_specs = (
        (token, token, P("exp", SEQ), token)
        + (dense, dense, expert, expert, P())
        + (dense,) * 4
        + (expert,) * 4
        + (P(), P())
    )
    out_specs = (token, token, P()) + (dense,) * 8 + (expert,) * 8 + (P(),) * 4
    rows, groups = mesh.devices.shape
    fine = Mesh(mesh.devices.reshape(rows // 4, 2, 2, groups), ALL)
    return jax.shard_map(body, mesh=fine, in_specs=in_specs, out_specs=out_specs, check_vma=False)
```

```python
import functools
import math

import jax
import jax.numpy as jnp
import numpy as np
from jax import lax
from jax.experimental import pallas as pl
from jax.experimental.pallas import tpu as pltpu
from jax.sharding import Mesh
from jax.sharding import PartitionSpec as P

HEADS = 12
CAP = 128
STEP = 10


EPSILON = 1e-05
CLIP = 1.0
BETA_ONE = 0.9
BETA_TWO = 0.99
ADAM_FLOOR = 1e-08
DECAY = 0.1
RATE_MATRIX = 0.04
RATE_OUTPUT = 0.1
RATE_GAIN = 0.5

SEQ = ("hi", "lo", "in")
EXP = ("exp",)
ALL = SEQ + EXP
TEAM = ("lo",)
SHARE = ("hi", "in")
LANES = 128
HALF = 64
FAR = -1e30
BF16 = jnp.bfloat16
F32 = jnp.float32
VMEM_LIMIT = 60 * 1024 * 1024


def head_plan(count):
    whole = math.lcm(HEADS, count)
    units, parts = whole // count, whole // HEADS
    first = np.zeros((count,), np.int64)
    active = np.zeros((count, 2, count), np.int32)
    for device in range(count):
        first[device] = min(units * device // parts, HEADS - 2)
        for unit in range(units * device, units * (device + 1)):
            slot = unit // parts - first[device]
            for block in range(count):
                turn = block % (2 * parts)
                if min(turn, 2 * parts - 1 - turn) == unit % parts:
                    active[device, slot, block] = 1
    return first, active


def three_parts(value):
    high = value.astype(BF16).astype(F32)
    middle = (value - high).astype(BF16).astype(F32)
    return high, middle, value - high - middle


def contract(left, right, left_axis, right_axis):
    return lax.dot_general(
        left, right, (((left_axis,), (right_axis,)), ((), ())), preferred_element_type=F32
    )


def slot_arrays(packed, documents, kind, slot):
    spare = HALF - HALF * slot
    lane = lax.broadcasted_iota(jnp.int32, packed.shape, 1)
    own = (lane < HALF) if slot == 0 else (lane >= HALF)
    place = (lane - spare).astype(F32)
    ours = place == documents
    first = (lane >= spare) & (lane < spare + 3)
    if kind == "query":
        extra = jnp.where(first & jnp.logical_not(ours), FAR, 0.0)
    elif kind == "key":
        extra = jnp.where(ours | ((lane >= spare + 3) & (lane < spare + 6)), 1.0, 0.0)
    else:
        extra = jnp.where(first, 1.0, 0.0)
    return jnp.where(own, packed, extra).astype(BF16)


def fill_slots(packed_of, documents_ref, wide_ref, kinds, place):
    documents = documents_ref[place, :].astype(F32)
    for number, kind in enumerate(kinds):
        packed = packed_of(kind).astype(F32)
        if kind == "query":
            packed = packed * 0.125
        for slot in range(2):
            column = (2 * number + slot) * LANES
            wide_ref[place, column : column + LANES] = slot_arrays(packed, documents, kind, slot)


def attend_kernel(active_ref, order_ref, *refs, block, chunk, held):
    row_refs = refs[:held]
    columns_ref, documents_ref = refs[held : held + 2]
    low_ref, full_ref, stat_ref, pair_ref, mixed_ref, wide_ref = refs[held + 2 :]
    at = pl.program_id(0)

    @pl.when(at == 0)
    def _():
        def fill(tokens, index):
            place = pl.ds(pl.multiple_of(order_ref[index] * block, block), block)
            packed = contract(tokens, columns_ref[...], 1, 0).astype(BF16)
            pair_ref[place, :] = packed[:, LANES:]
            parts = {
                kind: packed[:, part * LANES : (part + 1) * LANES]
                for part, kind in enumerate(("query", "key", "value"))
            }
            fill_slots(parts.get, documents_ref, wide_ref, tuple(parts), place)

        if held > 1:
            for index, row_ref in enumerate(row_refs):
                fill(row_ref[...], index)
        else:

            @pl.loop(0, pl.num_programs(0))
            def _(index):
                fill(row_refs[0][pl.ds(pl.multiple_of(index * block, block), block), :], index)

    rows = pl.ds(pl.multiple_of(at * block, block), block)
    lane = lax.broadcasted_iota(jnp.int32, (block, LANES), 1)
    last = lax.div(at * block, chunk)
    for slot in range(2):
        spare = HALF - HALF * slot
        own = (lane < HALF) if slot == 0 else (lane >= HALF)
        columns = slice(slot * LANES, (slot + 1) * LANES)

        @pl.when(active_ref[slot, at] != 0)
        def _():
            query = wide_ref[rows, columns]

            def step(index, carry, edge):
                top, weighted = carry
                place = pl.ds(pl.multiple_of(index * chunk, chunk), chunk)
                keys = wide_ref[place, 2 * LANES + slot * LANES : 3 * LANES + slot * LANES]
                values = wide_ref[place, 4 * LANES + slot * LANES : 5 * LANES + slot * LANES]
                scores = contract(query, keys, 1, 1)
                if edge:
                    key_at = index * chunk + lax.broadcasted_iota(jnp.int32, (block, chunk), 1)
                    query_at = at * block + lax.broadcasted_iota(jnp.int32, (block, chunk), 0)
                    scores = jnp.where(key_at <= query_at, scores, FAR)
                new_top = jnp.maximum(top, jnp.max(scores, axis=1, keepdims=True))
                weights = jnp.exp(scores - new_top).astype(BF16)
                weighted = weighted * jnp.exp(top - new_top) + contract(weights, values, 1, 0)
                return new_top, weighted

            carry = (jnp.full((block, 1), FAR, F32), jnp.zeros((block, LANES), F32))
            carry = lax.fori_loop(0, last, lambda index, state: step(index, state, False), carry)
            top, weighted = step(last, carry, True)
            total = weighted[:, spare : spare + 1]
            mixed_ref[slot] = jnp.where(own, weighted / total, 0.0)
            log_total = top + jnp.log(total)
            high, middle, small = three_parts(log_total)
            extra = jnp.where(lane == spare + 3, -high, 0.0)
            extra = jnp.where(lane == spare + 4, -middle, extra)
            extra = jnp.where(lane == spare + 5, -small, extra)
            stat_ref[:, columns] = (query.astype(F32) + extra).astype(BF16)

        @pl.when(active_ref[slot, at] == 0)
        def _():
            mixed_ref[slot] = jnp.zeros((block, LANES), F32)
            stat_ref[:, columns] = jnp.zeros((block, LANES), BF16)

    mixed = mixed_ref[0] + mixed_ref[1]
    full_ref[...] = mixed
    low_ref[...] = mixed.astype(BF16)


def attend_back_kernel(
    active_ref,
    order_ref,
    pair_ref,
    documents_ref,
    stat_ref,
    grad_ref,
    mixed_ref,
    out_ref,
    lying_ref,
    key_sum_ref,
    value_sum_ref,
    query_sum_ref,
    wide_ref,
    *,
    block,
    chunk,
    scaling,
):
    at = pl.program_id(0)
    rows = pl.ds(pl.multiple_of(at * block, block), block)
    lane = lax.broadcasted_iota(jnp.int32, (block, LANES), 1)
    last = lax.div(at * block, chunk)

    @pl.when(at == 0)
    def _():
        @pl.loop(0, pl.num_programs(0))
        def _(index):
            place = pl.ds(pl.multiple_of(index * block, block), block)
            parts = {"key": pair_ref[place, :LANES], "value": pair_ref[place, LANES:]}
            fill_slots(parts.get, documents_ref, wide_ref, tuple(parts), place)

        key_sum_ref[...] = jnp.zeros_like(key_sum_ref)
        value_sum_ref[...] = jnp.zeros_like(value_sum_ref)

    for slot in range(2):
        spare = HALF - HALF * slot
        own = (lane < HALF) if slot == 0 else (lane >= HALF)
        columns = slice(slot * LANES, (slot + 1) * LANES)
        query_sum_ref[slot] = jnp.zeros((block, LANES), F32)

        @pl.when(active_ref[slot, at] != 0)
        def _():
            query = stat_ref[:, columns]
            grad = grad_ref[...].astype(F32)
            delta = jnp.sum(jnp.where(own, grad * mixed_ref[...], 0.0), axis=1, keepdims=True)
            high, middle, small = three_parts(delta)
            extra = jnp.where(lane == spare, -high, 0.0)
            extra = jnp.where(lane == spare + 1, -middle, extra)
            extra = jnp.where(lane == spare + 2, -small, extra)
            grad_low = jnp.where(own, grad, extra).astype(BF16)

            def step(index, edge):
                place = pl.ds(pl.multiple_of(index * chunk, chunk), chunk)
                keys = wide_ref[place, slot * LANES : (slot + 1) * LANES]
                values = wide_ref[place, (2 + slot) * LANES : (3 + slot) * LANES]
                scores = contract(keys, query, 1, 1)
                if edge:
                    key_at = index * chunk + lax.broadcasted_iota(jnp.int32, (chunk, block), 0)
                    query_at = at * block + lax.broadcasted_iota(jnp.int32, (chunk, block), 1)
                    scores = jnp.where(key_at <= query_at, scores, FAR)
                weights = jnp.exp(scores)
                grad_weights = contract(values, grad_low, 1, 1)
                grad_scores = (weights * grad_weights).astype(BF16)
                value_sum_ref[slot, place, :] += contract(weights.astype(BF16), grad_low, 1, 0)
                key_sum_ref[slot, place, :] += contract(grad_scores, query, 1, 0)
                query_sum_ref[slot] += contract(grad_scores, keys, 0, 0)

            @pl.loop(0, last)
            def _(index):
                step(index, False)

            step(last, True)

    first_half = lane < HALF
    query_grad = jnp.where(first_half, query_sum_ref[0], query_sum_ref[1]) * scaling
    out_ref[rows, :LANES] = query_grad.astype(BF16)
    lying = pl.ds(pl.multiple_of(order_ref[at] * block, block), block)
    lying_ref[lying, :LANES] = query_grad.astype(BF16)

    @pl.when(at == pl.num_programs(0) - 1)
    def _():
        @pl.loop(0, pl.num_programs(0))
        def _(index):
            place = pl.ds(pl.multiple_of(index * block, block), block)
            key_grad = jnp.where(first_half, key_sum_ref[0, place, :], key_sum_ref[1, place, :])
            value_grad = jnp.where(
                first_half, value_sum_ref[0, place, :], value_sum_ref[1, place, :]
            )
            out_ref[place, LANES : 2 * LANES] = key_grad.astype(BF16)
            out_ref[place, 2 * LANES :] = value_grad.astype(BF16)
            lying = pl.ds(pl.multiple_of(order_ref[index] * block, block), block)
            lying_ref[lying, LANES : 2 * LANES] = key_grad.astype(BF16)
            lying_ref[lying, 2 * LANES :] = value_grad.astype(BF16)


def whole(value):
    return pl.BlockSpec(value.shape, lambda i, *unused: (0, 0), pipeline_mode=pl.Buffered(1))


SMALL = pl.CostEstimate(flops=1, bytes_accessed=1, transcendentals=0)


def attend(active, order, row_blocks, columns, documents, block):
    length = documents.shape[0]
    pair = jax.ShapeDtypeStruct((length, 2 * LANES), BF16)
    return pl.pallas_call(
        functools.partial(attend_kernel, block=block, chunk=2 * block, held=len(row_blocks)),
        grid_spec=pltpu.PrefetchScalarGridSpec(
            num_scalar_prefetch=2,
            grid=(length // block,),
            in_specs=[whole(value) for value in (*row_blocks, columns, documents)],
            out_specs=[
                pl.BlockSpec((block, LANES), lambda i, a, o: (i, 0)),
                pl.BlockSpec((block, LANES), lambda i, a, o: (i, 0)),
                pl.BlockSpec((block, 2 * LANES), lambda i, a, o: (i, 0)),
                whole(pair),
            ],
            scratch_shapes=[
                pltpu.VMEM((2, block, LANES), F32),
                pltpu.VMEM((length, 6 * LANES), BF16),
            ],
        ),
        out_shape=[
            jax.ShapeDtypeStruct((length, LANES), BF16),
            jax.ShapeDtypeStruct((length, LANES), F32),
            jax.ShapeDtypeStruct((length, 2 * LANES), BF16),
            pair,
        ],
        compiler_params=pltpu.CompilerParams(vmem_limit_bytes=VMEM_LIMIT),
        cost_estimate=SMALL,
    )(active, order, *row_blocks, columns, documents)


def attend_back(active, order, pair, documents, stat, grad, mixed, block, scaling):
    length = pair.shape[0]
    count = length // block
    return pl.pallas_call(
        functools.partial(attend_back_kernel, block=block, chunk=2 * block, scaling=scaling),
        grid_spec=pltpu.PrefetchScalarGridSpec(
            num_scalar_prefetch=2,
            grid=(count,),
            in_specs=[
                whole(pair),
                whole(documents),
                pl.BlockSpec((block, 2 * LANES), lambda i, a, o: (i, 0)),
                pl.BlockSpec((block, LANES), lambda i, a, o: (i, 0)),
                pl.BlockSpec((block, LANES), lambda i, a, o: (i, 0)),
            ],
            out_specs=[
                pl.BlockSpec(
                    (length, 3 * LANES), lambda i, a, o: (0, 0), pipeline_mode=pl.Buffered(1)
                )
            ]
            * 2,
            scratch_shapes=[
                pltpu.VMEM((2, length, LANES), F32),
                pltpu.VMEM((2, length, LANES), F32),
                pltpu.VMEM((2, block, LANES), F32),
                pltpu.VMEM((length, 4 * LANES), BF16),
            ],
        ),
        out_shape=[jax.ShapeDtypeStruct((length, 3 * LANES), BF16)] * 2,
        compiler_params=pltpu.CompilerParams(vmem_limit_bytes=VMEM_LIMIT),
        cost_estimate=SMALL,
    )(active, order, pair, documents, stat, grad, mixed)


def expert_kernel(arrived_ref, grad_ref, *refs, count):
    up_refs, down_refs = refs[:count], refs[count : 2 * count]
    total_ref, active_ref, hidden_ref = refs[2 * count :]
    arrived, grad_arrived = arrived_ref[...], grad_ref[...]
    scale = math.sqrt(2.0 / math.pi)
    total = jnp.zeros(total_ref.shape, F32)
    start = 0
    for up_ref, down_ref in zip(up_refs, down_refs, strict=True):
        up = up_ref[...]
        units = slice(start, start + up.shape[0])
        start += up.shape[0]
        hidden = contract(arrived, up, 1, 1)
        squared = hidden * hidden
        bend = jnp.tanh(scale * hidden * (1.0 + 0.044715 * squared))
        half = 0.5 + 0.5 * bend
        active_ref[:, units] = (hidden * half).astype(BF16)
        slope = half + (0.5 * scale) * hidden * (1.0 - bend * bend) * (1.0 + 3 * 0.044715 * squared)
        grad_hidden = (slope * contract(grad_arrived, down_ref[...], 1, 1)).astype(BF16)
        hidden_ref[:, units] = grad_hidden
        total = total + contract(grad_hidden, up, 1, 0)
    total_ref[...] = total.astype(BF16)


def rows_spec(value, block):
    return pl.BlockSpec((block, value.shape[1]), lambda i: (i, 0))


def expert_part(arrived, grad_arrived, ups, downs):
    slots, width = arrived.shape
    block = 256
    units = sum(up.shape[0] for up in ups)
    outs = [jax.ShapeDtypeStruct((slots, lanes), BF16) for lanes in (width, units, units)]
    return pl.pallas_call(
        functools.partial(expert_kernel, count=len(ups)),
        grid=(slots // block,),
        in_specs=[rows_spec(arrived, block), rows_spec(grad_arrived, block)]
        + [whole(value) for value in (*ups, *downs)],
        out_specs=[rows_spec(out, block) for out in outs],
        out_shape=outs,
        compiler_params=pltpu.CompilerParams(vmem_limit_bytes=VMEM_LIMIT),
        cost_estimate=SMALL,
    )(arrived, grad_arrived, *ups, *downs)


def produced_kernel(active_ref, *refs):
    total, start = 0.0, 0
    for down_ref in refs[:-1]:
        units = slice(start, start + down_ref.shape[0])
        start += down_ref.shape[0]
        total = total + contract(active_ref[:, units], down_ref[...], 1, 0)
    refs[-1][...] = total.astype(BF16)


def produced_part(active, downs):
    slots, width = active.shape[0], downs[0].shape[1]
    block = 256
    out = jax.ShapeDtypeStruct((slots, width), BF16)
    return pl.pallas_call(
        produced_kernel,
        grid=(slots // block,),
        in_specs=[rows_spec(active, block)] + [whole(down) for down in downs],
        out_specs=rows_spec(out, block),
        out_shape=out,
        compiler_params=pltpu.CompilerParams(vmem_limit_bytes=VMEM_LIMIT),
        cost_estimate=SMALL,
    )(active, *downs)


def unit_kernel(place_ref, active_ref, hidden_ref, grad_ref, arrived_ref, out_ref, *, half):
    @pl.when(pl.program_id(1) < half)
    def _():
        out_ref[...] = contract(active_ref[...], grad_ref[...], 0, 0).astype(BF16)

    @pl.when(pl.program_id(1) >= half)
    def _():
        out_ref[...] = contract(hidden_ref[...], arrived_ref[...], 0, 0).astype(BF16)


def unit_grads(places, active, grad_hidden, grad_arrived, arrived):
    slots, width = arrived.shape
    units = active.shape[1] // places.shape[0]
    block = 256
    half = width // block
    left = pl.BlockSpec((slots, units), lambda k, c, p: (0, k))
    right = pl.BlockSpec((slots, block), lambda k, c, p: (0, lax.rem(c, half)))
    return pl.pallas_call(
        functools.partial(unit_kernel, half=half),
        grid_spec=pltpu.PrefetchScalarGridSpec(
            num_scalar_prefetch=1,
            grid=(active.shape[1] // units, 2 * half),
            in_specs=[left, left, right, right],
            out_specs=pl.BlockSpec((units, block), lambda k, c, p: (p[k], c)),
        ),
        out_shape=jax.ShapeDtypeStruct((active.shape[1], 2 * width), BF16),
        compiler_params=pltpu.CompilerParams(vmem_limit_bytes=VMEM_LIMIT),
        cost_estimate=SMALL,
    )(places, active, grad_hidden, grad_arrived, arrived)


def column_kernel(*refs, held):
    row_refs = refs[:held]
    lying_ref, out_ref = refs[held:]
    start, total = 0, None
    for row_ref in row_refs:
        rows = row_ref.shape[0]
        part = contract(row_ref[...], lying_ref[start : start + rows, :], 0, 0)
        total = part if total is None else total + part
        start += rows
    out_ref[...] = total.astype(BF16)


def column_terms(row_blocks, grad_lying):
    width = row_blocks[0].shape[1]
    block = 256
    out = jax.ShapeDtypeStruct((width, 3 * LANES), BF16)
    return pl.pallas_call(
        functools.partial(column_kernel, held=len(row_blocks)),
        grid=(width // block,),
        in_specs=[
            pl.BlockSpec((value.shape[0], block), lambda i: (0, i)) for value in row_blocks
        ]
        + [whole(grad_lying)],
        out_specs=rows_spec(out, block),
        out_shape=out,
        compiler_params=pltpu.CompilerParams(vmem_limit_bytes=VMEM_LIMIT),
        cost_estimate=SMALL,
    )(*row_blocks, grad_lying)


def close_kernel(
    pieces_ref, matrix_ref, tokens_ref, gain_ref, residual_ref, out_ref, part_ref, sum_ref, *, starts
):
    width = tokens_ref.shape[1]
    lane = lax.broadcasted_iota(jnp.int32, (tokens_ref.shape[0], LANES), 1)
    sum_ref[...] = jnp.zeros_like(sum_ref)
    for device, start in enumerate(starts):
        for part in range(3):
            piece = pieces_ref[device, :, part * LANES : (part + 1) * LANES].astype(F32)
            column = part * width + start
            if column % LANES == 0:
                sum_ref[:, column : column + LANES] += piece
            else:
                turned = pltpu.roll(piece, HALF, 1)
                low, high = column - HALF, column + HALF
                sum_ref[:, low : low + LANES] += jnp.where(lane >= HALF, turned, 0.0)
                sum_ref[:, high : high + LANES] += jnp.where(lane < HALF, turned, 0.0)
    grad = contract(sum_ref[...].astype(BF16), matrix_ref[...], 1, 1)
    inputs = tokens_ref[...].astype(F32)
    scale = lax.rsqrt(jnp.mean(inputs * inputs, axis=-1, keepdims=True) + EPSILON)
    normed = inputs * scale
    scaled = grad * gain_ref[...]
    mean = jnp.mean(scaled * normed, axis=-1, keepdims=True)
    out_ref[...] = residual_ref[...] + scale * (scaled - normed * mean)
    part_ref[...] = jnp.sum(grad * normed, axis=0, keepdims=True)


def close_norm(pieces, starts, matrix, tokens, gain, residual):
    rows, width = tokens.shape
    outs = [
        jax.ShapeDtypeStruct((rows, width), F32),
        jax.ShapeDtypeStruct((1, width), F32),
    ]
    return pl.pallas_call(
        functools.partial(close_kernel, starts=starts),
        in_specs=[pl.BlockSpec(memory_space=pltpu.VMEM)] * 5,
        out_specs=[pl.BlockSpec(memory_space=pltpu.VMEM)] * 2,
        out_shape=outs,
        scratch_shapes=[pltpu.VMEM((rows, 3 * width), F32)],
        compiler_params=pltpu.CompilerParams(vmem_limit_bytes=VMEM_LIMIT),
        cost_estimate=SMALL,
    )(pieces, matrix, tokens, gain, residual)


def adam_update(weight, grad, first, second, factor, rate, decay):
    clipped = grad * factor
    first_new = BETA_ONE * first + (1.0 - BETA_ONE) * clipped
    second_new = BETA_TWO * second + (1.0 - BETA_TWO) * clipped * clipped
    first_hat = first_new / (1.0 - BETA_ONE**STEP)
    second_hat = second_new / (1.0 - BETA_TWO**STEP)
    weight_new = weight - rate * (first_hat / (jnp.sqrt(second_hat) + ADAM_FLOOR) + decay * weight)
    return (first_new, second_new, weight_new)


def together(*values):
    return lax.optimization_barrier(values)


def swap(value, axes):
    return lax.all_to_all(value, axes, split_axis=0, concat_axis=0, tiled=True)


def adam_kernel(factor_ref, *refs, rates):
    count = len(rates)
    factor = factor_ref[0]
    for index, rate in enumerate(rates):
        weight, grad, first, second = [ref[...] for ref in refs[4 * index : 4 * index + 4]]
        outs = refs[4 * count + 3 * index : 4 * count + 3 * index + 3]
        for out, value in zip(
            outs, adam_update(weight, grad, first, second, factor, rate, DECAY), strict=True
        ):
            out[...] = value


def adam_all(factor, leaves, rates, steps):
    flat = [value.reshape(value.shape[-2:]) for leaf in leaves for value in leaf]

    def spec(value):
        rows, columns = value.shape
        if rows % (8 * steps) == 0:
            return pl.BlockSpec((rows // steps, columns), lambda i: (i, 0))
        lanes = columns // steps
        return pl.BlockSpec((rows, lanes), lambda i: (0, i))

    shapes = [jax.ShapeDtypeStruct(value.shape, F32) for value in flat[::4] for _ in range(3)]
    outs = pl.pallas_call(
        functools.partial(adam_kernel, rates=rates),
        grid=(steps,),
        in_specs=[pl.BlockSpec(memory_space=pltpu.SMEM)] + [spec(value) for value in flat],
        out_specs=[spec(shape) for shape in shapes],
        out_shape=shapes,
        compiler_params=pltpu.CompilerParams(vmem_limit_bytes=VMEM_LIMIT),
        cost_estimate=pl.CostEstimate(
            flops=20 * sum(value.size for value in flat[::4]),
            bytes_accessed=28 * sum(value.size for value in flat[::4]),
            transcendentals=0,
        ),
    )(factor.reshape(1), *flat)
    return [
        [out.reshape(leaf[0].shape) for out in outs[3 * index : 3 * index + 3]]
        for index, leaf in enumerate(leaves)
    ]


def flip(value, bits):
    count = lax.axis_size(SEQ)
    return lax.ppermute(value, SEQ, [(index, index ^ bits) for index in range(count)])


def others(value, axis):
    size = lax.axis_size(axis)
    parts = [
        lax.ppermute(value, axis, [((i + step) % size, i) for i in range(size)])
        for step in range(1, size)
    ]
    return parts[0] if size == 2 else jnp.concatenate(parts, axis=0)


def to_owners(blocks, axis):
    size = lax.axis_size(axis)
    return [
        lax.ppermute(block, axis, [(i, (i + step) % size) for i in range(size)])
        for step, block in enumerate(blocks, 1)
    ]


def add_all(own, parts):
    return functools.reduce(lambda total, part: total + part.astype(F32), parts, own.astype(F32))


def spread_sum(value):
    count = lax.axis_size(ALL)
    return jnp.sum(swap(jnp.broadcast_to(value[None], (count, *value.shape)), ALL), axis=0)


def body(
    tokens,
    cotangent,
    segment_ids,
    expert_ids,
    projection,
    output_weight,
    expert_up,
    expert_down,
    norm_gains,
    projection_first,
    projection_second,
    output_first,
    output_second,
    up_first,
    up_second,
    down_first,
    down_second,
    gains_first,
    gains_second,
):
    inputs = tokens[0].astype(F32)
    upstream = cotangent[0].astype(F32)
    row_count = inputs.shape[0]
    width = inputs.shape[1]
    head_size = width // HEADS
    scaling = head_size ** (-0.5)
    count = lax.axis_size(SEQ)
    groups = lax.axis_size("exp")
    team = lax.axis_size(TEAM)
    position = lax.axis_index(SEQ)
    length = count * row_count
    weight_rows = projection.shape[0]
    first_heads, active_table = head_plan(count)
    starts = [int(head) * head_size for head in first_heads]
    active = lax.dynamic_index_in_dim(jnp.asarray(active_table), position, 0, keepdims=False)
    gain_first = norm_gains[0]
    gain_second = norm_gains[1]
    used = active_table.any(axis=2)

    scale_first = lax.rsqrt(jnp.mean(inputs * inputs, axis=-1, keepdims=True) + EPSILON)
    normed_first = inputs * scale_first
    attend_in = (normed_first * gain_first).astype(BF16)
    slots = groups * CAP
    chosen = expert_ids[0, :, 0]
    one_hot = (chosen[:, None] == jnp.arange(groups, dtype=jnp.int32)[None, :]).astype(jnp.int32)
    rank = jnp.sum(jnp.cumsum(one_hot, axis=0) * one_hot, axis=1) - 1
    target = chosen * CAP + rank
    placing = (target[:, None] == jnp.arange(slots, dtype=jnp.int32)[None, :]).astype(BF16)

    def to_slots(values):
        outgoing = jnp.einsum("ts,td->sd", placing, values, preferred_element_type=F32)
        return outgoing.astype(BF16)

    def dispatch(outgoing):
        outgoing = jnp.broadcast_to(
            outgoing.reshape(1, groups, CAP, width), (team, groups, CAP, width)
        )
        return swap(outgoing.reshape(team * groups, CAP, width), TEAM + EXP).reshape(
            team * slots, width
        )

    def send_back(values):
        return swap(values.reshape(team * groups, CAP, width), TEAM + EXP).reshape(
            team, slots, width
        )

    def collect(returned):
        return jnp.einsum("ts,jsd->td", placing, returned, preferred_element_type=F32)

    projection_low = projection.astype(BF16)
    sent_rows = weight_rows + 8
    own_documents = jnp.zeros((8, 3 * LANES + width), BF16)
    own_documents = own_documents.at[0, :row_count].set(segment_ids[0].astype(BF16))
    output_low = output_weight.astype(BF16)
    pieces = [
        jnp.concatenate(
            [projection_low[:, k * width + s : k * width + s + LANES] for k in range(3)]
            + [output_low],
            axis=1,
        )
        for s in starts
    ]
    pieces = jnp.stack([jnp.concatenate([piece, own_documents], axis=0) for piece in pieces])
    own_up = expert_up[0].astype(BF16)
    own_down = expert_down[0].astype(BF16)
    pairwise = count == 8
    if pairwise:
        order = jnp.arange(count, dtype=jnp.int32) ^ position
        beside, below, across = flip(attend_in, 1), flip(attend_in, 2), flip(attend_in, 4)
        got_rows, beside, below, across, own_up = together(
            swap(pieces, SEQ), beside, below, across, own_up
        )
        corner = flip(across, 2)
        row_blocks = [attend_in, beside]
        row_blocks += [part for block in (below, across, corner) for part in (block, flip(block, 1))]
    else:
        order = jnp.arange(count, dtype=jnp.int32)
        row_blocks = [lax.all_gather(attend_in, SEQ, axis=0, tiled=True)]
        got_rows = swap(pieces, SEQ)
    documents = jnp.broadcast_to(
        got_rows[:, weight_rows, :row_count].reshape(length, 1), (length, LANES)
    )
    own_copies = jnp.broadcast_to(
        got_rows[None, :, :weight_rows], (groups, count, weight_rows, 3 * LANES + width)
    )
    all_copies = swap(own_copies, EXP)

    peer_up = others(own_up, "hi")
    *row_blocks, all_copies, peer_up, own_up, own_down, grad_slots_out = together(
        *row_blocks, all_copies, peer_up, own_up, own_down, to_slots(cotangent[0])
    )
    all_copies = jnp.swapaxes(all_copies, 0, 1)
    columns = all_copies[..., : 3 * LANES].reshape(width, 3 * LANES)
    output_full = all_copies[..., 3 * LANES :].reshape(width, width)
    grad_arrived = dispatch(grad_slots_out)
    peer_down = others(own_down, "hi")
    side_up = others(own_up, "in")
    side_down = others(own_down, "in")
    far_up = others(peer_up, "in")

    mixed_low, mixed_full, stat, pair = attend(
        active, order, row_blocks, columns, documents, row_count
    )

    def place_heads():
        index = np.arange(LANES)
        matrix = np.zeros((count, LANES, width), np.float32)
        for device in range(count):
            for slot in range(2):
                if used[device, slot]:
                    own = index[slot * HALF : (slot + 1) * HALF]
                    matrix[device, own, starts[device] + own] = 1.0
        return jnp.asarray(matrix, BF16)

    head_places = place_heads()

    def to_tokens(values):
        return swap(values.reshape(count, row_count, values.shape[1]), SEQ)

    mixed_low, grad_arrived, peer_down, side_up, side_down, far_up = together(
        mixed_low, grad_arrived, peer_down, side_up, side_down, far_up
    )
    far_down = others(peer_down, "in")
    mixed_pieces, projection_low, far_down = together(
        to_tokens(mixed_low), projection_low, far_down
    )
    projection_full = lax.all_gather(projection_low, ALL, axis=0, tiled=True)
    attend_out = jnp.einsum(
        "jtc,jcd->td", mixed_pieces, head_places, preferred_element_type=F32
    ).astype(BF16)
    branch = jnp.dot(attend_out, output_full, preferred_element_type=F32)
    middle = inputs + branch
    scale_second = lax.rsqrt(jnp.mean(middle * middle, axis=-1, keepdims=True) + EPSILON)
    normed_second = middle * scale_second
    expert_in = (normed_second * gain_second).astype(BF16)

    arrived = dispatch(to_slots(expert_in))
    ups, downs = (own_up, peer_up, side_up, far_up), (own_down, peer_down, side_down, far_down)
    grad_slots, active_units, grad_hidden = expert_part(arrived, grad_arrived, ups, downs)
    returned_grad = send_back(grad_slots)
    at_hi, at_in = lax.axis_index("hi"), lax.axis_index("in")
    peers, sides = lax.axis_size("hi"), lax.axis_size("in")
    units = own_up.shape[0]
    places = jnp.arange(4, dtype=jnp.int32)
    if pairwise:
        places = (at_hi * sides + at_in) ^ jnp.asarray([0, 2, 1, 3], jnp.int32)
    unit_sums = unit_grads(places, active_units, grad_hidden, grad_arrived, arrived)
    if not pairwise:
        unit_sums = unit_sums.reshape(sides, peers, units, 2 * width)
        unit_sums = jnp.roll(unit_sums, (at_in, at_hi), axis=(0, 1))
        unit_sums = jnp.swapaxes(unit_sums, 0, 1).reshape(-1, 2 * width)
    produced = produced_part(active_units, downs)
    returned_grad, projection_full, produced, unit_sums = together(
        returned_grad, projection_full, produced, unit_sums
    )
    unit_sums = lax.psum_scatter(unit_sums, SHARE, scatter_dimension=0, tiled=True)
    grad_expert_in = collect(returned_grad)

    scaled_second = grad_expert_in * gain_second
    gain_second_part = jnp.sum(grad_expert_in * normed_second, axis=0)
    grad_middle = scale_second * (
        scaled_second
        - normed_second * jnp.mean(scaled_second * normed_second, axis=-1, keepdims=True)
    )
    residual_grad = upstream + grad_middle
    branch_grad = residual_grad.astype(BF16)
    grad_mixed = jnp.einsum(
        "td,ed->te", branch_grad, output_full, preferred_element_type=F32
    ).astype(BF16)

    sent_grad = jnp.stack([grad_mixed[:, s : s + LANES] for s in starts])
    row_grad = swap(sent_grad, SEQ).reshape(length, LANES)

    group = lax.axis_index(EXP)

    def group_rows(value):
        rows = value.reshape(count, groups, weight_rows, -1)
        own, *away = [
            lax.dynamic_index_in_dim(rows, lax.rem(group + step, groups), 1, keepdims=False)
            for step in range(groups)
        ]
        return own, away

    output_term = jnp.einsum("tc,te->ce", attend_out, branch_grad, preferred_element_type=F32)
    output_own, output_away = group_rows(output_term.astype(BF16))
    row_grad, produced, *output_away = together(row_grad, produced, *output_away)
    output_away = to_owners(output_away, "exp")
    returned = send_back(produced)
    grad_qkv, grad_lying = attend_back(
        active, order, pair, documents, stat, row_grad, mixed_full, row_count, scaling
    )
    grad_qkv, grad_lying, returned, *output_away = together(
        grad_qkv, grad_lying, returned, *output_away
    )
    block_output = (middle + collect(returned)).astype(BF16)[None]

    column_own, column_away = group_rows(column_terms(row_blocks, grad_lying))
    dense_rows = jnp.concatenate(
        [
            add_all(column_own, to_owners(column_away, "exp")).astype(BF16),
            add_all(output_own, output_away).astype(BF16),
        ],
        axis=2,
    )
    if pairwise:
        lying_terms = [
            lax.dynamic_index_in_dim(dense_rows, position ^ bits, 0, keepdims=False)
            for bits in range(count)
        ]
        lying_terms[1:] = [flip(lying_terms[bits], bits) for bits in range(1, count)]
        grad_pieces, unit_sums, *lying_terms = together(
            to_tokens(grad_qkv), unit_sums, *lying_terms
        )
        lying_terms = jnp.stack(lying_terms)
        got_terms = [
            lax.dynamic_index_in_dim(lying_terms, position ^ j, 0, keepdims=False)
            for j in range(count)
        ]
    else:
        grad_pieces, dense_rows = together(to_tokens(grad_qkv), dense_rows)
        got_terms = list(swap(dense_rows, SEQ))
    got_terms = [term.astype(F32) for term in got_terms]
    unit_sums = unit_sums.astype(F32)
    down_grad, up_grad = unit_sums[None, :, :width], unit_sums[None, :, width:]
    input_grad, gain_first_part = close_norm(
        grad_pieces, starts, projection_full, tokens[0], gain_first[None], residual_grad
    )
    input_grad, gain_first_part = input_grad[None], gain_first_part[0]
    output_grad = functools.reduce(jnp.add, [term[:, 3 * LANES :] for term in got_terms])
    head_grads = []
    for k in range(3):
        for head in range(HEADS):
            parts = [
                got_terms[j][:, k * LANES + slot * HALF : k * LANES + (slot + 1) * HALF]
                for j in range(count)
                for slot in range(2)
                if used[j, slot] and first_heads[j] + slot == head
            ]
            head_grads.append(functools.reduce(jnp.add, parts))
    projection_grad = jnp.concatenate(head_grads, axis=1)

    local_square = jnp.sum(projection_grad * projection_grad) + jnp.sum(output_grad * output_grad)
    local_square = local_square + jnp.sum(up_grad * up_grad) + jnp.sum(down_grad * down_grad)
    summed = spread_sum(
        jnp.concatenate(
            [gain_first_part, gain_second_part, jnp.broadcast_to(local_square, (LANES,))]
        )[None]
    )[0]
    gains_grad = summed[: 2 * width].reshape(2, width)
    grad_norm = jnp.sqrt(summed[2 * width] + jnp.sum(gains_grad * gains_grad))
    factor = jnp.minimum(1.0, CLIP / (grad_norm + 1e-06))
    (
        (projection_moment, projection_square, projection_new),
        (output_moment, output_square, output_new),
        (up_moment, up_square, up_new),
        (down_moment, down_square, down_new),
    ) = adam_all(
        factor,
        [
            (projection, projection_grad, projection_first, projection_second),
            (output_weight, output_grad, output_first, output_second),
            (expert_up, up_grad, up_first, up_second),
            (expert_down, down_grad, down_first, down_second),
        ],
        (RATE_MATRIX, RATE_OUTPUT, RATE_MATRIX, RATE_MATRIX),
        6,
    )
    gains_moment, gains_square, gains_new = adam_update(
        norm_gains, gains_grad, gains_first, gains_second, factor, RATE_GAIN, 0.0
    )
    return (
        block_output,
        input_grad,
        grad_norm,
        projection_grad,
        projection_moment,
        projection_square,
        projection_new,
        output_grad,
        output_moment,
        output_square,
        output_new,
        up_grad,
        up_moment,
        up_square,
        up_new,
        down_grad,
        down_moment,
        down_square,
        down_new,
        gains_grad,
        gains_moment,
        gains_square,
        gains_new,
    )


def solution(mesh):
    token = P("exp", SEQ, None)
    dense = P(ALL, None)
    expert = P("exp", SEQ, None)
    in_specs = (
        (token, token, P("exp", SEQ), token)
        + (dense, dense, expert, expert, P())
        + (dense,) * 4
        + (expert,) * 4
        + (P(), P())
    )
    out_specs = (token, token, P()) + (dense,) * 8 + (expert,) * 8 + (P(),) * 4
    rows, groups = mesh.devices.shape
    fine = Mesh(mesh.devices.reshape(rows // 4, 2, 2, groups), ALL)
    return jax.shard_map(body, mesh=fine, in_specs=in_specs, out_specs=out_specs, check_vma=False)
```

```python
import functools
import math

import jax
import jax.numpy as jnp
import numpy as np
from jax import lax
from jax.experimental import pallas as pl
from jax.experimental.pallas import tpu as pltpu
from jax.sharding import Mesh
from jax.sharding import PartitionSpec as P

HEADS = 12
CAP = 128
STEP = 10


EPSILON = 1e-05
CLIP = 1.0
BETA_ONE = 0.9
BETA_TWO = 0.99
ADAM_FLOOR = 1e-08
DECAY = 0.1
RATE_MATRIX = 0.04
RATE_OUTPUT = 0.1
RATE_GAIN = 0.5

SEQ = ("hi", "lo", "in")
EXP = ("exp",)
ALL = SEQ + EXP
TEAM = ("lo",)
SHARE = ("hi", "in")
LANES = 128
HALF = 64
FAR = -1e30
BF16 = jnp.bfloat16
F32 = jnp.float32
VMEM_LIMIT = 60 * 1024 * 1024


def head_plan(count):
    whole = math.lcm(HEADS, count)
    units, parts = whole // count, whole // HEADS
    first = np.zeros((count,), np.int64)
    active = np.zeros((count, 2, count), np.int32)
    for device in range(count):
        first[device] = min(units * device // parts, HEADS - 2)
        for unit in range(units * device, units * (device + 1)):
            slot = unit // parts - first[device]
            for block in range(count):
                turn = block % (2 * parts)
                if min(turn, 2 * parts - 1 - turn) == unit % parts:
                    active[device, slot, block] = 1
    return first, active


def three_parts(value):
    high = value.astype(BF16).astype(F32)
    middle = (value - high).astype(BF16).astype(F32)
    return high, middle, value - high - middle


def contract(left, right, left_axis, right_axis):
    return lax.dot_general(
        left, right, (((left_axis,), (right_axis,)), ((), ())), preferred_element_type=F32
    )


def slot_arrays(packed, documents, kind, slot):
    spare = HALF - HALF * slot
    lane = lax.broadcasted_iota(jnp.int32, packed.shape, 1)
    own = (lane < HALF) if slot == 0 else (lane >= HALF)
    place = (lane - spare).astype(F32)
    ours = place == documents
    first = (lane >= spare) & (lane < spare + 3)
    if kind == "query":
        extra = jnp.where(first & jnp.logical_not(ours), FAR, 0.0)
    elif kind == "key":
        extra = jnp.where(ours | ((lane >= spare + 3) & (lane < spare + 6)), 1.0, 0.0)
    else:
        extra = jnp.where(first, 1.0, 0.0)
    return jnp.where(own, packed, extra).astype(BF16)


def fill_slots(packed_of, documents_ref, wide_ref, kinds, place):
    documents = documents_ref[place, :].astype(F32)
    for number, kind in enumerate(kinds):
        packed = packed_of(kind).astype(F32)
        if kind == "query":
            packed = packed * 0.125
        for slot in range(2):
            column = (2 * number + slot) * LANES
            wide_ref[place, column : column + LANES] = slot_arrays(packed, documents, kind, slot)


def attend_kernel(active_ref, order_ref, *refs, block, chunk, held):
    row_refs = refs[:held]
    columns_ref, documents_ref = refs[held : held + 2]
    low_ref, full_ref, stat_ref, pair_ref, mixed_ref, wide_ref = refs[held + 2 :]
    at = pl.program_id(0)

    @pl.when(at == 0)
    def _():
        def fill(tokens, index):
            place = pl.ds(pl.multiple_of(order_ref[index] * block, block), block)
            packed = contract(tokens, columns_ref[...], 1, 0).astype(BF16)
            pair_ref[place, :] = packed[:, LANES:]
            parts = {
                kind: packed[:, part * LANES : (part + 1) * LANES]
                for part, kind in enumerate(("query", "key", "value"))
            }
            fill_slots(parts.get, documents_ref, wide_ref, tuple(parts), place)

        if held > 1:
            for index, row_ref in enumerate(row_refs):
                fill(row_ref[...], index)
        else:

            @pl.loop(0, pl.num_programs(0))
            def _(index):
                fill(row_refs[0][pl.ds(pl.multiple_of(index * block, block), block), :], index)

    rows = pl.ds(pl.multiple_of(at * block, block), block)
    lane = lax.broadcasted_iota(jnp.int32, (block, LANES), 1)
    last = lax.div(at * block, chunk)
    for slot in range(2):
        spare = HALF - HALF * slot
        own = (lane < HALF) if slot == 0 else (lane >= HALF)
        columns = slice(slot * LANES, (slot + 1) * LANES)

        @pl.when(active_ref[slot, at] != 0)
        def _():
            query = wide_ref[rows, columns]

            def step(index, carry, edge):
                top, weighted = carry
                place = pl.ds(pl.multiple_of(index * chunk, chunk), chunk)
                keys = wide_ref[place, 2 * LANES + slot * LANES : 3 * LANES + slot * LANES]
                values = wide_ref[place, 4 * LANES + slot * LANES : 5 * LANES + slot * LANES]
                scores = contract(query, keys, 1, 1)
                if edge:
                    key_at = index * chunk + lax.broadcasted_iota(jnp.int32, (block, chunk), 1)
                    query_at = at * block + lax.broadcasted_iota(jnp.int32, (block, chunk), 0)
                    scores = jnp.where(key_at <= query_at, scores, FAR)
                new_top = jnp.maximum(top, jnp.max(scores, axis=1, keepdims=True))
                weights = jnp.exp(scores - new_top).astype(BF16)
                weighted = weighted * jnp.exp(top - new_top) + contract(weights, values, 1, 0)
                return new_top, weighted

            carry = (jnp.full((block, 1), FAR, F32), jnp.zeros((block, LANES), F32))
            carry = lax.fori_loop(0, last, lambda index, state: step(index, state, False), carry)
            top, weighted = step(last, carry, True)
            total = weighted[:, spare : spare + 1]
            mixed_ref[slot] = jnp.where(own, weighted / total, 0.0)
            log_total = top + jnp.log(total)
            high, middle, small = three_parts(log_total)
            extra = jnp.where(lane == spare + 3, -high, 0.0)
            extra = jnp.where(lane == spare + 4, -middle, extra)
            extra = jnp.where(lane == spare + 5, -small, extra)
            stat_ref[:, columns] = (query.astype(F32) + extra).astype(BF16)

        @pl.when(active_ref[slot, at] == 0)
        def _():
            mixed_ref[slot] = jnp.zeros((block, LANES), F32)
            stat_ref[:, columns] = jnp.zeros((block, LANES), BF16)

    mixed = mixed_ref[0] + mixed_ref[1]
    full_ref[...] = mixed
    low_ref[...] = mixed.astype(BF16)


def attend_back_kernel(
    active_ref,
    order_ref,
    pair_ref,
    documents_ref,
    stat_ref,
    grad_ref,
    mixed_ref,
    out_ref,
    lying_ref,
    key_sum_ref,
    value_sum_ref,
    query_sum_ref,
    wide_ref,
    *,
    block,
    chunk,
    scaling,
):
    at = pl.program_id(0)
    rows = pl.ds(pl.multiple_of(at * block, block), block)
    lane = lax.broadcasted_iota(jnp.int32, (block, LANES), 1)
    last = lax.div(at * block, chunk)

    @pl.when(at == 0)
    def _():
        @pl.loop(0, pl.num_programs(0))
        def _(index):
            place = pl.ds(pl.multiple_of(index * block, block), block)
            parts = {"key": pair_ref[place, :LANES], "value": pair_ref[place, LANES:]}
            fill_slots(parts.get, documents_ref, wide_ref, tuple(parts), place)

        key_sum_ref[...] = jnp.zeros_like(key_sum_ref)
        value_sum_ref[...] = jnp.zeros_like(value_sum_ref)

    for slot in range(2):
        spare = HALF - HALF * slot
        own = (lane < HALF) if slot == 0 else (lane >= HALF)
        columns = slice(slot * LANES, (slot + 1) * LANES)
        query_sum_ref[slot] = jnp.zeros((block, LANES), F32)

        @pl.when(active_ref[slot, at] != 0)
        def _():
            query = stat_ref[:, columns]
            grad = grad_ref[...].astype(F32)
            delta = jnp.sum(jnp.where(own, grad * mixed_ref[...], 0.0), axis=1, keepdims=True)
            high, middle, small = three_parts(delta)
            extra = jnp.where(lane == spare, -high, 0.0)
            extra = jnp.where(lane == spare + 1, -middle, extra)
            extra = jnp.where(lane == spare + 2, -small, extra)
            grad_low = jnp.where(own, grad, extra).astype(BF16)

            def step(index, edge):
                place = pl.ds(pl.multiple_of(index * chunk, chunk), chunk)
                keys = wide_ref[place, slot * LANES : (slot + 1) * LANES]
                values = wide_ref[place, (2 + slot) * LANES : (3 + slot) * LANES]
                scores = contract(keys, query, 1, 1)
                if edge:
                    key_at = index * chunk + lax.broadcasted_iota(jnp.int32, (chunk, block), 0)
                    query_at = at * block + lax.broadcasted_iota(jnp.int32, (chunk, block), 1)
                    scores = jnp.where(key_at <= query_at, scores, FAR)
                weights = jnp.exp(scores)
                grad_weights = contract(values, grad_low, 1, 1)
                grad_scores = (weights * grad_weights).astype(BF16)
                value_sum_ref[slot, place, :] += contract(weights.astype(BF16), grad_low, 1, 0)
                key_sum_ref[slot, place, :] += contract(grad_scores, query, 1, 0)
                query_sum_ref[slot] += contract(grad_scores, keys, 0, 0)

            @pl.loop(0, last)
            def _(index):
                step(index, False)

            step(last, True)

    first_half = lane < HALF
    query_grad = jnp.where(first_half, query_sum_ref[0], query_sum_ref[1]) * scaling
    out_ref[rows, :LANES] = query_grad.astype(BF16)
    lying = pl.ds(pl.multiple_of(order_ref[at] * block, block), block)
    lying_ref[lying, :LANES] = query_grad.astype(BF16)

    @pl.when(at == pl.num_programs(0) - 1)
    def _():
        @pl.loop(0, pl.num_programs(0))
        def _(index):
            place = pl.ds(pl.multiple_of(index * block, block), block)
            key_grad = jnp.where(first_half, key_sum_ref[0, place, :], key_sum_ref[1, place, :])
            value_grad = jnp.where(
                first_half, value_sum_ref[0, place, :], value_sum_ref[1, place, :]
            )
            out_ref[place, LANES : 2 * LANES] = key_grad.astype(BF16)
            out_ref[place, 2 * LANES :] = value_grad.astype(BF16)
            lying = pl.ds(pl.multiple_of(order_ref[index] * block, block), block)
            lying_ref[lying, LANES : 2 * LANES] = key_grad.astype(BF16)
            lying_ref[lying, 2 * LANES :] = value_grad.astype(BF16)


def whole(value):
    return pl.BlockSpec(value.shape, lambda i, *unused: (0, 0), pipeline_mode=pl.Buffered(1))


SMALL = pl.CostEstimate(flops=1, bytes_accessed=1, transcendentals=0)


def attend(active, order, row_blocks, columns, documents, block):
    length = documents.shape[0]
    pair = jax.ShapeDtypeStruct((length, 2 * LANES), BF16)
    return pl.pallas_call(
        functools.partial(attend_kernel, block=block, chunk=2 * block, held=len(row_blocks)),
        grid_spec=pltpu.PrefetchScalarGridSpec(
            num_scalar_prefetch=2,
            grid=(length // block,),
            in_specs=[whole(value) for value in (*row_blocks, columns, documents)],
            out_specs=[
                pl.BlockSpec((block, LANES), lambda i, a, o: (i, 0)),
                pl.BlockSpec((block, LANES), lambda i, a, o: (i, 0)),
                pl.BlockSpec((block, 2 * LANES), lambda i, a, o: (i, 0)),
                whole(pair),
            ],
            scratch_shapes=[
                pltpu.VMEM((2, block, LANES), F32),
                pltpu.VMEM((length, 6 * LANES), BF16),
            ],
        ),
        out_shape=[
            jax.ShapeDtypeStruct((length, LANES), BF16),
            jax.ShapeDtypeStruct((length, LANES), F32),
            jax.ShapeDtypeStruct((length, 2 * LANES), BF16),
            pair,
        ],
        compiler_params=pltpu.CompilerParams(vmem_limit_bytes=VMEM_LIMIT),
        cost_estimate=SMALL,
    )(active, order, *row_blocks, columns, documents)


def attend_back(active, order, pair, documents, stat, grad, mixed, block, scaling):
    length = pair.shape[0]
    count = length // block
    return pl.pallas_call(
        functools.partial(attend_back_kernel, block=block, chunk=2 * block, scaling=scaling),
        grid_spec=pltpu.PrefetchScalarGridSpec(
            num_scalar_prefetch=2,
            grid=(count,),
            in_specs=[
                whole(pair),
                whole(documents),
                pl.BlockSpec((block, 2 * LANES), lambda i, a, o: (i, 0)),
                pl.BlockSpec((block, LANES), lambda i, a, o: (i, 0)),
                pl.BlockSpec((block, LANES), lambda i, a, o: (i, 0)),
            ],
            out_specs=[
                pl.BlockSpec(
                    (length, 3 * LANES), lambda i, a, o: (0, 0), pipeline_mode=pl.Buffered(1)
                )
            ]
            * 2,
            scratch_shapes=[
                pltpu.VMEM((2, length, LANES), F32),
                pltpu.VMEM((2, length, LANES), F32),
                pltpu.VMEM((2, block, LANES), F32),
                pltpu.VMEM((length, 4 * LANES), BF16),
            ],
        ),
        out_shape=[jax.ShapeDtypeStruct((length, 3 * LANES), BF16)] * 2,
        compiler_params=pltpu.CompilerParams(vmem_limit_bytes=VMEM_LIMIT),
        cost_estimate=SMALL,
    )(active, order, pair, documents, stat, grad, mixed)


def expert_kernel(arrived_ref, grad_ref, *refs, count):
    up_refs, down_refs = refs[:count], refs[count : 2 * count]
    total_ref = refs[2 * count]
    active_refs, hidden_refs = refs[2 * count + 1 : 3 * count + 1], refs[3 * count + 1 :]
    arrived, grad_arrived = arrived_ref[...], grad_ref[...]
    scale = math.sqrt(2.0 / math.pi)
    total = jnp.zeros(total_ref.shape, F32)
    for up_ref, down_ref, active_ref, hidden_ref in zip(
        up_refs, down_refs, active_refs, hidden_refs, strict=True
    ):
        up = up_ref[...]
        hidden = contract(arrived, up, 1, 1)
        squared = hidden * hidden
        bend = jnp.tanh(scale * hidden * (1.0 + 0.044715 * squared))
        half = 0.5 + 0.5 * bend
        active_ref[...] = (hidden * half).astype(BF16)
        slope = half + (0.5 * scale) * hidden * (1.0 - bend * bend) * (1.0 + 3 * 0.044715 * squared)
        grad_hidden = (slope * contract(grad_arrived, down_ref[...], 1, 1)).astype(BF16)
        hidden_ref[...] = grad_hidden
        total = total + contract(grad_hidden, up, 1, 0)
    total_ref[...] = total.astype(BF16)


def rows_spec(value, block):
    return pl.BlockSpec((block, value.shape[1]), lambda i: (i, 0))


def expert_part(arrived, grad_arrived, ups, downs):
    slots, width = arrived.shape
    block = 256
    units = [jax.ShapeDtypeStruct((slots, up.shape[0]), BF16) for up in ups]
    outs = [jax.ShapeDtypeStruct((slots, width), BF16), *units, *units]
    total, *parts = pl.pallas_call(
        functools.partial(expert_kernel, count=len(ups)),
        grid=(slots // block,),
        in_specs=[rows_spec(arrived, block), rows_spec(grad_arrived, block)]
        + [whole(value) for value in (*ups, *downs)],
        out_specs=[rows_spec(out, block) for out in outs],
        out_shape=outs,
        compiler_params=pltpu.CompilerParams(vmem_limit_bytes=VMEM_LIMIT),
        cost_estimate=SMALL,
    )(arrived, grad_arrived, *ups, *downs)
    return total, parts[: len(ups)], parts[len(ups) :]


def produced_kernel(*refs, count):
    total = contract(refs[0][...], refs[count][...], 1, 0)
    for index in range(1, count):
        total = total + contract(refs[index][...], refs[count + index][...], 1, 0)
    refs[-1][...] = total.astype(BF16)


def produced_part(actives, downs):
    slots, width = actives[0].shape[0], downs[0].shape[1]
    block = 256
    out = jax.ShapeDtypeStruct((slots, width), BF16)
    return pl.pallas_call(
        functools.partial(produced_kernel, count=len(actives)),
        grid=(slots // block,),
        in_specs=[rows_spec(value, block) for value in actives] + [whole(down) for down in downs],
        out_specs=rows_spec(out, block),
        out_shape=out,
        compiler_params=pltpu.CompilerParams(vmem_limit_bytes=VMEM_LIMIT),
        cost_estimate=SMALL,
    )(*actives, *downs)


def unit_kernel(grad_ref, arrived_ref, *refs, count):
    for index in range(count):
        active_ref, hidden_ref = refs[2 * index : 2 * index + 2]
        down_ref, up_ref = refs[2 * count + 2 * index : 2 * count + 2 * index + 2]
        down_ref[...] = contract(active_ref[...], grad_ref[...], 0, 0).astype(down_ref.dtype)
        up_ref[...] = contract(hidden_ref[...], arrived_ref[...], 0, 0).astype(up_ref.dtype)


def unit_grads(grad_arrived, arrived, blocks, kinds):
    slots, width = arrived.shape
    block = 256
    right = pl.BlockSpec((slots, block), lambda i: (0, i))
    outs = [
        jax.ShapeDtypeStruct((active.shape[1], width), kind)
        for (active, unused), kind in zip(blocks, kinds, strict=True)
        for part in range(2)
    ]
    flat = [value for pair in blocks for value in pair]
    return pl.pallas_call(
        functools.partial(unit_kernel, count=len(blocks)),
        grid=(width // block,),
        in_specs=[right, right] + [whole(value) for value in flat],
        out_specs=[pl.BlockSpec((out.shape[0], block), lambda i: (0, i)) for out in outs],
        out_shape=outs,
        compiler_params=pltpu.CompilerParams(vmem_limit_bytes=VMEM_LIMIT),
        cost_estimate=SMALL,
    )(grad_arrived, arrived, *flat)


def column_kernel(*refs, held):
    row_refs = refs[:held]
    lying_ref, out_ref = refs[held:]
    start, total = 0, None
    for row_ref in row_refs:
        rows = row_ref.shape[0]
        part = contract(row_ref[...], lying_ref[start : start + rows, :], 0, 0)
        total = part if total is None else total + part
        start += rows
    out_ref[...] = total.astype(BF16)


def column_terms(row_blocks, grad_lying):
    width = row_blocks[0].shape[1]
    block = 256
    out = jax.ShapeDtypeStruct((width, 3 * LANES), BF16)
    return pl.pallas_call(
        functools.partial(column_kernel, held=len(row_blocks)),
        grid=(width // block,),
        in_specs=[
            pl.BlockSpec((value.shape[0], block), lambda i: (0, i)) for value in row_blocks
        ]
        + [whole(grad_lying)],
        out_specs=rows_spec(out, block),
        out_shape=out,
        compiler_params=pltpu.CompilerParams(vmem_limit_bytes=VMEM_LIMIT),
        cost_estimate=SMALL,
    )(*row_blocks, grad_lying)


def close_kernel(
    pieces_ref, matrix_ref, tokens_ref, gain_ref, residual_ref, out_ref, part_ref, sum_ref, *, starts
):
    width = tokens_ref.shape[1]
    lane = lax.broadcasted_iota(jnp.int32, (tokens_ref.shape[0], LANES), 1)
    sum_ref[...] = jnp.zeros_like(sum_ref)
    for device, start in enumerate(starts):
        for part in range(3):
            piece = pieces_ref[device, :, part * LANES : (part + 1) * LANES].astype(F32)
            column = part * width + start
            if column % LANES == 0:
                sum_ref[:, column : column + LANES] += piece
            else:
                turned = pltpu.roll(piece, HALF, 1)
                low, high = column - HALF, column + HALF
                sum_ref[:, low : low + LANES] += jnp.where(lane >= HALF, turned, 0.0)
                sum_ref[:, high : high + LANES] += jnp.where(lane < HALF, turned, 0.0)
    grad = contract(sum_ref[...].astype(BF16), matrix_ref[...], 1, 1)
    inputs = tokens_ref[...].astype(F32)
    scale = lax.rsqrt(jnp.mean(inputs * inputs, axis=-1, keepdims=True) + EPSILON)
    normed = inputs * scale
    scaled = grad * gain_ref[...]
    mean = jnp.mean(scaled * normed, axis=-1, keepdims=True)
    out_ref[...] = residual_ref[...] + scale * (scaled - normed * mean)
    part_ref[...] = jnp.sum(grad * normed, axis=0, keepdims=True)


def close_norm(pieces, starts, matrix, tokens, gain, residual):
    rows, width = tokens.shape
    outs = [
        jax.ShapeDtypeStruct((rows, width), F32),
        jax.ShapeDtypeStruct((1, width), F32),
    ]
    return pl.pallas_call(
        functools.partial(close_kernel, starts=starts),
        in_specs=[pl.BlockSpec(memory_space=pltpu.VMEM)] * 5,
        out_specs=[pl.BlockSpec(memory_space=pltpu.VMEM)] * 2,
        out_shape=outs,
        scratch_shapes=[pltpu.VMEM((rows, 3 * width), F32)],
        compiler_params=pltpu.CompilerParams(vmem_limit_bytes=VMEM_LIMIT),
        cost_estimate=SMALL,
    )(pieces, matrix, tokens, gain, residual)


def adam_update(weight, grad, first, second, factor, rate, decay):
    clipped = grad * factor
    first_new = BETA_ONE * first + (1.0 - BETA_ONE) * clipped
    second_new = BETA_TWO * second + (1.0 - BETA_TWO) * clipped * clipped
    first_hat = first_new / (1.0 - BETA_ONE**STEP)
    second_hat = second_new / (1.0 - BETA_TWO**STEP)
    weight_new = weight - rate * (first_hat / (jnp.sqrt(second_hat) + ADAM_FLOOR) + decay * weight)
    return (first_new, second_new, weight_new)


def together(*values):
    return lax.optimization_barrier(values)


def swap(value, axes):
    return lax.all_to_all(value, axes, split_axis=0, concat_axis=0, tiled=True)


def adam_kernel(factor_ref, *refs, rates):
    count = len(rates)
    factor = factor_ref[0]
    for index, rate in enumerate(rates):
        weight, grad, first, second = [ref[...] for ref in refs[4 * index : 4 * index + 4]]
        outs = refs[4 * count + 3 * index : 4 * count + 3 * index + 3]
        for out, value in zip(
            outs, adam_update(weight, grad, first, second, factor, rate, DECAY), strict=True
        ):
            out[...] = value


def adam_all(factor, leaves, rates, steps):
    flat = [value.reshape(value.shape[-2:]) for leaf in leaves for value in leaf]

    def spec(value):
        rows, columns = value.shape
        if rows % (8 * steps) == 0:
            return pl.BlockSpec((rows // steps, columns), lambda i: (i, 0))
        lanes = columns // steps
        return pl.BlockSpec((rows, lanes), lambda i: (0, i))

    shapes = [jax.ShapeDtypeStruct(value.shape, F32) for value in flat[::4] for _ in range(3)]
    outs = pl.pallas_call(
        functools.partial(adam_kernel, rates=rates),
        grid=(steps,),
        in_specs=[pl.BlockSpec(memory_space=pltpu.SMEM)] + [spec(value) for value in flat],
        out_specs=[spec(shape) for shape in shapes],
        out_shape=shapes,
        compiler_params=pltpu.CompilerParams(vmem_limit_bytes=VMEM_LIMIT),
        cost_estimate=pl.CostEstimate(
            flops=20 * sum(value.size for value in flat[::4]),
            bytes_accessed=28 * sum(value.size for value in flat[::4]),
            transcendentals=0,
        ),
    )(factor.reshape(1), *flat)
    return [
        [out.reshape(leaf[0].shape) for out in outs[3 * index : 3 * index + 3]]
        for index, leaf in enumerate(leaves)
    ]


def flip(value, bits):
    count = lax.axis_size(SEQ)
    return lax.ppermute(value, SEQ, [(index, index ^ bits) for index in range(count)])


def others(value, axis):
    size = lax.axis_size(axis)
    parts = [
        lax.ppermute(value, axis, [((i + step) % size, i) for i in range(size)])
        for step in range(1, size)
    ]
    return parts[0] if size == 2 else jnp.concatenate(parts, axis=0)


def to_owners(blocks, axis):
    size = lax.axis_size(axis)
    return [
        lax.ppermute(block, axis, [(i, (i + step) % size) for i in range(size)])
        for step, block in enumerate(blocks, 1)
    ]


def add_all(own, parts):
    return functools.reduce(lambda total, part: total + part.astype(F32), parts, own.astype(F32))


def spread_sum(value):
    count = lax.axis_size(ALL)
    return jnp.sum(swap(jnp.broadcast_to(value[None], (count, *value.shape)), ALL), axis=0)


def body(
    tokens,
    cotangent,
    segment_ids,
    expert_ids,
    projection,
    output_weight,
    expert_up,
    expert_down,
    norm_gains,
    projection_first,
    projection_second,
    output_first,
    output_second,
    up_first,
    up_second,
    down_first,
    down_second,
    gains_first,
    gains_second,
):
    inputs = tokens[0].astype(F32)
    upstream = cotangent[0].astype(F32)
    row_count = inputs.shape[0]
    width = inputs.shape[1]
    head_size = width // HEADS
    scaling = head_size ** (-0.5)
    count = lax.axis_size(SEQ)
    groups = lax.axis_size("exp")
    team = lax.axis_size(TEAM)
    position = lax.axis_index(SEQ)
    length = count * row_count
    weight_rows = projection.shape[0]
    first_heads, active_table = head_plan(count)
    starts = [int(head) * head_size for head in first_heads]
    active = lax.dynamic_index_in_dim(jnp.asarray(active_table), position, 0, keepdims=False)
    gain_first = norm_gains[0]
    gain_second = norm_gains[1]
    used = active_table.any(axis=2)

    scale_first = lax.rsqrt(jnp.mean(inputs * inputs, axis=-1, keepdims=True) + EPSILON)
    normed_first = inputs * scale_first
    attend_in = (normed_first * gain_first).astype(BF16)
    slots = groups * CAP
    chosen = expert_ids[0, :, 0]
    one_hot = (chosen[:, None] == jnp.arange(groups, dtype=jnp.int32)[None, :]).astype(jnp.int32)
    rank = jnp.sum(jnp.cumsum(one_hot, axis=0) * one_hot, axis=1) - 1
    target = chosen * CAP + rank
    placing = (target[:, None] == jnp.arange(slots, dtype=jnp.int32)[None, :]).astype(BF16)

    def to_slots(values):
        outgoing = jnp.einsum("ts,td->sd", placing, values, preferred_element_type=F32)
        return outgoing.astype(BF16)

    def dispatch(outgoing):
        outgoing = jnp.broadcast_to(
            outgoing.reshape(1, groups, CAP, width), (team, groups, CAP, width)
        )
        return swap(outgoing.reshape(team * groups, CAP, width), TEAM + EXP).reshape(
            team * slots, width
        )

    def send_back(values):
        return swap(values.reshape(team * groups, CAP, width), TEAM + EXP).reshape(
            team, slots, width
        )

    def collect(returned):
        return jnp.einsum("ts,jsd->td", placing, returned, preferred_element_type=F32)

    projection_low = projection.astype(BF16)
    sent_rows = weight_rows + 8
    own_documents = jnp.zeros((8, 3 * LANES + width), BF16)
    own_documents = own_documents.at[0, :row_count].set(segment_ids[0].astype(BF16))
    output_low = output_weight.astype(BF16)
    pieces = [
        jnp.concatenate(
            [projection_low[:, k * width + s : k * width + s + LANES] for k in range(3)]
            + [output_low],
            axis=1,
        )
        for s in starts
    ]
    pieces = jnp.stack([jnp.concatenate([piece, own_documents], axis=0) for piece in pieces])
    own_up = expert_up[0].astype(BF16)
    own_down = expert_down[0].astype(BF16)
    pairwise = count == 8
    if pairwise:
        order = jnp.arange(count, dtype=jnp.int32) ^ position
        beside, below, across = flip(attend_in, 1), flip(attend_in, 2), flip(attend_in, 4)
        grad_arrived = dispatch(to_slots(cotangent[0]))
        pieces, beside, below, across, grad_arrived, own_up = together(
            pieces, beside, below, across, grad_arrived, own_up
        )
        corner = flip(across, 2)
        row_blocks = [attend_in, beside]
        row_blocks += [part for block in (below, across, corner) for part in (block, flip(block, 1))]
    else:
        order = jnp.arange(count, dtype=jnp.int32)
        row_blocks = [lax.all_gather(attend_in, SEQ, axis=0, tiled=True)]
        grad_arrived = dispatch(to_slots(cotangent[0]))
    got_rows = swap(pieces, SEQ)
    documents = jnp.broadcast_to(
        got_rows[:, weight_rows, :row_count].reshape(length, 1), (length, LANES)
    )

    def group_copies(value):
        return swap(jnp.broadcast_to(value[None], (groups, *value.shape)), EXP)

    column_copies = group_copies(got_rows[:, :weight_rows, : 3 * LANES])

    peer_up = others(own_up, "hi")
    *row_blocks, column_copies, output_rows, peer_up, own_up, own_down = together(
        *row_blocks,
        column_copies,
        got_rows[:, :weight_rows, 3 * LANES :],
        peer_up,
        own_up,
        own_down,
    )
    columns = jnp.swapaxes(column_copies, 0, 1).reshape(width, 3 * LANES)
    output_copies = group_copies(output_rows)
    peer_down = others(own_down, "hi")
    side_up = others(own_up, "in")
    side_down = others(own_down, "in")
    far_up = others(peer_up, "in")

    mixed_low, mixed_full, stat, pair = attend(
        active, order, row_blocks, columns, documents, row_count
    )

    def place_heads():
        index = np.arange(LANES)
        matrix = np.zeros((count, LANES, width), np.float32)
        for device in range(count):
            for slot in range(2):
                if used[device, slot]:
                    own = index[slot * HALF : (slot + 1) * HALF]
                    matrix[device, own, starts[device] + own] = 1.0
        return jnp.asarray(matrix, BF16)

    head_places = place_heads()

    def to_tokens(values):
        return swap(values.reshape(count, row_count, values.shape[1]), SEQ)

    mixed_low, output_copies, peer_down, side_up, side_down, far_up = together(
        mixed_low, output_copies, peer_down, side_up, side_down, far_up
    )
    output_full = jnp.swapaxes(output_copies, 0, 1).reshape(width, width)
    far_down = others(peer_down, "in")
    mixed_pieces, projection_low = together(to_tokens(mixed_low), projection_low)
    projection_full = lax.all_gather(projection_low, ALL, axis=0, tiled=True)
    attend_out = jnp.einsum(
        "jtc,jcd->td", mixed_pieces, head_places, preferred_element_type=F32
    ).astype(BF16)
    branch = jnp.dot(attend_out, output_full, preferred_element_type=F32)
    middle = inputs + branch
    scale_second = lax.rsqrt(jnp.mean(middle * middle, axis=-1, keepdims=True) + EPSILON)
    normed_second = middle * scale_second
    expert_in = (normed_second * gain_second).astype(BF16)

    expert_slots, far_down = together(to_slots(expert_in), far_down)
    arrived = dispatch(expert_slots)
    ups, downs = (own_up, peer_up, side_up, far_up), (own_down, peer_down, side_down, far_down)
    grad_slots, actives, hiddens = expert_part(arrived, grad_arrived, ups, downs)
    returned_grad = send_back(grad_slots)

    blocks = list(zip(actives, hiddens, strict=True))
    down_far, up_far, down_peer, up_peer = unit_grads(
        grad_arrived, arrived, (blocks[3], blocks[1]), (BF16, F32)
    )
    (down_part,) = to_owners([down_far], "in")
    down_side, up_side, down_own, up_own = unit_grads(
        grad_arrived, arrived, (blocks[2], blocks[0]), (BF16, F32)
    )
    produced = produced_part(actives, downs)
    returned_grad, down_part, up_far, up_peer, projection_full, produced, down_side, up_own = (
        together(
            returned_grad, down_part, up_far, up_peer, projection_full, produced, down_side, up_own
        )
    )
    grad_expert_in = collect(returned_grad)
    (up_part,) = to_owners([up_far], "in")
    peers = lax.axis_size("hi")

    def hi_parts(value):
        return to_owners(list(value.astype(BF16).reshape(peers - 1, -1, width)), "hi")

    down_hi = hi_parts(add_all(down_peer, [down_part]))

    scaled_second = grad_expert_in * gain_second
    gain_second_part = jnp.sum(grad_expert_in * normed_second, axis=0)
    grad_middle = scale_second * (
        scaled_second
        - normed_second * jnp.mean(scaled_second * normed_second, axis=-1, keepdims=True)
    )
    residual_grad = upstream + grad_middle
    branch_grad = residual_grad.astype(BF16)
    grad_mixed = jnp.einsum(
        "td,ed->te", branch_grad, output_full, preferred_element_type=F32
    ).astype(BF16)

    sent_grad = jnp.stack([grad_mixed[:, s : s + LANES] for s in starts])
    row_grad = swap(sent_grad, SEQ).reshape(length, LANES)

    group = lax.axis_index(EXP)

    def group_rows(value):
        rows = value.reshape(count, groups, weight_rows, -1)
        own, *away = [
            lax.dynamic_index_in_dim(rows, lax.rem(group + step, groups), 1, keepdims=False)
            for step in range(groups)
        ]
        return own, away

    output_term = jnp.einsum("tc,te->ce", attend_out, branch_grad, preferred_element_type=F32)
    output_own, output_away = group_rows(output_term.astype(BF16))
    output_away = to_owners(output_away, "exp")
    row_grad, produced, down_side, up_side, up_part, *output_away = together(
        row_grad, produced, down_side, up_side, up_part, *output_away
    )
    (down_early,) = to_owners([down_side], "in")
    (up_early,) = to_owners([up_side], "in")
    up_hi = hi_parts(add_all(up_peer, [up_part]))
    returned = send_back(produced)
    grad_qkv, grad_lying = attend_back(
        active, order, pair, documents, stat, row_grad, mixed_full, row_count, scaling
    )
    grad_qkv, grad_lying, returned, down_early, up_early, *held = together(
        grad_qkv, grad_lying, returned, down_early, up_early, *down_hi, *up_hi
    )
    down_hi, up_hi = held[: len(up_hi)], held[len(up_hi) :]
    up_grad = add_all(up_own, [up_early, *up_hi])[None]
    down_grad = add_all(down_own, [down_early, *down_hi])[None]
    block_output = (middle + collect(returned)).astype(BF16)[None]

    column_own, column_away = group_rows(column_terms(row_blocks, grad_lying))
    dense_rows = jnp.concatenate(
        [
            add_all(column_own, to_owners(column_away, "exp")).astype(BF16),
            add_all(output_own, output_away).astype(BF16),
        ],
        axis=2,
    )
    if pairwise:
        lying_terms = [
            lax.dynamic_index_in_dim(dense_rows, position ^ bits, 0, keepdims=False)
            for bits in range(count)
        ]
        lying_terms[1:] = [flip(lying_terms[bits], bits) for bits in range(1, count)]
        grad_pieces, *lying_terms = together(to_tokens(grad_qkv), *lying_terms)
        lying_terms = jnp.stack(lying_terms)
        got_terms = [
            lax.dynamic_index_in_dim(lying_terms, position ^ j, 0, keepdims=False)
            for j in range(count)
        ]
    else:
        grad_pieces, dense_rows = together(to_tokens(grad_qkv), dense_rows)
        got_terms = list(swap(dense_rows, SEQ))
    got_terms = [term.astype(F32) for term in got_terms]
    input_grad, gain_first_part = close_norm(
        grad_pieces, starts, projection_full, tokens[0], gain_first[None], residual_grad
    )
    input_grad, gain_first_part = input_grad[None], gain_first_part[0]
    output_grad = functools.reduce(jnp.add, [term[:, 3 * LANES :] for term in got_terms])
    head_grads = []
    for k in range(3):
        for head in range(HEADS):
            parts = [
                got_terms[j][:, k * LANES + slot * HALF : k * LANES + (slot + 1) * HALF]
                for j in range(count)
                for slot in range(2)
                if used[j, slot] and first_heads[j] + slot == head
            ]
            head_grads.append(functools.reduce(jnp.add, parts))
    projection_grad = jnp.concatenate(head_grads, axis=1)

    local_square = jnp.sum(projection_grad * projection_grad) + jnp.sum(output_grad * output_grad)
    local_square = local_square + jnp.sum(up_grad * up_grad) + jnp.sum(down_grad * down_grad)
    summed = spread_sum(
        jnp.concatenate(
            [gain_first_part, gain_second_part, jnp.broadcast_to(local_square, (LANES,))]
        )[None]
    )[0]
    gains_grad = summed[: 2 * width].reshape(2, width)
    grad_norm = jnp.sqrt(summed[2 * width] + jnp.sum(gains_grad * gains_grad))
    factor = jnp.minimum(1.0, CLIP / (grad_norm + 1e-06))
    (
        (projection_moment, projection_square, projection_new),
        (output_moment, output_square, output_new),
        (up_moment, up_square, up_new),
        (down_moment, down_square, down_new),
    ) = adam_all(
        factor,
        [
            (projection, projection_grad, projection_first, projection_second),
            (output_weight, output_grad, output_first, output_second),
            (expert_up, up_grad, up_first, up_second),
            (expert_down, down_grad, down_first, down_second),
        ],
        (RATE_MATRIX, RATE_OUTPUT, RATE_MATRIX, RATE_MATRIX),
        6,
    )
    gains_moment, gains_square, gains_new = adam_update(
        norm_gains, gains_grad, gains_first, gains_second, factor, RATE_GAIN, 0.0
    )
    return (
        block_output,
        input_grad,
        grad_norm,
        projection_grad,
        projection_moment,
        projection_square,
        projection_new,
        output_grad,
        output_moment,
        output_square,
        output_new,
        up_grad,
        up_moment,
        up_square,
        up_new,
        down_grad,
        down_moment,
        down_square,
        down_new,
        gains_grad,
        gains_moment,
        gains_square,
        gains_new,
    )


def solution(mesh):
    token = P("exp", SEQ, None)
    dense = P(ALL, None)
    expert = P("exp", SEQ, None)
    in_specs = (
        (token, token, P("exp", SEQ), token)
        + (dense, dense, expert, expert, P())
        + (dense,) * 4
        + (expert,) * 4
        + (P(), P())
    )
    out_specs = (token, token, P()) + (dense,) * 8 + (expert,) * 8 + (P(),) * 4
    rows, groups = mesh.devices.shape
    fine = Mesh(mesh.devices.reshape(rows // 4, 2, 2, groups), ALL)
    return jax.shard_map(body, mesh=fine, in_specs=in_specs, out_specs=out_specs, check_vma=False)
```

```python
import functools
import math

import jax
import jax.numpy as jnp
import numpy as np
from jax import lax
from jax.experimental import pallas as pl
from jax.experimental.pallas import tpu as pltpu
from jax.sharding import Mesh
from jax.sharding import PartitionSpec as P

HEADS = 12
CAP = 128
STEP = 10


EPSILON = 1e-05
CLIP = 1.0
BETA_ONE = 0.9
BETA_TWO = 0.99
ADAM_FLOOR = 1e-08
DECAY = 0.1
RATE_MATRIX = 0.04
RATE_OUTPUT = 0.1
RATE_GAIN = 0.5

SEQ = ("hi", "lo", "in")
EXP = ("exp",)
ALL = SEQ + EXP
TEAM = ("lo",)
SHARE = ("hi", "in")
LANES = 128
HALF = 64
FAR = -1e30
BF16 = jnp.bfloat16
F32 = jnp.float32
VMEM_LIMIT = 60 * 1024 * 1024


def head_plan(count):
    whole = math.lcm(HEADS, count)
    units, parts = whole // count, whole // HEADS
    first = np.zeros((count,), np.int64)
    active = np.zeros((count, 2, count), np.int32)
    for device in range(count):
        first[device] = min(units * device // parts, HEADS - 2)
        for unit in range(units * device, units * (device + 1)):
            slot = unit // parts - first[device]
            for block in range(count):
                turn = block % (2 * parts)
                if min(turn, 2 * parts - 1 - turn) == unit % parts:
                    active[device, slot, block] = 1
    return first, active


def three_parts(value):
    high = value.astype(BF16).astype(F32)
    middle = (value - high).astype(BF16).astype(F32)
    return high, middle, value - high - middle


def contract(left, right, left_axis, right_axis):
    return lax.dot_general(
        left, right, (((left_axis,), (right_axis,)), ((), ())), preferred_element_type=F32
    )


def slot_arrays(packed, documents, kind, slot):
    spare = HALF - HALF * slot
    lane = lax.broadcasted_iota(jnp.int32, packed.shape, 1)
    own = (lane < HALF) if slot == 0 else (lane >= HALF)
    place = (lane - spare).astype(F32)
    ours = place == documents
    first = (lane >= spare) & (lane < spare + 3)
    if kind == "query":
        extra = jnp.where(first & jnp.logical_not(ours), FAR, 0.0)
    elif kind == "key":
        extra = jnp.where(ours | ((lane >= spare + 3) & (lane < spare + 6)), 1.0, 0.0)
    else:
        extra = jnp.where(first, 1.0, 0.0)
    return jnp.where(own, packed, extra).astype(BF16)


def fill_slots(packed_of, documents_ref, wide_ref, kinds, place):
    documents = documents_ref[place, :].astype(F32)
    for number, kind in enumerate(kinds):
        packed = packed_of(kind).astype(F32)
        if kind == "query":
            packed = packed * 0.125
        for slot in range(2):
            column = (2 * number + slot) * LANES
            wide_ref[place, column : column + LANES] = slot_arrays(packed, documents, kind, slot)


def attend_kernel(active_ref, order_ref, *refs, block, chunk, held):
    row_refs = refs[:held]
    columns_ref, documents_ref = refs[held : held + 2]
    low_ref, full_ref, stat_ref, pair_ref, mixed_ref, wide_ref = refs[held + 2 :]
    at = pl.program_id(0)

    @pl.when(at == 0)
    def _():
        def fill(tokens, index):
            place = pl.ds(pl.multiple_of(order_ref[index] * block, block), block)
            packed = contract(tokens, columns_ref[...], 1, 0).astype(BF16)
            pair_ref[place, :] = packed[:, LANES:]
            parts = {
                kind: packed[:, part * LANES : (part + 1) * LANES]
                for part, kind in enumerate(("query", "key", "value"))
            }
            fill_slots(parts.get, documents_ref, wide_ref, tuple(parts), place)

        if held > 1:
            for index, row_ref in enumerate(row_refs):
                fill(row_ref[...], index)
        else:

            @pl.loop(0, pl.num_programs(0))
            def _(index):
                fill(row_refs[0][pl.ds(pl.multiple_of(index * block, block), block), :], index)

    rows = pl.ds(pl.multiple_of(at * block, block), block)
    lane = lax.broadcasted_iota(jnp.int32, (block, LANES), 1)
    last = lax.div(at * block, chunk)
    for slot in range(2):
        spare = HALF - HALF * slot
        own = (lane < HALF) if slot == 0 else (lane >= HALF)
        columns = slice(slot * LANES, (slot + 1) * LANES)

        @pl.when(active_ref[slot, at] != 0)
        def _():
            query = wide_ref[rows, columns]

            def step(index, carry, edge):
                top, weighted = carry
                place = pl.ds(pl.multiple_of(index * chunk, chunk), chunk)
                keys = wide_ref[place, 2 * LANES + slot * LANES : 3 * LANES + slot * LANES]
                values = wide_ref[place, 4 * LANES + slot * LANES : 5 * LANES + slot * LANES]
                scores = contract(query, keys, 1, 1)
                if edge:
                    key_at = index * chunk + lax.broadcasted_iota(jnp.int32, (block, chunk), 1)
                    query_at = at * block + lax.broadcasted_iota(jnp.int32, (block, chunk), 0)
                    scores = jnp.where(key_at <= query_at, scores, FAR)
                new_top = jnp.maximum(top, jnp.max(scores, axis=1, keepdims=True))
                weights = jnp.exp(scores - new_top).astype(BF16)
                weighted = weighted * jnp.exp(top - new_top) + contract(weights, values, 1, 0)
                return new_top, weighted

            carry = (jnp.full((block, 1), FAR, F32), jnp.zeros((block, LANES), F32))
            carry = lax.fori_loop(0, last, lambda index, state: step(index, state, False), carry)
            top, weighted = step(last, carry, True)
            total = weighted[:, spare : spare + 1]
            mixed_ref[slot] = jnp.where(own, weighted / total, 0.0)
            log_total = top + jnp.log(total)
            high, middle, small = three_parts(log_total)
            extra = jnp.where(lane == spare + 3, -high, 0.0)
            extra = jnp.where(lane == spare + 4, -middle, extra)
            extra = jnp.where(lane == spare + 5, -small, extra)
            stat_ref[:, columns] = (query.astype(F32) + extra).astype(BF16)

        @pl.when(active_ref[slot, at] == 0)
        def _():
            mixed_ref[slot] = jnp.zeros((block, LANES), F32)
            stat_ref[:, columns] = jnp.zeros((block, LANES), BF16)

    mixed = mixed_ref[0] + mixed_ref[1]
    full_ref[...] = mixed
    low_ref[...] = mixed.astype(BF16)


def attend_back_kernel(
    active_ref,
    order_ref,
    pair_ref,
    documents_ref,
    stat_ref,
    grad_ref,
    mixed_ref,
    out_ref,
    lying_ref,
    key_sum_ref,
    value_sum_ref,
    query_sum_ref,
    wide_ref,
    *,
    block,
    chunk,
    scaling,
):
    at = pl.program_id(0)
    rows = pl.ds(pl.multiple_of(at * block, block), block)
    lane = lax.broadcasted_iota(jnp.int32, (block, LANES), 1)
    last = lax.div(at * block, chunk)

    @pl.when(at == 0)
    def _():
        @pl.loop(0, pl.num_programs(0))
        def _(index):
            place = pl.ds(pl.multiple_of(index * block, block), block)
            parts = {"key": pair_ref[place, :LANES], "value": pair_ref[place, LANES:]}
            fill_slots(parts.get, documents_ref, wide_ref, tuple(parts), place)

        key_sum_ref[...] = jnp.zeros_like(key_sum_ref)
        value_sum_ref[...] = jnp.zeros_like(value_sum_ref)

    for slot in range(2):
        spare = HALF - HALF * slot
        own = (lane < HALF) if slot == 0 else (lane >= HALF)
        columns = slice(slot * LANES, (slot + 1) * LANES)
        query_sum_ref[slot] = jnp.zeros((block, LANES), F32)

        @pl.when(active_ref[slot, at] != 0)
        def _():
            query = stat_ref[:, columns]
            grad = grad_ref[...].astype(F32)
            delta = jnp.sum(jnp.where(own, grad * mixed_ref[...], 0.0), axis=1, keepdims=True)
            high, middle, small = three_parts(delta)
            extra = jnp.where(lane == spare, -high, 0.0)
            extra = jnp.where(lane == spare + 1, -middle, extra)
            extra = jnp.where(lane == spare + 2, -small, extra)
            grad_low = jnp.where(own, grad, extra).astype(BF16)

            def step(index, edge):
                place = pl.ds(pl.multiple_of(index * chunk, chunk), chunk)
                keys = wide_ref[place, slot * LANES : (slot + 1) * LANES]
                values = wide_ref[place, (2 + slot) * LANES : (3 + slot) * LANES]
                scores = contract(keys, query, 1, 1)
                if edge:
                    key_at = index * chunk + lax.broadcasted_iota(jnp.int32, (chunk, block), 0)
                    query_at = at * block + lax.broadcasted_iota(jnp.int32, (chunk, block), 1)
                    scores = jnp.where(key_at <= query_at, scores, FAR)
                weights = jnp.exp(scores)
                grad_weights = contract(values, grad_low, 1, 1)
                grad_scores = (weights * grad_weights).astype(BF16)
                value_sum_ref[slot, place, :] += contract(weights.astype(BF16), grad_low, 1, 0)
                key_sum_ref[slot, place, :] += contract(grad_scores, query, 1, 0)
                query_sum_ref[slot] += contract(grad_scores, keys, 0, 0)

            @pl.loop(0, last)
            def _(index):
                step(index, False)

            step(last, True)

    first_half = lane < HALF
    query_grad = jnp.where(first_half, query_sum_ref[0], query_sum_ref[1]) * scaling
    out_ref[rows, :LANES] = query_grad.astype(BF16)
    lying = pl.ds(pl.multiple_of(order_ref[at] * block, block), block)
    lying_ref[lying, :LANES] = query_grad.astype(BF16)

    @pl.when(at == pl.num_programs(0) - 1)
    def _():
        @pl.loop(0, pl.num_programs(0))
        def _(index):
            place = pl.ds(pl.multiple_of(index * block, block), block)
            key_grad = jnp.where(first_half, key_sum_ref[0, place, :], key_sum_ref[1, place, :])
            value_grad = jnp.where(
                first_half, value_sum_ref[0, place, :], value_sum_ref[1, place, :]
            )
            out_ref[place, LANES : 2 * LANES] = key_grad.astype(BF16)
            out_ref[place, 2 * LANES :] = value_grad.astype(BF16)
            lying = pl.ds(pl.multiple_of(order_ref[index] * block, block), block)
            lying_ref[lying, LANES : 2 * LANES] = key_grad.astype(BF16)
            lying_ref[lying, 2 * LANES :] = value_grad.astype(BF16)


def whole(value):
    return pl.BlockSpec(value.shape, lambda i, *unused: (0, 0), pipeline_mode=pl.Buffered(1))


SMALL = pl.CostEstimate(flops=1, bytes_accessed=1, transcendentals=0)


def attend(active, order, row_blocks, columns, documents, block):
    length = documents.shape[0]
    pair = jax.ShapeDtypeStruct((length, 2 * LANES), BF16)
    return pl.pallas_call(
        functools.partial(attend_kernel, block=block, chunk=2 * block, held=len(row_blocks)),
        grid_spec=pltpu.PrefetchScalarGridSpec(
            num_scalar_prefetch=2,
            grid=(length // block,),
            in_specs=[whole(value) for value in (*row_blocks, columns, documents)],
            out_specs=[
                pl.BlockSpec((block, LANES), lambda i, a, o: (i, 0)),
                pl.BlockSpec((block, LANES), lambda i, a, o: (i, 0)),
                pl.BlockSpec((block, 2 * LANES), lambda i, a, o: (i, 0)),
                whole(pair),
            ],
            scratch_shapes=[
                pltpu.VMEM((2, block, LANES), F32),
                pltpu.VMEM((length, 6 * LANES), BF16),
            ],
        ),
        out_shape=[
            jax.ShapeDtypeStruct((length, LANES), BF16),
            jax.ShapeDtypeStruct((length, LANES), F32),
            jax.ShapeDtypeStruct((length, 2 * LANES), BF16),
            pair,
        ],
        compiler_params=pltpu.CompilerParams(vmem_limit_bytes=VMEM_LIMIT),
        cost_estimate=SMALL,
    )(active, order, *row_blocks, columns, documents)


def attend_back(active, order, pair, documents, stat, grad, mixed, block, scaling):
    length = pair.shape[0]
    count = length // block
    return pl.pallas_call(
        functools.partial(attend_back_kernel, block=block, chunk=2 * block, scaling=scaling),
        grid_spec=pltpu.PrefetchScalarGridSpec(
            num_scalar_prefetch=2,
            grid=(count,),
            in_specs=[
                whole(pair),
                whole(documents),
                pl.BlockSpec((block, 2 * LANES), lambda i, a, o: (i, 0)),
                pl.BlockSpec((block, LANES), lambda i, a, o: (i, 0)),
                pl.BlockSpec((block, LANES), lambda i, a, o: (i, 0)),
            ],
            out_specs=[
                pl.BlockSpec(
                    (length, 3 * LANES), lambda i, a, o: (0, 0), pipeline_mode=pl.Buffered(1)
                )
            ]
            * 2,
            scratch_shapes=[
                pltpu.VMEM((2, length, LANES), F32),
                pltpu.VMEM((2, length, LANES), F32),
                pltpu.VMEM((2, block, LANES), F32),
                pltpu.VMEM((length, 4 * LANES), BF16),
            ],
        ),
        out_shape=[jax.ShapeDtypeStruct((length, 3 * LANES), BF16)] * 2,
        compiler_params=pltpu.CompilerParams(vmem_limit_bytes=VMEM_LIMIT),
        cost_estimate=SMALL,
    )(active, order, pair, documents, stat, grad, mixed)


def expert_kernel(arrived_ref, grad_ref, *refs, count):
    up_refs, down_refs = refs[:count], refs[count : 2 * count]
    total_ref = refs[2 * count]
    active_refs, hidden_refs = refs[2 * count + 1 : 3 * count + 1], refs[3 * count + 1 :]
    arrived, grad_arrived = arrived_ref[...], grad_ref[...]
    scale = math.sqrt(2.0 / math.pi)
    total = jnp.zeros(total_ref.shape, F32)
    for up_ref, down_ref, active_ref, hidden_ref in zip(
        up_refs, down_refs, active_refs, hidden_refs, strict=True
    ):
        up = up_ref[...]
        hidden = contract(arrived, up, 1, 1)
        squared = hidden * hidden
        bend = jnp.tanh(scale * hidden * (1.0 + 0.044715 * squared))
        half = 0.5 + 0.5 * bend
        active_ref[...] = (hidden * half).astype(BF16)
        slope = half + (0.5 * scale) * hidden * (1.0 - bend * bend) * (1.0 + 3 * 0.044715 * squared)
        grad_hidden = (slope * contract(grad_arrived, down_ref[...], 1, 1)).astype(BF16)
        hidden_ref[...] = grad_hidden
        total = total + contract(grad_hidden, up, 1, 0)
    total_ref[...] = total.astype(BF16)


def rows_spec(value, block):
    return pl.BlockSpec((block, value.shape[1]), lambda i: (i, 0))


def expert_part(arrived, grad_arrived, ups, downs):
    slots, width = arrived.shape
    block = 256
    units = [jax.ShapeDtypeStruct((slots, up.shape[0]), BF16) for up in ups]
    outs = [jax.ShapeDtypeStruct((slots, width), BF16), *units, *units]
    total, *parts = pl.pallas_call(
        functools.partial(expert_kernel, count=len(ups)),
        grid=(slots // block,),
        in_specs=[rows_spec(arrived, block), rows_spec(grad_arrived, block)]
        + [whole(value) for value in (*ups, *downs)],
        out_specs=[rows_spec(out, block) for out in outs],
        out_shape=outs,
        compiler_params=pltpu.CompilerParams(vmem_limit_bytes=VMEM_LIMIT),
        cost_estimate=SMALL,
    )(arrived, grad_arrived, *ups, *downs)
    return total, parts[: len(ups)], parts[len(ups) :]


def produced_kernel(*refs, count):
    total = contract(refs[0][...], refs[count][...], 1, 0)
    for index in range(1, count):
        total = total + contract(refs[index][...], refs[count + index][...], 1, 0)
    refs[-1][...] = total.astype(BF16)


def produced_part(actives, downs):
    slots, width = actives[0].shape[0], downs[0].shape[1]
    block = 256
    out = jax.ShapeDtypeStruct((slots, width), BF16)
    return pl.pallas_call(
        functools.partial(produced_kernel, count=len(actives)),
        grid=(slots // block,),
        in_specs=[rows_spec(value, block) for value in actives] + [whole(down) for down in downs],
        out_specs=rows_spec(out, block),
        out_shape=out,
        compiler_params=pltpu.CompilerParams(vmem_limit_bytes=VMEM_LIMIT),
        cost_estimate=SMALL,
    )(*actives, *downs)


def unit_kernel(grad_ref, arrived_ref, *refs, count):
    for index in range(count):
        active_ref, hidden_ref = refs[2 * index : 2 * index + 2]
        down_ref, up_ref = refs[2 * count + 2 * index : 2 * count + 2 * index + 2]
        down_ref[...] = contract(active_ref[...], grad_ref[...], 0, 0).astype(down_ref.dtype)
        up_ref[...] = contract(hidden_ref[...], arrived_ref[...], 0, 0).astype(up_ref.dtype)


def unit_grads(grad_arrived, arrived, blocks, kinds):
    slots, width = arrived.shape
    block = 256
    right = pl.BlockSpec((slots, block), lambda i: (0, i))
    outs = [
        jax.ShapeDtypeStruct((active.shape[1], width), kind)
        for (active, unused), kind in zip(blocks, kinds, strict=True)
        for part in range(2)
    ]
    flat = [value for pair in blocks for value in pair]
    return pl.pallas_call(
        functools.partial(unit_kernel, count=len(blocks)),
        grid=(width // block,),
        in_specs=[right, right] + [whole(value) for value in flat],
        out_specs=[pl.BlockSpec((out.shape[0], block), lambda i: (0, i)) for out in outs],
        out_shape=outs,
        compiler_params=pltpu.CompilerParams(vmem_limit_bytes=VMEM_LIMIT),
        cost_estimate=SMALL,
    )(grad_arrived, arrived, *flat)


def column_kernel(*refs, held):
    row_refs = refs[:held]
    lying_ref, out_ref = refs[held:]
    start, total = 0, None
    for row_ref in row_refs:
        rows = row_ref.shape[0]
        part = contract(row_ref[...], lying_ref[start : start + rows, :], 0, 0)
        total = part if total is None else total + part
        start += rows
    out_ref[...] = total.astype(BF16)


def column_terms(row_blocks, grad_lying):
    width = row_blocks[0].shape[1]
    block = 256
    out = jax.ShapeDtypeStruct((width, 3 * LANES), BF16)
    return pl.pallas_call(
        functools.partial(column_kernel, held=len(row_blocks)),
        grid=(width // block,),
        in_specs=[
            pl.BlockSpec((value.shape[0], block), lambda i: (0, i)) for value in row_blocks
        ]
        + [whole(grad_lying)],
        out_specs=rows_spec(out, block),
        out_shape=out,
        compiler_params=pltpu.CompilerParams(vmem_limit_bytes=VMEM_LIMIT),
        cost_estimate=SMALL,
    )(*row_blocks, grad_lying)


def close_kernel(
    pieces_ref, matrix_ref, tokens_ref, gain_ref, residual_ref, out_ref, part_ref, sum_ref, *, starts
):
    width = tokens_ref.shape[1]
    lane = lax.broadcasted_iota(jnp.int32, (tokens_ref.shape[0], LANES), 1)
    sum_ref[...] = jnp.zeros_like(sum_ref)
    for device, start in enumerate(starts):
        for part in range(3):
            piece = pieces_ref[device, :, part * LANES : (part + 1) * LANES].astype(F32)
            column = part * width + start
            if column % LANES == 0:
                sum_ref[:, column : column + LANES] += piece
            else:
                turned = pltpu.roll(piece, HALF, 1)
                low, high = column - HALF, column + HALF
                sum_ref[:, low : low + LANES] += jnp.where(lane >= HALF, turned, 0.0)
                sum_ref[:, high : high + LANES] += jnp.where(lane < HALF, turned, 0.0)
    grad = contract(sum_ref[...].astype(BF16), matrix_ref[...], 1, 1)
    inputs = tokens_ref[...].astype(F32)
    scale = lax.rsqrt(jnp.mean(inputs * inputs, axis=-1, keepdims=True) + EPSILON)
    normed = inputs * scale
    scaled = grad * gain_ref[...]
    mean = jnp.mean(scaled * normed, axis=-1, keepdims=True)
    out_ref[...] = residual_ref[...] + scale * (scaled - normed * mean)
    part_ref[...] = jnp.sum(grad * normed, axis=0, keepdims=True)


def close_norm(pieces, starts, matrix, tokens, gain, residual):
    rows, width = tokens.shape
    outs = [
        jax.ShapeDtypeStruct((rows, width), F32),
        jax.ShapeDtypeStruct((1, width), F32),
    ]
    return pl.pallas_call(
        functools.partial(close_kernel, starts=starts),
        in_specs=[pl.BlockSpec(memory_space=pltpu.VMEM)] * 5,
        out_specs=[pl.BlockSpec(memory_space=pltpu.VMEM)] * 2,
        out_shape=outs,
        scratch_shapes=[pltpu.VMEM((rows, 3 * width), F32)],
        compiler_params=pltpu.CompilerParams(vmem_limit_bytes=VMEM_LIMIT),
        cost_estimate=SMALL,
    )(pieces, matrix, tokens, gain, residual)


def dense_kernel(order_ref, *refs, starts):
    count = len(starts)
    term_refs = refs[:count]
    columns_ref, output_ref, square_ref, terms_ref = refs[count:]
    width = output_ref.shape[1]
    for index, term_ref in enumerate(term_refs):
        terms_ref[order_ref[index]] = term_ref[...].astype(F32)
    columns_ref[...] = jnp.zeros_like(columns_ref)
    lane = lax.broadcasted_iota(jnp.int32, (columns_ref.shape[0], LANES), 1)
    output = jnp.zeros(output_ref.shape, F32)
    for device, start in enumerate(starts):
        output = output + terms_ref[device, :, 3 * LANES :]
        for part in range(3):
            piece = terms_ref[device, :, part * LANES : (part + 1) * LANES]
            column = part * width + start
            if column % LANES == 0:
                columns_ref[:, column : column + LANES] += piece
            else:
                turned = pltpu.roll(piece, HALF, 1)
                low, high = column - HALF, column + HALF
                columns_ref[:, low : low + LANES] += jnp.where(lane >= HALF, turned, 0.0)
                columns_ref[:, high : high + LANES] += jnp.where(lane < HALF, turned, 0.0)
    output_ref[...] = output
    columns = columns_ref[...]
    square_ref[...] = jnp.zeros_like(square_ref) + (
        jnp.sum(columns * columns) + jnp.sum(output * output)
    )


def dense_grads(order, terms, starts):
    rows, lanes = terms[0].shape
    width = lanes - 3 * LANES
    outs = [jax.ShapeDtypeStruct((rows, columns), F32) for columns in (3 * width, width)]
    outs.append(jax.ShapeDtypeStruct((1, LANES), F32))
    return pl.pallas_call(
        functools.partial(dense_kernel, starts=starts),
        in_specs=[pl.BlockSpec(memory_space=pltpu.SMEM)]
        + [pl.BlockSpec(memory_space=pltpu.VMEM)] * len(terms),
        out_specs=[pl.BlockSpec(memory_space=pltpu.VMEM)] * 3,
        out_shape=outs,
        scratch_shapes=[pltpu.VMEM((len(terms), rows, lanes), F32)],
        compiler_params=pltpu.CompilerParams(vmem_limit_bytes=VMEM_LIMIT),
        cost_estimate=SMALL,
    )(order, *terms)


def adam_update(weight, grad, first, second, factor, rate, decay):
    clipped = grad * factor
    first_new = BETA_ONE * first + (1.0 - BETA_ONE) * clipped
    second_new = BETA_TWO * second + (1.0 - BETA_TWO) * clipped * clipped
    first_hat = first_new / (1.0 - BETA_ONE**STEP)
    second_hat = second_new / (1.0 - BETA_TWO**STEP)
    weight_new = weight - rate * (first_hat / (jnp.sqrt(second_hat) + ADAM_FLOOR) + decay * weight)
    return (first_new, second_new, weight_new)


def together(*values):
    return lax.optimization_barrier(values)


def swap(value, axes):
    return lax.all_to_all(value, axes, split_axis=0, concat_axis=0, tiled=True)


def adam_kernel(factor_ref, *refs, rates):
    count = len(rates)
    factor = factor_ref[0]
    for index, rate in enumerate(rates):
        weight, grad, first, second = [ref[...] for ref in refs[4 * index : 4 * index + 4]]
        outs = refs[4 * count + 3 * index : 4 * count + 3 * index + 3]
        for out, value in zip(
            outs, adam_update(weight, grad, first, second, factor, rate, DECAY), strict=True
        ):
            out[...] = value


def adam_all(factor, leaves, rates, steps):
    flat = [value.reshape(value.shape[-2:]) for leaf in leaves for value in leaf]

    def spec(value):
        rows, columns = value.shape
        if rows % (8 * steps) == 0:
            return pl.BlockSpec((rows // steps, columns), lambda i: (i, 0))
        lanes = columns // steps
        return pl.BlockSpec((rows, lanes), lambda i: (0, i))

    shapes = [jax.ShapeDtypeStruct(value.shape, F32) for value in flat[::4] for _ in range(3)]
    outs = pl.pallas_call(
        functools.partial(adam_kernel, rates=rates),
        grid=(steps,),
        in_specs=[pl.BlockSpec(memory_space=pltpu.SMEM)] + [spec(value) for value in flat],
        out_specs=[spec(shape) for shape in shapes],
        out_shape=shapes,
        compiler_params=pltpu.CompilerParams(vmem_limit_bytes=VMEM_LIMIT),
        cost_estimate=pl.CostEstimate(
            flops=20 * sum(value.size for value in flat[::4]),
            bytes_accessed=28 * sum(value.size for value in flat[::4]),
            transcendentals=0,
        ),
    )(factor.reshape(1), *flat)
    return [
        [out.reshape(leaf[0].shape) for out in outs[3 * index : 3 * index + 3]]
        for index, leaf in enumerate(leaves)
    ]


def flip(value, bits):
    count = lax.axis_size(SEQ)
    return lax.ppermute(value, SEQ, [(index, index ^ bits) for index in range(count)])


def others(value, axis):
    size = lax.axis_size(axis)
    parts = [
        lax.ppermute(value, axis, [((i + step) % size, i) for i in range(size)])
        for step in range(1, size)
    ]
    return parts[0] if size == 2 else jnp.concatenate(parts, axis=0)


def to_owners(blocks, axis):
    size = lax.axis_size(axis)
    return [
        lax.ppermute(block, axis, [(i, (i + step) % size) for i in range(size)])
        for step, block in enumerate(blocks, 1)
    ]


def add_all(own, parts):
    return functools.reduce(lambda total, part: total + part.astype(F32), parts, own.astype(F32))


def spread_sum(value):
    count = lax.axis_size(ALL)
    return jnp.sum(swap(jnp.broadcast_to(value[None], (count, *value.shape)), ALL), axis=0)


def body(
    tokens,
    cotangent,
    segment_ids,
    expert_ids,
    projection,
    output_weight,
    expert_up,
    expert_down,
    norm_gains,
    projection_first,
    projection_second,
    output_first,
    output_second,
    up_first,
    up_second,
    down_first,
    down_second,
    gains_first,
    gains_second,
):
    inputs = tokens[0].astype(F32)
    upstream = cotangent[0].astype(F32)
    row_count = inputs.shape[0]
    width = inputs.shape[1]
    head_size = width // HEADS
    scaling = head_size ** (-0.5)
    count = lax.axis_size(SEQ)
    groups = lax.axis_size("exp")
    team = lax.axis_size(TEAM)
    position = lax.axis_index(SEQ)
    length = count * row_count
    weight_rows = projection.shape[0]
    first_heads, active_table = head_plan(count)
    starts = [int(head) * head_size for head in first_heads]
    active = lax.dynamic_index_in_dim(jnp.asarray(active_table), position, 0, keepdims=False)
    gain_first = norm_gains[0]
    gain_second = norm_gains[1]
    used = active_table.any(axis=2)

    scale_first = lax.rsqrt(jnp.mean(inputs * inputs, axis=-1, keepdims=True) + EPSILON)
    normed_first = inputs * scale_first
    attend_in = (normed_first * gain_first).astype(BF16)
    slots = groups * CAP
    chosen = expert_ids[0, :, 0]
    one_hot = (chosen[:, None] == jnp.arange(groups, dtype=jnp.int32)[None, :]).astype(jnp.int32)
    rank = jnp.sum(jnp.cumsum(one_hot, axis=0) * one_hot, axis=1) - 1
    target = chosen * CAP + rank
    placing = (target[:, None] == jnp.arange(slots, dtype=jnp.int32)[None, :]).astype(BF16)

    def to_slots(values):
        outgoing = jnp.einsum("ts,td->sd", placing, values, preferred_element_type=F32)
        return outgoing.astype(BF16)

    def dispatch(outgoing):
        outgoing = jnp.broadcast_to(
            outgoing.reshape(1, groups, CAP, width), (team, groups, CAP, width)
        )
        return swap(outgoing.reshape(team * groups, CAP, width), TEAM + EXP).reshape(
            team * slots, width
        )

    def send_back(values):
        return swap(values.reshape(team * groups, CAP, width), TEAM + EXP).reshape(
            team, slots, width
        )

    def collect(returned):
        return jnp.einsum("ts,jsd->td", placing, returned, preferred_element_type=F32)

    projection_low = projection.astype(BF16)
    sent_rows = weight_rows + 8
    own_documents = jnp.zeros((8, 3 * LANES + width), BF16)
    own_documents = own_documents.at[0, :row_count].set(segment_ids[0].astype(BF16))
    output_low = output_weight.astype(BF16)
    pieces = [
        jnp.concatenate(
            [projection_low[:, k * width + s : k * width + s + LANES] for k in range(3)]
            + [output_low],
            axis=1,
        )
        for s in starts
    ]
    pieces = jnp.stack([jnp.concatenate([piece, own_documents], axis=0) for piece in pieces])
    own_up = expert_up[0].astype(BF16)
    own_down = expert_down[0].astype(BF16)
    pairwise = count == 8
    if pairwise:
        order = jnp.arange(count, dtype=jnp.int32) ^ position
        beside, below, across = flip(attend_in, 1), flip(attend_in, 2), flip(attend_in, 4)
        side_up, side_down = flip(own_up, 1), flip(own_down, 1)
        got_rows, beside, below, across, side_up, side_down, own_up = together(
            swap(pieces, SEQ), beside, below, across, side_up, side_down, own_up
        )
        corner = flip(across, 2)
        row_blocks = [attend_in, beside]
        row_blocks += [part for block in (below, across, corner) for part in (block, flip(block, 1))]
    else:
        order = jnp.arange(count, dtype=jnp.int32)
        row_blocks = [lax.all_gather(attend_in, SEQ, axis=0, tiled=True)]
        got_rows = swap(pieces, SEQ)
        side_up, side_down = others(own_up, "in"), others(own_down, "in")
    documents = jnp.broadcast_to(
        got_rows[:, weight_rows, :row_count].reshape(length, 1), (length, LANES)
    )
    own_copies = jnp.broadcast_to(
        got_rows[None, :, :weight_rows], (groups, count, weight_rows, 3 * LANES + width)
    )
    all_copies = swap(own_copies, EXP)

    peer_up = others(own_up, "hi")
    *row_blocks, all_copies, peer_up, own_up, own_down, grad_slots_out = together(
        *row_blocks, all_copies, peer_up, own_up, own_down, to_slots(cotangent[0])
    )
    all_copies = jnp.swapaxes(all_copies, 0, 1)
    columns = all_copies[..., : 3 * LANES].reshape(width, 3 * LANES)
    output_full = all_copies[..., 3 * LANES :].reshape(width, width)
    grad_arrived = dispatch(grad_slots_out)
    peer_down = others(own_down, "hi")
    far_up = others(peer_up, "in")

    mixed_low, mixed_full, stat, pair = attend(
        active, order, row_blocks, columns, documents, row_count
    )

    def place_heads():
        index = np.arange(LANES)
        matrix = np.zeros((count, LANES, width), np.float32)
        for device in range(count):
            for slot in range(2):
                if used[device, slot]:
                    own = index[slot * HALF : (slot + 1) * HALF]
                    matrix[device, own, starts[device] + own] = 1.0
        return jnp.asarray(matrix, BF16)

    head_places = place_heads()

    def to_tokens(values):
        return swap(values.reshape(count, row_count, values.shape[1]), SEQ)

    mixed_low, grad_arrived, peer_down, far_up = together(
        mixed_low, grad_arrived, peer_down, far_up
    )
    far_down = others(peer_down, "in")
    mixed_pieces, projection_low, far_down = together(
        to_tokens(mixed_low), projection_low, far_down
    )
    projection_full = lax.all_gather(projection_low, ALL, axis=0, tiled=True)
    attend_out = jnp.einsum(
        "jtc,jcd->td", mixed_pieces, head_places, preferred_element_type=F32
    ).astype(BF16)
    branch = jnp.dot(attend_out, output_full, preferred_element_type=F32)
    middle = inputs + branch
    scale_second = lax.rsqrt(jnp.mean(middle * middle, axis=-1, keepdims=True) + EPSILON)
    normed_second = middle * scale_second
    expert_in = (normed_second * gain_second).astype(BF16)

    arrived = dispatch(to_slots(expert_in))
    ups, downs = (own_up, peer_up, side_up, far_up), (own_down, peer_down, side_down, far_down)
    grad_slots, actives, hiddens = expert_part(arrived, grad_arrived, ups, downs)
    returned_grad = send_back(grad_slots)

    blocks = list(zip(actives, hiddens, strict=True))
    down_far, up_far, down_peer, up_peer = unit_grads(
        grad_arrived, arrived, (blocks[3], blocks[1]), (BF16, F32)
    )
    (down_part,) = to_owners([down_far], "in")
    down_side, up_side, down_own, up_own = unit_grads(
        grad_arrived, arrived, (blocks[2], blocks[0]), (BF16, F32)
    )
    produced = produced_part(actives, downs)
    returned_grad, down_part, up_far, up_peer, projection_full, produced, down_side, up_own = (
        together(
            returned_grad, down_part, up_far, up_peer, projection_full, produced, down_side, up_own
        )
    )
    grad_expert_in = collect(returned_grad)
    (up_part,) = to_owners([up_far], "in")
    peers = lax.axis_size("hi")

    def hi_parts(value):
        return to_owners(list(value.astype(BF16).reshape(peers - 1, -1, width)), "hi")

    down_hi = hi_parts(add_all(down_peer, [down_part]))

    scaled_second = grad_expert_in * gain_second
    gain_second_part = jnp.sum(grad_expert_in * normed_second, axis=0)
    grad_middle = scale_second * (
        scaled_second
        - normed_second * jnp.mean(scaled_second * normed_second, axis=-1, keepdims=True)
    )
    residual_grad = upstream + grad_middle
    branch_grad = residual_grad.astype(BF16)
    grad_mixed = jnp.einsum(
        "td,ed->te", branch_grad, output_full, preferred_element_type=F32
    ).astype(BF16)

    sent_grad = jnp.stack([grad_mixed[:, s : s + LANES] for s in starts])
    sent_grad, *down_hi = together(sent_grad, *down_hi)
    row_grad = swap(sent_grad, SEQ).reshape(length, LANES)

    group = lax.axis_index(EXP)

    def group_rows(value):
        rows = value.reshape(count, groups, weight_rows, -1)
        own, *away = [
            lax.dynamic_index_in_dim(rows, lax.rem(group + step, groups), 1, keepdims=False)
            for step in range(groups)
        ]
        return own, away

    output_term = jnp.einsum("tc,te->ce", attend_out, branch_grad, preferred_element_type=F32)
    output_own, output_away = group_rows(output_term.astype(BF16))
    row_grad, produced, down_side, up_side, up_part, *output_away = together(
        row_grad, produced, down_side, up_side, up_part, *output_away
    )
    output_away = to_owners(output_away, "exp")
    (down_early,) = to_owners([down_side], "in")
    (up_early,) = to_owners([up_side], "in")
    up_hi = hi_parts(add_all(up_peer, [up_part]))
    returned = send_back(produced)
    grad_qkv, grad_lying = attend_back(
        active, order, pair, documents, stat, row_grad, mixed_full, row_count, scaling
    )
    grad_qkv, grad_lying, returned, down_early, up_early, *held = together(
        grad_qkv, grad_lying, returned, down_early, up_early, *up_hi, *output_away
    )
    up_hi, output_away = held[: len(up_hi)], held[len(up_hi) :]
    up_grad = add_all(up_own, [up_early, *up_hi])[None]
    down_grad = add_all(down_own, [down_early, *down_hi])[None]
    block_output = (middle + collect(returned)).astype(BF16)[None]

    column_own, column_away = group_rows(column_terms(row_blocks, grad_lying))
    dense_rows = jnp.concatenate(
        [
            add_all(column_own, to_owners(column_away, "exp")).astype(BF16),
            add_all(output_own, output_away).astype(BF16),
        ],
        axis=2,
    )
    if pairwise:
        lying_terms = [
            lax.dynamic_index_in_dim(dense_rows, position ^ bits, 0, keepdims=False)
            for bits in range(count)
        ]
        lying_terms[1:] = [flip(lying_terms[bits], bits) for bits in range(1, count)]
        grad_pieces, *lying_terms = together(to_tokens(grad_qkv), *lying_terms)
    else:
        grad_pieces, dense_rows = together(to_tokens(grad_qkv), dense_rows)
        lying_terms = list(swap(dense_rows, SEQ))
    projection_grad, output_grad, dense_square = dense_grads(order, lying_terms, starts)
    input_grad, gain_first_part = close_norm(
        grad_pieces, starts, projection_full, tokens[0], gain_first[None], residual_grad
    )
    input_grad, gain_first_part = input_grad[None], gain_first_part[0]
    local_square = jnp.sum(up_grad * up_grad) + jnp.sum(down_grad * down_grad)
    summed = spread_sum(
        jnp.concatenate(
            [gain_first_part, gain_second_part, dense_square[0] + local_square]
        )[None]
    )[0]
    gains_grad = summed[: 2 * width].reshape(2, width)
    grad_norm = jnp.sqrt(summed[2 * width] + jnp.sum(gains_grad * gains_grad))
    factor = jnp.minimum(1.0, CLIP / (grad_norm + 1e-06))
    (
        (projection_moment, projection_square, projection_new),
        (output_moment, output_square, output_new),
        (up_moment, up_square, up_new),
        (down_moment, down_square, down_new),
    ) = adam_all(
        factor,
        [
            (projection, projection_grad, projection_first, projection_second),
            (output_weight, output_grad, output_first, output_second),
            (expert_up, up_grad, up_first, up_second),
            (expert_down, down_grad, down_first, down_second),
        ],
        (RATE_MATRIX, RATE_OUTPUT, RATE_MATRIX, RATE_MATRIX),
        6,
    )
    gains_moment, gains_square, gains_new = adam_update(
        norm_gains, gains_grad, gains_first, gains_second, factor, RATE_GAIN, 0.0
    )
    return (
        block_output,
        input_grad,
        grad_norm,
        projection_grad,
        projection_moment,
        projection_square,
        projection_new,
        output_grad,
        output_moment,
        output_square,
        output_new,
        up_grad,
        up_moment,
        up_square,
        up_new,
        down_grad,
        down_moment,
        down_square,
        down_new,
        gains_grad,
        gains_moment,
        gains_square,
        gains_new,
    )


def solution(mesh):
    token = P("exp", SEQ, None)
    dense = P(ALL, None)
    expert = P("exp", SEQ, None)
    in_specs = (
        (token, token, P("exp", SEQ), token)
        + (dense, dense, expert, expert, P())
        + (dense,) * 4
        + (expert,) * 4
        + (P(), P())
    )
    out_specs = (token, token, P()) + (dense,) * 8 + (expert,) * 8 + (P(),) * 4
    rows, groups = mesh.devices.shape
    fine = Mesh(mesh.devices.reshape(rows // 4, 2, 2, groups), ALL)
    return jax.shard_map(body, mesh=fine, in_specs=in_specs, out_specs=out_specs, check_vma=False)
```

```python
import functools
import math

import jax
import jax.numpy as jnp
import numpy as np
from jax import lax
from jax.experimental import pallas as pl
from jax.experimental.pallas import tpu as pltpu
from jax.sharding import Mesh
from jax.sharding import PartitionSpec as P

HEADS = 12
CAP = 128
STEP = 10


EPSILON = 1e-05
CLIP = 1.0
BETA_ONE = 0.9
BETA_TWO = 0.99
ADAM_FLOOR = 1e-08
DECAY = 0.1
RATE_MATRIX = 0.04
RATE_OUTPUT = 0.1
RATE_GAIN = 0.5

SEQ = ("hi", "lo", "in")
EXP = ("exp",)
ALL = SEQ + EXP
TEAM = ("lo",)
SHARE = ("hi", "in")
LANES = 128
HALF = 64
FAR = -1e30
BF16 = jnp.bfloat16
F32 = jnp.float32
VMEM_LIMIT = 60 * 1024 * 1024


def head_plan(count):
    whole = math.lcm(HEADS, count)
    units, parts = whole // count, whole // HEADS
    first = np.zeros((count,), np.int64)
    active = np.zeros((count, 2, count), np.int32)
    for device in range(count):
        first[device] = min(units * device // parts, HEADS - 2)
        for unit in range(units * device, units * (device + 1)):
            slot = unit // parts - first[device]
            for block in range(count):
                turn = block % (2 * parts)
                if min(turn, 2 * parts - 1 - turn) == unit % parts:
                    active[device, slot, block] = 1
    return first, active


def three_parts(value):
    high = value.astype(BF16).astype(F32)
    middle = (value - high).astype(BF16).astype(F32)
    return high, middle, value - high - middle


def contract(left, right, left_axis, right_axis):
    return lax.dot_general(
        left, right, (((left_axis,), (right_axis,)), ((), ())), preferred_element_type=F32
    )


def slot_arrays(packed, documents, kind, slot):
    spare = HALF - HALF * slot
    lane = lax.broadcasted_iota(jnp.int32, packed.shape, 1)
    own = (lane < HALF) if slot == 0 else (lane >= HALF)
    place = (lane - spare).astype(F32)
    ours = place == documents
    first = (lane >= spare) & (lane < spare + 3)
    if kind == "query":
        extra = jnp.where(first & jnp.logical_not(ours), FAR, 0.0)
    elif kind == "key":
        extra = jnp.where(ours | ((lane >= spare + 3) & (lane < spare + 6)), 1.0, 0.0)
    else:
        extra = jnp.where(first, 1.0, 0.0)
    return jnp.where(own, packed, extra).astype(BF16)


def fill_slots(packed_of, documents_ref, wide_ref, kinds, place):
    documents = documents_ref[place, :].astype(F32)
    for number, kind in enumerate(kinds):
        packed = packed_of(kind).astype(F32)
        if kind == "query":
            packed = packed * 0.125
        for slot in range(2):
            column = (2 * number + slot) * LANES
            wide_ref[place, column : column + LANES] = slot_arrays(packed, documents, kind, slot)


def attend_kernel(active_ref, order_ref, *refs, block, chunk, held):
    row_refs = refs[:held]
    columns_ref, documents_ref = refs[held : held + 2]
    low_ref, full_ref, stat_ref, pair_ref, mixed_ref, wide_ref = refs[held + 2 :]
    at = pl.program_id(0)

    @pl.when(at == 0)
    def _():
        def fill(tokens, index):
            place = pl.ds(pl.multiple_of(order_ref[index] * block, block), block)
            packed = contract(tokens, columns_ref[...], 1, 0).astype(BF16)
            pair_ref[place, :] = packed[:, LANES:]
            parts = {
                kind: packed[:, part * LANES : (part + 1) * LANES]
                for part, kind in enumerate(("query", "key", "value"))
            }
            fill_slots(parts.get, documents_ref, wide_ref, tuple(parts), place)

        if held > 1:
            for index, row_ref in enumerate(row_refs):
                fill(row_ref[...], index)
        else:

            @pl.loop(0, pl.num_programs(0))
            def _(index):
                fill(row_refs[0][pl.ds(pl.multiple_of(index * block, block), block), :], index)

    rows = pl.ds(pl.multiple_of(at * block, block), block)
    lane = lax.broadcasted_iota(jnp.int32, (block, LANES), 1)
    last = lax.div(at * block, chunk)
    for slot in range(2):
        spare = HALF - HALF * slot
        own = (lane < HALF) if slot == 0 else (lane >= HALF)
        columns = slice(slot * LANES, (slot + 1) * LANES)

        @pl.when(active_ref[slot, at] != 0)
        def _():
            query = wide_ref[rows, columns]

            def step(index, carry, edge):
                top, weighted = carry
                place = pl.ds(pl.multiple_of(index * chunk, chunk), chunk)
                keys = wide_ref[place, 2 * LANES + slot * LANES : 3 * LANES + slot * LANES]
                values = wide_ref[place, 4 * LANES + slot * LANES : 5 * LANES + slot * LANES]
                scores = contract(query, keys, 1, 1)
                if edge:
                    key_at = index * chunk + lax.broadcasted_iota(jnp.int32, (block, chunk), 1)
                    query_at = at * block + lax.broadcasted_iota(jnp.int32, (block, chunk), 0)
                    scores = jnp.where(key_at <= query_at, scores, FAR)
                new_top = jnp.maximum(top, jnp.max(scores, axis=1, keepdims=True))
                weights = jnp.exp(scores - new_top).astype(BF16)
                weighted = weighted * jnp.exp(top - new_top) + contract(weights, values, 1, 0)
                return new_top, weighted

            carry = (jnp.full((block, 1), FAR, F32), jnp.zeros((block, LANES), F32))
            carry = lax.fori_loop(0, last, lambda index, state: step(index, state, False), carry)
            top, weighted = step(last, carry, True)
            total = weighted[:, spare : spare + 1]
            mixed_ref[slot] = jnp.where(own, weighted / total, 0.0)
            log_total = top + jnp.log(total)
            high, middle, small = three_parts(log_total)
            extra = jnp.where(lane == spare + 3, -high, 0.0)
            extra = jnp.where(lane == spare + 4, -middle, extra)
            extra = jnp.where(lane == spare + 5, -small, extra)
            stat_ref[:, columns] = (query.astype(F32) + extra).astype(BF16)

        @pl.when(active_ref[slot, at] == 0)
        def _():
            mixed_ref[slot] = jnp.zeros((block, LANES), F32)
            stat_ref[:, columns] = jnp.zeros((block, LANES), BF16)

    mixed = mixed_ref[0] + mixed_ref[1]
    full_ref[...] = mixed
    low_ref[...] = mixed.astype(BF16)


def attend_back_kernel(
    active_ref,
    order_ref,
    pair_ref,
    documents_ref,
    stat_ref,
    grad_ref,
    mixed_ref,
    out_ref,
    lying_ref,
    key_sum_ref,
    value_sum_ref,
    query_sum_ref,
    wide_ref,
    *,
    block,
    chunk,
    scaling,
):
    at = pl.program_id(0)
    rows = pl.ds(pl.multiple_of(at * block, block), block)
    lane = lax.broadcasted_iota(jnp.int32, (block, LANES), 1)
    last = lax.div(at * block, chunk)

    @pl.when(at == 0)
    def _():
        @pl.loop(0, pl.num_programs(0))
        def _(index):
            place = pl.ds(pl.multiple_of(index * block, block), block)
            parts = {"key": pair_ref[place, :LANES], "value": pair_ref[place, LANES:]}
            fill_slots(parts.get, documents_ref, wide_ref, tuple(parts), place)

        key_sum_ref[...] = jnp.zeros_like(key_sum_ref)
        value_sum_ref[...] = jnp.zeros_like(value_sum_ref)

    for slot in range(2):
        spare = HALF - HALF * slot
        own = (lane < HALF) if slot == 0 else (lane >= HALF)
        columns = slice(slot * LANES, (slot + 1) * LANES)
        query_sum_ref[slot] = jnp.zeros((block, LANES), F32)

        @pl.when(active_ref[slot, at] != 0)
        def _():
            query = stat_ref[:, columns]
            grad = grad_ref[...].astype(F32)
            delta = jnp.sum(jnp.where(own, grad * mixed_ref[...], 0.0), axis=1, keepdims=True)
            high, middle, small = three_parts(delta)
            extra = jnp.where(lane == spare, -high, 0.0)
            extra = jnp.where(lane == spare + 1, -middle, extra)
            extra = jnp.where(lane == spare + 2, -small, extra)
            grad_low = jnp.where(own, grad, extra).astype(BF16)

            def step(index, edge):
                place = pl.ds(pl.multiple_of(index * chunk, chunk), chunk)
                keys = wide_ref[place, slot * LANES : (slot + 1) * LANES]
                values = wide_ref[place, (2 + slot) * LANES : (3 + slot) * LANES]
                scores = contract(keys, query, 1, 1)
                if edge:
                    key_at = index * chunk + lax.broadcasted_iota(jnp.int32, (chunk, block), 0)
                    query_at = at * block + lax.broadcasted_iota(jnp.int32, (chunk, block), 1)
                    scores = jnp.where(key_at <= query_at, scores, FAR)
                weights = jnp.exp(scores)
                grad_weights = contract(values, grad_low, 1, 1)
                grad_scores = (weights * grad_weights).astype(BF16)
                value_sum_ref[slot, place, :] += contract(weights.astype(BF16), grad_low, 1, 0)
                key_sum_ref[slot, place, :] += contract(grad_scores, query, 1, 0)
                query_sum_ref[slot] += contract(grad_scores, keys, 0, 0)

            @pl.loop(0, last)
            def _(index):
                step(index, False)

            step(last, True)

    first_half = lane < HALF
    query_grad = jnp.where(first_half, query_sum_ref[0], query_sum_ref[1]) * scaling
    out_ref[rows, :LANES] = query_grad.astype(BF16)
    lying = pl.ds(pl.multiple_of(order_ref[at] * block, block), block)
    lying_ref[lying, :LANES] = query_grad.astype(BF16)

    @pl.when(at == pl.num_programs(0) - 1)
    def _():
        @pl.loop(0, pl.num_programs(0))
        def _(index):
            place = pl.ds(pl.multiple_of(index * block, block), block)
            key_grad = jnp.where(first_half, key_sum_ref[0, place, :], key_sum_ref[1, place, :])
            value_grad = jnp.where(
                first_half, value_sum_ref[0, place, :], value_sum_ref[1, place, :]
            )
            out_ref[place, LANES : 2 * LANES] = key_grad.astype(BF16)
            out_ref[place, 2 * LANES :] = value_grad.astype(BF16)
            lying = pl.ds(pl.multiple_of(order_ref[index] * block, block), block)
            lying_ref[lying, LANES : 2 * LANES] = key_grad.astype(BF16)
            lying_ref[lying, 2 * LANES :] = value_grad.astype(BF16)


def whole(value):
    return pl.BlockSpec(value.shape, lambda i, *unused: (0, 0), pipeline_mode=pl.Buffered(1))


SMALL = pl.CostEstimate(flops=1, bytes_accessed=1, transcendentals=0)


def attend(active, order, row_blocks, columns, documents, block):
    length = documents.shape[0]
    pair = jax.ShapeDtypeStruct((length, 2 * LANES), BF16)
    return pl.pallas_call(
        functools.partial(attend_kernel, block=block, chunk=2 * block, held=len(row_blocks)),
        grid_spec=pltpu.PrefetchScalarGridSpec(
            num_scalar_prefetch=2,
            grid=(length // block,),
            in_specs=[whole(value) for value in (*row_blocks, columns, documents)],
            out_specs=[
                pl.BlockSpec((block, LANES), lambda i, a, o: (i, 0)),
                pl.BlockSpec((block, LANES), lambda i, a, o: (i, 0)),
                pl.BlockSpec((block, 2 * LANES), lambda i, a, o: (i, 0)),
                whole(pair),
            ],
            scratch_shapes=[
                pltpu.VMEM((2, block, LANES), F32),
                pltpu.VMEM((length, 6 * LANES), BF16),
            ],
        ),
        out_shape=[
            jax.ShapeDtypeStruct((length, LANES), BF16),
            jax.ShapeDtypeStruct((length, LANES), F32),
            jax.ShapeDtypeStruct((length, 2 * LANES), BF16),
            pair,
        ],
        compiler_params=pltpu.CompilerParams(vmem_limit_bytes=VMEM_LIMIT),
        cost_estimate=SMALL,
    )(active, order, *row_blocks, columns, documents)


def attend_back(active, order, pair, documents, stat, grad, mixed, block, scaling):
    length = pair.shape[0]
    count = length // block
    return pl.pallas_call(
        functools.partial(attend_back_kernel, block=block, chunk=2 * block, scaling=scaling),
        grid_spec=pltpu.PrefetchScalarGridSpec(
            num_scalar_prefetch=2,
            grid=(count,),
            in_specs=[
                whole(pair),
                whole(documents),
                pl.BlockSpec((block, 2 * LANES), lambda i, a, o: (i, 0)),
                pl.BlockSpec((block, LANES), lambda i, a, o: (i, 0)),
                pl.BlockSpec((block, LANES), lambda i, a, o: (i, 0)),
            ],
            out_specs=[
                pl.BlockSpec(
                    (length, 3 * LANES), lambda i, a, o: (0, 0), pipeline_mode=pl.Buffered(1)
                )
            ]
            * 2,
            scratch_shapes=[
                pltpu.VMEM((2, length, LANES), F32),
                pltpu.VMEM((2, length, LANES), F32),
                pltpu.VMEM((2, block, LANES), F32),
                pltpu.VMEM((length, 4 * LANES), BF16),
            ],
        ),
        out_shape=[jax.ShapeDtypeStruct((length, 3 * LANES), BF16)] * 2,
        compiler_params=pltpu.CompilerParams(vmem_limit_bytes=VMEM_LIMIT),
        cost_estimate=SMALL,
    )(active, order, pair, documents, stat, grad, mixed)


def expert_kernel(arrived_ref, grad_ref, *refs, count):
    up_refs, down_refs = refs[:count], refs[count : 2 * count]
    total_ref = refs[2 * count]
    active_refs, hidden_refs = refs[2 * count + 1 : 3 * count + 1], refs[3 * count + 1 :]
    arrived, grad_arrived = arrived_ref[...], grad_ref[...]
    scale = math.sqrt(2.0 / math.pi)
    total = jnp.zeros(total_ref.shape, F32)
    for up_ref, down_ref, active_ref, hidden_ref in zip(
        up_refs, down_refs, active_refs, hidden_refs, strict=True
    ):
        up = up_ref[...]
        hidden = contract(arrived, up, 1, 1)
        squared = hidden * hidden
        bend = jnp.tanh(scale * hidden * (1.0 + 0.044715 * squared))
        half = 0.5 + 0.5 * bend
        active_ref[...] = (hidden * half).astype(BF16)
        slope = half + (0.5 * scale) * hidden * (1.0 - bend * bend) * (1.0 + 3 * 0.044715 * squared)
        grad_hidden = (slope * contract(grad_arrived, down_ref[...], 1, 1)).astype(BF16)
        hidden_ref[...] = grad_hidden
        total = total + contract(grad_hidden, up, 1, 0)
    total_ref[...] = total.astype(BF16)


def rows_spec(value, block):
    return pl.BlockSpec((block, value.shape[1]), lambda i: (i, 0))


def expert_part(arrived, grad_arrived, ups, downs):
    slots, width = arrived.shape
    block = 256
    units = [jax.ShapeDtypeStruct((slots, up.shape[0]), BF16) for up in ups]
    outs = [jax.ShapeDtypeStruct((slots, width), BF16), *units, *units]
    total, *parts = pl.pallas_call(
        functools.partial(expert_kernel, count=len(ups)),
        grid=(slots // block,),
        in_specs=[rows_spec(arrived, block), rows_spec(grad_arrived, block)]
        + [whole(value) for value in (*ups, *downs)],
        out_specs=[rows_spec(out, block) for out in outs],
        out_shape=outs,
        compiler_params=pltpu.CompilerParams(vmem_limit_bytes=VMEM_LIMIT),
        cost_estimate=SMALL,
    )(arrived, grad_arrived, *ups, *downs)
    return total, parts[: len(ups)], parts[len(ups) :]


def produced_kernel(*refs, count):
    total = contract(refs[0][...], refs[count][...], 1, 0)
    for index in range(1, count):
        total = total + contract(refs[index][...], refs[count + index][...], 1, 0)
    refs[-1][...] = total.astype(BF16)


def produced_part(actives, downs):
    slots, width = actives[0].shape[0], downs[0].shape[1]
    block = 256
    out = jax.ShapeDtypeStruct((slots, width), BF16)
    return pl.pallas_call(
        functools.partial(produced_kernel, count=len(actives)),
        grid=(slots // block,),
        in_specs=[rows_spec(value, block) for value in actives] + [whole(down) for down in downs],
        out_specs=rows_spec(out, block),
        out_shape=out,
        compiler_params=pltpu.CompilerParams(vmem_limit_bytes=VMEM_LIMIT),
        cost_estimate=SMALL,
    )(*actives, *downs)


def unit_kernel(grad_ref, arrived_ref, *refs, count):
    for index in range(count):
        active_ref, hidden_ref = refs[2 * index : 2 * index + 2]
        down_ref, up_ref = refs[2 * count + 2 * index : 2 * count + 2 * index + 2]
        down_ref[...] = contract(active_ref[...], grad_ref[...], 0, 0).astype(down_ref.dtype)
        up_ref[...] = contract(hidden_ref[...], arrived_ref[...], 0, 0).astype(up_ref.dtype)


def unit_grads(grad_arrived, arrived, blocks, kinds):
    slots, width = arrived.shape
    block = 256
    right = pl.BlockSpec((slots, block), lambda i: (0, i))
    outs = [
        jax.ShapeDtypeStruct((active.shape[1], width), kind)
        for (active, unused), kind in zip(blocks, kinds, strict=True)
        for part in range(2)
    ]
    flat = [value for pair in blocks for value in pair]
    return pl.pallas_call(
        functools.partial(unit_kernel, count=len(blocks)),
        grid=(width // block,),
        in_specs=[right, right] + [whole(value) for value in flat],
        out_specs=[pl.BlockSpec((out.shape[0], block), lambda i: (0, i)) for out in outs],
        out_shape=outs,
        compiler_params=pltpu.CompilerParams(vmem_limit_bytes=VMEM_LIMIT),
        cost_estimate=SMALL,
    )(grad_arrived, arrived, *flat)


def column_kernel(*refs, held):
    row_refs = refs[:held]
    lying_ref, out_ref = refs[held:]
    start, total = 0, None
    for row_ref in row_refs:
        rows = row_ref.shape[0]
        part = contract(row_ref[...], lying_ref[start : start + rows, :], 0, 0)
        total = part if total is None else total + part
        start += rows
    out_ref[...] = total.astype(BF16)


def column_terms(row_blocks, grad_lying):
    width = row_blocks[0].shape[1]
    block = 256
    out = jax.ShapeDtypeStruct((width, 3 * LANES), BF16)
    return pl.pallas_call(
        functools.partial(column_kernel, held=len(row_blocks)),
        grid=(width // block,),
        in_specs=[
            pl.BlockSpec((value.shape[0], block), lambda i: (0, i)) for value in row_blocks
        ]
        + [whole(grad_lying)],
        out_specs=rows_spec(out, block),
        out_shape=out,
        compiler_params=pltpu.CompilerParams(vmem_limit_bytes=VMEM_LIMIT),
        cost_estimate=SMALL,
    )(*row_blocks, grad_lying)


def close_kernel(
    pieces_ref, matrix_ref, tokens_ref, gain_ref, residual_ref, out_ref, part_ref, sum_ref, *, starts
):
    width = tokens_ref.shape[1]
    lane = lax.broadcasted_iota(jnp.int32, (tokens_ref.shape[0], LANES), 1)
    sum_ref[...] = jnp.zeros_like(sum_ref)
    for device, start in enumerate(starts):
        for part in range(3):
            piece = pieces_ref[device, :, part * LANES : (part + 1) * LANES].astype(F32)
            column = part * width + start
            if column % LANES == 0:
                sum_ref[:, column : column + LANES] += piece
            else:
                turned = pltpu.roll(piece, HALF, 1)
                low, high = column - HALF, column + HALF
                sum_ref[:, low : low + LANES] += jnp.where(lane >= HALF, turned, 0.0)
                sum_ref[:, high : high + LANES] += jnp.where(lane < HALF, turned, 0.0)
    grad = contract(sum_ref[...].astype(BF16), matrix_ref[...], 1, 1)
    inputs = tokens_ref[...].astype(F32)
    scale = lax.rsqrt(jnp.mean(inputs * inputs, axis=-1, keepdims=True) + EPSILON)
    normed = inputs * scale
    scaled = grad * gain_ref[...]
    mean = jnp.mean(scaled * normed, axis=-1, keepdims=True)
    out_ref[...] = residual_ref[...] + scale * (scaled - normed * mean)
    part_ref[...] = jnp.sum(grad * normed, axis=0, keepdims=True)


def close_norm(pieces, starts, matrix, tokens, gain, residual):
    rows, width = tokens.shape
    outs = [
        jax.ShapeDtypeStruct((rows, width), F32),
        jax.ShapeDtypeStruct((1, width), F32),
    ]
    return pl.pallas_call(
        functools.partial(close_kernel, starts=starts),
        in_specs=[pl.BlockSpec(memory_space=pltpu.VMEM)] * 5,
        out_specs=[pl.BlockSpec(memory_space=pltpu.VMEM)] * 2,
        out_shape=outs,
        scratch_shapes=[pltpu.VMEM((rows, 3 * width), F32)],
        compiler_params=pltpu.CompilerParams(vmem_limit_bytes=VMEM_LIMIT),
        cost_estimate=SMALL,
    )(pieces, matrix, tokens, gain, residual)


def dense_kernel(order_ref, *refs, starts):
    count = len(starts)
    term_refs = refs[:count]
    columns_ref, output_ref, square_ref, terms_ref = refs[count:]
    width = output_ref.shape[1]
    for index, term_ref in enumerate(term_refs):
        terms_ref[order_ref[index]] = term_ref[...].astype(F32)
    columns_ref[...] = jnp.zeros_like(columns_ref)
    lane = lax.broadcasted_iota(jnp.int32, (columns_ref.shape[0], LANES), 1)
    output = jnp.zeros(output_ref.shape, F32)
    for device, start in enumerate(starts):
        output = output + terms_ref[device, :, 3 * LANES :]
        for part in range(3):
            piece = terms_ref[device, :, part * LANES : (part + 1) * LANES]
            column = part * width + start
            if column % LANES == 0:
                columns_ref[:, column : column + LANES] += piece
            else:
                turned = pltpu.roll(piece, HALF, 1)
                low, high = column - HALF, column + HALF
                columns_ref[:, low : low + LANES] += jnp.where(lane >= HALF, turned, 0.0)
                columns_ref[:, high : high + LANES] += jnp.where(lane < HALF, turned, 0.0)
    output_ref[...] = output
    columns = columns_ref[...]
    square_ref[...] = jnp.zeros_like(square_ref) + (
        jnp.sum(columns * columns) + jnp.sum(output * output)
    )


def dense_grads(order, terms, starts):
    rows, lanes = terms[0].shape
    width = lanes - 3 * LANES
    outs = [jax.ShapeDtypeStruct((rows, columns), F32) for columns in (3 * width, width)]
    outs.append(jax.ShapeDtypeStruct((1, LANES), F32))
    return pl.pallas_call(
        functools.partial(dense_kernel, starts=starts),
        in_specs=[pl.BlockSpec(memory_space=pltpu.SMEM)]
        + [pl.BlockSpec(memory_space=pltpu.VMEM)] * len(terms),
        out_specs=[pl.BlockSpec(memory_space=pltpu.VMEM)] * 3,
        out_shape=outs,
        scratch_shapes=[pltpu.VMEM((len(terms), rows, lanes), F32)],
        compiler_params=pltpu.CompilerParams(vmem_limit_bytes=VMEM_LIMIT),
        cost_estimate=SMALL,
    )(order, *terms)


def adam_update(weight, grad, first, second, factor, rate, decay):
    clipped = grad * factor
    first_new = BETA_ONE * first + (1.0 - BETA_ONE) * clipped
    second_new = BETA_TWO * second + (1.0 - BETA_TWO) * clipped * clipped
    first_hat = first_new / (1.0 - BETA_ONE**STEP)
    second_hat = second_new / (1.0 - BETA_TWO**STEP)
    weight_new = weight - rate * (first_hat / (jnp.sqrt(second_hat) + ADAM_FLOOR) + decay * weight)
    return (first_new, second_new, weight_new)


def together(*values):
    return lax.optimization_barrier(values)


def swap(value, axes):
    return lax.all_to_all(value, axes, split_axis=0, concat_axis=0, tiled=True)


def adam_kernel(factor_ref, *refs, rates):
    count = len(rates)
    factor = factor_ref[0]
    for index, rate in enumerate(rates):
        weight, grad, first, second = [ref[...] for ref in refs[4 * index : 4 * index + 4]]
        outs = refs[4 * count + 3 * index : 4 * count + 3 * index + 3]
        for out, value in zip(
            outs, adam_update(weight, grad, first, second, factor, rate, DECAY), strict=True
        ):
            out[...] = value


def adam_all(factor, leaves, rates, steps):
    flat = [value.reshape(value.shape[-2:]) for leaf in leaves for value in leaf]

    def spec(value):
        rows, columns = value.shape
        if rows % (8 * steps) == 0:
            return pl.BlockSpec((rows // steps, columns), lambda i: (i, 0))
        lanes = columns // steps
        return pl.BlockSpec((rows, lanes), lambda i: (0, i))

    shapes = [jax.ShapeDtypeStruct(value.shape, F32) for value in flat[::4] for _ in range(3)]
    outs = pl.pallas_call(
        functools.partial(adam_kernel, rates=rates),
        grid=(steps,),
        in_specs=[pl.BlockSpec(memory_space=pltpu.SMEM)] + [spec(value) for value in flat],
        out_specs=[spec(shape) for shape in shapes],
        out_shape=shapes,
        compiler_params=pltpu.CompilerParams(vmem_limit_bytes=VMEM_LIMIT),
        cost_estimate=pl.CostEstimate(
            flops=20 * sum(value.size for value in flat[::4]),
            bytes_accessed=28 * sum(value.size for value in flat[::4]),
            transcendentals=0,
        ),
    )(factor.reshape(1), *flat)
    return [
        [out.reshape(leaf[0].shape) for out in outs[3 * index : 3 * index + 3]]
        for index, leaf in enumerate(leaves)
    ]


def flip(value, bits):
    count = lax.axis_size(SEQ)
    return lax.ppermute(value, SEQ, [(index, index ^ bits) for index in range(count)])


def others(value, axis):
    size = lax.axis_size(axis)
    parts = [
        lax.ppermute(value, axis, [((i + step) % size, i) for i in range(size)])
        for step in range(1, size)
    ]
    return parts[0] if size == 2 else jnp.concatenate(parts, axis=0)


def to_owners(blocks, axis):
    size = lax.axis_size(axis)
    return [
        lax.ppermute(block, axis, [(i, (i + step) % size) for i in range(size)])
        for step, block in enumerate(blocks, 1)
    ]


def add_all(own, parts):
    return functools.reduce(lambda total, part: total + part.astype(F32), parts, own.astype(F32))


def spread_sum(value):
    count = lax.axis_size(ALL)
    return jnp.sum(swap(jnp.broadcast_to(value[None], (count, *value.shape)), ALL), axis=0)


def body(
    tokens,
    cotangent,
    segment_ids,
    expert_ids,
    projection,
    output_weight,
    expert_up,
    expert_down,
    norm_gains,
    projection_first,
    projection_second,
    output_first,
    output_second,
    up_first,
    up_second,
    down_first,
    down_second,
    gains_first,
    gains_second,
):
    inputs = tokens[0].astype(F32)
    upstream = cotangent[0].astype(F32)
    row_count = inputs.shape[0]
    width = inputs.shape[1]
    head_size = width // HEADS
    scaling = head_size ** (-0.5)
    count = lax.axis_size(SEQ)
    groups = lax.axis_size("exp")
    team = lax.axis_size(TEAM)
    position = lax.axis_index(SEQ)
    length = count * row_count
    weight_rows = projection.shape[0]
    first_heads, active_table = head_plan(count)
    starts = [int(head) * head_size for head in first_heads]
    active = lax.dynamic_index_in_dim(jnp.asarray(active_table), position, 0, keepdims=False)
    gain_first = norm_gains[0]
    gain_second = norm_gains[1]
    used = active_table.any(axis=2)

    scale_first = lax.rsqrt(jnp.mean(inputs * inputs, axis=-1, keepdims=True) + EPSILON)
    normed_first = inputs * scale_first
    attend_in = (normed_first * gain_first).astype(BF16)
    slots = groups * CAP
    chosen = expert_ids[0, :, 0]
    one_hot = (chosen[:, None] == jnp.arange(groups, dtype=jnp.int32)[None, :]).astype(jnp.int32)
    rank = jnp.sum(jnp.cumsum(one_hot, axis=0) * one_hot, axis=1) - 1
    target = chosen * CAP + rank
    placing = (target[:, None] == jnp.arange(slots, dtype=jnp.int32)[None, :]).astype(BF16)

    def to_slots(values):
        outgoing = jnp.einsum("ts,td->sd", placing, values, preferred_element_type=F32)
        return outgoing.astype(BF16)

    def dispatch(outgoing):
        outgoing = jnp.broadcast_to(
            outgoing.reshape(1, groups, CAP, width), (team, groups, CAP, width)
        )
        return swap(outgoing.reshape(team * groups, CAP, width), TEAM + EXP).reshape(
            team * slots, width
        )

    def send_back(values):
        return swap(values.reshape(team * groups, CAP, width), TEAM + EXP).reshape(
            team, slots, width
        )

    def collect(returned):
        return jnp.einsum("ts,jsd->td", placing, returned, preferred_element_type=F32)

    projection_low = projection.astype(BF16)
    sent_rows = weight_rows + 8
    own_documents = jnp.zeros((8, 3 * LANES + width), BF16)
    own_documents = own_documents.at[0, :row_count].set(segment_ids[0].astype(BF16))
    output_low = output_weight.astype(BF16)
    pieces = [
        jnp.concatenate(
            [projection_low[:, k * width + s : k * width + s + LANES] for k in range(3)]
            + [output_low],
            axis=1,
        )
        for s in starts
    ]
    pieces = jnp.stack([jnp.concatenate([piece, own_documents], axis=0) for piece in pieces])
    own_up = expert_up[0].astype(BF16)
    own_down = expert_down[0].astype(BF16)
    pairwise = count == 8
    if pairwise:
        order = jnp.arange(count, dtype=jnp.int32) ^ position
        beside, below, across = flip(attend_in, 1), flip(attend_in, 2), flip(attend_in, 4)
        got_rows, beside, below, across, own_up = together(
            swap(pieces, SEQ), beside, below, across, own_up
        )
        corner = flip(across, 2)
        row_blocks = [attend_in, beside]
        row_blocks += [part for block in (below, across, corner) for part in (block, flip(block, 1))]
    else:
        order = jnp.arange(count, dtype=jnp.int32)
        row_blocks = [lax.all_gather(attend_in, SEQ, axis=0, tiled=True)]
        got_rows = swap(pieces, SEQ)
    documents = jnp.broadcast_to(
        got_rows[:, weight_rows, :row_count].reshape(length, 1), (length, LANES)
    )
    own_copies = jnp.broadcast_to(
        got_rows[None, :, :weight_rows], (groups, count, weight_rows, 3 * LANES + width)
    )
    all_copies = swap(own_copies, EXP)

    peer_up = others(own_up, "hi")
    *row_blocks, all_copies, peer_up, own_up, own_down, grad_slots_out = together(
        *row_blocks, all_copies, peer_up, own_up, own_down, to_slots(cotangent[0])
    )
    all_copies = jnp.swapaxes(all_copies, 0, 1)
    columns = all_copies[..., : 3 * LANES].reshape(width, 3 * LANES)
    output_full = all_copies[..., 3 * LANES :].reshape(width, width)
    grad_arrived = dispatch(grad_slots_out)
    peer_down = others(own_down, "hi")
    side_up = others(own_up, "in")
    far_up = others(peer_up, "in")

    mixed_low, mixed_full, stat, pair = attend(
        active, order, row_blocks, columns, documents, row_count
    )

    def place_heads():
        index = np.arange(LANES)
        matrix = np.zeros((count, LANES, width), np.float32)
        for device in range(count):
            for slot in range(2):
                if used[device, slot]:
                    own = index[slot * HALF : (slot + 1) * HALF]
                    matrix[device, own, starts[device] + own] = 1.0
        return jnp.asarray(matrix, BF16)

    head_places = place_heads()

    def to_tokens(values):
        return swap(values.reshape(count, row_count, values.shape[1]), SEQ)

    mixed_low, grad_arrived, peer_down, side_up, far_up, own_down = together(
        mixed_low, grad_arrived, peer_down, side_up, far_up, own_down
    )
    side_down = others(own_down, "in")
    far_down = others(peer_down, "in")
    mixed_pieces, projection_low, far_down, side_down = together(
        to_tokens(mixed_low), projection_low, far_down, side_down
    )
    projection_full = lax.all_gather(projection_low, ALL, axis=0, tiled=True)
    attend_out = jnp.einsum(
        "jtc,jcd->td", mixed_pieces, head_places, preferred_element_type=F32
    ).astype(BF16)
    branch = jnp.dot(attend_out, output_full, preferred_element_type=F32)
    middle = inputs + branch
    scale_second = lax.rsqrt(jnp.mean(middle * middle, axis=-1, keepdims=True) + EPSILON)
    normed_second = middle * scale_second
    expert_in = (normed_second * gain_second).astype(BF16)

    arrived = dispatch(to_slots(expert_in))
    ups, downs = (own_up, peer_up, side_up, far_up), (own_down, peer_down, side_down, far_down)
    grad_slots, actives, hiddens = expert_part(arrived, grad_arrived, ups, downs)
    returned_grad = send_back(grad_slots)

    blocks = list(zip(actives, hiddens, strict=True))
    down_far, up_far, down_peer, up_peer = unit_grads(
        grad_arrived, arrived, (blocks[3], blocks[1]), (BF16, F32)
    )
    (down_part,) = to_owners([down_far], "in")
    down_side, up_side, down_own, up_own = unit_grads(
        grad_arrived, arrived, (blocks[2], blocks[0]), (BF16, F32)
    )
    produced = produced_part(actives, downs)
    returned_grad, down_part, up_far, up_peer, projection_full, produced, down_side, up_own = (
        together(
            returned_grad, down_part, up_far, up_peer, projection_full, produced, down_side, up_own
        )
    )
    grad_expert_in = collect(returned_grad)
    (up_part,) = to_owners([up_far], "in")
    peers = lax.axis_size("hi")

    def hi_parts(value):
        return to_owners(list(value.astype(BF16).reshape(peers - 1, -1, width)), "hi")

    down_hi = hi_parts(add_all(down_peer, [down_part]))

    scaled_second = grad_expert_in * gain_second
    gain_second_part = jnp.sum(grad_expert_in * normed_second, axis=0)
    grad_middle = scale_second * (
        scaled_second
        - normed_second * jnp.mean(scaled_second * normed_second, axis=-1, keepdims=True)
    )
    residual_grad = upstream + grad_middle
    branch_grad = residual_grad.astype(BF16)
    grad_mixed = jnp.einsum(
        "td,ed->te", branch_grad, output_full, preferred_element_type=F32
    ).astype(BF16)

    sent_grad = jnp.stack([grad_mixed[:, s : s + LANES] for s in starts])
    row_grad = swap(sent_grad, SEQ).reshape(length, LANES)

    group = lax.axis_index(EXP)

    def group_rows(value):
        rows = value.reshape(count, groups, weight_rows, -1)
        own, *away = [
            lax.dynamic_index_in_dim(rows, lax.rem(group + step, groups), 1, keepdims=False)
            for step in range(groups)
        ]
        return own, away

    output_term = jnp.einsum("tc,te->ce", attend_out, branch_grad, preferred_element_type=F32)
    output_own, output_away = group_rows(output_term.astype(BF16))
    row_grad, produced, down_side, up_side, up_part, *output_away = together(
        row_grad, produced, down_side, up_side, up_part, *output_away
    )
    output_away = to_owners(output_away, "exp")
    (down_early,) = to_owners([down_side], "in")
    up_hi = hi_parts(add_all(up_peer, [up_part]))
    returned = send_back(produced)
    grad_qkv, grad_lying = attend_back(
        active, order, pair, documents, stat, row_grad, mixed_full, row_count, scaling
    )
    grad_qkv, grad_lying, returned, down_early, up_side, *held = together(
        grad_qkv, grad_lying, returned, down_early, up_side, *down_hi, *output_away
    )
    down_hi, output_away = held[: len(down_hi)], held[len(down_hi) :]
    (up_early,) = to_owners([up_side], "in")
    down_grad = add_all(down_own, [down_early, *down_hi])[None]
    block_output = (middle + collect(returned)).astype(BF16)[None]

    column_own, column_away = group_rows(column_terms(row_blocks, grad_lying))
    dense_rows = jnp.concatenate(
        [
            add_all(column_own, to_owners(column_away, "exp")).astype(BF16),
            add_all(output_own, output_away).astype(BF16),
        ],
        axis=2,
    )
    if pairwise:
        lying_terms = [
            lax.dynamic_index_in_dim(dense_rows, position ^ bits, 0, keepdims=False)
            for bits in range(count)
        ]
        lying_terms[1:] = [flip(lying_terms[bits], bits) for bits in range(1, count)]
        grad_pieces, *lying_terms = together(to_tokens(grad_qkv), *lying_terms)
    else:
        grad_pieces, dense_rows = together(to_tokens(grad_qkv), dense_rows)
        lying_terms = list(swap(dense_rows, SEQ))
    grad_pieces, up_early, *up_hi = together(grad_pieces, up_early, *up_hi)
    up_grad = add_all(up_own, [up_early, *up_hi])[None]
    projection_grad, output_grad, dense_square = dense_grads(order, lying_terms, starts)
    input_grad, gain_first_part = close_norm(
        grad_pieces, starts, projection_full, tokens[0], gain_first[None], residual_grad
    )
    input_grad, gain_first_part = input_grad[None], gain_first_part[0]
    local_square = jnp.sum(up_grad * up_grad) + jnp.sum(down_grad * down_grad)
    summed = spread_sum(
        jnp.concatenate(
            [gain_first_part, gain_second_part, dense_square[0] + local_square]
        )[None]
    )[0]
    gains_grad = summed[: 2 * width].reshape(2, width)
    grad_norm = jnp.sqrt(summed[2 * width] + jnp.sum(gains_grad * gains_grad))
    factor = jnp.minimum(1.0, CLIP / (grad_norm + 1e-06))
    (
        (projection_moment, projection_square, projection_new),
        (output_moment, output_square, output_new),
        (up_moment, up_square, up_new),
        (down_moment, down_square, down_new),
    ) = adam_all(
        factor,
        [
            (projection, projection_grad, projection_first, projection_second),
            (output_weight, output_grad, output_first, output_second),
            (expert_up, up_grad, up_first, up_second),
            (expert_down, down_grad, down_first, down_second),
        ],
        (RATE_MATRIX, RATE_OUTPUT, RATE_MATRIX, RATE_MATRIX),
        6,
    )
    gains_moment, gains_square, gains_new = adam_update(
        norm_gains, gains_grad, gains_first, gains_second, factor, RATE_GAIN, 0.0
    )
    return (
        block_output,
        input_grad,
        grad_norm,
        projection_grad,
        projection_moment,
        projection_square,
        projection_new,
        output_grad,
        output_moment,
        output_square,
        output_new,
        up_grad,
        up_moment,
        up_square,
        up_new,
        down_grad,
        down_moment,
        down_square,
        down_new,
        gains_grad,
        gains_moment,
        gains_square,
        gains_new,
    )


def solution(mesh):
    token = P("exp", SEQ, None)
    dense = P(ALL, None)
    expert = P("exp", SEQ, None)
    in_specs = (
        (token, token, P("exp", SEQ), token)
        + (dense, dense, expert, expert, P())
        + (dense,) * 4
        + (expert,) * 4
        + (P(), P())
    )
    out_specs = (token, token, P()) + (dense,) * 8 + (expert,) * 8 + (P(),) * 4
    rows, groups = mesh.devices.shape
    fine = Mesh(mesh.devices.reshape(rows // 4, 2, 2, groups), ALL)
    return jax.shard_map(body, mesh=fine, in_specs=in_specs, out_specs=out_specs, check_vma=False)
```

```python
import functools
import math

import jax
import jax.numpy as jnp
import numpy as np
from jax import lax
from jax.experimental import pallas as pl
from jax.experimental.pallas import tpu as pltpu
from jax.sharding import Mesh
from jax.sharding import PartitionSpec as P

HEADS = 12
CAP = 128
STEP = 10


EPSILON = 1e-05
CLIP = 1.0
BETA_ONE = 0.9
BETA_TWO = 0.99
ADAM_FLOOR = 1e-08
DECAY = 0.1
RATE_MATRIX = 0.04
RATE_OUTPUT = 0.1
RATE_GAIN = 0.5

SEQ = ("hi", "lo", "in")
EXP = ("exp",)
ALL = SEQ + EXP
TEAM = ("lo",)
SHARE = ("hi", "in")
LANES = 128
HALF = 64
FAR = -1e30
BF16 = jnp.bfloat16
F32 = jnp.float32
VMEM_LIMIT = 60 * 1024 * 1024


def head_plan(count):
    whole = math.lcm(HEADS, count)
    units, parts = whole // count, whole // HEADS
    first = np.zeros((count,), np.int64)
    active = np.zeros((count, 2, count), np.int32)
    for device in range(count):
        first[device] = min(units * device // parts, HEADS - 2)
        for unit in range(units * device, units * (device + 1)):
            slot = unit // parts - first[device]
            for block in range(count):
                turn = block % (2 * parts)
                if min(turn, 2 * parts - 1 - turn) == unit % parts:
                    active[device, slot, block] = 1
    return first, active


def three_parts(value):
    high = value.astype(BF16).astype(F32)
    middle = (value - high).astype(BF16).astype(F32)
    return high, middle, value - high - middle


def contract(left, right, left_axis, right_axis):
    return lax.dot_general(
        left, right, (((left_axis,), (right_axis,)), ((), ())), preferred_element_type=F32
    )


def slot_arrays(packed, documents, kind, slot):
    spare = HALF - HALF * slot
    lane = lax.broadcasted_iota(jnp.int32, packed.shape, 1)
    own = (lane < HALF) if slot == 0 else (lane >= HALF)
    place = (lane - spare).astype(F32)
    ours = place == documents
    first = (lane >= spare) & (lane < spare + 3)
    if kind == "query":
        extra = jnp.where(first & jnp.logical_not(ours), FAR, 0.0)
    elif kind == "key":
        extra = jnp.where(ours | ((lane >= spare + 3) & (lane < spare + 6)), 1.0, 0.0)
    else:
        extra = jnp.where(first, 1.0, 0.0)
    return jnp.where(own, packed, extra).astype(BF16)


def fill_slots(packed_of, documents_ref, wide_ref, kinds, place):
    documents = documents_ref[place, :].astype(F32)
    for number, kind in enumerate(kinds):
        packed = packed_of(kind).astype(F32)
        if kind == "query":
            packed = packed * 0.125
        for slot in range(2):
            column = (2 * number + slot) * LANES
            wide_ref[place, column : column + LANES] = slot_arrays(packed, documents, kind, slot)


def attend_kernel(active_ref, order_ref, *refs, block, chunk, held):
    row_refs = refs[:held]
    columns_ref, documents_ref = refs[held : held + 2]
    low_ref, full_ref, stat_ref, pair_ref, mixed_ref, wide_ref = refs[held + 2 :]
    at = pl.program_id(0)

    @pl.when(at == 0)
    def _():
        def fill(tokens, index):
            place = pl.ds(pl.multiple_of(order_ref[index] * block, block), block)
            packed = contract(tokens, columns_ref[...], 1, 0).astype(BF16)
            pair_ref[place, :] = packed[:, LANES:]
            parts = {
                kind: packed[:, part * LANES : (part + 1) * LANES]
                for part, kind in enumerate(("query", "key", "value"))
            }
            fill_slots(parts.get, documents_ref, wide_ref, tuple(parts), place)

        if held > 1:
            for index, row_ref in enumerate(row_refs):
                fill(row_ref[...], index)
        else:

            @pl.loop(0, pl.num_programs(0))
            def _(index):
                fill(row_refs[0][pl.ds(pl.multiple_of(index * block, block), block), :], index)

    rows = pl.ds(pl.multiple_of(at * block, block), block)
    lane = lax.broadcasted_iota(jnp.int32, (block, LANES), 1)
    last = lax.div(at * block, chunk)
    for slot in range(2):
        spare = HALF - HALF * slot
        own = (lane < HALF) if slot == 0 else (lane >= HALF)
        columns = slice(slot * LANES, (slot + 1) * LANES)

        @pl.when(active_ref[slot, at] != 0)
        def _():
            query = wide_ref[rows, columns]

            def step(index, carry, edge):
                top, weighted = carry
                place = pl.ds(pl.multiple_of(index * chunk, chunk), chunk)
                keys = wide_ref[place, 2 * LANES + slot * LANES : 3 * LANES + slot * LANES]
                values = wide_ref[place, 4 * LANES + slot * LANES : 5 * LANES + slot * LANES]
                scores = contract(query, keys, 1, 1)
                if edge:
                    key_at = index * chunk + lax.broadcasted_iota(jnp.int32, (block, chunk), 1)
                    query_at = at * block + lax.broadcasted_iota(jnp.int32, (block, chunk), 0)
                    scores = jnp.where(key_at <= query_at, scores, FAR)
                new_top = jnp.maximum(top, jnp.max(scores, axis=1, keepdims=True))
                weights = jnp.exp(scores - new_top).astype(BF16)
                weighted = weighted * jnp.exp(top - new_top) + contract(weights, values, 1, 0)
                return new_top, weighted

            carry = (jnp.full((block, 1), FAR, F32), jnp.zeros((block, LANES), F32))
            carry = lax.fori_loop(0, last, lambda index, state: step(index, state, False), carry)
            top, weighted = step(last, carry, True)
            total = weighted[:, spare : spare + 1]
            mixed_ref[slot] = jnp.where(own, weighted / total, 0.0)
            log_total = top + jnp.log(total)
            high, middle, small = three_parts(log_total)
            extra = jnp.where(lane == spare + 3, -high, 0.0)
            extra = jnp.where(lane == spare + 4, -middle, extra)
            extra = jnp.where(lane == spare + 5, -small, extra)
            stat_ref[:, columns] = (query.astype(F32) + extra).astype(BF16)

        @pl.when(active_ref[slot, at] == 0)
        def _():
            mixed_ref[slot] = jnp.zeros((block, LANES), F32)
            stat_ref[:, columns] = jnp.zeros((block, LANES), BF16)

    mixed = mixed_ref[0] + mixed_ref[1]
    full_ref[...] = mixed
    low_ref[...] = mixed.astype(BF16)


def attend_back_kernel(
    active_ref,
    order_ref,
    pair_ref,
    documents_ref,
    stat_ref,
    grad_ref,
    mixed_ref,
    out_ref,
    lying_ref,
    key_sum_ref,
    value_sum_ref,
    query_sum_ref,
    wide_ref,
    *,
    block,
    chunk,
    scaling,
):
    at = pl.program_id(0)
    rows = pl.ds(pl.multiple_of(at * block, block), block)
    lane = lax.broadcasted_iota(jnp.int32, (block, LANES), 1)
    last = lax.div(at * block, chunk)

    @pl.when(at == 0)
    def _():
        @pl.loop(0, pl.num_programs(0))
        def _(index):
            place = pl.ds(pl.multiple_of(index * block, block), block)
            parts = {"key": pair_ref[place, :LANES], "value": pair_ref[place, LANES:]}
            fill_slots(parts.get, documents_ref, wide_ref, tuple(parts), place)

        key_sum_ref[...] = jnp.zeros_like(key_sum_ref)
        value_sum_ref[...] = jnp.zeros_like(value_sum_ref)

    for slot in range(2):
        spare = HALF - HALF * slot
        own = (lane < HALF) if slot == 0 else (lane >= HALF)
        columns = slice(slot * LANES, (slot + 1) * LANES)
        query_sum_ref[slot] = jnp.zeros((block, LANES), F32)

        @pl.when(active_ref[slot, at] != 0)
        def _():
            query = stat_ref[:, columns]
            grad = grad_ref[...].astype(F32)
            delta = jnp.sum(jnp.where(own, grad * mixed_ref[...], 0.0), axis=1, keepdims=True)
            high, middle, small = three_parts(delta)
            extra = jnp.where(lane == spare, -high, 0.0)
            extra = jnp.where(lane == spare + 1, -middle, extra)
            extra = jnp.where(lane == spare + 2, -small, extra)
            grad_low = jnp.where(own, grad, extra).astype(BF16)

            def step(index, edge):
                place = pl.ds(pl.multiple_of(index * chunk, chunk), chunk)
                keys = wide_ref[place, slot * LANES : (slot + 1) * LANES]
                values = wide_ref[place, (2 + slot) * LANES : (3 + slot) * LANES]
                scores = contract(keys, query, 1, 1)
                if edge:
                    key_at = index * chunk + lax.broadcasted_iota(jnp.int32, (chunk, block), 0)
                    query_at = at * block + lax.broadcasted_iota(jnp.int32, (chunk, block), 1)
                    scores = jnp.where(key_at <= query_at, scores, FAR)
                weights = jnp.exp(scores)
                grad_weights = contract(values, grad_low, 1, 1)
                grad_scores = (weights * grad_weights).astype(BF16)
                value_sum_ref[slot, place, :] += contract(weights.astype(BF16), grad_low, 1, 0)
                key_sum_ref[slot, place, :] += contract(grad_scores, query, 1, 0)
                query_sum_ref[slot] += contract(grad_scores, keys, 0, 0)

            @pl.loop(0, last)
            def _(index):
                step(index, False)

            step(last, True)

    first_half = lane < HALF
    query_grad = jnp.where(first_half, query_sum_ref[0], query_sum_ref[1]) * scaling
    out_ref[rows, :LANES] = query_grad.astype(BF16)
    lying = pl.ds(pl.multiple_of(order_ref[at] * block, block), block)
    lying_ref[lying, :LANES] = query_grad.astype(BF16)

    @pl.when(at == pl.num_programs(0) - 1)
    def _():
        @pl.loop(0, pl.num_programs(0))
        def _(index):
            place = pl.ds(pl.multiple_of(index * block, block), block)
            key_grad = jnp.where(first_half, key_sum_ref[0, place, :], key_sum_ref[1, place, :])
            value_grad = jnp.where(
                first_half, value_sum_ref[0, place, :], value_sum_ref[1, place, :]
            )
            out_ref[place, LANES : 2 * LANES] = key_grad.astype(BF16)
            out_ref[place, 2 * LANES :] = value_grad.astype(BF16)
            lying = pl.ds(pl.multiple_of(order_ref[index] * block, block), block)
            lying_ref[lying, LANES : 2 * LANES] = key_grad.astype(BF16)
            lying_ref[lying, 2 * LANES :] = value_grad.astype(BF16)


def whole(value):
    return pl.BlockSpec(value.shape, lambda i, *unused: (0, 0), pipeline_mode=pl.Buffered(1))


SMALL = pl.CostEstimate(flops=1, bytes_accessed=1, transcendentals=0)


def attend(active, order, row_blocks, columns, documents, block):
    length = documents.shape[0]
    pair = jax.ShapeDtypeStruct((length, 2 * LANES), BF16)
    return pl.pallas_call(
        functools.partial(attend_kernel, block=block, chunk=2 * block, held=len(row_blocks)),
        grid_spec=pltpu.PrefetchScalarGridSpec(
            num_scalar_prefetch=2,
            grid=(length // block,),
            in_specs=[whole(value) for value in (*row_blocks, columns, documents)],
            out_specs=[
                pl.BlockSpec((block, LANES), lambda i, a, o: (i, 0)),
                pl.BlockSpec((block, LANES), lambda i, a, o: (i, 0)),
                pl.BlockSpec((block, 2 * LANES), lambda i, a, o: (i, 0)),
                whole(pair),
            ],
            scratch_shapes=[
                pltpu.VMEM((2, block, LANES), F32),
                pltpu.VMEM((length, 6 * LANES), BF16),
            ],
        ),
        out_shape=[
            jax.ShapeDtypeStruct((length, LANES), BF16),
            jax.ShapeDtypeStruct((length, LANES), F32),
            jax.ShapeDtypeStruct((length, 2 * LANES), BF16),
            pair,
        ],
        compiler_params=pltpu.CompilerParams(vmem_limit_bytes=VMEM_LIMIT),
        cost_estimate=SMALL,
    )(active, order, *row_blocks, columns, documents)


def attend_back(active, order, pair, documents, stat, grad, mixed, block, scaling):
    length = pair.shape[0]
    count = length // block
    return pl.pallas_call(
        functools.partial(attend_back_kernel, block=block, chunk=2 * block, scaling=scaling),
        grid_spec=pltpu.PrefetchScalarGridSpec(
            num_scalar_prefetch=2,
            grid=(count,),
            in_specs=[
                whole(pair),
                whole(documents),
                pl.BlockSpec((block, 2 * LANES), lambda i, a, o: (i, 0)),
                pl.BlockSpec((block, LANES), lambda i, a, o: (i, 0)),
                pl.BlockSpec((block, LANES), lambda i, a, o: (i, 0)),
            ],
            out_specs=[
                pl.BlockSpec(
                    (length, 3 * LANES), lambda i, a, o: (0, 0), pipeline_mode=pl.Buffered(1)
                )
            ]
            * 2,
            scratch_shapes=[
                pltpu.VMEM((2, length, LANES), F32),
                pltpu.VMEM((2, length, LANES), F32),
                pltpu.VMEM((2, block, LANES), F32),
                pltpu.VMEM((length, 4 * LANES), BF16),
            ],
        ),
        out_shape=[jax.ShapeDtypeStruct((length, 3 * LANES), BF16)] * 2,
        compiler_params=pltpu.CompilerParams(vmem_limit_bytes=VMEM_LIMIT),
        cost_estimate=SMALL,
    )(active, order, pair, documents, stat, grad, mixed)


def expert_kernel(arrived_ref, grad_ref, *refs, count):
    up_refs, down_refs = refs[:count], refs[count : 2 * count]
    total_ref = refs[2 * count]
    active_refs, hidden_refs = refs[2 * count + 1 : 3 * count + 1], refs[3 * count + 1 :]
    arrived, grad_arrived = arrived_ref[...], grad_ref[...]
    scale = math.sqrt(2.0 / math.pi)
    total = jnp.zeros(total_ref.shape, F32)
    for up_ref, down_ref, active_ref, hidden_ref in zip(
        up_refs, down_refs, active_refs, hidden_refs, strict=True
    ):
        up = up_ref[...]
        hidden = contract(arrived, up, 1, 1)
        squared = hidden * hidden
        bend = jnp.tanh(scale * hidden * (1.0 + 0.044715 * squared))
        half = 0.5 + 0.5 * bend
        active_ref[...] = (hidden * half).astype(BF16)
        slope = half + (0.5 * scale) * hidden * (1.0 - bend * bend) * (1.0 + 3 * 0.044715 * squared)
        grad_hidden = (slope * contract(grad_arrived, down_ref[...], 1, 1)).astype(BF16)
        hidden_ref[...] = grad_hidden
        total = total + contract(grad_hidden, up, 1, 0)
    total_ref[...] = total.astype(BF16)


def rows_spec(value, block):
    return pl.BlockSpec((block, value.shape[1]), lambda i: (i, 0))


def expert_part(arrived, grad_arrived, ups, downs):
    slots, width = arrived.shape
    block = 256
    units = [jax.ShapeDtypeStruct((slots, up.shape[0]), BF16) for up in ups]
    outs = [jax.ShapeDtypeStruct((slots, width), BF16), *units, *units]
    total, *parts = pl.pallas_call(
        functools.partial(expert_kernel, count=len(ups)),
        grid=(slots // block,),
        in_specs=[rows_spec(arrived, block), rows_spec(grad_arrived, block)]
        + [whole(value) for value in (*ups, *downs)],
        out_specs=[rows_spec(out, block) for out in outs],
        out_shape=outs,
        compiler_params=pltpu.CompilerParams(vmem_limit_bytes=VMEM_LIMIT),
        cost_estimate=SMALL,
    )(arrived, grad_arrived, *ups, *downs)
    return total, parts[: len(ups)], parts[len(ups) :]


def produced_kernel(*refs, count):
    total = contract(refs[0][...], refs[count][...], 1, 0)
    for index in range(1, count):
        total = total + contract(refs[index][...], refs[count + index][...], 1, 0)
    refs[-1][...] = total.astype(BF16)


def produced_part(actives, downs):
    slots, width = actives[0].shape[0], downs[0].shape[1]
    block = 256
    out = jax.ShapeDtypeStruct((slots, width), BF16)
    return pl.pallas_call(
        functools.partial(produced_kernel, count=len(actives)),
        grid=(slots // block,),
        in_specs=[rows_spec(value, block) for value in actives] + [whole(down) for down in downs],
        out_specs=rows_spec(out, block),
        out_shape=out,
        compiler_params=pltpu.CompilerParams(vmem_limit_bytes=VMEM_LIMIT),
        cost_estimate=SMALL,
    )(*actives, *downs)


def unit_kernel(grad_ref, arrived_ref, *refs, count):
    for index in range(count):
        active_ref, hidden_ref = refs[2 * index : 2 * index + 2]
        down_ref, up_ref = refs[2 * count + 2 * index : 2 * count + 2 * index + 2]
        down_ref[...] = contract(active_ref[...], grad_ref[...], 0, 0).astype(down_ref.dtype)
        up_ref[...] = contract(hidden_ref[...], arrived_ref[...], 0, 0).astype(up_ref.dtype)


def unit_grads(grad_arrived, arrived, blocks, kinds):
    slots, width = arrived.shape
    block = 256
    right = pl.BlockSpec((slots, block), lambda i: (0, i))
    outs = [
        jax.ShapeDtypeStruct((active.shape[1], width), kind)
        for (active, unused), kind in zip(blocks, kinds, strict=True)
        for part in range(2)
    ]
    flat = [value for pair in blocks for value in pair]
    return pl.pallas_call(
        functools.partial(unit_kernel, count=len(blocks)),
        grid=(width // block,),
        in_specs=[right, right] + [whole(value) for value in flat],
        out_specs=[pl.BlockSpec((out.shape[0], block), lambda i: (0, i)) for out in outs],
        out_shape=outs,
        compiler_params=pltpu.CompilerParams(vmem_limit_bytes=VMEM_LIMIT),
        cost_estimate=SMALL,
    )(grad_arrived, arrived, *flat)


def column_kernel(*refs, held):
    row_refs = refs[:held]
    lying_ref, out_ref = refs[held:]
    start, total = 0, None
    for row_ref in row_refs:
        rows = row_ref.shape[0]
        part = contract(row_ref[...], lying_ref[start : start + rows, :], 0, 0)
        total = part if total is None else total + part
        start += rows
    out_ref[...] = total.astype(BF16)


def column_terms(row_blocks, grad_lying):
    width = row_blocks[0].shape[1]
    block = 256
    out = jax.ShapeDtypeStruct((width, 3 * LANES), BF16)
    return pl.pallas_call(
        functools.partial(column_kernel, held=len(row_blocks)),
        grid=(width // block,),
        in_specs=[
            pl.BlockSpec((value.shape[0], block), lambda i: (0, i)) for value in row_blocks
        ]
        + [whole(grad_lying)],
        out_specs=rows_spec(out, block),
        out_shape=out,
        compiler_params=pltpu.CompilerParams(vmem_limit_bytes=VMEM_LIMIT),
        cost_estimate=SMALL,
    )(*row_blocks, grad_lying)


def close_kernel(
    pieces_ref, matrix_ref, tokens_ref, gain_ref, residual_ref, out_ref, part_ref, sum_ref, *, starts
):
    width = tokens_ref.shape[1]
    lane = lax.broadcasted_iota(jnp.int32, (tokens_ref.shape[0], LANES), 1)
    sum_ref[...] = jnp.zeros_like(sum_ref)
    for device, start in enumerate(starts):
        for part in range(3):
            piece = pieces_ref[device, :, part * LANES : (part + 1) * LANES].astype(F32)
            column = part * width + start
            if column % LANES == 0:
                sum_ref[:, column : column + LANES] += piece
            else:
                turned = pltpu.roll(piece, HALF, 1)
                low, high = column - HALF, column + HALF
                sum_ref[:, low : low + LANES] += jnp.where(lane >= HALF, turned, 0.0)
                sum_ref[:, high : high + LANES] += jnp.where(lane < HALF, turned, 0.0)
    grad = contract(sum_ref[...].astype(BF16), matrix_ref[...], 1, 1)
    inputs = tokens_ref[...].astype(F32)
    scale = lax.rsqrt(jnp.mean(inputs * inputs, axis=-1, keepdims=True) + EPSILON)
    normed = inputs * scale
    scaled = grad * gain_ref[...]
    mean = jnp.mean(scaled * normed, axis=-1, keepdims=True)
    out_ref[...] = residual_ref[...] + scale * (scaled - normed * mean)
    part_ref[...] = jnp.sum(grad * normed, axis=0, keepdims=True)


def close_norm(pieces, starts, matrix, tokens, gain, residual):
    rows, width = tokens.shape
    outs = [
        jax.ShapeDtypeStruct((rows, width), F32),
        jax.ShapeDtypeStruct((1, width), F32),
    ]
    return pl.pallas_call(
        functools.partial(close_kernel, starts=starts),
        in_specs=[pl.BlockSpec(memory_space=pltpu.VMEM)] * 5,
        out_specs=[pl.BlockSpec(memory_space=pltpu.VMEM)] * 2,
        out_shape=outs,
        scratch_shapes=[pltpu.VMEM((rows, 3 * width), F32)],
        compiler_params=pltpu.CompilerParams(vmem_limit_bytes=VMEM_LIMIT),
        cost_estimate=SMALL,
    )(pieces, matrix, tokens, gain, residual)


def dense_kernel(terms_ref, columns_ref, output_ref, square_ref, *, starts):
    width = output_ref.shape[1]
    columns_ref[...] = jnp.zeros_like(columns_ref)
    lane = lax.broadcasted_iota(jnp.int32, (columns_ref.shape[0], LANES), 1)
    output = jnp.zeros(output_ref.shape, F32)
    for device, start in enumerate(starts):
        output = output + terms_ref[device, :, 3 * LANES :].astype(F32)
        for part in range(3):
            piece = terms_ref[device, :, part * LANES : (part + 1) * LANES].astype(F32)
            column = part * width + start
            if column % LANES == 0:
                columns_ref[:, column : column + LANES] += piece
            else:
                turned = pltpu.roll(piece, HALF, 1)
                low, high = column - HALF, column + HALF
                columns_ref[:, low : low + LANES] += jnp.where(lane >= HALF, turned, 0.0)
                columns_ref[:, high : high + LANES] += jnp.where(lane < HALF, turned, 0.0)
    output_ref[...] = output
    columns = columns_ref[...]
    square_ref[...] = jnp.zeros_like(square_ref) + (
        jnp.sum(columns * columns) + jnp.sum(output * output)
    )


def dense_grads(terms, starts):
    unused, rows, lanes = terms.shape
    width = lanes - 3 * LANES
    outs = [jax.ShapeDtypeStruct((rows, columns), F32) for columns in (3 * width, width)]
    outs.append(jax.ShapeDtypeStruct((1, LANES), F32))
    return pl.pallas_call(
        functools.partial(dense_kernel, starts=starts),
        in_specs=[pl.BlockSpec(memory_space=pltpu.VMEM)],
        out_specs=[pl.BlockSpec(memory_space=pltpu.VMEM)] * 3,
        out_shape=outs,
        compiler_params=pltpu.CompilerParams(vmem_limit_bytes=VMEM_LIMIT),
        cost_estimate=SMALL,
    )(terms)


def adam_update(weight, grad, first, second, factor, rate, decay):
    clipped = grad * factor
    first_new = BETA_ONE * first + (1.0 - BETA_ONE) * clipped
    second_new = BETA_TWO * second + (1.0 - BETA_TWO) * clipped * clipped
    first_hat = first_new / (1.0 - BETA_ONE**STEP)
    second_hat = second_new / (1.0 - BETA_TWO**STEP)
    weight_new = weight - rate * (first_hat / (jnp.sqrt(second_hat) + ADAM_FLOOR) + decay * weight)
    return (first_new, second_new, weight_new)


def together(*values):
    return lax.optimization_barrier(values)


def swap(value, axes):
    return lax.all_to_all(value, axes, split_axis=0, concat_axis=0, tiled=True)


def adam_kernel(factor_ref, *refs, rates):
    count = len(rates)
    factor = factor_ref[0]
    for index, rate in enumerate(rates):
        weight, grad, first, second = [ref[...] for ref in refs[4 * index : 4 * index + 4]]
        outs = refs[4 * count + 3 * index : 4 * count + 3 * index + 3]
        for out, value in zip(
            outs, adam_update(weight, grad, first, second, factor, rate, DECAY), strict=True
        ):
            out[...] = value


def adam_all(factor, leaves, rates, steps):
    flat = [value.reshape(value.shape[-2:]) for leaf in leaves for value in leaf]

    def spec(value):
        rows, columns = value.shape
        if rows % (8 * steps) == 0:
            return pl.BlockSpec((rows // steps, columns), lambda i: (i, 0))
        lanes = columns // steps
        return pl.BlockSpec((rows, lanes), lambda i: (0, i))

    shapes = [jax.ShapeDtypeStruct(value.shape, F32) for value in flat[::4] for _ in range(3)]
    outs = pl.pallas_call(
        functools.partial(adam_kernel, rates=rates),
        grid=(steps,),
        in_specs=[pl.BlockSpec(memory_space=pltpu.SMEM)] + [spec(value) for value in flat],
        out_specs=[spec(shape) for shape in shapes],
        out_shape=shapes,
        compiler_params=pltpu.CompilerParams(vmem_limit_bytes=VMEM_LIMIT),
        cost_estimate=pl.CostEstimate(
            flops=20 * sum(value.size for value in flat[::4]),
            bytes_accessed=28 * sum(value.size for value in flat[::4]),
            transcendentals=0,
        ),
    )(factor.reshape(1), *flat)
    return [
        [out.reshape(leaf[0].shape) for out in outs[3 * index : 3 * index + 3]]
        for index, leaf in enumerate(leaves)
    ]


def flip(value, bits):
    count = lax.axis_size(SEQ)
    return lax.ppermute(value, SEQ, [(index, index ^ bits) for index in range(count)])


def others(value, axis):
    size = lax.axis_size(axis)
    parts = [
        lax.ppermute(value, axis, [((i + step) % size, i) for i in range(size)])
        for step in range(1, size)
    ]
    return parts[0] if size == 2 else jnp.concatenate(parts, axis=0)


def to_owners(blocks, axis):
    size = lax.axis_size(axis)
    return [
        lax.ppermute(block, axis, [(i, (i + step) % size) for i in range(size)])
        for step, block in enumerate(blocks, 1)
    ]


def add_all(own, parts):
    return functools.reduce(lambda total, part: total + part.astype(F32), parts, own.astype(F32))


def spread_sum(value):
    count = lax.axis_size(ALL)
    return jnp.sum(swap(jnp.broadcast_to(value[None], (count, *value.shape)), ALL), axis=0)


def body(
    tokens,
    cotangent,
    segment_ids,
    expert_ids,
    projection,
    output_weight,
    expert_up,
    expert_down,
    norm_gains,
    projection_first,
    projection_second,
    output_first,
    output_second,
    up_first,
    up_second,
    down_first,
    down_second,
    gains_first,
    gains_second,
):
    inputs = tokens[0].astype(F32)
    upstream = cotangent[0].astype(F32)
    row_count = inputs.shape[0]
    width = inputs.shape[1]
    head_size = width // HEADS
    scaling = head_size ** (-0.5)
    count = lax.axis_size(SEQ)
    groups = lax.axis_size("exp")
    team = lax.axis_size(TEAM)
    position = lax.axis_index(SEQ)
    length = count * row_count
    weight_rows = projection.shape[0]
    first_heads, active_table = head_plan(count)
    starts = [int(head) * head_size for head in first_heads]
    active = lax.dynamic_index_in_dim(jnp.asarray(active_table), position, 0, keepdims=False)
    gain_first = norm_gains[0]
    gain_second = norm_gains[1]
    used = active_table.any(axis=2)

    scale_first = lax.rsqrt(jnp.mean(inputs * inputs, axis=-1, keepdims=True) + EPSILON)
    normed_first = inputs * scale_first
    attend_in = (normed_first * gain_first).astype(BF16)
    slots = groups * CAP
    chosen = expert_ids[0, :, 0]
    one_hot = (chosen[:, None] == jnp.arange(groups, dtype=jnp.int32)[None, :]).astype(jnp.int32)
    rank = jnp.sum(jnp.cumsum(one_hot, axis=0) * one_hot, axis=1) - 1
    target = chosen * CAP + rank
    placing = (target[:, None] == jnp.arange(slots, dtype=jnp.int32)[None, :]).astype(BF16)

    def to_slots(values):
        outgoing = jnp.einsum("ts,td->sd", placing, values, preferred_element_type=F32)
        return outgoing.astype(BF16)

    def dispatch(outgoing):
        outgoing = jnp.broadcast_to(
            outgoing.reshape(1, groups, CAP, width), (team, groups, CAP, width)
        )
        return swap(outgoing.reshape(team * groups, CAP, width), TEAM + EXP).reshape(
            team * slots, width
        )

    def send_back(values):
        return swap(values.reshape(team * groups, CAP, width), TEAM + EXP).reshape(
            team, slots, width
        )

    def collect(returned):
        return jnp.einsum("ts,jsd->td", placing, returned, preferred_element_type=F32)

    projection_low = projection.astype(BF16)
    sent_rows = weight_rows + 8
    own_documents = jnp.zeros((8, 3 * LANES + width), BF16)
    own_documents = own_documents.at[0, :row_count].set(segment_ids[0].astype(BF16))
    output_low = output_weight.astype(BF16)
    pieces = [
        jnp.concatenate(
            [projection_low[:, k * width + s : k * width + s + LANES] for k in range(3)]
            + [output_low],
            axis=1,
        )
        for s in starts
    ]
    pieces = jnp.stack([jnp.concatenate([piece, own_documents], axis=0) for piece in pieces])
    own_up = expert_up[0].astype(BF16)
    own_down = expert_down[0].astype(BF16)
    pairwise = count == 8
    if pairwise:
        order = jnp.arange(count, dtype=jnp.int32) ^ position
        beside, below, across = flip(attend_in, 1), flip(attend_in, 2), flip(attend_in, 4)
        got_rows, beside, below, across, own_up = together(
            swap(pieces, SEQ), beside, below, across, own_up
        )
        corner = flip(across, 2)
        row_blocks = [attend_in, beside]
        row_blocks += [part for block in (below, across, corner) for part in (block, flip(block, 1))]
    else:
        order = jnp.arange(count, dtype=jnp.int32)
        row_blocks = [lax.all_gather(attend_in, SEQ, axis=0, tiled=True)]
        got_rows = swap(pieces, SEQ)
    documents = jnp.broadcast_to(
        got_rows[:, weight_rows, :row_count].reshape(length, 1), (length, LANES)
    )
    own_copies = jnp.broadcast_to(
        got_rows[None, :, :weight_rows], (groups, count, weight_rows, 3 * LANES + width)
    )
    all_copies = swap(own_copies, EXP)

    peer_up = others(own_up, "hi")
    *row_blocks, all_copies, peer_up, own_up, own_down, grad_slots_out = together(
        *row_blocks, all_copies, peer_up, own_up, own_down, to_slots(cotangent[0])
    )
    all_copies = jnp.swapaxes(all_copies, 0, 1)
    columns = all_copies[..., : 3 * LANES].reshape(width, 3 * LANES)
    output_full = all_copies[..., 3 * LANES :].reshape(width, width)
    grad_arrived = dispatch(grad_slots_out)
    peer_down = others(own_down, "hi")
    side_up = others(own_up, "in")
    side_down = others(own_down, "in")
    far_up = others(peer_up, "in")

    mixed_low, mixed_full, stat, pair = attend(
        active, order, row_blocks, columns, documents, row_count
    )

    def place_heads():
        index = np.arange(LANES)
        matrix = np.zeros((count, LANES, width), np.float32)
        for device in range(count):
            for slot in range(2):
                if used[device, slot]:
                    own = index[slot * HALF : (slot + 1) * HALF]
                    matrix[device, own, starts[device] + own] = 1.0
        return jnp.asarray(matrix, BF16)

    head_places = place_heads()

    def to_tokens(values):
        return swap(values.reshape(count, row_count, values.shape[1]), SEQ)

    mixed_low, grad_arrived, peer_down, side_up, side_down, far_up = together(
        mixed_low, grad_arrived, peer_down, side_up, side_down, far_up
    )
    far_down = others(peer_down, "in")
    mixed_pieces, projection_low, far_down = together(
        to_tokens(mixed_low), projection_low, far_down
    )
    projection_full = lax.all_gather(projection_low, ALL, axis=0, tiled=True)
    attend_out = jnp.einsum(
        "jtc,jcd->td", mixed_pieces, head_places, preferred_element_type=F32
    ).astype(BF16)
    branch = jnp.dot(attend_out, output_full, preferred_element_type=F32)
    middle = inputs + branch
    scale_second = lax.rsqrt(jnp.mean(middle * middle, axis=-1, keepdims=True) + EPSILON)
    normed_second = middle * scale_second
    expert_in = (normed_second * gain_second).astype(BF16)

    arrived = dispatch(to_slots(expert_in))
    ups, downs = (own_up, peer_up, side_up, far_up), (own_down, peer_down, side_down, far_down)
    grad_slots, actives, hiddens = expert_part(arrived, grad_arrived, ups, downs)
    returned_grad = send_back(grad_slots)

    blocks = list(zip(actives, hiddens, strict=True))
    down_far, up_far, down_peer, up_peer = unit_grads(
        grad_arrived, arrived, (blocks[3], blocks[1]), (BF16, F32)
    )
    (down_part,) = to_owners([down_far], "in")
    down_side, up_side, down_own, up_own = unit_grads(
        grad_arrived, arrived, (blocks[2], blocks[0]), (BF16, F32)
    )
    produced = produced_part(actives, downs)
    returned_grad, down_part, up_far, up_peer, projection_full, produced, down_side, up_own = (
        together(
            returned_grad, down_part, up_far, up_peer, projection_full, produced, down_side, up_own
        )
    )
    grad_expert_in = collect(returned_grad)
    (up_part,) = to_owners([up_far], "in")
    peers = lax.axis_size("hi")

    def hi_parts(value):
        return to_owners(list(value.astype(BF16).reshape(peers - 1, -1, width)), "hi")

    down_hi = hi_parts(add_all(down_peer, [down_part]))

    scaled_second = grad_expert_in * gain_second
    gain_second_part = jnp.sum(grad_expert_in * normed_second, axis=0)
    grad_middle = scale_second * (
        scaled_second
        - normed_second * jnp.mean(scaled_second * normed_second, axis=-1, keepdims=True)
    )
    residual_grad = upstream + grad_middle
    branch_grad = residual_grad.astype(BF16)
    grad_mixed = jnp.einsum(
        "td,ed->te", branch_grad, output_full, preferred_element_type=F32
    ).astype(BF16)

    sent_grad = jnp.stack([grad_mixed[:, s : s + LANES] for s in starts])
    row_grad = swap(sent_grad, SEQ).reshape(length, LANES)

    group = lax.axis_index(EXP)

    def group_rows(value):
        rows = value.reshape(count, groups, weight_rows, -1)
        own, *away = [
            lax.dynamic_index_in_dim(rows, lax.rem(group + step, groups), 1, keepdims=False)
            for step in range(groups)
        ]
        return own, away

    output_term = jnp.einsum("tc,te->ce", attend_out, branch_grad, preferred_element_type=F32)
    output_own, output_away = group_rows(output_term.astype(BF16))
    row_grad, produced, down_side, up_side, up_part, *output_away = together(
        row_grad, produced, down_side, up_side, up_part, *output_away
    )
    output_away = to_owners(output_away, "exp")
    up_head, up_tail = [
        list(part)
        for part in zip(
            *(
                jnp.split(block, 2, axis=0)
                for block in add_all(up_peer, [up_part]).astype(BF16).reshape(peers - 1, -1, width)
            ),
            strict=True,
        )
    ]
    up_head = to_owners(up_head, "hi")
    returned = send_back(produced)
    grad_qkv, grad_lying = attend_back(
        active, order, pair, documents, stat, row_grad, mixed_full, row_count, scaling
    )
    grad_qkv, grad_lying, returned, down_side, up_side, *held = together(
        grad_qkv, grad_lying, returned, down_side, up_side, *down_hi, *up_head, *output_away
    )
    down_hi, up_head = held[: peers - 1], held[peers - 1 : 2 * peers - 2]
    output_away = held[2 * peers - 2 :]
    (down_early,) = to_owners([down_side], "in")
    (up_early,) = to_owners([up_side], "in")
    block_output = (middle + collect(returned)).astype(BF16)[None]

    column_own, column_away = group_rows(column_terms(row_blocks, grad_lying))
    dense_rows = jnp.concatenate(
        [
            add_all(column_own, to_owners(column_away, "exp")).astype(BF16),
            add_all(output_own, output_away).astype(BF16),
        ],
        axis=2,
    )
    grad_pieces, dense_rows, down_early, up_early, *up_tail = together(
        to_tokens(grad_qkv), dense_rows, down_early, up_early, *up_tail
    )
    up_tail = to_owners(up_tail, "hi")
    projection_grad, output_grad, dense_square = dense_grads(swap(dense_rows, SEQ), starts)
    down_grad = add_all(down_own, [down_early, *down_hi])[None]
    up_half = up_own.shape[0] // 2
    up_grad = add_all(up_own, [up_early])
    up_grad = jnp.concatenate(
        [add_all(up_grad[:up_half], up_head), add_all(up_grad[up_half:], up_tail)], axis=0
    )[None]
    input_grad, gain_first_part = close_norm(
        grad_pieces, starts, projection_full, tokens[0], gain_first[None], residual_grad
    )
    input_grad, gain_first_part = input_grad[None], gain_first_part[0]
    local_square = jnp.sum(up_grad * up_grad) + jnp.sum(down_grad * down_grad)
    summed = spread_sum(
        jnp.concatenate(
            [gain_first_part, gain_second_part, dense_square[0] + local_square]
        )[None]
    )[0]
    gains_grad = summed[: 2 * width].reshape(2, width)
    grad_norm = jnp.sqrt(summed[2 * width] + jnp.sum(gains_grad * gains_grad))
    factor = jnp.minimum(1.0, CLIP / (grad_norm + 1e-06))
    (
        (projection_moment, projection_square, projection_new),
        (output_moment, output_square, output_new),
        (up_moment, up_square, up_new),
        (down_moment, down_square, down_new),
    ) = adam_all(
        factor,
        [
            (projection, projection_grad, projection_first, projection_second),
            (output_weight, output_grad, output_first, output_second),
            (expert_up, up_grad, up_first, up_second),
            (expert_down, down_grad, down_first, down_second),
        ],
        (RATE_MATRIX, RATE_OUTPUT, RATE_MATRIX, RATE_MATRIX),
        6,
    )
    gains_moment, gains_square, gains_new = adam_update(
        norm_gains, gains_grad, gains_first, gains_second, factor, RATE_GAIN, 0.0
    )
    return (
        block_output,
        input_grad,
        grad_norm,
        projection_grad,
        projection_moment,
        projection_square,
        projection_new,
        output_grad,
        output_moment,
        output_square,
        output_new,
        up_grad,
        up_moment,
        up_square,
        up_new,
        down_grad,
        down_moment,
        down_square,
        down_new,
        gains_grad,
        gains_moment,
        gains_square,
        gains_new,
    )


def solution(mesh):
    token = P("exp", SEQ, None)
    dense = P(ALL, None)
    expert = P("exp", SEQ, None)
    in_specs = (
        (token, token, P("exp", SEQ), token)
        + (dense, dense, expert, expert, P())
        + (dense,) * 4
        + (expert,) * 4
        + (P(), P())
    )
    out_specs = (token, token, P()) + (dense,) * 8 + (expert,) * 8 + (P(),) * 4
    rows, groups = mesh.devices.shape
    fine = Mesh(mesh.devices.reshape(rows // 4, 2, 2, groups), ALL)
    return jax.shard_map(body, mesh=fine, in_specs=in_specs, out_specs=out_specs, check_vma=False)
```

```python
import functools
import math

import jax
import jax.numpy as jnp
import numpy as np
from jax import lax
from jax.experimental import pallas as pl
from jax.experimental.pallas import tpu as pltpu
from jax.sharding import Mesh
from jax.sharding import PartitionSpec as P

HEADS = 12
CAP = 128
STEP = 10


EPSILON = 1e-05
CLIP = 1.0
BETA_ONE = 0.9
BETA_TWO = 0.99
ADAM_FLOOR = 1e-08
DECAY = 0.1
RATE_MATRIX = 0.04
RATE_OUTPUT = 0.1
RATE_GAIN = 0.5

SEQ = ("hi", "lo", "in")
EXP = ("exp",)
ALL = SEQ + EXP
TEAM = ("lo",)
SHARE = ("hi", "in")
LANES = 128
HALF = 64
FAR = -1e30
BF16 = jnp.bfloat16
F32 = jnp.float32
VMEM_LIMIT = 60 * 1024 * 1024


def head_plan(count):
    whole = math.lcm(HEADS, count)
    units, parts = whole // count, whole // HEADS
    first = np.zeros((count,), np.int64)
    active = np.zeros((count, 2, count), np.int32)
    for device in range(count):
        first[device] = min(units * device // parts, HEADS - 2)
        for unit in range(units * device, units * (device + 1)):
            slot = unit // parts - first[device]
            for block in range(count):
                turn = block % (2 * parts)
                if min(turn, 2 * parts - 1 - turn) == unit % parts:
                    active[device, slot, block] = 1
    return first, active


def three_parts(value):
    high = value.astype(BF16).astype(F32)
    middle = (value - high).astype(BF16).astype(F32)
    return high, middle, value - high - middle


def contract(left, right, left_axis, right_axis):
    return lax.dot_general(
        left, right, (((left_axis,), (right_axis,)), ((), ())), preferred_element_type=F32
    )


def slot_arrays(packed, documents, kind, slot):
    spare = HALF - HALF * slot
    lane = lax.broadcasted_iota(jnp.int32, packed.shape, 1)
    own = (lane < HALF) if slot == 0 else (lane >= HALF)
    place = (lane - spare).astype(F32)
    ours = place == documents
    first = (lane >= spare) & (lane < spare + 3)
    if kind == "query":
        extra = jnp.where(first & jnp.logical_not(ours), FAR, 0.0)
    elif kind == "key":
        extra = jnp.where(ours | ((lane >= spare + 3) & (lane < spare + 6)), 1.0, 0.0)
    else:
        extra = jnp.where(first, 1.0, 0.0)
    return jnp.where(own, packed, extra).astype(BF16)


def fill_slots(packed_of, documents_ref, wide_ref, kinds, place):
    documents = documents_ref[place, :].astype(F32)
    for number, kind in enumerate(kinds):
        packed = packed_of(kind).astype(F32)
        if kind == "query":
            packed = packed * 0.125
        for slot in range(2):
            column = (2 * number + slot) * LANES
            wide_ref[place, column : column + LANES] = slot_arrays(packed, documents, kind, slot)


def attend_kernel(active_ref, order_ref, *refs, block, chunk, held):
    row_refs = refs[:held]
    columns_ref, documents_ref = refs[held : held + 2]
    low_ref, full_ref, stat_ref, pair_ref, mixed_ref, wide_ref = refs[held + 2 :]
    at = pl.program_id(0)

    @pl.when(at == 0)
    def _():
        def fill(tokens, index):
            place = pl.ds(pl.multiple_of(order_ref[index] * block, block), block)
            packed = contract(tokens, columns_ref[...], 1, 0).astype(BF16)
            pair_ref[place, :] = packed[:, LANES:]
            parts = {
                kind: packed[:, part * LANES : (part + 1) * LANES]
                for part, kind in enumerate(("query", "key", "value"))
            }
            fill_slots(parts.get, documents_ref, wide_ref, tuple(parts), place)

        if held > 1:
            for index, row_ref in enumerate(row_refs):
                fill(row_ref[...], index)
        else:

            @pl.loop(0, pl.num_programs(0))
            def _(index):
                fill(row_refs[0][pl.ds(pl.multiple_of(index * block, block), block), :], index)

    rows = pl.ds(pl.multiple_of(at * block, block), block)
    lane = lax.broadcasted_iota(jnp.int32, (block, LANES), 1)
    last = lax.div(at * block, chunk)
    for slot in range(2):
        spare = HALF - HALF * slot
        own = (lane < HALF) if slot == 0 else (lane >= HALF)
        columns = slice(slot * LANES, (slot + 1) * LANES)

        @pl.when(active_ref[slot, at] != 0)
        def _():
            query = wide_ref[rows, columns]

            def step(index, carry, edge):
                top, weighted = carry
                place = pl.ds(pl.multiple_of(index * chunk, chunk), chunk)
                keys = wide_ref[place, 2 * LANES + slot * LANES : 3 * LANES + slot * LANES]
                values = wide_ref[place, 4 * LANES + slot * LANES : 5 * LANES + slot * LANES]
                scores = contract(query, keys, 1, 1)
                if edge:
                    key_at = index * chunk + lax.broadcasted_iota(jnp.int32, (block, chunk), 1)
                    query_at = at * block + lax.broadcasted_iota(jnp.int32, (block, chunk), 0)
                    scores = jnp.where(key_at <= query_at, scores, FAR)
                new_top = jnp.maximum(top, jnp.max(scores, axis=1, keepdims=True))
                weights = jnp.exp(scores - new_top).astype(BF16)
                weighted = weighted * jnp.exp(top - new_top) + contract(weights, values, 1, 0)
                return new_top, weighted

            carry = (jnp.full((block, 1), FAR, F32), jnp.zeros((block, LANES), F32))
            carry = lax.fori_loop(0, last, lambda index, state: step(index, state, False), carry)
            top, weighted = step(last, carry, True)
            total = weighted[:, spare : spare + 1]
            mixed_ref[slot] = jnp.where(own, weighted / total, 0.0)
            log_total = top + jnp.log(total)
            high, middle, small = three_parts(log_total)
            extra = jnp.where(lane == spare + 3, -high, 0.0)
            extra = jnp.where(lane == spare + 4, -middle, extra)
            extra = jnp.where(lane == spare + 5, -small, extra)
            stat_ref[:, columns] = (query.astype(F32) + extra).astype(BF16)

        @pl.when(active_ref[slot, at] == 0)
        def _():
            mixed_ref[slot] = jnp.zeros((block, LANES), F32)
            stat_ref[:, columns] = jnp.zeros((block, LANES), BF16)

    mixed = mixed_ref[0] + mixed_ref[1]
    full_ref[...] = mixed
    low_ref[...] = mixed.astype(BF16)


def attend_back_kernel(
    active_ref,
    order_ref,
    pair_ref,
    documents_ref,
    stat_ref,
    grad_ref,
    mixed_ref,
    out_ref,
    lying_ref,
    key_sum_ref,
    value_sum_ref,
    query_sum_ref,
    wide_ref,
    *,
    block,
    chunk,
    scaling,
):
    at = pl.program_id(0)
    rows = pl.ds(pl.multiple_of(at * block, block), block)
    lane = lax.broadcasted_iota(jnp.int32, (block, LANES), 1)
    last = lax.div(at * block, chunk)

    @pl.when(at == 0)
    def _():
        @pl.loop(0, pl.num_programs(0))
        def _(index):
            place = pl.ds(pl.multiple_of(index * block, block), block)
            parts = {"key": pair_ref[place, :LANES], "value": pair_ref[place, LANES:]}
            fill_slots(parts.get, documents_ref, wide_ref, tuple(parts), place)

        key_sum_ref[...] = jnp.zeros_like(key_sum_ref)
        value_sum_ref[...] = jnp.zeros_like(value_sum_ref)

    for slot in range(2):
        spare = HALF - HALF * slot
        own = (lane < HALF) if slot == 0 else (lane >= HALF)
        columns = slice(slot * LANES, (slot + 1) * LANES)
        query_sum_ref[slot] = jnp.zeros((block, LANES), F32)

        @pl.when(active_ref[slot, at] != 0)
        def _():
            query = stat_ref[:, columns]
            grad = grad_ref[...].astype(F32)
            delta = jnp.sum(jnp.where(own, grad * mixed_ref[...], 0.0), axis=1, keepdims=True)
            high, middle, small = three_parts(delta)
            extra = jnp.where(lane == spare, -high, 0.0)
            extra = jnp.where(lane == spare + 1, -middle, extra)
            extra = jnp.where(lane == spare + 2, -small, extra)
            grad_low = jnp.where(own, grad, extra).astype(BF16)

            def step(index, edge):
                place = pl.ds(pl.multiple_of(index * chunk, chunk), chunk)
                keys = wide_ref[place, slot * LANES : (slot + 1) * LANES]
                values = wide_ref[place, (2 + slot) * LANES : (3 + slot) * LANES]
                scores = contract(keys, query, 1, 1)
                if edge:
                    key_at = index * chunk + lax.broadcasted_iota(jnp.int32, (chunk, block), 0)
                    query_at = at * block + lax.broadcasted_iota(jnp.int32, (chunk, block), 1)
                    scores = jnp.where(key_at <= query_at, scores, FAR)
                weights = jnp.exp(scores)
                grad_weights = contract(values, grad_low, 1, 1)
                grad_scores = (weights * grad_weights).astype(BF16)
                value_sum_ref[slot, place, :] += contract(weights.astype(BF16), grad_low, 1, 0)
                key_sum_ref[slot, place, :] += contract(grad_scores, query, 1, 0)
                query_sum_ref[slot] += contract(grad_scores, keys, 0, 0)

            @pl.loop(0, last)
            def _(index):
                step(index, False)

            step(last, True)

    first_half = lane < HALF
    query_grad = jnp.where(first_half, query_sum_ref[0], query_sum_ref[1]) * scaling
    out_ref[rows, :LANES] = query_grad.astype(BF16)
    lying = pl.ds(pl.multiple_of(order_ref[at] * block, block), block)
    lying_ref[lying, :LANES] = query_grad.astype(BF16)

    @pl.when(at == pl.num_programs(0) - 1)
    def _():
        @pl.loop(0, pl.num_programs(0))
        def _(index):
            place = pl.ds(pl.multiple_of(index * block, block), block)
            key_grad = jnp.where(first_half, key_sum_ref[0, place, :], key_sum_ref[1, place, :])
            value_grad = jnp.where(
                first_half, value_sum_ref[0, place, :], value_sum_ref[1, place, :]
            )
            out_ref[place, LANES : 2 * LANES] = key_grad.astype(BF16)
            out_ref[place, 2 * LANES :] = value_grad.astype(BF16)
            lying = pl.ds(pl.multiple_of(order_ref[index] * block, block), block)
            lying_ref[lying, LANES : 2 * LANES] = key_grad.astype(BF16)
            lying_ref[lying, 2 * LANES :] = value_grad.astype(BF16)


def whole(value):
    return pl.BlockSpec(value.shape, lambda i, *unused: (0, 0), pipeline_mode=pl.Buffered(1))


SMALL = pl.CostEstimate(flops=1, bytes_accessed=1, transcendentals=0)


def attend(active, order, row_blocks, columns, documents, block):
    length = documents.shape[0]
    pair = jax.ShapeDtypeStruct((length, 2 * LANES), BF16)
    return pl.pallas_call(
        functools.partial(attend_kernel, block=block, chunk=2 * block, held=len(row_blocks)),
        grid_spec=pltpu.PrefetchScalarGridSpec(
            num_scalar_prefetch=2,
            grid=(length // block,),
            in_specs=[whole(value) for value in (*row_blocks, columns, documents)],
            out_specs=[
                pl.BlockSpec((block, LANES), lambda i, a, o: (i, 0)),
                pl.BlockSpec((block, LANES), lambda i, a, o: (i, 0)),
                pl.BlockSpec((block, 2 * LANES), lambda i, a, o: (i, 0)),
                whole(pair),
            ],
            scratch_shapes=[
                pltpu.VMEM((2, block, LANES), F32),
                pltpu.VMEM((length, 6 * LANES), BF16),
            ],
        ),
        out_shape=[
            jax.ShapeDtypeStruct((length, LANES), BF16),
            jax.ShapeDtypeStruct((length, LANES), F32),
            jax.ShapeDtypeStruct((length, 2 * LANES), BF16),
            pair,
        ],
        compiler_params=pltpu.CompilerParams(vmem_limit_bytes=VMEM_LIMIT),
        cost_estimate=SMALL,
    )(active, order, *row_blocks, columns, documents)


def attend_back(active, order, pair, documents, stat, grad, mixed, block, scaling):
    length = pair.shape[0]
    count = length // block
    return pl.pallas_call(
        functools.partial(attend_back_kernel, block=block, chunk=2 * block, scaling=scaling),
        grid_spec=pltpu.PrefetchScalarGridSpec(
            num_scalar_prefetch=2,
            grid=(count,),
            in_specs=[
                whole(pair),
                whole(documents),
                pl.BlockSpec((block, 2 * LANES), lambda i, a, o: (i, 0)),
                pl.BlockSpec((block, LANES), lambda i, a, o: (i, 0)),
                pl.BlockSpec((block, LANES), lambda i, a, o: (i, 0)),
            ],
            out_specs=[
                pl.BlockSpec(
                    (length, 3 * LANES), lambda i, a, o: (0, 0), pipeline_mode=pl.Buffered(1)
                )
            ]
            * 2,
            scratch_shapes=[
                pltpu.VMEM((2, length, LANES), F32),
                pltpu.VMEM((2, length, LANES), F32),
                pltpu.VMEM((2, block, LANES), F32),
                pltpu.VMEM((length, 4 * LANES), BF16),
            ],
        ),
        out_shape=[jax.ShapeDtypeStruct((length, 3 * LANES), BF16)] * 2,
        compiler_params=pltpu.CompilerParams(vmem_limit_bytes=VMEM_LIMIT),
        cost_estimate=SMALL,
    )(active, order, pair, documents, stat, grad, mixed)


def expert_kernel(arrived_ref, grad_ref, *refs, count):
    up_refs, down_refs = refs[:count], refs[count : 2 * count]
    total_ref = refs[2 * count]
    active_refs, hidden_refs = refs[2 * count + 1 : 3 * count + 1], refs[3 * count + 1 :]
    arrived, grad_arrived = arrived_ref[...], grad_ref[...]
    scale = math.sqrt(2.0 / math.pi)
    total = jnp.zeros(total_ref.shape, F32)
    for up_ref, down_ref, active_ref, hidden_ref in zip(
        up_refs, down_refs, active_refs, hidden_refs, strict=True
    ):
        up = up_ref[...]
        hidden = contract(arrived, up, 1, 1)
        squared = hidden * hidden
        bend = jnp.tanh(scale * hidden * (1.0 + 0.044715 * squared))
        half = 0.5 + 0.5 * bend
        active_ref[...] = (hidden * half).astype(BF16)
        slope = half + (0.5 * scale) * hidden * (1.0 - bend * bend) * (1.0 + 3 * 0.044715 * squared)
        grad_hidden = (slope * contract(grad_arrived, down_ref[...], 1, 1)).astype(BF16)
        hidden_ref[...] = grad_hidden
        total = total + contract(grad_hidden, up, 1, 0)
    total_ref[...] = total.astype(BF16)


def rows_spec(value, block):
    return pl.BlockSpec((block, value.shape[1]), lambda i: (i, 0))


def expert_part(arrived, grad_arrived, ups, downs):
    slots, width = arrived.shape
    block = 256
    units = [jax.ShapeDtypeStruct((slots, up.shape[0]), BF16) for up in ups]
    outs = [jax.ShapeDtypeStruct((slots, width), BF16), *units, *units]
    total, *parts = pl.pallas_call(
        functools.partial(expert_kernel, count=len(ups)),
        grid=(slots // block,),
        in_specs=[rows_spec(arrived, block), rows_spec(grad_arrived, block)]
        + [whole(value) for value in (*ups, *downs)],
        out_specs=[rows_spec(out, block) for out in outs],
        out_shape=outs,
        compiler_params=pltpu.CompilerParams(vmem_limit_bytes=VMEM_LIMIT),
        cost_estimate=SMALL,
    )(arrived, grad_arrived, *ups, *downs)
    return total, parts[: len(ups)], parts[len(ups) :]


def produced_kernel(*refs, count):
    total = contract(refs[0][...], refs[count][...], 1, 0)
    for index in range(1, count):
        total = total + contract(refs[index][...], refs[count + index][...], 1, 0)
    refs[-1][...] = total.astype(BF16)


def produced_part(actives, downs):
    slots, width = actives[0].shape[0], downs[0].shape[1]
    block = 256
    out = jax.ShapeDtypeStruct((slots, width), BF16)
    return pl.pallas_call(
        functools.partial(produced_kernel, count=len(actives)),
        grid=(slots // block,),
        in_specs=[rows_spec(value, block) for value in actives] + [whole(down) for down in downs],
        out_specs=rows_spec(out, block),
        out_shape=out,
        compiler_params=pltpu.CompilerParams(vmem_limit_bytes=VMEM_LIMIT),
        cost_estimate=SMALL,
    )(*actives, *downs)


def unit_kernel(grad_ref, arrived_ref, *refs, count):
    for index in range(count):
        active_ref, hidden_ref = refs[2 * index : 2 * index + 2]
        down_ref, up_ref = refs[2 * count + 2 * index : 2 * count + 2 * index + 2]
        down_ref[...] = contract(active_ref[...], grad_ref[...], 0, 0).astype(down_ref.dtype)
        up_ref[...] = contract(hidden_ref[...], arrived_ref[...], 0, 0).astype(up_ref.dtype)


def unit_grads(grad_arrived, arrived, blocks, kinds):
    slots, width = arrived.shape
    block = 256
    right = pl.BlockSpec((slots, block), lambda i: (0, i))
    outs = [
        jax.ShapeDtypeStruct((active.shape[1], width), kind)
        for (active, unused), kind in zip(blocks, kinds, strict=True)
        for part in range(2)
    ]
    flat = [value for pair in blocks for value in pair]
    return pl.pallas_call(
        functools.partial(unit_kernel, count=len(blocks)),
        grid=(width // block,),
        in_specs=[right, right] + [whole(value) for value in flat],
        out_specs=[pl.BlockSpec((out.shape[0], block), lambda i: (0, i)) for out in outs],
        out_shape=outs,
        compiler_params=pltpu.CompilerParams(vmem_limit_bytes=VMEM_LIMIT),
        cost_estimate=SMALL,
    )(grad_arrived, arrived, *flat)


def column_kernel(*refs, held):
    row_refs = refs[:held]
    lying_ref, out_ref = refs[held:]
    start, total = 0, None
    for row_ref in row_refs:
        rows = row_ref.shape[0]
        part = contract(row_ref[...], lying_ref[start : start + rows, :], 0, 0)
        total = part if total is None else total + part
        start += rows
    out_ref[...] = total.astype(BF16)


def column_terms(row_blocks, grad_lying):
    width = row_blocks[0].shape[1]
    block = 256
    out = jax.ShapeDtypeStruct((width, 3 * LANES), BF16)
    return pl.pallas_call(
        functools.partial(column_kernel, held=len(row_blocks)),
        grid=(width // block,),
        in_specs=[
            pl.BlockSpec((value.shape[0], block), lambda i: (0, i)) for value in row_blocks
        ]
        + [whole(grad_lying)],
        out_specs=rows_spec(out, block),
        out_shape=out,
        compiler_params=pltpu.CompilerParams(vmem_limit_bytes=VMEM_LIMIT),
        cost_estimate=SMALL,
    )(*row_blocks, grad_lying)


def close_kernel(
    pieces_ref, matrix_ref, tokens_ref, gain_ref, residual_ref, out_ref, part_ref, sum_ref, *, starts
):
    width = tokens_ref.shape[1]
    lane = lax.broadcasted_iota(jnp.int32, (tokens_ref.shape[0], LANES), 1)
    sum_ref[...] = jnp.zeros_like(sum_ref)
    for device, start in enumerate(starts):
        for part in range(3):
            piece = pieces_ref[device, :, part * LANES : (part + 1) * LANES].astype(F32)
            column = part * width + start
            if column % LANES == 0:
                sum_ref[:, column : column + LANES] += piece
            else:
                turned = pltpu.roll(piece, HALF, 1)
                low, high = column - HALF, column + HALF
                sum_ref[:, low : low + LANES] += jnp.where(lane >= HALF, turned, 0.0)
                sum_ref[:, high : high + LANES] += jnp.where(lane < HALF, turned, 0.0)
    grad = contract(sum_ref[...].astype(BF16), matrix_ref[...], 1, 1)
    inputs = tokens_ref[...].astype(F32)
    scale = lax.rsqrt(jnp.mean(inputs * inputs, axis=-1, keepdims=True) + EPSILON)
    normed = inputs * scale
    scaled = grad * gain_ref[...]
    mean = jnp.mean(scaled * normed, axis=-1, keepdims=True)
    out_ref[...] = residual_ref[...] + scale * (scaled - normed * mean)
    part_ref[...] = jnp.sum(grad * normed, axis=0, keepdims=True)


def close_norm(pieces, starts, matrix, tokens, gain, residual):
    rows, width = tokens.shape
    outs = [
        jax.ShapeDtypeStruct((rows, width), F32),
        jax.ShapeDtypeStruct((1, width), F32),
    ]
    return pl.pallas_call(
        functools.partial(close_kernel, starts=starts),
        in_specs=[pl.BlockSpec(memory_space=pltpu.VMEM)] * 5,
        out_specs=[pl.BlockSpec(memory_space=pltpu.VMEM)] * 2,
        out_shape=outs,
        scratch_shapes=[pltpu.VMEM((rows, 3 * width), F32)],
        compiler_params=pltpu.CompilerParams(vmem_limit_bytes=VMEM_LIMIT),
        cost_estimate=SMALL,
    )(pieces, matrix, tokens, gain, residual)


def dense_kernel(terms_ref, columns_ref, output_ref, square_ref, *, starts):
    width = output_ref.shape[1]
    columns_ref[...] = jnp.zeros_like(columns_ref)
    lane = lax.broadcasted_iota(jnp.int32, (columns_ref.shape[0], LANES), 1)
    output = jnp.zeros(output_ref.shape, F32)
    for device, start in enumerate(starts):
        output = output + terms_ref[device, :, 3 * LANES :].astype(F32)
        for part in range(3):
            piece = terms_ref[device, :, part * LANES : (part + 1) * LANES].astype(F32)
            column = part * width + start
            if column % LANES == 0:
                columns_ref[:, column : column + LANES] += piece
            else:
                turned = pltpu.roll(piece, HALF, 1)
                low, high = column - HALF, column + HALF
                columns_ref[:, low : low + LANES] += jnp.where(lane >= HALF, turned, 0.0)
                columns_ref[:, high : high + LANES] += jnp.where(lane < HALF, turned, 0.0)
    output_ref[...] = output
    columns = columns_ref[...]
    square_ref[...] = jnp.zeros_like(square_ref) + (
        jnp.sum(columns * columns) + jnp.sum(output * output)
    )


def dense_grads(terms, starts):
    unused, rows, lanes = terms.shape
    width = lanes - 3 * LANES
    outs = [jax.ShapeDtypeStruct((rows, columns), F32) for columns in (3 * width, width)]
    outs.append(jax.ShapeDtypeStruct((1, LANES), F32))
    return pl.pallas_call(
        functools.partial(dense_kernel, starts=starts),
        in_specs=[pl.BlockSpec(memory_space=pltpu.VMEM)],
        out_specs=[pl.BlockSpec(memory_space=pltpu.VMEM)] * 3,
        out_shape=outs,
        compiler_params=pltpu.CompilerParams(vmem_limit_bytes=VMEM_LIMIT),
        cost_estimate=SMALL,
    )(terms)


def adam_update(weight, grad, first, second, factor, rate, decay):
    clipped = grad * factor
    first_new = BETA_ONE * first + (1.0 - BETA_ONE) * clipped
    second_new = BETA_TWO * second + (1.0 - BETA_TWO) * clipped * clipped
    first_hat = first_new / (1.0 - BETA_ONE**STEP)
    second_hat = second_new / (1.0 - BETA_TWO**STEP)
    weight_new = weight - rate * (first_hat / (jnp.sqrt(second_hat) + ADAM_FLOOR) + decay * weight)
    return (first_new, second_new, weight_new)


def together(*values):
    return lax.optimization_barrier(values)


def swap(value, axes):
    return lax.all_to_all(value, axes, split_axis=0, concat_axis=0, tiled=True)


def adam_kernel(factor_ref, *refs, rates):
    count = len(rates)
    factor = factor_ref[0]
    for index, rate in enumerate(rates):
        weight, grad, first, second = [ref[...] for ref in refs[4 * index : 4 * index + 4]]
        outs = refs[4 * count + 3 * index : 4 * count + 3 * index + 3]
        for out, value in zip(
            outs, adam_update(weight, grad, first, second, factor, rate, DECAY), strict=True
        ):
            out[...] = value


def adam_all(factor, leaves, rates, steps):
    flat = [value.reshape(value.shape[-2:]) for leaf in leaves for value in leaf]

    def spec(value):
        rows, columns = value.shape
        if rows % (8 * steps) == 0:
            return pl.BlockSpec((rows // steps, columns), lambda i: (i, 0))
        lanes = columns // steps
        return pl.BlockSpec((rows, lanes), lambda i: (0, i))

    shapes = [jax.ShapeDtypeStruct(value.shape, F32) for value in flat[::4] for _ in range(3)]
    outs = pl.pallas_call(
        functools.partial(adam_kernel, rates=rates),
        grid=(steps,),
        in_specs=[pl.BlockSpec(memory_space=pltpu.SMEM)] + [spec(value) for value in flat],
        out_specs=[spec(shape) for shape in shapes],
        out_shape=shapes,
        compiler_params=pltpu.CompilerParams(vmem_limit_bytes=VMEM_LIMIT),
        cost_estimate=pl.CostEstimate(
            flops=20 * sum(value.size for value in flat[::4]),
            bytes_accessed=28 * sum(value.size for value in flat[::4]),
            transcendentals=0,
        ),
    )(factor.reshape(1), *flat)
    return [
        [out.reshape(leaf[0].shape) for out in outs[3 * index : 3 * index + 3]]
        for index, leaf in enumerate(leaves)
    ]


def flip(value, bits):
    count = lax.axis_size(SEQ)
    return lax.ppermute(value, SEQ, [(index, index ^ bits) for index in range(count)])


def others(value, axis):
    size = lax.axis_size(axis)
    parts = [
        lax.ppermute(value, axis, [((i + step) % size, i) for i in range(size)])
        for step in range(1, size)
    ]
    return parts[0] if size == 2 else jnp.concatenate(parts, axis=0)


def to_owners(blocks, axis):
    size = lax.axis_size(axis)
    return [
        lax.ppermute(block, axis, [(i, (i + step) % size) for i in range(size)])
        for step, block in enumerate(blocks, 1)
    ]


def add_all(own, parts):
    return functools.reduce(lambda total, part: total + part.astype(F32), parts, own.astype(F32))


def spread_sum(value):
    count = lax.axis_size(ALL)
    return jnp.sum(swap(jnp.broadcast_to(value[None], (count, *value.shape)), ALL), axis=0)


def body(
    tokens,
    cotangent,
    segment_ids,
    expert_ids,
    projection,
    output_weight,
    expert_up,
    expert_down,
    norm_gains,
    projection_first,
    projection_second,
    output_first,
    output_second,
    up_first,
    up_second,
    down_first,
    down_second,
    gains_first,
    gains_second,
):
    inputs = tokens[0].astype(F32)
    upstream = cotangent[0].astype(F32)
    row_count = inputs.shape[0]
    width = inputs.shape[1]
    head_size = width // HEADS
    scaling = head_size ** (-0.5)
    count = lax.axis_size(SEQ)
    groups = lax.axis_size("exp")
    team = lax.axis_size(TEAM)
    position = lax.axis_index(SEQ)
    length = count * row_count
    weight_rows = projection.shape[0]
    first_heads, active_table = head_plan(count)
    starts = [int(head) * head_size for head in first_heads]
    active = lax.dynamic_index_in_dim(jnp.asarray(active_table), position, 0, keepdims=False)
    gain_first = norm_gains[0]
    gain_second = norm_gains[1]
    used = active_table.any(axis=2)

    scale_first = lax.rsqrt(jnp.mean(inputs * inputs, axis=-1, keepdims=True) + EPSILON)
    normed_first = inputs * scale_first
    attend_in = (normed_first * gain_first).astype(BF16)
    slots = groups * CAP
    chosen = expert_ids[0, :, 0]
    one_hot = (chosen[:, None] == jnp.arange(groups, dtype=jnp.int32)[None, :]).astype(jnp.int32)
    rank = jnp.sum(jnp.cumsum(one_hot, axis=0) * one_hot, axis=1) - 1
    target = chosen * CAP + rank
    placing = (target[:, None] == jnp.arange(slots, dtype=jnp.int32)[None, :]).astype(BF16)

    def to_slots(values):
        outgoing = jnp.einsum("ts,td->sd", placing, values, preferred_element_type=F32)
        return outgoing.astype(BF16)

    def dispatch(outgoing):
        outgoing = jnp.broadcast_to(
            outgoing.reshape(1, groups, CAP, width), (team, groups, CAP, width)
        )
        return swap(outgoing.reshape(team * groups, CAP, width), TEAM + EXP).reshape(
            team * slots, width
        )

    def send_back(values):
        return swap(values.reshape(team * groups, CAP, width), TEAM + EXP).reshape(
            team, slots, width
        )

    def collect(returned):
        return jnp.einsum("ts,jsd->td", placing, returned, preferred_element_type=F32)

    projection_low = projection.astype(BF16)
    sent_rows = weight_rows + 8
    own_documents = jnp.zeros((8, 3 * LANES + width), BF16)
    own_documents = own_documents.at[0, :row_count].set(segment_ids[0].astype(BF16))
    output_low = output_weight.astype(BF16)
    pieces = [
        jnp.concatenate(
            [projection_low[:, k * width + s : k * width + s + LANES] for k in range(3)]
            + [output_low],
            axis=1,
        )
        for s in starts
    ]
    pieces = jnp.stack([jnp.concatenate([piece, own_documents], axis=0) for piece in pieces])
    own_up = expert_up[0].astype(BF16)
    own_down = expert_down[0].astype(BF16)
    pairwise = count == 8
    if pairwise:
        order = jnp.arange(count, dtype=jnp.int32) ^ position
        beside, below, across = flip(attend_in, 1), flip(attend_in, 2), flip(attend_in, 4)
        got_rows, beside, below, across, own_up = together(
            swap(pieces, SEQ), beside, below, across, own_up
        )
        corner = flip(across, 2)
        row_blocks = [attend_in, beside]
        row_blocks += [part for block in (below, across, corner) for part in (block, flip(block, 1))]
    else:
        order = jnp.arange(count, dtype=jnp.int32)
        row_blocks = [lax.all_gather(attend_in, SEQ, axis=0, tiled=True)]
        got_rows = swap(pieces, SEQ)
    documents = jnp.broadcast_to(
        got_rows[:, weight_rows, :row_count].reshape(length, 1), (length, LANES)
    )
    own_copies = jnp.broadcast_to(
        got_rows[None, :, :weight_rows], (groups, count, weight_rows, 3 * LANES + width)
    )
    all_copies = swap(own_copies, EXP)

    peer_up = others(own_up, "hi")
    *row_blocks, all_copies, peer_up, own_up, own_down, grad_slots_out = together(
        *row_blocks, all_copies, peer_up, own_up, own_down, to_slots(cotangent[0])
    )
    all_copies = jnp.swapaxes(all_copies, 0, 1)
    columns = all_copies[..., : 3 * LANES].reshape(width, 3 * LANES)
    output_full = all_copies[..., 3 * LANES :].reshape(width, width)
    grad_arrived = dispatch(grad_slots_out)
    peer_down = others(own_down, "hi")
    side_up = others(own_up, "in")
    side_down = others(own_down, "in")
    far_up = others(peer_up, "in")

    mixed_low, mixed_full, stat, pair = attend(
        active, order, row_blocks, columns, documents, row_count
    )

    def place_heads():
        index = np.arange(LANES)
        matrix = np.zeros((count, LANES, width), np.float32)
        for device in range(count):
            for slot in range(2):
                if used[device, slot]:
                    own = index[slot * HALF : (slot + 1) * HALF]
                    matrix[device, own, starts[device] + own] = 1.0
        return jnp.asarray(matrix, BF16)

    head_places = place_heads()

    def to_tokens(values):
        return swap(values.reshape(count, row_count, values.shape[1]), SEQ)

    mixed_low, grad_arrived, peer_down, side_up, side_down, far_up = together(
        mixed_low, grad_arrived, peer_down, side_up, side_down, far_up
    )
    far_down = others(peer_down, "in")
    mixed_pieces, projection_low, far_down = together(
        to_tokens(mixed_low), projection_low, far_down
    )
    projection_full = lax.all_gather(projection_low, ALL, axis=0, tiled=True)
    attend_out = jnp.einsum(
        "jtc,jcd->td", mixed_pieces, head_places, preferred_element_type=F32
    ).astype(BF16)
    branch = jnp.dot(attend_out, output_full, preferred_element_type=F32)
    middle = inputs + branch
    scale_second = lax.rsqrt(jnp.mean(middle * middle, axis=-1, keepdims=True) + EPSILON)
    normed_second = middle * scale_second
    expert_in = (normed_second * gain_second).astype(BF16)

    arrived = dispatch(to_slots(expert_in))
    ups, downs = (own_up, peer_up, side_up, far_up), (own_down, peer_down, side_down, far_down)
    grad_slots, actives, hiddens = expert_part(arrived, grad_arrived, ups, downs)
    returned_grad = send_back(grad_slots)

    blocks = list(zip(actives, hiddens, strict=True))
    down_far, up_far, down_peer, up_peer = unit_grads(
        grad_arrived, arrived, (blocks[3], blocks[1]), (BF16, F32)
    )
    (down_part,) = to_owners([down_far], "in")
    down_side, up_side, down_own, up_own = unit_grads(
        grad_arrived, arrived, (blocks[2], blocks[0]), (BF16, F32)
    )
    produced = produced_part(actives, downs)
    returned_grad, down_part, up_far, up_peer, projection_full, produced, down_side, up_own = (
        together(
            returned_grad, down_part, up_far, up_peer, projection_full, produced, down_side, up_own
        )
    )
    grad_expert_in = collect(returned_grad)
    (up_part,) = to_owners([up_far], "in")
    peers = lax.axis_size("hi")

    def hi_parts(value):
        return to_owners(list(value.astype(BF16).reshape(peers - 1, -1, width)), "hi")

    down_hi = hi_parts(add_all(down_peer, [down_part]))

    scaled_second = grad_expert_in * gain_second
    gain_second_part = jnp.sum(grad_expert_in * normed_second, axis=0)
    grad_middle = scale_second * (
        scaled_second
        - normed_second * jnp.mean(scaled_second * normed_second, axis=-1, keepdims=True)
    )
    residual_grad = upstream + grad_middle
    branch_grad = residual_grad.astype(BF16)
    grad_mixed = jnp.einsum(
        "td,ed->te", branch_grad, output_full, preferred_element_type=F32
    ).astype(BF16)

    sent_grad = jnp.stack([grad_mixed[:, s : s + LANES] for s in starts])
    row_grad = swap(sent_grad, SEQ).reshape(length, LANES)

    group = lax.axis_index(EXP)

    def group_rows(value):
        rows = value.reshape(count, groups, weight_rows, -1)
        own, *away = [
            lax.dynamic_index_in_dim(rows, lax.rem(group + step, groups), 1, keepdims=False)
            for step in range(groups)
        ]
        return own, away

    output_term = jnp.einsum("tc,te->ce", attend_out, branch_grad, preferred_element_type=F32)
    output_own, output_away = group_rows(output_term.astype(BF16))
    output_away = to_owners(output_away, "exp")
    row_grad, produced, down_side, up_side, up_part, *held = together(
        row_grad, produced, down_side, up_side, up_part, *down_hi, *output_away
    )
    down_hi, output_away = held[: peers - 1], held[peers - 1 :]
    (down_early,) = to_owners([down_side], "in")
    (up_early,) = to_owners([up_side], "in")
    up_hi = hi_parts(add_all(up_peer, [up_part]))
    returned = send_back(produced)
    grad_qkv, grad_lying = attend_back(
        active, order, pair, documents, stat, row_grad, mixed_full, row_count, scaling
    )
    grad_qkv, grad_lying, returned, down_early, up_early, *up_hi = together(
        grad_qkv, grad_lying, returned, down_early, up_early, *up_hi
    )
    down_grad = add_all(down_own, [down_early, *down_hi])[None]
    up_grad = add_all(up_own, [up_early, *up_hi])[None]
    block_output = (middle + collect(returned)).astype(BF16)[None]

    column_own, column_away = group_rows(column_terms(row_blocks, grad_lying))
    dense_rows = jnp.concatenate(
        [
            add_all(column_own, to_owners(column_away, "exp")).astype(BF16),
            add_all(output_own, output_away).astype(BF16),
        ],
        axis=2,
    )
    grad_pieces, dense_rows = together(to_tokens(grad_qkv), dense_rows)
    projection_grad, output_grad, dense_square = dense_grads(swap(dense_rows, SEQ), starts)
    input_grad, gain_first_part = close_norm(
        grad_pieces, starts, projection_full, tokens[0], gain_first[None], residual_grad
    )
    input_grad, gain_first_part = input_grad[None], gain_first_part[0]
    local_square = jnp.sum(up_grad * up_grad) + jnp.sum(down_grad * down_grad)
    summed = spread_sum(
        jnp.concatenate(
            [gain_first_part, gain_second_part, dense_square[0] + local_square]
        )[None]
    )[0]
    gains_grad = summed[: 2 * width].reshape(2, width)
    grad_norm = jnp.sqrt(summed[2 * width] + jnp.sum(gains_grad * gains_grad))
    factor = jnp.minimum(1.0, CLIP / (grad_norm + 1e-06))
    (
        (projection_moment, projection_square, projection_new),
        (output_moment, output_square, output_new),
        (up_moment, up_square, up_new),
        (down_moment, down_square, down_new),
    ) = adam_all(
        factor,
        [
            (projection, projection_grad, projection_first, projection_second),
            (output_weight, output_grad, output_first, output_second),
            (expert_up, up_grad, up_first, up_second),
            (expert_down, down_grad, down_first, down_second),
        ],
        (RATE_MATRIX, RATE_OUTPUT, RATE_MATRIX, RATE_MATRIX),
        6,
    )
    gains_moment, gains_square, gains_new = adam_update(
        norm_gains, gains_grad, gains_first, gains_second, factor, RATE_GAIN, 0.0
    )
    return (
        block_output,
        input_grad,
        grad_norm,
        projection_grad,
        projection_moment,
        projection_square,
        projection_new,
        output_grad,
        output_moment,
        output_square,
        output_new,
        up_grad,
        up_moment,
        up_square,
        up_new,
        down_grad,
        down_moment,
        down_square,
        down_new,
        gains_grad,
        gains_moment,
        gains_square,
        gains_new,
    )


def solution(mesh):
    token = P("exp", SEQ, None)
    dense = P(ALL, None)
    expert = P("exp", SEQ, None)
    in_specs = (
        (token, token, P("exp", SEQ), token)
        + (dense, dense, expert, expert, P())
        + (dense,) * 4
        + (expert,) * 4
        + (P(), P())
    )
    out_specs = (token, token, P()) + (dense,) * 8 + (expert,) * 8 + (P(),) * 4
    rows, groups = mesh.devices.shape
    fine = Mesh(mesh.devices.reshape(rows // 4, 2, 2, groups), ALL)
    return jax.shard_map(body, mesh=fine, in_specs=in_specs, out_specs=out_specs, check_vma=False)
```

```python
import functools
import math

import jax
import jax.numpy as jnp
import numpy as np
from jax import lax
from jax.experimental import pallas as pl
from jax.experimental.pallas import tpu as pltpu
from jax.sharding import Mesh
from jax.sharding import PartitionSpec as P

HEADS = 12
CAP = 128
STEP = 10


EPSILON = 1e-05
CLIP = 1.0
BETA_ONE = 0.9
BETA_TWO = 0.99
ADAM_FLOOR = 1e-08
DECAY = 0.1
RATE_MATRIX = 0.04
RATE_OUTPUT = 0.1
RATE_GAIN = 0.5

SEQ = ("hi", "lo", "in")
EXP = ("exp",)
ALL = SEQ + EXP
TEAM = ("lo",)
SHARE = ("hi", "in")
LANES = 128
HALF = 64
FAR = -1e30
BF16 = jnp.bfloat16
F32 = jnp.float32
MIB = 1024 * 1024


def room(length=0):
    return (24 if length <= 2048 else 60) * MIB


def head_plan(count):
    whole = math.lcm(HEADS, count)
    units, parts = whole // count, whole // HEADS
    first = np.zeros((count,), np.int64)
    active = np.zeros((count, 2, count), np.int32)
    for device in range(count):
        first[device] = min(units * device // parts, HEADS - 2)
        for unit in range(units * device, units * (device + 1)):
            slot = unit // parts - first[device]
            for block in range(count):
                turn = block % (2 * parts)
                if min(turn, 2 * parts - 1 - turn) == unit % parts:
                    active[device, slot, block] = 1
    return first, active


def three_parts(value):
    high = value.astype(BF16).astype(F32)
    middle = (value - high).astype(BF16).astype(F32)
    return high, middle, value - high - middle


def contract(left, right, left_axis, right_axis):
    return lax.dot_general(
        left, right, (((left_axis,), (right_axis,)), ((), ())), preferred_element_type=F32
    )


def slot_arrays(packed, documents, kind, slot):
    spare = HALF - HALF * slot
    lane = lax.broadcasted_iota(jnp.int32, packed.shape, 1)
    own = (lane < HALF) if slot == 0 else (lane >= HALF)
    place = (lane - spare).astype(F32)
    ours = place == documents
    first = (lane >= spare) & (lane < spare + 3)
    if kind == "query":
        extra = jnp.where(first & jnp.logical_not(ours), FAR, 0.0)
    elif kind == "key":
        extra = jnp.where(ours | ((lane >= spare + 3) & (lane < spare + 6)), 1.0, 0.0)
    else:
        extra = jnp.where(first, 1.0, 0.0)
    return jnp.where(own, packed, extra).astype(BF16)


def fill_slots(packed_of, documents_ref, wide_ref, kinds, place):
    documents = documents_ref[place, :].astype(F32)
    for number, kind in enumerate(kinds):
        packed = packed_of(kind).astype(F32)
        if kind == "query":
            packed = packed * 0.125
        for slot in range(2):
            column = (2 * number + slot) * LANES
            wide_ref[place, column : column + LANES] = slot_arrays(packed, documents, kind, slot)


def attend_kernel(active_ref, order_ref, *refs, block, chunk, held):
    row_refs = refs[:held]
    columns_ref, documents_ref = refs[held : held + 2]
    low_ref, full_ref, stat_ref, pair_ref, mixed_ref, wide_ref = refs[held + 2 :]
    at = pl.program_id(0)

    @pl.when(at == 0)
    def _():
        def fill(tokens, index):
            place = pl.ds(pl.multiple_of(order_ref[index] * block, block), block)
            packed = contract(tokens, columns_ref[...], 1, 0).astype(BF16)
            pair_ref[place, :] = packed[:, LANES:]
            parts = {
                kind: packed[:, part * LANES : (part + 1) * LANES]
                for part, kind in enumerate(("query", "key", "value"))
            }
            fill_slots(parts.get, documents_ref, wide_ref, tuple(parts), place)

        if held > 1:
            for index, row_ref in enumerate(row_refs):
                fill(row_ref[...], index)
        else:

            @pl.loop(0, pl.num_programs(0))
            def _(index):
                fill(row_refs[0][pl.ds(pl.multiple_of(index * block, block), block), :], index)

    rows = pl.ds(pl.multiple_of(at * block, block), block)
    lane = lax.broadcasted_iota(jnp.int32, (block, LANES), 1)
    last = lax.div(at * block, chunk)
    for slot in range(2):
        spare = HALF - HALF * slot
        own = (lane < HALF) if slot == 0 else (lane >= HALF)
        columns = slice(slot * LANES, (slot + 1) * LANES)

        @pl.when(active_ref[slot, at] != 0)
        def _():
            query = wide_ref[rows, columns]

            def step(index, carry, edge):
                top, weighted = carry
                place = pl.ds(pl.multiple_of(index * chunk, chunk), chunk)
                keys = wide_ref[place, 2 * LANES + slot * LANES : 3 * LANES + slot * LANES]
                values = wide_ref[place, 4 * LANES + slot * LANES : 5 * LANES + slot * LANES]
                scores = contract(query, keys, 1, 1)
                if edge:
                    key_at = index * chunk + lax.broadcasted_iota(jnp.int32, (block, chunk), 1)
                    query_at = at * block + lax.broadcasted_iota(jnp.int32, (block, chunk), 0)
                    scores = jnp.where(key_at <= query_at, scores, FAR)
                new_top = jnp.maximum(top, jnp.max(scores, axis=1, keepdims=True))
                weights = jnp.exp(scores - new_top).astype(BF16)
                weighted = weighted * jnp.exp(top - new_top) + contract(weights, values, 1, 0)
                return new_top, weighted

            carry = (jnp.full((block, 1), FAR, F32), jnp.zeros((block, LANES), F32))
            carry = lax.fori_loop(0, last, lambda index, state: step(index, state, False), carry)
            top, weighted = step(last, carry, True)
            total = weighted[:, spare : spare + 1]
            mixed_ref[slot] = jnp.where(own, weighted / total, 0.0)
            log_total = top + jnp.log(total)
            high, middle, small = three_parts(log_total)
            extra = jnp.where(lane == spare + 3, -high, 0.0)
            extra = jnp.where(lane == spare + 4, -middle, extra)
            extra = jnp.where(lane == spare + 5, -small, extra)
            stat_ref[:, columns] = (query.astype(F32) + extra).astype(BF16)

        @pl.when(active_ref[slot, at] == 0)
        def _():
            mixed_ref[slot] = jnp.zeros((block, LANES), F32)
            stat_ref[:, columns] = jnp.zeros((block, LANES), BF16)

    mixed = mixed_ref[0] + mixed_ref[1]
    full_ref[...] = mixed
    low_ref[...] = mixed.astype(BF16)


def attend_back_kernel(
    active_ref,
    order_ref,
    pair_ref,
    documents_ref,
    stat_ref,
    grad_ref,
    mixed_ref,
    out_ref,
    lying_ref,
    key_sum_ref,
    value_sum_ref,
    query_sum_ref,
    wide_ref,
    *,
    block,
    chunk,
    scaling,
):
    at = pl.program_id(0)
    rows = pl.ds(pl.multiple_of(at * block, block), block)
    lane = lax.broadcasted_iota(jnp.int32, (block, LANES), 1)
    last = lax.div(at * block, chunk)

    @pl.when(at == 0)
    def _():
        @pl.loop(0, pl.num_programs(0))
        def _(index):
            place = pl.ds(pl.multiple_of(index * block, block), block)
            parts = {"key": pair_ref[place, :LANES], "value": pair_ref[place, LANES:]}
            fill_slots(parts.get, documents_ref, wide_ref, tuple(parts), place)

        key_sum_ref[...] = jnp.zeros_like(key_sum_ref)
        value_sum_ref[...] = jnp.zeros_like(value_sum_ref)

    for slot in range(2):
        spare = HALF - HALF * slot
        own = (lane < HALF) if slot == 0 else (lane >= HALF)
        columns = slice(slot * LANES, (slot + 1) * LANES)
        query_sum_ref[slot] = jnp.zeros((block, LANES), F32)

        @pl.when(active_ref[slot, at] != 0)
        def _():
            query = stat_ref[:, columns]
            grad = grad_ref[...].astype(F32)
            delta = jnp.sum(jnp.where(own, grad * mixed_ref[...], 0.0), axis=1, keepdims=True)
            high, middle, small = three_parts(delta)
            extra = jnp.where(lane == spare, -high, 0.0)
            extra = jnp.where(lane == spare + 1, -middle, extra)
            extra = jnp.where(lane == spare + 2, -small, extra)
            grad_low = jnp.where(own, grad, extra).astype(BF16)

            def step(index, edge):
                place = pl.ds(pl.multiple_of(index * chunk, chunk), chunk)
                keys = wide_ref[place, slot * LANES : (slot + 1) * LANES]
                values = wide_ref[place, (2 + slot) * LANES : (3 + slot) * LANES]
                scores = contract(keys, query, 1, 1)
                if edge:
                    key_at = index * chunk + lax.broadcasted_iota(jnp.int32, (chunk, block), 0)
                    query_at = at * block + lax.broadcasted_iota(jnp.int32, (chunk, block), 1)
                    scores = jnp.where(key_at <= query_at, scores, FAR)
                weights = jnp.exp(scores)
                grad_weights = contract(values, grad_low, 1, 1)
                grad_scores = (weights * grad_weights).astype(BF16)
                value_sum_ref[slot, place, :] += contract(weights.astype(BF16), grad_low, 1, 0)
                key_sum_ref[slot, place, :] += contract(grad_scores, query, 1, 0)
                query_sum_ref[slot] += contract(grad_scores, keys, 0, 0)

            @pl.loop(0, last)
            def _(index):
                step(index, False)

            step(last, True)

    first_half = lane < HALF
    query_grad = jnp.where(first_half, query_sum_ref[0], query_sum_ref[1]) * scaling
    out_ref[rows, :LANES] = query_grad.astype(BF16)
    lying = pl.ds(pl.multiple_of(order_ref[at] * block, block), block)
    lying_ref[lying, :LANES] = query_grad.astype(BF16)

    @pl.when(at == pl.num_programs(0) - 1)
    def _():
        @pl.loop(0, pl.num_programs(0))
        def _(index):
            place = pl.ds(pl.multiple_of(index * block, block), block)
            key_grad = jnp.where(first_half, key_sum_ref[0, place, :], key_sum_ref[1, place, :])
            value_grad = jnp.where(
                first_half, value_sum_ref[0, place, :], value_sum_ref[1, place, :]
            )
            out_ref[place, LANES : 2 * LANES] = key_grad.astype(BF16)
            out_ref[place, 2 * LANES :] = value_grad.astype(BF16)
            lying = pl.ds(pl.multiple_of(order_ref[index] * block, block), block)
            lying_ref[lying, LANES : 2 * LANES] = key_grad.astype(BF16)
            lying_ref[lying, 2 * LANES :] = value_grad.astype(BF16)


def whole(value):
    return pl.BlockSpec(value.shape, lambda i, *unused: (0, 0), pipeline_mode=pl.Buffered(1))


SMALL = pl.CostEstimate(flops=1, bytes_accessed=1, transcendentals=0)


def attend(active, order, row_blocks, columns, documents, block):
    length = documents.shape[0]
    pair = jax.ShapeDtypeStruct((length, 2 * LANES), BF16)
    return pl.pallas_call(
        functools.partial(attend_kernel, block=block, chunk=2 * block, held=len(row_blocks)),
        grid_spec=pltpu.PrefetchScalarGridSpec(
            num_scalar_prefetch=2,
            grid=(length // block,),
            in_specs=[whole(value) for value in (*row_blocks, columns, documents)],
            out_specs=[
                pl.BlockSpec((block, LANES), lambda i, a, o: (i, 0)),
                pl.BlockSpec((block, LANES), lambda i, a, o: (i, 0)),
                pl.BlockSpec((block, 2 * LANES), lambda i, a, o: (i, 0)),
                whole(pair),
            ],
            scratch_shapes=[
                pltpu.VMEM((2, block, LANES), F32),
                pltpu.VMEM((length, 6 * LANES), BF16),
            ],
        ),
        out_shape=[
            jax.ShapeDtypeStruct((length, LANES), BF16),
            jax.ShapeDtypeStruct((length, LANES), F32),
            jax.ShapeDtypeStruct((length, 2 * LANES), BF16),
            pair,
        ],
        compiler_params=pltpu.CompilerParams(vmem_limit_bytes=room(length)),
        cost_estimate=SMALL,
    )(active, order, *row_blocks, columns, documents)


def attend_back(active, order, pair, documents, stat, grad, mixed, block, scaling):
    length = pair.shape[0]
    count = length // block
    return pl.pallas_call(
        functools.partial(attend_back_kernel, block=block, chunk=2 * block, scaling=scaling),
        grid_spec=pltpu.PrefetchScalarGridSpec(
            num_scalar_prefetch=2,
            grid=(count,),
            in_specs=[
                whole(pair),
                whole(documents),
                pl.BlockSpec((block, 2 * LANES), lambda i, a, o: (i, 0)),
                pl.BlockSpec((block, LANES), lambda i, a, o: (i, 0)),
                pl.BlockSpec((block, LANES), lambda i, a, o: (i, 0)),
            ],
            out_specs=[
                pl.BlockSpec(
                    (length, 3 * LANES), lambda i, a, o: (0, 0), pipeline_mode=pl.Buffered(1)
                )
            ]
            * 2,
            scratch_shapes=[
                pltpu.VMEM((2, length, LANES), F32),
                pltpu.VMEM((2, length, LANES), F32),
                pltpu.VMEM((2, block, LANES), F32),
                pltpu.VMEM((length, 4 * LANES), BF16),
            ],
        ),
        out_shape=[jax.ShapeDtypeStruct((length, 3 * LANES), BF16)] * 2,
        compiler_params=pltpu.CompilerParams(vmem_limit_bytes=room(length)),
        cost_estimate=SMALL,
    )(active, order, pair, documents, stat, grad, mixed)


def expert_kernel(arrived_ref, grad_ref, *refs, count):
    up_refs, down_refs = refs[:count], refs[count : 2 * count]
    total_ref = refs[2 * count]
    active_refs, hidden_refs = refs[2 * count + 1 : 3 * count + 1], refs[3 * count + 1 :]
    arrived, grad_arrived = arrived_ref[...], grad_ref[...]
    scale = math.sqrt(2.0 / math.pi)
    total = jnp.zeros(total_ref.shape, F32)
    for up_ref, down_ref, active_ref, hidden_ref in zip(
        up_refs, down_refs, active_refs, hidden_refs, strict=True
    ):
        up = up_ref[...]
        hidden = contract(arrived, up, 1, 1)
        squared = hidden * hidden
        bend = jnp.tanh(scale * hidden * (1.0 + 0.044715 * squared))
        half = 0.5 + 0.5 * bend
        active_ref[...] = (hidden * half).astype(BF16)
        slope = half + (0.5 * scale) * hidden * (1.0 - bend * bend) * (1.0 + 3 * 0.044715 * squared)
        grad_hidden = (slope * contract(grad_arrived, down_ref[...], 1, 1)).astype(BF16)
        hidden_ref[...] = grad_hidden
        total = total + contract(grad_hidden, up, 1, 0)
    total_ref[...] = total.astype(BF16)


def rows_spec(value, block):
    return pl.BlockSpec((block, value.shape[1]), lambda i: (i, 0))


def expert_part(arrived, grad_arrived, ups, downs):
    slots, width = arrived.shape
    block = 256
    units = [jax.ShapeDtypeStruct((slots, up.shape[0]), BF16) for up in ups]
    outs = [jax.ShapeDtypeStruct((slots, width), BF16), *units, *units]
    total, *parts = pl.pallas_call(
        functools.partial(expert_kernel, count=len(ups)),
        grid=(slots // block,),
        in_specs=[rows_spec(arrived, block), rows_spec(grad_arrived, block)]
        + [whole(value) for value in (*ups, *downs)],
        out_specs=[rows_spec(out, block) for out in outs],
        out_shape=outs,
        compiler_params=pltpu.CompilerParams(vmem_limit_bytes=room()),
        cost_estimate=SMALL,
    )(arrived, grad_arrived, *ups, *downs)
    return total, parts[: len(ups)], parts[len(ups) :]


def produced_kernel(*refs, count):
    total = contract(refs[0][...], refs[count][...], 1, 0)
    for index in range(1, count):
        total = total + contract(refs[index][...], refs[count + index][...], 1, 0)
    refs[-1][...] = total.astype(BF16)


def produced_part(actives, downs):
    slots, width = actives[0].shape[0], downs[0].shape[1]
    block = 256
    out = jax.ShapeDtypeStruct((slots, width), BF16)
    return pl.pallas_call(
        functools.partial(produced_kernel, count=len(actives)),
        grid=(slots // block,),
        in_specs=[rows_spec(value, block) for value in actives] + [whole(down) for down in downs],
        out_specs=rows_spec(out, block),
        out_shape=out,
        compiler_params=pltpu.CompilerParams(vmem_limit_bytes=room()),
        cost_estimate=SMALL,
    )(*actives, *downs)


def unit_kernel(grad_ref, arrived_ref, *refs, count):
    for index in range(count):
        active_ref, hidden_ref = refs[2 * index : 2 * index + 2]
        down_ref, up_ref = refs[2 * count + 2 * index : 2 * count + 2 * index + 2]
        down_ref[...] = contract(active_ref[...], grad_ref[...], 0, 0).astype(down_ref.dtype)
        up_ref[...] = contract(hidden_ref[...], arrived_ref[...], 0, 0).astype(up_ref.dtype)


def unit_grads(grad_arrived, arrived, blocks, kinds):
    slots, width = arrived.shape
    block = 256
    right = pl.BlockSpec((slots, block), lambda i: (0, i))
    outs = [
        jax.ShapeDtypeStruct((active.shape[1], width), kind)
        for (active, unused), kind in zip(blocks, kinds, strict=True)
        for part in range(2)
    ]
    flat = [value for pair in blocks for value in pair]
    return pl.pallas_call(
        functools.partial(unit_kernel, count=len(blocks)),
        grid=(width // block,),
        in_specs=[right, right] + [whole(value) for value in flat],
        out_specs=[pl.BlockSpec((out.shape[0], block), lambda i: (0, i)) for out in outs],
        out_shape=outs,
        compiler_params=pltpu.CompilerParams(vmem_limit_bytes=room()),
        cost_estimate=SMALL,
    )(grad_arrived, arrived, *flat)


def column_kernel(*refs, held):
    row_refs = refs[:held]
    lying_ref, out_ref = refs[held:]
    start, total = 0, None
    for row_ref in row_refs:
        rows = row_ref.shape[0]
        part = contract(row_ref[...], lying_ref[start : start + rows, :], 0, 0)
        total = part if total is None else total + part
        start += rows
    out_ref[...] = total.astype(BF16)


def column_terms(row_blocks, grad_lying):
    width = row_blocks[0].shape[1]
    block = 256
    out = jax.ShapeDtypeStruct((width, 3 * LANES), BF16)
    return pl.pallas_call(
        functools.partial(column_kernel, held=len(row_blocks)),
        grid=(width // block,),
        in_specs=[
            pl.BlockSpec((value.shape[0], block), lambda i: (0, i)) for value in row_blocks
        ]
        + [whole(grad_lying)],
        out_specs=rows_spec(out, block),
        out_shape=out,
        compiler_params=pltpu.CompilerParams(vmem_limit_bytes=room()),
        cost_estimate=SMALL,
    )(*row_blocks, grad_lying)


def close_kernel(
    pieces_ref, matrix_ref, tokens_ref, gain_ref, residual_ref, out_ref, part_ref, sum_ref, *, starts
):
    width = tokens_ref.shape[1]
    lane = lax.broadcasted_iota(jnp.int32, (tokens_ref.shape[0], LANES), 1)
    sum_ref[...] = jnp.zeros_like(sum_ref)
    for device, start in enumerate(starts):
        for part in range(3):
            piece = pieces_ref[device, :, part * LANES : (part + 1) * LANES].astype(F32)
            column = part * width + start
            if column % LANES == 0:
                sum_ref[:, column : column + LANES] += piece
            else:
                turned = pltpu.roll(piece, HALF, 1)
                low, high = column - HALF, column + HALF
                sum_ref[:, low : low + LANES] += jnp.where(lane >= HALF, turned, 0.0)
                sum_ref[:, high : high + LANES] += jnp.where(lane < HALF, turned, 0.0)
    grad = contract(sum_ref[...].astype(BF16), matrix_ref[...], 1, 1)
    inputs = tokens_ref[...].astype(F32)
    scale = lax.rsqrt(jnp.mean(inputs * inputs, axis=-1, keepdims=True) + EPSILON)
    normed = inputs * scale
    scaled = grad * gain_ref[...]
    mean = jnp.mean(scaled * normed, axis=-1, keepdims=True)
    out_ref[...] = residual_ref[...] + scale * (scaled - normed * mean)
    part_ref[...] = jnp.sum(grad * normed, axis=0, keepdims=True)


def close_norm(pieces, starts, matrix, tokens, gain, residual):
    rows, width = tokens.shape
    outs = [
        jax.ShapeDtypeStruct((rows, width), F32),
        jax.ShapeDtypeStruct((1, width), F32),
    ]
    return pl.pallas_call(
        functools.partial(close_kernel, starts=starts),
        in_specs=[pl.BlockSpec(memory_space=pltpu.VMEM)] * 5,
        out_specs=[pl.BlockSpec(memory_space=pltpu.VMEM)] * 2,
        out_shape=outs,
        scratch_shapes=[pltpu.VMEM((rows, 3 * width), F32)],
        compiler_params=pltpu.CompilerParams(vmem_limit_bytes=room()),
        cost_estimate=SMALL,
    )(pieces, matrix, tokens, gain, residual)


def dense_kernel(terms_ref, columns_ref, output_ref, square_ref, *, starts):
    width = output_ref.shape[1]
    columns_ref[...] = jnp.zeros_like(columns_ref)
    lane = lax.broadcasted_iota(jnp.int32, (columns_ref.shape[0], LANES), 1)
    output = jnp.zeros(output_ref.shape, F32)
    for device, start in enumerate(starts):
        output = output + terms_ref[device, :, 3 * LANES :].astype(F32)
        for part in range(3):
            piece = terms_ref[device, :, part * LANES : (part + 1) * LANES].astype(F32)
            column = part * width + start
            if column % LANES == 0:
                columns_ref[:, column : column + LANES] += piece
            else:
                turned = pltpu.roll(piece, HALF, 1)
                low, high = column - HALF, column + HALF
                columns_ref[:, low : low + LANES] += jnp.where(lane >= HALF, turned, 0.0)
                columns_ref[:, high : high + LANES] += jnp.where(lane < HALF, turned, 0.0)
    output_ref[...] = output
    columns = columns_ref[...]
    square_ref[...] = jnp.zeros_like(square_ref) + (
        jnp.sum(columns * columns) + jnp.sum(output * output)
    )


def dense_grads(terms, starts):
    unused, rows, lanes = terms.shape
    width = lanes - 3 * LANES
    outs = [jax.ShapeDtypeStruct((rows, columns), F32) for columns in (3 * width, width)]
    outs.append(jax.ShapeDtypeStruct((1, LANES), F32))
    return pl.pallas_call(
        functools.partial(dense_kernel, starts=starts),
        in_specs=[pl.BlockSpec(memory_space=pltpu.VMEM)],
        out_specs=[pl.BlockSpec(memory_space=pltpu.VMEM)] * 3,
        out_shape=outs,
        compiler_params=pltpu.CompilerParams(vmem_limit_bytes=room()),
        cost_estimate=SMALL,
    )(terms)


def adam_update(weight, grad, first, second, factor, rate, decay):
    clipped = grad * factor
    first_new = BETA_ONE * first + (1.0 - BETA_ONE) * clipped
    second_new = BETA_TWO * second + (1.0 - BETA_TWO) * clipped * clipped
    first_hat = first_new / (1.0 - BETA_ONE**STEP)
    second_hat = second_new / (1.0 - BETA_TWO**STEP)
    weight_new = weight - rate * (first_hat / (jnp.sqrt(second_hat) + ADAM_FLOOR) + decay * weight)
    return (first_new, second_new, weight_new)


def together(*values):
    return lax.optimization_barrier(values)


def swap(value, axes):
    return lax.all_to_all(value, axes, split_axis=0, concat_axis=0, tiled=True)


def adam_kernel(factor_ref, *refs, rates):
    count = len(rates)
    factor = factor_ref[0]
    for index, rate in enumerate(rates):
        weight, grad, first, second = [ref[...] for ref in refs[4 * index : 4 * index + 4]]
        outs = refs[4 * count + 3 * index : 4 * count + 3 * index + 3]
        for out, value in zip(
            outs, adam_update(weight, grad, first, second, factor, rate, DECAY), strict=True
        ):
            out[...] = value


def adam_all(factor, leaves, rates, steps):
    flat = [value.reshape(value.shape[-2:]) for leaf in leaves for value in leaf]

    def spec(value):
        rows, columns = value.shape
        if rows % (8 * steps) == 0:
            return pl.BlockSpec((rows // steps, columns), lambda i: (i, 0))
        lanes = columns // steps
        return pl.BlockSpec((rows, lanes), lambda i: (0, i))

    shapes = [jax.ShapeDtypeStruct(value.shape, F32) for value in flat[::4] for _ in range(3)]
    outs = pl.pallas_call(
        functools.partial(adam_kernel, rates=rates),
        grid=(steps,),
        in_specs=[pl.BlockSpec(memory_space=pltpu.SMEM)] + [spec(value) for value in flat],
        out_specs=[spec(shape) for shape in shapes],
        out_shape=shapes,
        compiler_params=pltpu.CompilerParams(vmem_limit_bytes=room()),
        cost_estimate=pl.CostEstimate(
            flops=20 * sum(value.size for value in flat[::4]),
            bytes_accessed=28 * sum(value.size for value in flat[::4]),
            transcendentals=0,
        ),
    )(factor.reshape(1), *flat)
    return [
        [out.reshape(leaf[0].shape) for out in outs[3 * index : 3 * index + 3]]
        for index, leaf in enumerate(leaves)
    ]


def flip(value, bits):
    count = lax.axis_size(SEQ)
    return lax.ppermute(value, SEQ, [(index, index ^ bits) for index in range(count)])


def others(value, axis):
    size = lax.axis_size(axis)
    parts = [
        lax.ppermute(value, axis, [((i + step) % size, i) for i in range(size)])
        for step in range(1, size)
    ]
    return parts[0] if size == 2 else jnp.concatenate(parts, axis=0)


def to_owners(blocks, axis):
    size = lax.axis_size(axis)
    return [
        lax.ppermute(block, axis, [(i, (i + step) % size) for i in range(size)])
        for step, block in enumerate(blocks, 1)
    ]


def add_all(own, parts):
    return functools.reduce(lambda total, part: total + part.astype(F32), parts, own.astype(F32))


def spread_sum(value):
    count = lax.axis_size(ALL)
    return jnp.sum(swap(jnp.broadcast_to(value[None], (count, *value.shape)), ALL), axis=0)


def body(
    tokens,
    cotangent,
    segment_ids,
    expert_ids,
    projection,
    output_weight,
    expert_up,
    expert_down,
    norm_gains,
    projection_first,
    projection_second,
    output_first,
    output_second,
    up_first,
    up_second,
    down_first,
    down_second,
    gains_first,
    gains_second,
):
    inputs = tokens[0].astype(F32)
    upstream = cotangent[0].astype(F32)
    row_count = inputs.shape[0]
    width = inputs.shape[1]
    head_size = width // HEADS
    scaling = head_size ** (-0.5)
    count = lax.axis_size(SEQ)
    groups = lax.axis_size("exp")
    team = lax.axis_size(TEAM)
    position = lax.axis_index(SEQ)
    length = count * row_count
    weight_rows = projection.shape[0]
    first_heads, active_table = head_plan(count)
    starts = [int(head) * head_size for head in first_heads]
    active = lax.dynamic_index_in_dim(jnp.asarray(active_table), position, 0, keepdims=False)
    gain_first = norm_gains[0]
    gain_second = norm_gains[1]
    used = active_table.any(axis=2)

    scale_first = lax.rsqrt(jnp.mean(inputs * inputs, axis=-1, keepdims=True) + EPSILON)
    normed_first = inputs * scale_first
    attend_in = (normed_first * gain_first).astype(BF16)
    slots = groups * CAP
    chosen = expert_ids[0, :, 0]
    one_hot = (chosen[:, None] == jnp.arange(groups, dtype=jnp.int32)[None, :]).astype(F32)
    token = jnp.arange(row_count, dtype=jnp.int32)
    earlier = (token[None, :] < token[:, None]).astype(BF16)
    counts = jnp.dot(earlier, one_hot.astype(BF16), preferred_element_type=F32)
    rank = jnp.sum(counts * one_hot, axis=1).astype(jnp.int32)
    target = chosen * CAP + rank
    placing = (target[:, None] == jnp.arange(slots, dtype=jnp.int32)[None, :]).astype(BF16)

    def to_slots(values):
        outgoing = jnp.einsum("ts,td->sd", placing, values, preferred_element_type=F32)
        return outgoing.astype(BF16)

    def dispatch(outgoing):
        outgoing = jnp.broadcast_to(
            outgoing.reshape(1, groups, CAP, width), (team, groups, CAP, width)
        )
        return swap(outgoing.reshape(team * groups, CAP, width), TEAM + EXP).reshape(
            team * slots, width
        )

    def send_back(values):
        return swap(values.reshape(team * groups, CAP, width), TEAM + EXP).reshape(
            team, slots, width
        )

    def collect(returned):
        return jnp.einsum("ts,jsd->td", placing, returned, preferred_element_type=F32)

    projection_low = projection.astype(BF16)
    sent_rows = weight_rows + 8
    own_documents = jnp.zeros((8, 3 * LANES + width), BF16)
    own_documents = own_documents.at[0, :row_count].set(segment_ids[0].astype(BF16))
    output_low = output_weight.astype(BF16)
    pieces = [
        jnp.concatenate(
            [projection_low[:, k * width + s : k * width + s + LANES] for k in range(3)]
            + [output_low],
            axis=1,
        )
        for s in starts
    ]
    pieces = jnp.stack([jnp.concatenate([piece, own_documents], axis=0) for piece in pieces])
    own_up = expert_up[0].astype(BF16)
    own_down = expert_down[0].astype(BF16)
    pairwise = count == 8
    if pairwise:
        order = jnp.arange(count, dtype=jnp.int32) ^ position
        beside, below, across = flip(attend_in, 1), flip(attend_in, 2), flip(attend_in, 4)
        got_rows, beside, below, across, own_up = together(
            swap(pieces, SEQ), beside, below, across, own_up
        )
        corner = flip(across, 2)
        row_blocks = [attend_in, beside]
        row_blocks += [part for block in (below, across, corner) for part in (block, flip(block, 1))]
    else:
        order = jnp.arange(count, dtype=jnp.int32)
        row_blocks = [lax.all_gather(attend_in, SEQ, axis=0, tiled=True)]
        got_rows = swap(pieces, SEQ)
    documents = jnp.broadcast_to(
        got_rows[:, weight_rows, :row_count].reshape(length, 1), (length, LANES)
    )
    own_copies = jnp.broadcast_to(
        got_rows[None, :, :weight_rows], (groups, count, weight_rows, 3 * LANES + width)
    )
    all_copies = swap(own_copies, EXP)

    peer_up = others(own_up, "hi")
    *row_blocks, all_copies, peer_up, own_up, own_down, grad_slots_out = together(
        *row_blocks, all_copies, peer_up, own_up, own_down, to_slots(cotangent[0])
    )
    all_copies = jnp.swapaxes(all_copies, 0, 1)
    columns = all_copies[..., : 3 * LANES].reshape(width, 3 * LANES)
    output_full = all_copies[..., 3 * LANES :].reshape(width, width)
    grad_arrived = dispatch(grad_slots_out)
    peer_down = others(own_down, "hi")
    side_up = others(own_up, "in")
    side_down = others(own_down, "in")
    far_up = others(peer_up, "in")

    mixed_low, mixed_full, stat, pair = attend(
        active, order, row_blocks, columns, documents, row_count
    )

    def place_heads():
        index = np.arange(LANES)
        matrix = np.zeros((count, LANES, width), np.float32)
        for device in range(count):
            for slot in range(2):
                if used[device, slot]:
                    own = index[slot * HALF : (slot + 1) * HALF]
                    matrix[device, own, starts[device] + own] = 1.0
        return jnp.asarray(matrix, BF16)

    head_places = place_heads()

    def to_tokens(values):
        return swap(values.reshape(count, row_count, values.shape[1]), SEQ)

    mixed_low, grad_arrived, peer_down, side_up, side_down, far_up = together(
        mixed_low, grad_arrived, peer_down, side_up, side_down, far_up
    )
    far_down = others(peer_down, "in")
    mixed_pieces, projection_low, far_down = together(
        to_tokens(mixed_low), projection_low, far_down
    )
    projection_full = lax.all_gather(projection_low, ALL, axis=0, tiled=True)
    attend_out = jnp.einsum(
        "jtc,jcd->td", mixed_pieces, head_places, preferred_element_type=F32
    ).astype(BF16)
    branch = jnp.dot(attend_out, output_full, preferred_element_type=F32)
    middle = inputs + branch
    scale_second = lax.rsqrt(jnp.mean(middle * middle, axis=-1, keepdims=True) + EPSILON)
    normed_second = middle * scale_second
    expert_in = (normed_second * gain_second).astype(BF16)

    arrived = dispatch(to_slots(expert_in))
    ups, downs = (own_up, peer_up, side_up, far_up), (own_down, peer_down, side_down, far_down)
    grad_slots, actives, hiddens = expert_part(arrived, grad_arrived, ups, downs)
    returned_grad = send_back(grad_slots)

    blocks = list(zip(actives, hiddens, strict=True))
    down_far, up_far, down_peer, up_peer = unit_grads(
        grad_arrived, arrived, (blocks[3], blocks[1]), (BF16, F32)
    )
    (down_part,) = to_owners([down_far], "in")
    down_side, up_side, down_own, up_own = unit_grads(
        grad_arrived, arrived, (blocks[2], blocks[0]), (BF16, F32)
    )
    produced = produced_part(actives, downs)
    returned_grad, down_part, up_far, up_peer, projection_full, produced, down_side, up_own = (
        together(
            returned_grad, down_part, up_far, up_peer, projection_full, produced, down_side, up_own
        )
    )
    grad_expert_in = collect(returned_grad)
    (up_part,) = to_owners([up_far], "in")
    peers = lax.axis_size("hi")

    def hi_parts(value):
        return to_owners(list(value.astype(BF16).reshape(peers - 1, -1, width)), "hi")

    down_hi = hi_parts(add_all(down_peer, [down_part]))

    scaled_second = grad_expert_in * gain_second
    gain_second_part = jnp.sum(grad_expert_in * normed_second, axis=0)
    grad_middle = scale_second * (
        scaled_second
        - normed_second * jnp.mean(scaled_second * normed_second, axis=-1, keepdims=True)
    )
    residual_grad = upstream + grad_middle
    branch_grad = residual_grad.astype(BF16)
    grad_mixed = jnp.einsum(
        "td,ed->te", branch_grad, output_full, preferred_element_type=F32
    ).astype(BF16)

    sent_grad = jnp.stack([grad_mixed[:, s : s + LANES] for s in starts])
    row_grad = swap(sent_grad, SEQ).reshape(length, LANES)

    group = lax.axis_index(EXP)

    def group_rows(value):
        rows = value.reshape(count, groups, weight_rows, -1)
        own, *away = [
            lax.dynamic_index_in_dim(rows, lax.rem(group + step, groups), 1, keepdims=False)
            for step in range(groups)
        ]
        return own, away

    output_term = jnp.einsum("tc,te->ce", attend_out, branch_grad, preferred_element_type=F32)
    output_own, output_away = group_rows(output_term.astype(BF16))
    output_away = to_owners(output_away, "exp")
    row_grad, produced, down_side, up_side, up_part, *held = together(
        row_grad, produced, down_side, up_side, up_part, *down_hi, *output_away
    )
    down_hi, output_away = held[: peers - 1], held[peers - 1 :]
    (down_early,) = to_owners([down_side], "in")
    (up_early,) = to_owners([up_side], "in")
    up_hi = hi_parts(add_all(up_peer, [up_part]))
    returned = send_back(produced)
    grad_qkv, grad_lying = attend_back(
        active, order, pair, documents, stat, row_grad, mixed_full, row_count, scaling
    )
    grad_qkv, grad_lying, returned, down_early, up_early, *up_hi = together(
        grad_qkv, grad_lying, returned, down_early, up_early, *up_hi
    )
    down_grad = add_all(down_own, [down_early, *down_hi])[None]
    up_grad = add_all(up_own, [up_early, *up_hi])[None]
    block_output = (middle + collect(returned)).astype(BF16)[None]

    column_own, column_away = group_rows(column_terms(row_blocks, grad_lying))
    dense_rows = jnp.concatenate(
        [
            add_all(column_own, to_owners(column_away, "exp")).astype(BF16),
            add_all(output_own, output_away).astype(BF16),
        ],
        axis=2,
    )
    local_square = jnp.sum(up_grad * up_grad) + jnp.sum(down_grad * down_grad)
    grad_pieces, dense_rows, local_square = together(
        to_tokens(grad_qkv), dense_rows, local_square
    )
    projection_grad, output_grad, dense_square = dense_grads(swap(dense_rows, SEQ), starts)
    input_grad, gain_first_part = close_norm(
        grad_pieces, starts, projection_full, tokens[0], gain_first[None], residual_grad
    )
    input_grad, gain_first_part = input_grad[None], gain_first_part[0]
    summed = spread_sum(
        jnp.concatenate(
            [gain_first_part, gain_second_part, dense_square[0] + local_square]
        )[None]
    )[0]
    gains_grad = summed[: 2 * width].reshape(2, width)
    grad_norm = jnp.sqrt(summed[2 * width] + jnp.sum(gains_grad * gains_grad))
    factor = jnp.minimum(1.0, CLIP / (grad_norm + 1e-06))
    (
        (projection_moment, projection_square, projection_new),
        (output_moment, output_square, output_new),
        (up_moment, up_square, up_new),
        (down_moment, down_square, down_new),
    ) = adam_all(
        factor,
        [
            (projection, projection_grad, projection_first, projection_second),
            (output_weight, output_grad, output_first, output_second),
            (expert_up, up_grad, up_first, up_second),
            (expert_down, down_grad, down_first, down_second),
        ],
        (RATE_MATRIX, RATE_OUTPUT, RATE_MATRIX, RATE_MATRIX),
        6,
    )
    gains_moment, gains_square, gains_new = adam_update(
        norm_gains, gains_grad, gains_first, gains_second, factor, RATE_GAIN, 0.0
    )
    return (
        block_output,
        input_grad,
        grad_norm,
        projection_grad,
        projection_moment,
        projection_square,
        projection_new,
        output_grad,
        output_moment,
        output_square,
        output_new,
        up_grad,
        up_moment,
        up_square,
        up_new,
        down_grad,
        down_moment,
        down_square,
        down_new,
        gains_grad,
        gains_moment,
        gains_square,
        gains_new,
    )


def solution(mesh):
    token = P("exp", SEQ, None)
    dense = P(ALL, None)
    expert = P("exp", SEQ, None)
    in_specs = (
        (token, token, P("exp", SEQ), token)
        + (dense, dense, expert, expert, P())
        + (dense,) * 4
        + (expert,) * 4
        + (P(), P())
    )
    out_specs = (token, token, P()) + (dense,) * 8 + (expert,) * 8 + (P(),) * 4
    rows, groups = mesh.devices.shape
    fine = Mesh(mesh.devices.reshape(rows // 4, 2, 2, groups), ALL)
    return jax.shard_map(body, mesh=fine, in_specs=in_specs, out_specs=out_specs, check_vma=False)
```

```python
import functools
import math

import jax
import jax.numpy as jnp
import numpy as np
from jax import lax
from jax.experimental import pallas as pl
from jax.experimental.pallas import tpu as pltpu
from jax.sharding import Mesh
from jax.sharding import PartitionSpec as P

HEADS = 12
CAP = 128
STEP = 10


EPSILON = 1e-05
CLIP = 1.0
BETA_ONE = 0.9
BETA_TWO = 0.99
ADAM_FLOOR = 1e-08
DECAY = 0.1
RATE_MATRIX = 0.04
RATE_OUTPUT = 0.1
RATE_GAIN = 0.5

SEQ = ("hi", "lo", "in")
EXP = ("exp",)
ALL = SEQ + EXP
TEAM = ("lo",)
SHARE = ("hi", "in")
LANES = 128
HALF = 64
FAR = -1e30
BF16 = jnp.bfloat16
F32 = jnp.float32
VMEM_LIMIT = 60 * 1024 * 1024


def head_plan(count):
    whole = math.lcm(HEADS, count)
    units, parts = whole // count, whole // HEADS
    first = np.zeros((count,), np.int64)
    active = np.zeros((count, 2, count), np.int32)
    for device in range(count):
        first[device] = min(units * device // parts, HEADS - 2)
        for unit in range(units * device, units * (device + 1)):
            slot = unit // parts - first[device]
            for block in range(count):
                turn = block % (2 * parts)
                if min(turn, 2 * parts - 1 - turn) == unit % parts:
                    active[device, slot, block] = 1
    return first, active


def three_parts(value):
    high = value.astype(BF16).astype(F32)
    middle = (value - high).astype(BF16).astype(F32)
    return high, middle, value - high - middle


def contract(left, right, left_axis, right_axis):
    return lax.dot_general(
        left, right, (((left_axis,), (right_axis,)), ((), ())), preferred_element_type=F32
    )


def slot_arrays(packed, documents, kind, slot):
    spare = HALF - HALF * slot
    lane = lax.broadcasted_iota(jnp.int32, packed.shape, 1)
    own = (lane < HALF) if slot == 0 else (lane >= HALF)
    place = (lane - spare).astype(F32)
    ours = place == documents
    first = (lane >= spare) & (lane < spare + 3)
    if kind == "query":
        extra = jnp.where(first & jnp.logical_not(ours), FAR, 0.0)
    elif kind == "key":
        extra = jnp.where(ours | ((lane >= spare + 3) & (lane < spare + 6)), 1.0, 0.0)
    else:
        extra = jnp.where(first, 1.0, 0.0)
    return jnp.where(own, packed, extra).astype(BF16)


def fill_slots(packed_of, documents_ref, wide_ref, kinds, place):
    documents = documents_ref[place, :].astype(F32)
    for number, kind in enumerate(kinds):
        packed = packed_of(kind).astype(F32)
        if kind == "query":
            packed = packed * 0.125
        for slot in range(2):
            column = (2 * number + slot) * LANES
            wide_ref[place, column : column + LANES] = slot_arrays(packed, documents, kind, slot)


def attend_kernel(active_ref, order_ref, *refs, block, chunk, held):
    row_refs = refs[:held]
    columns_ref, documents_ref = refs[held : held + 2]
    low_ref, full_ref, stat_ref, pair_ref, mixed_ref, wide_ref = refs[held + 2 :]
    at = pl.program_id(0)

    @pl.when(at == 0)
    def _():
        def fill(tokens, index):
            place = pl.ds(pl.multiple_of(order_ref[index] * block, block), block)
            packed = contract(tokens, columns_ref[...], 1, 0).astype(BF16)
            pair_ref[place, :] = packed[:, LANES:]
            parts = {
                kind: packed[:, part * LANES : (part + 1) * LANES]
                for part, kind in enumerate(("query", "key", "value"))
            }
            fill_slots(parts.get, documents_ref, wide_ref, tuple(parts), place)

        if held > 1:
            for index, row_ref in enumerate(row_refs):
                fill(row_ref[...], index)
        else:

            @pl.loop(0, pl.num_programs(0))
            def _(index):
                fill(row_refs[0][pl.ds(pl.multiple_of(index * block, block), block), :], index)

    rows = pl.ds(pl.multiple_of(at * block, block), block)
    lane = lax.broadcasted_iota(jnp.int32, (block, LANES), 1)
    last = lax.div(at * block, chunk)
    for slot in range(2):
        spare = HALF - HALF * slot
        own = (lane < HALF) if slot == 0 else (lane >= HALF)
        columns = slice(slot * LANES, (slot + 1) * LANES)

        @pl.when(active_ref[slot, at] != 0)
        def _():
            query = wide_ref[rows, columns]

            def step(index, carry, edge):
                top, weighted = carry
                place = pl.ds(pl.multiple_of(index * chunk, chunk), chunk)
                keys = wide_ref[place, 2 * LANES + slot * LANES : 3 * LANES + slot * LANES]
                values = wide_ref[place, 4 * LANES + slot * LANES : 5 * LANES + slot * LANES]
                scores = contract(query, keys, 1, 1)
                if edge:
                    key_at = index * chunk + lax.broadcasted_iota(jnp.int32, (block, chunk), 1)
                    query_at = at * block + lax.broadcasted_iota(jnp.int32, (block, chunk), 0)
                    scores = jnp.where(key_at <= query_at, scores, FAR)
                new_top = jnp.maximum(top, jnp.max(scores, axis=1, keepdims=True))
                weights = jnp.exp(scores - new_top).astype(BF16)
                weighted = weighted * jnp.exp(top - new_top) + contract(weights, values, 1, 0)
                return new_top, weighted

            carry = (jnp.full((block, 1), FAR, F32), jnp.zeros((block, LANES), F32))
            carry = lax.fori_loop(0, last, lambda index, state: step(index, state, False), carry)
            top, weighted = step(last, carry, True)
            total = weighted[:, spare : spare + 1]
            mixed_ref[slot] = jnp.where(own, weighted / total, 0.0)
            log_total = top + jnp.log(total)
            high, middle, small = three_parts(log_total)
            extra = jnp.where(lane == spare + 3, -high, 0.0)
            extra = jnp.where(lane == spare + 4, -middle, extra)
            extra = jnp.where(lane == spare + 5, -small, extra)
            stat_ref[:, columns] = (query.astype(F32) + extra).astype(BF16)

        @pl.when(active_ref[slot, at] == 0)
        def _():
            mixed_ref[slot] = jnp.zeros((block, LANES), F32)
            stat_ref[:, columns] = jnp.zeros((block, LANES), BF16)

    mixed = mixed_ref[0] + mixed_ref[1]
    full_ref[...] = mixed
    low_ref[...] = mixed.astype(BF16)


def attend_back_kernel(
    active_ref,
    order_ref,
    pair_ref,
    documents_ref,
    stat_ref,
    grad_ref,
    mixed_ref,
    out_ref,
    lying_ref,
    key_sum_ref,
    value_sum_ref,
    query_sum_ref,
    wide_ref,
    *,
    block,
    chunk,
    scaling,
):
    at = pl.program_id(0)
    rows = pl.ds(pl.multiple_of(at * block, block), block)
    lane = lax.broadcasted_iota(jnp.int32, (block, LANES), 1)
    last = lax.div(at * block, chunk)

    @pl.when(at == 0)
    def _():
        @pl.loop(0, pl.num_programs(0))
        def _(index):
            place = pl.ds(pl.multiple_of(index * block, block), block)
            parts = {"key": pair_ref[place, :LANES], "value": pair_ref[place, LANES:]}
            fill_slots(parts.get, documents_ref, wide_ref, tuple(parts), place)

        key_sum_ref[...] = jnp.zeros_like(key_sum_ref)
        value_sum_ref[...] = jnp.zeros_like(value_sum_ref)

    for slot in range(2):
        spare = HALF - HALF * slot
        own = (lane < HALF) if slot == 0 else (lane >= HALF)
        columns = slice(slot * LANES, (slot + 1) * LANES)
        query_sum_ref[slot] = jnp.zeros((block, LANES), F32)

        @pl.when(active_ref[slot, at] != 0)
        def _():
            query = stat_ref[:, columns]
            grad = grad_ref[...].astype(F32)
            delta = jnp.sum(jnp.where(own, grad * mixed_ref[...], 0.0), axis=1, keepdims=True)
            high, middle, small = three_parts(delta)
            extra = jnp.where(lane == spare, -high, 0.0)
            extra = jnp.where(lane == spare + 1, -middle, extra)
            extra = jnp.where(lane == spare + 2, -small, extra)
            grad_low = jnp.where(own, grad, extra).astype(BF16)

            def step(index, edge):
                place = pl.ds(pl.multiple_of(index * chunk, chunk), chunk)
                keys = wide_ref[place, slot * LANES : (slot + 1) * LANES]
                values = wide_ref[place, (2 + slot) * LANES : (3 + slot) * LANES]
                scores = contract(keys, query, 1, 1)
                if edge:
                    key_at = index * chunk + lax.broadcasted_iota(jnp.int32, (chunk, block), 0)
                    query_at = at * block + lax.broadcasted_iota(jnp.int32, (chunk, block), 1)
                    scores = jnp.where(key_at <= query_at, scores, FAR)
                weights = jnp.exp(scores)
                grad_weights = contract(values, grad_low, 1, 1)
                grad_scores = (weights * grad_weights).astype(BF16)
                value_sum_ref[slot, place, :] += contract(weights.astype(BF16), grad_low, 1, 0)
                key_sum_ref[slot, place, :] += contract(grad_scores, query, 1, 0)
                query_sum_ref[slot] += contract(grad_scores, keys, 0, 0)

            @pl.loop(0, last)
            def _(index):
                step(index, False)

            step(last, True)

    first_half = lane < HALF
    query_grad = jnp.where(first_half, query_sum_ref[0], query_sum_ref[1]) * scaling
    out_ref[rows, :LANES] = query_grad.astype(BF16)
    lying = pl.ds(pl.multiple_of(order_ref[at] * block, block), block)
    lying_ref[lying, :LANES] = query_grad.astype(BF16)

    @pl.when(at == pl.num_programs(0) - 1)
    def _():
        @pl.loop(0, pl.num_programs(0))
        def _(index):
            place = pl.ds(pl.multiple_of(index * block, block), block)
            key_grad = jnp.where(first_half, key_sum_ref[0, place, :], key_sum_ref[1, place, :])
            value_grad = jnp.where(
                first_half, value_sum_ref[0, place, :], value_sum_ref[1, place, :]
            )
            out_ref[place, LANES : 2 * LANES] = key_grad.astype(BF16)
            out_ref[place, 2 * LANES :] = value_grad.astype(BF16)
            lying = pl.ds(pl.multiple_of(order_ref[index] * block, block), block)
            lying_ref[lying, LANES : 2 * LANES] = key_grad.astype(BF16)
            lying_ref[lying, 2 * LANES :] = value_grad.astype(BF16)


def whole(value):
    return pl.BlockSpec(value.shape, lambda i, *unused: (0, 0), pipeline_mode=pl.Buffered(1))


SMALL = pl.CostEstimate(flops=1, bytes_accessed=1, transcendentals=0)


def attend(active, order, row_blocks, columns, documents, block):
    length = documents.shape[0]
    pair = jax.ShapeDtypeStruct((length, 2 * LANES), BF16)
    return pl.pallas_call(
        functools.partial(attend_kernel, block=block, chunk=2 * block, held=len(row_blocks)),
        grid_spec=pltpu.PrefetchScalarGridSpec(
            num_scalar_prefetch=2,
            grid=(length // block,),
            in_specs=[whole(value) for value in (*row_blocks, columns, documents)],
            out_specs=[
                pl.BlockSpec((block, LANES), lambda i, a, o: (i, 0)),
                pl.BlockSpec((block, LANES), lambda i, a, o: (i, 0)),
                pl.BlockSpec((block, 2 * LANES), lambda i, a, o: (i, 0)),
                whole(pair),
            ],
            scratch_shapes=[
                pltpu.VMEM((2, block, LANES), F32),
                pltpu.VMEM((length, 6 * LANES), BF16),
            ],
        ),
        out_shape=[
            jax.ShapeDtypeStruct((length, LANES), BF16),
            jax.ShapeDtypeStruct((length, LANES), F32),
            jax.ShapeDtypeStruct((length, 2 * LANES), BF16),
            pair,
        ],
        compiler_params=pltpu.CompilerParams(vmem_limit_bytes=VMEM_LIMIT),
        cost_estimate=SMALL,
    )(active, order, *row_blocks, columns, documents)


def attend_back(active, order, pair, documents, stat, grad, mixed, block, scaling):
    length = pair.shape[0]
    count = length // block
    return pl.pallas_call(
        functools.partial(attend_back_kernel, block=block, chunk=2 * block, scaling=scaling),
        grid_spec=pltpu.PrefetchScalarGridSpec(
            num_scalar_prefetch=2,
            grid=(count,),
            in_specs=[
                whole(pair),
                whole(documents),
                pl.BlockSpec((block, 2 * LANES), lambda i, a, o: (i, 0)),
                pl.BlockSpec((block, LANES), lambda i, a, o: (i, 0)),
                pl.BlockSpec((block, LANES), lambda i, a, o: (i, 0)),
            ],
            out_specs=[
                pl.BlockSpec(
                    (length, 3 * LANES), lambda i, a, o: (0, 0), pipeline_mode=pl.Buffered(1)
                )
            ]
            * 2,
            scratch_shapes=[
                pltpu.VMEM((2, length, LANES), F32),
                pltpu.VMEM((2, length, LANES), F32),
                pltpu.VMEM((2, block, LANES), F32),
                pltpu.VMEM((length, 4 * LANES), BF16),
            ],
        ),
        out_shape=[jax.ShapeDtypeStruct((length, 3 * LANES), BF16)] * 2,
        compiler_params=pltpu.CompilerParams(vmem_limit_bytes=VMEM_LIMIT),
        cost_estimate=SMALL,
    )(active, order, pair, documents, stat, grad, mixed)


def expert_kernel(arrived_ref, grad_ref, *refs, count):
    up_refs, down_refs = refs[:count], refs[count : 2 * count]
    total_ref = refs[2 * count]
    active_refs, hidden_refs = refs[2 * count + 1 : 3 * count + 1], refs[3 * count + 1 :]
    arrived, grad_arrived = arrived_ref[...], grad_ref[...]
    scale = math.sqrt(2.0 / math.pi)
    total = jnp.zeros(total_ref.shape, F32)
    for up_ref, down_ref, active_ref, hidden_ref in zip(
        up_refs, down_refs, active_refs, hidden_refs, strict=True
    ):
        up = up_ref[...]
        hidden = contract(arrived, up, 1, 1)
        squared = hidden * hidden
        bend = jnp.tanh(scale * hidden * (1.0 + 0.044715 * squared))
        half = 0.5 + 0.5 * bend
        active_ref[...] = (hidden * half).astype(BF16)
        slope = half + (0.5 * scale) * hidden * (1.0 - bend * bend) * (1.0 + 3 * 0.044715 * squared)
        grad_hidden = (slope * contract(grad_arrived, down_ref[...], 1, 1)).astype(BF16)
        hidden_ref[...] = grad_hidden
        total = total + contract(grad_hidden, up, 1, 0)
    total_ref[...] = total.astype(BF16)


def rows_spec(value, block):
    return pl.BlockSpec((block, value.shape[1]), lambda i: (i, 0))


def expert_part(arrived, grad_arrived, ups, downs):
    slots, width = arrived.shape
    block = 256
    units = [jax.ShapeDtypeStruct((slots, up.shape[0]), BF16) for up in ups]
    outs = [jax.ShapeDtypeStruct((slots, width), BF16), *units, *units]
    total, *parts = pl.pallas_call(
        functools.partial(expert_kernel, count=len(ups)),
        grid=(slots // block,),
        in_specs=[rows_spec(arrived, block), rows_spec(grad_arrived, block)]
        + [whole(value) for value in (*ups, *downs)],
        out_specs=[rows_spec(out, block) for out in outs],
        out_shape=outs,
        compiler_params=pltpu.CompilerParams(vmem_limit_bytes=VMEM_LIMIT),
        cost_estimate=SMALL,
    )(arrived, grad_arrived, *ups, *downs)
    return total, parts[: len(ups)], parts[len(ups) :]


def produced_kernel(*refs, count):
    total = contract(refs[0][...], refs[count][...], 1, 0)
    for index in range(1, count):
        total = total + contract(refs[index][...], refs[count + index][...], 1, 0)
    refs[-1][...] = total.astype(BF16)


def produced_part(actives, downs):
    slots, width = actives[0].shape[0], downs[0].shape[1]
    block = 256
    out = jax.ShapeDtypeStruct((slots, width), BF16)
    return pl.pallas_call(
        functools.partial(produced_kernel, count=len(actives)),
        grid=(slots // block,),
        in_specs=[rows_spec(value, block) for value in actives] + [whole(down) for down in downs],
        out_specs=rows_spec(out, block),
        out_shape=out,
        compiler_params=pltpu.CompilerParams(vmem_limit_bytes=VMEM_LIMIT),
        cost_estimate=SMALL,
    )(*actives, *downs)


def unit_kernel(grad_ref, arrived_ref, *refs, count):
    for index in range(count):
        active_ref, hidden_ref = refs[2 * index : 2 * index + 2]
        down_ref, up_ref = refs[2 * count + 2 * index : 2 * count + 2 * index + 2]
        down_ref[...] = contract(active_ref[...], grad_ref[...], 0, 0).astype(down_ref.dtype)
        up_ref[...] = contract(hidden_ref[...], arrived_ref[...], 0, 0).astype(up_ref.dtype)


def unit_grads(grad_arrived, arrived, blocks, kinds):
    slots, width = arrived.shape
    block = 256
    right = pl.BlockSpec((slots, block), lambda i: (0, i))
    outs = [
        jax.ShapeDtypeStruct((active.shape[1], width), kind)
        for (active, unused), kind in zip(blocks, kinds, strict=True)
        for part in range(2)
    ]
    flat = [value for pair in blocks for value in pair]
    return pl.pallas_call(
        functools.partial(unit_kernel, count=len(blocks)),
        grid=(width // block,),
        in_specs=[right, right] + [whole(value) for value in flat],
        out_specs=[pl.BlockSpec((out.shape[0], block), lambda i: (0, i)) for out in outs],
        out_shape=outs,
        compiler_params=pltpu.CompilerParams(vmem_limit_bytes=VMEM_LIMIT),
        cost_estimate=SMALL,
    )(grad_arrived, arrived, *flat)


def column_kernel(*refs, held):
    row_refs = refs[:held]
    lying_ref, out_ref = refs[held:]
    start, total = 0, None
    for row_ref in row_refs:
        rows = row_ref.shape[0]
        part = contract(row_ref[...], lying_ref[start : start + rows, :], 0, 0)
        total = part if total is None else total + part
        start += rows
    out_ref[...] = total.astype(BF16)


def column_terms(row_blocks, grad_lying):
    width = row_blocks[0].shape[1]
    block = 256
    out = jax.ShapeDtypeStruct((width, 3 * LANES), BF16)
    return pl.pallas_call(
        functools.partial(column_kernel, held=len(row_blocks)),
        grid=(width // block,),
        in_specs=[
            pl.BlockSpec((value.shape[0], block), lambda i: (0, i)) for value in row_blocks
        ]
        + [whole(grad_lying)],
        out_specs=rows_spec(out, block),
        out_shape=out,
        compiler_params=pltpu.CompilerParams(vmem_limit_bytes=VMEM_LIMIT),
        cost_estimate=SMALL,
    )(*row_blocks, grad_lying)


def close_kernel(
    pieces_ref, matrix_ref, tokens_ref, gain_ref, residual_ref, out_ref, part_ref, sum_ref, *, starts
):
    width = tokens_ref.shape[1]
    lane = lax.broadcasted_iota(jnp.int32, (tokens_ref.shape[0], LANES), 1)
    sum_ref[...] = jnp.zeros_like(sum_ref)
    for device, start in enumerate(starts):
        for part in range(3):
            piece = pieces_ref[device, :, part * LANES : (part + 1) * LANES].astype(F32)
            column = part * width + start
            if column % LANES == 0:
                sum_ref[:, column : column + LANES] += piece
            else:
                turned = pltpu.roll(piece, HALF, 1)
                low, high = column - HALF, column + HALF
                sum_ref[:, low : low + LANES] += jnp.where(lane >= HALF, turned, 0.0)
                sum_ref[:, high : high + LANES] += jnp.where(lane < HALF, turned, 0.0)
    grad = contract(sum_ref[...].astype(BF16), matrix_ref[...], 1, 1)
    inputs = tokens_ref[...].astype(F32)
    scale = lax.rsqrt(jnp.mean(inputs * inputs, axis=-1, keepdims=True) + EPSILON)
    normed = inputs * scale
    scaled = grad * gain_ref[...]
    mean = jnp.mean(scaled * normed, axis=-1, keepdims=True)
    out_ref[...] = residual_ref[...] + scale * (scaled - normed * mean)
    part_ref[...] = jnp.sum(grad * normed, axis=0, keepdims=True)


def close_norm(pieces, starts, matrix, tokens, gain, residual):
    rows, width = tokens.shape
    outs = [
        jax.ShapeDtypeStruct((rows, width), F32),
        jax.ShapeDtypeStruct((1, width), F32),
    ]
    return pl.pallas_call(
        functools.partial(close_kernel, starts=starts),
        in_specs=[pl.BlockSpec(memory_space=pltpu.VMEM)] * 5,
        out_specs=[pl.BlockSpec(memory_space=pltpu.VMEM)] * 2,
        out_shape=outs,
        scratch_shapes=[pltpu.VMEM((rows, 3 * width), F32)],
        compiler_params=pltpu.CompilerParams(vmem_limit_bytes=VMEM_LIMIT),
        cost_estimate=SMALL,
    )(pieces, matrix, tokens, gain, residual)


def dense_kernel(terms_ref, columns_ref, output_ref, square_ref, *, starts):
    width = output_ref.shape[1]
    columns_ref[...] = jnp.zeros_like(columns_ref)
    lane = lax.broadcasted_iota(jnp.int32, (columns_ref.shape[0], LANES), 1)
    output = jnp.zeros(output_ref.shape, F32)
    for device, start in enumerate(starts):
        output = output + terms_ref[device, :, 3 * LANES :].astype(F32)
        for part in range(3):
            piece = terms_ref[device, :, part * LANES : (part + 1) * LANES].astype(F32)
            column = part * width + start
            if column % LANES == 0:
                columns_ref[:, column : column + LANES] += piece
            else:
                turned = pltpu.roll(piece, HALF, 1)
                low, high = column - HALF, column + HALF
                columns_ref[:, low : low + LANES] += jnp.where(lane >= HALF, turned, 0.0)
                columns_ref[:, high : high + LANES] += jnp.where(lane < HALF, turned, 0.0)
    output_ref[...] = output
    columns = columns_ref[...]
    square_ref[...] = jnp.zeros_like(square_ref) + (
        jnp.sum(columns * columns) + jnp.sum(output * output)
    )


def dense_grads(terms, starts):
    unused, rows, lanes = terms.shape
    width = lanes - 3 * LANES
    outs = [jax.ShapeDtypeStruct((rows, columns), F32) for columns in (3 * width, width)]
    outs.append(jax.ShapeDtypeStruct((1, LANES), F32))
    return pl.pallas_call(
        functools.partial(dense_kernel, starts=starts),
        in_specs=[pl.BlockSpec(memory_space=pltpu.VMEM)],
        out_specs=[pl.BlockSpec(memory_space=pltpu.VMEM)] * 3,
        out_shape=outs,
        compiler_params=pltpu.CompilerParams(vmem_limit_bytes=VMEM_LIMIT),
        cost_estimate=SMALL,
    )(terms)


def adam_update(weight, grad, first, second, factor, rate, decay):
    clipped = grad * factor
    first_new = BETA_ONE * first + (1.0 - BETA_ONE) * clipped
    second_new = BETA_TWO * second + (1.0 - BETA_TWO) * clipped * clipped
    first_hat = first_new / (1.0 - BETA_ONE**STEP)
    second_hat = second_new / (1.0 - BETA_TWO**STEP)
    weight_new = weight - rate * (first_hat / (jnp.sqrt(second_hat) + ADAM_FLOOR) + decay * weight)
    return (first_new, second_new, weight_new)


def together(*values):
    return lax.optimization_barrier(values)


def swap(value, axes):
    return lax.all_to_all(value, axes, split_axis=0, concat_axis=0, tiled=True)


def adam_kernel(factor_ref, *refs, rates):
    count = len(rates)
    factor = factor_ref[0]
    for index, rate in enumerate(rates):
        weight, grad, first, second = [ref[...] for ref in refs[4 * index : 4 * index + 4]]
        outs = refs[4 * count + 3 * index : 4 * count + 3 * index + 3]
        for out, value in zip(
            outs, adam_update(weight, grad, first, second, factor, rate, DECAY), strict=True
        ):
            out[...] = value


def adam_all(factor, leaves, rates, steps):
    flat = [value.reshape(value.shape[-2:]) for leaf in leaves for value in leaf]

    def spec(value):
        rows, columns = value.shape
        if rows % (8 * steps) == 0:
            return pl.BlockSpec((rows // steps, columns), lambda i: (i, 0))
        lanes = columns // steps
        return pl.BlockSpec((rows, lanes), lambda i: (0, i))

    shapes = [jax.ShapeDtypeStruct(value.shape, F32) for value in flat[::4] for _ in range(3)]
    outs = pl.pallas_call(
        functools.partial(adam_kernel, rates=rates),
        grid=(steps,),
        in_specs=[pl.BlockSpec(memory_space=pltpu.SMEM)] + [spec(value) for value in flat],
        out_specs=[spec(shape) for shape in shapes],
        out_shape=shapes,
        compiler_params=pltpu.CompilerParams(vmem_limit_bytes=VMEM_LIMIT),
        cost_estimate=pl.CostEstimate(
            flops=20 * sum(value.size for value in flat[::4]),
            bytes_accessed=28 * sum(value.size for value in flat[::4]),
            transcendentals=0,
        ),
    )(factor.reshape(1), *flat)
    return [
        [out.reshape(leaf[0].shape) for out in outs[3 * index : 3 * index + 3]]
        for index, leaf in enumerate(leaves)
    ]


def flip(value, bits):
    count = lax.axis_size(SEQ)
    return lax.ppermute(value, SEQ, [(index, index ^ bits) for index in range(count)])


def others(value, axis):
    size = lax.axis_size(axis)
    parts = [
        lax.ppermute(value, axis, [((i + step) % size, i) for i in range(size)])
        for step in range(1, size)
    ]
    return parts[0] if size == 2 else jnp.concatenate(parts, axis=0)


def to_owners(blocks, axis):
    size = lax.axis_size(axis)
    return [
        lax.ppermute(block, axis, [(i, (i + step) % size) for i in range(size)])
        for step, block in enumerate(blocks, 1)
    ]


def add_all(own, parts):
    return functools.reduce(lambda total, part: total + part.astype(F32), parts, own.astype(F32))


def spread_sum(value):
    count = lax.axis_size(ALL)
    return jnp.sum(swap(jnp.broadcast_to(value[None], (count, *value.shape)), ALL), axis=0)


def body(
    tokens,
    cotangent,
    segment_ids,
    expert_ids,
    projection,
    output_weight,
    expert_up,
    expert_down,
    norm_gains,
    projection_first,
    projection_second,
    output_first,
    output_second,
    up_first,
    up_second,
    down_first,
    down_second,
    gains_first,
    gains_second,
):
    inputs = tokens[0].astype(F32)
    upstream = cotangent[0].astype(F32)
    row_count = inputs.shape[0]
    width = inputs.shape[1]
    head_size = width // HEADS
    scaling = head_size ** (-0.5)
    count = lax.axis_size(SEQ)
    groups = lax.axis_size("exp")
    team = lax.axis_size(TEAM)
    position = lax.axis_index(SEQ)
    length = count * row_count
    weight_rows = projection.shape[0]
    first_heads, active_table = head_plan(count)
    starts = [int(head) * head_size for head in first_heads]
    active = lax.dynamic_index_in_dim(jnp.asarray(active_table), position, 0, keepdims=False)
    gain_first = norm_gains[0]
    gain_second = norm_gains[1]
    used = active_table.any(axis=2)

    scale_first = lax.rsqrt(jnp.mean(inputs * inputs, axis=-1, keepdims=True) + EPSILON)
    normed_first = inputs * scale_first
    attend_in = (normed_first * gain_first).astype(BF16)
    slots = groups * CAP
    chosen = expert_ids[0, :, 0]
    one_hot = (chosen[:, None] == jnp.arange(groups, dtype=jnp.int32)[None, :]).astype(F32)
    token = jnp.arange(row_count, dtype=jnp.int32)
    earlier = (token[None, :] < token[:, None]).astype(BF16)
    counts = jnp.dot(earlier, one_hot.astype(BF16), preferred_element_type=F32)
    rank = jnp.sum(counts * one_hot, axis=1).astype(jnp.int32)
    target = chosen * CAP + rank
    placing = (target[:, None] == jnp.arange(slots, dtype=jnp.int32)[None, :]).astype(BF16)

    def to_slots(values):
        outgoing = jnp.einsum("ts,td->sd", placing, values, preferred_element_type=F32)
        return outgoing.astype(BF16)

    def dispatch(outgoing):
        outgoing = jnp.broadcast_to(
            outgoing.reshape(1, groups, CAP, width), (team, groups, CAP, width)
        )
        return swap(outgoing.reshape(team * groups, CAP, width), TEAM + EXP).reshape(
            team * slots, width
        )

    def send_back(values):
        return swap(values.reshape(team * groups, CAP, width), TEAM + EXP).reshape(
            team, slots, width
        )

    def collect(returned):
        return jnp.einsum("ts,jsd->td", placing, returned, preferred_element_type=F32)

    projection_low = projection.astype(BF16)
    sent_rows = weight_rows + 8
    own_documents = jnp.zeros((8, 3 * LANES + width), BF16)
    own_documents = own_documents.at[0, :row_count].set(segment_ids[0].astype(BF16))
    output_low = output_weight.astype(BF16)
    pieces = [
        jnp.concatenate(
            [projection_low[:, k * width + s : k * width + s + LANES] for k in range(3)]
            + [output_low],
            axis=1,
        )
        for s in starts
    ]
    pieces = jnp.stack([jnp.concatenate([piece, own_documents], axis=0) for piece in pieces])
    own_up = expert_up[0].astype(BF16)
    own_down = expert_down[0].astype(BF16)
    pairwise = count == 8
    if pairwise:
        order = jnp.arange(count, dtype=jnp.int32) ^ position
        beside, below, across = flip(attend_in, 1), flip(attend_in, 2), flip(attend_in, 4)
        got_rows, beside, below, across, own_up = together(
            swap(pieces, SEQ), beside, below, across, own_up
        )
        corner = flip(across, 2)
        row_blocks = [attend_in, beside]
        row_blocks += [part for block in (below, across, corner) for part in (block, flip(block, 1))]
    else:
        order = jnp.arange(count, dtype=jnp.int32)
        row_blocks = [lax.all_gather(attend_in, SEQ, axis=0, tiled=True)]
        got_rows = swap(pieces, SEQ)
    documents = jnp.broadcast_to(
        got_rows[:, weight_rows, :row_count].reshape(length, 1), (length, LANES)
    )
    own_copies = jnp.broadcast_to(
        got_rows[None, :, :weight_rows], (groups, count, weight_rows, 3 * LANES + width)
    )
    all_copies = swap(own_copies, EXP)

    peer_up = others(own_up, "hi")
    *row_blocks, all_copies, peer_up, own_up, own_down, grad_slots_out = together(
        *row_blocks, all_copies, peer_up, own_up, own_down, to_slots(cotangent[0])
    )
    all_copies = jnp.swapaxes(all_copies, 0, 1)
    columns = all_copies[..., : 3 * LANES].reshape(width, 3 * LANES)
    output_full = all_copies[..., 3 * LANES :].reshape(width, width)
    grad_arrived = dispatch(grad_slots_out)
    peer_down = others(own_down, "hi")
    side_up = others(own_up, "in")
    side_down = others(own_down, "in")
    far_up = others(peer_up, "in")

    mixed_low, mixed_full, stat, pair = attend(
        active, order, row_blocks, columns, documents, row_count
    )

    def place_heads():
        index = np.arange(LANES)
        matrix = np.zeros((count, LANES, width), np.float32)
        for device in range(count):
            for slot in range(2):
                if used[device, slot]:
                    own = index[slot * HALF : (slot + 1) * HALF]
                    matrix[device, own, starts[device] + own] = 1.0
        return jnp.asarray(matrix, BF16)

    head_places = place_heads()

    def to_tokens(values):
        return swap(values.reshape(count, row_count, values.shape[1]), SEQ)

    mixed_low, grad_arrived, peer_down, side_up, side_down, far_up = together(
        mixed_low, grad_arrived, peer_down, side_up, side_down, far_up
    )
    far_down = others(peer_down, "in")
    mixed_pieces, projection_low, far_down = together(
        to_tokens(mixed_low), projection_low, far_down
    )
    projection_full = lax.all_gather(projection_low, ALL, axis=0, tiled=True)
    attend_out = jnp.einsum(
        "jtc,jcd->td", mixed_pieces, head_places, preferred_element_type=F32
    ).astype(BF16)
    branch = jnp.dot(attend_out, output_full, preferred_element_type=F32)
    middle = inputs + branch
    scale_second = lax.rsqrt(jnp.mean(middle * middle, axis=-1, keepdims=True) + EPSILON)
    normed_second = middle * scale_second
    expert_in = (normed_second * gain_second).astype(BF16)

    arrived = dispatch(to_slots(expert_in))
    ups, downs = (own_up, peer_up, side_up, far_up), (own_down, peer_down, side_down, far_down)
    grad_slots, actives, hiddens = expert_part(arrived, grad_arrived, ups, downs)
    returned_grad = send_back(grad_slots)

    blocks = list(zip(actives, hiddens, strict=True))
    down_far, up_far, down_peer, up_peer = unit_grads(
        grad_arrived, arrived, (blocks[3], blocks[1]), (BF16, F32)
    )
    (down_part,) = to_owners([down_far], "in")
    down_side, up_side, down_own, up_own = unit_grads(
        grad_arrived, arrived, (blocks[2], blocks[0]), (BF16, F32)
    )
    produced = produced_part(actives, downs)
    returned_grad, down_part, up_far, up_peer, projection_full, produced, down_side, up_own = (
        together(
            returned_grad, down_part, up_far, up_peer, projection_full, produced, down_side, up_own
        )
    )
    grad_expert_in = collect(returned_grad)
    (up_part,) = to_owners([up_far], "in")
    peers = lax.axis_size("hi")

    def hi_parts(value):
        return to_owners(list(value.astype(BF16).reshape(peers - 1, -1, width)), "hi")

    down_hi = hi_parts(add_all(down_peer, [down_part]))

    scaled_second = grad_expert_in * gain_second
    gain_second_part = jnp.sum(grad_expert_in * normed_second, axis=0)
    grad_middle = scale_second * (
        scaled_second
        - normed_second * jnp.mean(scaled_second * normed_second, axis=-1, keepdims=True)
    )
    residual_grad = upstream + grad_middle
    branch_grad = residual_grad.astype(BF16)
    grad_mixed = jnp.einsum(
        "td,ed->te", branch_grad, output_full, preferred_element_type=F32
    ).astype(BF16)

    sent_grad = jnp.stack([grad_mixed[:, s : s + LANES] for s in starts])
    row_grad = swap(sent_grad, SEQ).reshape(length, LANES)

    group = lax.axis_index(EXP)

    def group_rows(value):
        rows = value.reshape(count, groups, weight_rows, -1)
        own, *away = [
            lax.dynamic_index_in_dim(rows, lax.rem(group + step, groups), 1, keepdims=False)
            for step in range(groups)
        ]
        return own, away

    output_term = jnp.einsum("tc,te->ce", attend_out, branch_grad, preferred_element_type=F32)
    output_own, output_away = group_rows(output_term.astype(BF16))
    output_away = to_owners(output_away, "exp")
    row_grad, produced, down_side, up_side, up_part, *held = together(
        row_grad, produced, down_side, up_side, up_part, *down_hi, *output_away
    )
    down_hi, output_away = held[: peers - 1], held[peers - 1 :]
    (down_early,) = to_owners([down_side], "in")
    (up_early,) = to_owners([up_side], "in")
    up_hi = hi_parts(add_all(up_peer, [up_part]))
    returned = send_back(produced)
    grad_qkv, grad_lying = attend_back(
        active, order, pair, documents, stat, row_grad, mixed_full, row_count, scaling
    )
    grad_qkv, grad_lying, returned, down_early, up_early, *up_hi = together(
        grad_qkv, grad_lying, returned, down_early, up_early, *up_hi
    )
    down_grad = add_all(down_own, [down_early, *down_hi])[None]
    up_grad = add_all(up_own, [up_early, *up_hi])[None]
    block_output = (middle + collect(returned)).astype(BF16)[None]

    column_own, column_away = group_rows(column_terms(row_blocks, grad_lying))
    dense_rows = jnp.concatenate(
        [
            add_all(column_own, to_owners(column_away, "exp")).astype(BF16),
            add_all(output_own, output_away).astype(BF16),
        ],
        axis=2,
    )
    local_square = jnp.sum(up_grad * up_grad) + jnp.sum(down_grad * down_grad)
    grad_pieces, dense_rows, local_square = together(
        to_tokens(grad_qkv), dense_rows, local_square
    )
    projection_grad, output_grad, dense_square = dense_grads(swap(dense_rows, SEQ), starts)
    input_grad, gain_first_part = close_norm(
        grad_pieces, starts, projection_full, tokens[0], gain_first[None], residual_grad
    )
    input_grad, gain_first_part = input_grad[None], gain_first_part[0]
    summed = spread_sum(
        jnp.concatenate(
            [gain_first_part, gain_second_part, dense_square[0] + local_square]
        )[None]
    )[0]
    gains_grad = summed[: 2 * width].reshape(2, width)
    grad_norm = jnp.sqrt(summed[2 * width] + jnp.sum(gains_grad * gains_grad))
    factor = jnp.minimum(1.0, CLIP / (grad_norm + 1e-06))
    (
        (projection_moment, projection_square, projection_new),
        (output_moment, output_square, output_new),
        (up_moment, up_square, up_new),
        (down_moment, down_square, down_new),
    ) = adam_all(
        factor,
        [
            (projection, projection_grad, projection_first, projection_second),
            (output_weight, output_grad, output_first, output_second),
            (expert_up, up_grad, up_first, up_second),
            (expert_down, down_grad, down_first, down_second),
        ],
        (RATE_MATRIX, RATE_OUTPUT, RATE_MATRIX, RATE_MATRIX),
        6,
    )
    gains_moment, gains_square, gains_new = adam_update(
        norm_gains, gains_grad, gains_first, gains_second, factor, RATE_GAIN, 0.0
    )
    return (
        block_output,
        input_grad,
        grad_norm,
        projection_grad,
        projection_moment,
        projection_square,
        projection_new,
        output_grad,
        output_moment,
        output_square,
        output_new,
        up_grad,
        up_moment,
        up_square,
        up_new,
        down_grad,
        down_moment,
        down_square,
        down_new,
        gains_grad,
        gains_moment,
        gains_square,
        gains_new,
    )


def solution(mesh):
    token = P("exp", SEQ, None)
    dense = P(ALL, None)
    expert = P("exp", SEQ, None)
    in_specs = (
        (token, token, P("exp", SEQ), token)
        + (dense, dense, expert, expert, P())
        + (dense,) * 4
        + (expert,) * 4
        + (P(), P())
    )
    out_specs = (token, token, P()) + (dense,) * 8 + (expert,) * 8 + (P(),) * 4
    rows, groups = mesh.devices.shape
    fine = Mesh(mesh.devices.reshape(rows // 4, 2, 2, groups), ALL)
    return jax.shard_map(body, mesh=fine, in_specs=in_specs, out_specs=out_specs, check_vma=False)
```

```python
import functools
import math

import jax
import jax.numpy as jnp
import numpy as np
from jax import lax
from jax.experimental import pallas as pl
from jax.experimental.pallas import tpu as pltpu
from jax.sharding import Mesh
from jax.sharding import PartitionSpec as P

HEADS = 12
CAP = 128
STEP = 10


EPSILON = 1e-05
CLIP = 1.0
BETA_ONE = 0.9
BETA_TWO = 0.99
ADAM_FLOOR = 1e-08
DECAY = 0.1
RATE_MATRIX = 0.04
RATE_OUTPUT = 0.1
RATE_GAIN = 0.5

SEQ = ("hi", "lo", "in")
EXP = ("exp",)
ALL = SEQ + EXP
TEAM = ("lo",)
SHARE = ("hi", "in")
LANES = 128
HALF = 64
FAR = -1e30
BF16 = jnp.bfloat16
F32 = jnp.float32
VMEM_LIMIT = 60 * 1024 * 1024


def head_plan(count):
    whole = math.lcm(HEADS, count)
    units, parts = whole // count, whole // HEADS
    first = np.zeros((count,), np.int64)
    active = np.zeros((count, 2, count), np.int32)
    for device in range(count):
        first[device] = min(units * device // parts, HEADS - 2)
        for unit in range(units * device, units * (device + 1)):
            slot = unit // parts - first[device]
            for block in range(count):
                turn = block % (2 * parts)
                if min(turn, 2 * parts - 1 - turn) == unit % parts:
                    active[device, slot, block] = 1
    return first, active


def three_parts(value):
    high = value.astype(BF16).astype(F32)
    middle = (value - high).astype(BF16).astype(F32)
    return high, middle, value - high - middle


def contract(left, right, left_axis, right_axis):
    return lax.dot_general(
        left, right, (((left_axis,), (right_axis,)), ((), ())), preferred_element_type=F32
    )


def slot_arrays(packed, documents, kind, slot):
    spare = HALF - HALF * slot
    lane = lax.broadcasted_iota(jnp.int32, packed.shape, 1)
    own = (lane < HALF) if slot == 0 else (lane >= HALF)
    place = (lane - spare).astype(F32)
    ours = place == documents
    first = (lane >= spare) & (lane < spare + 3)
    if kind == "query":
        extra = jnp.where(first & jnp.logical_not(ours), FAR, 0.0)
    elif kind == "key":
        extra = jnp.where(ours | ((lane >= spare + 3) & (lane < spare + 6)), 1.0, 0.0)
    else:
        extra = jnp.where(first, 1.0, 0.0)
    return jnp.where(own, packed, extra).astype(BF16)


def fill_slots(packed_of, documents_ref, wide_ref, kinds, place):
    documents = documents_ref[place, :].astype(F32)
    for number, kind in enumerate(kinds):
        packed = packed_of(kind).astype(F32)
        if kind == "query":
            packed = packed * 0.125
        for slot in range(2):
            column = (2 * number + slot) * LANES
            wide_ref[place, column : column + LANES] = slot_arrays(packed, documents, kind, slot)


def attend_kernel(active_ref, order_ref, *refs, block, chunk, held):
    row_refs = refs[:held]
    columns_ref, documents_ref = refs[held : held + 2]
    low_ref, full_ref, stat_ref, pair_ref, mixed_ref, wide_ref = refs[held + 2 :]
    at = pl.program_id(0)

    @pl.when(at == 0)
    def _():
        def fill(tokens, index):
            place = pl.ds(pl.multiple_of(order_ref[index] * block, block), block)
            packed = contract(tokens, columns_ref[...], 1, 0).astype(BF16)
            pair_ref[place, :] = packed[:, LANES:]
            parts = {
                kind: packed[:, part * LANES : (part + 1) * LANES]
                for part, kind in enumerate(("query", "key", "value"))
            }
            fill_slots(parts.get, documents_ref, wide_ref, tuple(parts), place)

        if held > 1:
            for index, row_ref in enumerate(row_refs):
                fill(row_ref[...], index)
        else:

            @pl.loop(0, pl.num_programs(0))
            def _(index):
                fill(row_refs[0][pl.ds(pl.multiple_of(index * block, block), block), :], index)

    rows = pl.ds(pl.multiple_of(at * block, block), block)
    lane = lax.broadcasted_iota(jnp.int32, (block, LANES), 1)
    last = lax.div(at * block, chunk)
    for slot in range(2):
        spare = HALF - HALF * slot
        own = (lane < HALF) if slot == 0 else (lane >= HALF)
        columns = slice(slot * LANES, (slot + 1) * LANES)

        @pl.when(active_ref[slot, at] != 0)
        def _():
            query = wide_ref[rows, columns]

            def step(index, carry, edge):
                top, weighted = carry
                place = pl.ds(pl.multiple_of(index * chunk, chunk), chunk)
                keys = wide_ref[place, 2 * LANES + slot * LANES : 3 * LANES + slot * LANES]
                values = wide_ref[place, 4 * LANES + slot * LANES : 5 * LANES + slot * LANES]
                scores = contract(query, keys, 1, 1)
                if edge:
                    key_at = index * chunk + lax.broadcasted_iota(jnp.int32, (block, chunk), 1)
                    query_at = at * block + lax.broadcasted_iota(jnp.int32, (block, chunk), 0)
                    scores = jnp.where(key_at <= query_at, scores, FAR)
                new_top = jnp.maximum(top, jnp.max(scores, axis=1, keepdims=True))
                weights = jnp.exp(scores - new_top).astype(BF16)
                weighted = weighted * jnp.exp(top - new_top) + contract(weights, values, 1, 0)
                return new_top, weighted

            carry = (jnp.full((block, 1), FAR, F32), jnp.zeros((block, LANES), F32))
            carry = lax.fori_loop(0, last, lambda index, state: step(index, state, False), carry)
            top, weighted = step(last, carry, True)
            total = weighted[:, spare : spare + 1]
            mixed_ref[slot] = jnp.where(own, weighted / total, 0.0)
            log_total = top + jnp.log(total)
            high, middle, small = three_parts(log_total)
            extra = jnp.where(lane == spare + 3, -high, 0.0)
            extra = jnp.where(lane == spare + 4, -middle, extra)
            extra = jnp.where(lane == spare + 5, -small, extra)
            stat_ref[:, columns] = (query.astype(F32) + extra).astype(BF16)

        @pl.when(active_ref[slot, at] == 0)
        def _():
            mixed_ref[slot] = jnp.zeros((block, LANES), F32)
            stat_ref[:, columns] = jnp.zeros((block, LANES), BF16)

    mixed = mixed_ref[0] + mixed_ref[1]
    full_ref[...] = mixed
    low_ref[...] = mixed.astype(BF16)


def attend_back_kernel(
    active_ref,
    order_ref,
    pair_ref,
    documents_ref,
    stat_ref,
    grad_ref,
    mixed_ref,
    out_ref,
    lying_ref,
    key_sum_ref,
    value_sum_ref,
    query_sum_ref,
    wide_ref,
    *,
    block,
    chunk,
    scaling,
):
    at = pl.program_id(0)
    rows = pl.ds(pl.multiple_of(at * block, block), block)
    lane = lax.broadcasted_iota(jnp.int32, (block, LANES), 1)
    last = lax.div(at * block, chunk)

    @pl.when(at == 0)
    def _():
        @pl.loop(0, pl.num_programs(0))
        def _(index):
            place = pl.ds(pl.multiple_of(index * block, block), block)
            parts = {"key": pair_ref[place, :LANES], "value": pair_ref[place, LANES:]}
            fill_slots(parts.get, documents_ref, wide_ref, tuple(parts), place)

        key_sum_ref[...] = jnp.zeros_like(key_sum_ref)
        value_sum_ref[...] = jnp.zeros_like(value_sum_ref)

    for slot in range(2):
        spare = HALF - HALF * slot
        own = (lane < HALF) if slot == 0 else (lane >= HALF)
        columns = slice(slot * LANES, (slot + 1) * LANES)
        query_sum_ref[slot] = jnp.zeros((block, LANES), F32)

        @pl.when(active_ref[slot, at] != 0)
        def _():
            query = stat_ref[:, columns]
            grad = grad_ref[...].astype(F32)
            delta = jnp.sum(jnp.where(own, grad * mixed_ref[...], 0.0), axis=1, keepdims=True)
            high, middle, small = three_parts(delta)
            extra = jnp.where(lane == spare, -high, 0.0)
            extra = jnp.where(lane == spare + 1, -middle, extra)
            extra = jnp.where(lane == spare + 2, -small, extra)
            grad_low = jnp.where(own, grad, extra).astype(BF16)

            def step(index, edge):
                place = pl.ds(pl.multiple_of(index * chunk, chunk), chunk)
                keys = wide_ref[place, slot * LANES : (slot + 1) * LANES]
                values = wide_ref[place, (2 + slot) * LANES : (3 + slot) * LANES]
                scores = contract(keys, query, 1, 1)
                if edge:
                    key_at = index * chunk + lax.broadcasted_iota(jnp.int32, (chunk, block), 0)
                    query_at = at * block + lax.broadcasted_iota(jnp.int32, (chunk, block), 1)
                    scores = jnp.where(key_at <= query_at, scores, FAR)
                weights = jnp.exp(scores)
                grad_weights = contract(values, grad_low, 1, 1)
                grad_scores = (weights * grad_weights).astype(BF16)
                value_sum_ref[slot, place, :] += contract(weights.astype(BF16), grad_low, 1, 0)
                key_sum_ref[slot, place, :] += contract(grad_scores, query, 1, 0)
                query_sum_ref[slot] += contract(grad_scores, keys, 0, 0)

            @pl.loop(0, last)
            def _(index):
                step(index, False)

            step(last, True)

    first_half = lane < HALF
    query_grad = jnp.where(first_half, query_sum_ref[0], query_sum_ref[1]) * scaling
    out_ref[rows, :LANES] = query_grad.astype(BF16)
    lying = pl.ds(pl.multiple_of(order_ref[at] * block, block), block)
    lying_ref[lying, :LANES] = query_grad.astype(BF16)

    @pl.when(at == pl.num_programs(0) - 1)
    def _():
        @pl.loop(0, pl.num_programs(0))
        def _(index):
            place = pl.ds(pl.multiple_of(index * block, block), block)
            key_grad = jnp.where(first_half, key_sum_ref[0, place, :], key_sum_ref[1, place, :])
            value_grad = jnp.where(
                first_half, value_sum_ref[0, place, :], value_sum_ref[1, place, :]
            )
            out_ref[place, LANES : 2 * LANES] = key_grad.astype(BF16)
            out_ref[place, 2 * LANES :] = value_grad.astype(BF16)
            lying = pl.ds(pl.multiple_of(order_ref[index] * block, block), block)
            lying_ref[lying, LANES : 2 * LANES] = key_grad.astype(BF16)
            lying_ref[lying, 2 * LANES :] = value_grad.astype(BF16)


def whole(value):
    return pl.BlockSpec(value.shape, lambda i, *unused: (0, 0), pipeline_mode=pl.Buffered(1))


SMALL = pl.CostEstimate(flops=1, bytes_accessed=1, transcendentals=0)


def attend(active, order, row_blocks, columns, documents, block):
    length = documents.shape[0]
    pair = jax.ShapeDtypeStruct((length, 2 * LANES), BF16)
    return pl.pallas_call(
        functools.partial(attend_kernel, block=block, chunk=2 * block, held=len(row_blocks)),
        grid_spec=pltpu.PrefetchScalarGridSpec(
            num_scalar_prefetch=2,
            grid=(length // block,),
            in_specs=[whole(value) for value in (*row_blocks, columns, documents)],
            out_specs=[
                pl.BlockSpec((block, LANES), lambda i, a, o: (i, 0)),
                pl.BlockSpec((block, LANES), lambda i, a, o: (i, 0)),
                pl.BlockSpec((block, 2 * LANES), lambda i, a, o: (i, 0)),
                whole(pair),
            ],
            scratch_shapes=[
                pltpu.VMEM((2, block, LANES), F32),
                pltpu.VMEM((length, 6 * LANES), BF16),
            ],
        ),
        out_shape=[
            jax.ShapeDtypeStruct((length, LANES), BF16),
            jax.ShapeDtypeStruct((length, LANES), F32),
            jax.ShapeDtypeStruct((length, 2 * LANES), BF16),
            pair,
        ],
        compiler_params=pltpu.CompilerParams(vmem_limit_bytes=VMEM_LIMIT),
        cost_estimate=SMALL,
    )(active, order, *row_blocks, columns, documents)


def attend_back(active, order, pair, documents, stat, grad, mixed, block, scaling):
    length = pair.shape[0]
    count = length // block
    return pl.pallas_call(
        functools.partial(attend_back_kernel, block=block, chunk=2 * block, scaling=scaling),
        grid_spec=pltpu.PrefetchScalarGridSpec(
            num_scalar_prefetch=2,
            grid=(count,),
            in_specs=[
                whole(pair),
                whole(documents),
                pl.BlockSpec((block, 2 * LANES), lambda i, a, o: (i, 0)),
                pl.BlockSpec((block, LANES), lambda i, a, o: (i, 0)),
                pl.BlockSpec((block, LANES), lambda i, a, o: (i, 0)),
            ],
            out_specs=[
                pl.BlockSpec(
                    (length, 3 * LANES), lambda i, a, o: (0, 0), pipeline_mode=pl.Buffered(1)
                )
            ]
            * 2,
            scratch_shapes=[
                pltpu.VMEM((2, length, LANES), F32),
                pltpu.VMEM((2, length, LANES), F32),
                pltpu.VMEM((2, block, LANES), F32),
                pltpu.VMEM((length, 4 * LANES), BF16),
            ],
        ),
        out_shape=[jax.ShapeDtypeStruct((length, 3 * LANES), BF16)] * 2,
        compiler_params=pltpu.CompilerParams(vmem_limit_bytes=VMEM_LIMIT),
        cost_estimate=SMALL,
    )(active, order, pair, documents, stat, grad, mixed)


def expert_kernel(arrived_ref, grad_ref, *refs, count):
    up_refs, down_refs = refs[:count], refs[count : 2 * count]
    total_ref = refs[2 * count]
    active_refs, hidden_refs = refs[2 * count + 1 : 3 * count + 1], refs[3 * count + 1 :]
    arrived, grad_arrived = arrived_ref[...], grad_ref[...]
    scale = math.sqrt(2.0 / math.pi)
    total = jnp.zeros(total_ref.shape, F32)
    for up_ref, down_ref, active_ref, hidden_ref in zip(
        up_refs, down_refs, active_refs, hidden_refs, strict=True
    ):
        up = up_ref[...]
        hidden = contract(arrived, up, 1, 1)
        squared = hidden * hidden
        bend = jnp.tanh(scale * hidden * (1.0 + 0.044715 * squared))
        half = 0.5 + 0.5 * bend
        active_ref[...] = (hidden * half).astype(BF16)
        slope = half + (0.5 * scale) * hidden * (1.0 - bend * bend) * (1.0 + 3 * 0.044715 * squared)
        grad_hidden = (slope * contract(grad_arrived, down_ref[...], 1, 1)).astype(BF16)
        hidden_ref[...] = grad_hidden
        total = total + contract(grad_hidden, up, 1, 0)
    total_ref[...] = total.astype(BF16)


def rows_spec(value, block):
    return pl.BlockSpec((block, value.shape[1]), lambda i: (i, 0))


def expert_part(arrived, grad_arrived, ups, downs):
    slots, width = arrived.shape
    block = 256
    units = [jax.ShapeDtypeStruct((slots, up.shape[0]), BF16) for up in ups]
    outs = [jax.ShapeDtypeStruct((slots, width), BF16), *units, *units]
    total, *parts = pl.pallas_call(
        functools.partial(expert_kernel, count=len(ups)),
        grid=(slots // block,),
        in_specs=[rows_spec(arrived, block), rows_spec(grad_arrived, block)]
        + [whole(value) for value in (*ups, *downs)],
        out_specs=[rows_spec(out, block) for out in outs],
        out_shape=outs,
        compiler_params=pltpu.CompilerParams(vmem_limit_bytes=VMEM_LIMIT),
        cost_estimate=SMALL,
    )(arrived, grad_arrived, *ups, *downs)
    return total, parts[: len(ups)], parts[len(ups) :]


def produced_kernel(*refs, count):
    total = contract(refs[0][...], refs[count][...], 1, 0)
    for index in range(1, count):
        total = total + contract(refs[index][...], refs[count + index][...], 1, 0)
    refs[-1][...] = total.astype(BF16)


def produced_part(actives, downs):
    slots, width = actives[0].shape[0], downs[0].shape[1]
    block = 256
    out = jax.ShapeDtypeStruct((slots, width), BF16)
    return pl.pallas_call(
        functools.partial(produced_kernel, count=len(actives)),
        grid=(slots // block,),
        in_specs=[rows_spec(value, block) for value in actives] + [whole(down) for down in downs],
        out_specs=rows_spec(out, block),
        out_shape=out,
        compiler_params=pltpu.CompilerParams(vmem_limit_bytes=VMEM_LIMIT),
        cost_estimate=SMALL,
    )(*actives, *downs)


def unit_kernel(grad_ref, arrived_ref, *refs, count):
    for index in range(count):
        active_ref, hidden_ref = refs[2 * index : 2 * index + 2]
        down_ref, up_ref = refs[2 * count + 2 * index : 2 * count + 2 * index + 2]
        down_ref[...] = contract(active_ref[...], grad_ref[...], 0, 0).astype(down_ref.dtype)
        up_ref[...] = contract(hidden_ref[...], arrived_ref[...], 0, 0).astype(up_ref.dtype)


def unit_grads(grad_arrived, arrived, blocks, kinds):
    slots, width = arrived.shape
    block = 256
    right = pl.BlockSpec((slots, block), lambda i: (0, i))
    outs = [
        jax.ShapeDtypeStruct((active.shape[1], width), kind)
        for (active, unused), kind in zip(blocks, kinds, strict=True)
        for part in range(2)
    ]
    flat = [value for pair in blocks for value in pair]
    return pl.pallas_call(
        functools.partial(unit_kernel, count=len(blocks)),
        grid=(width // block,),
        in_specs=[right, right] + [whole(value) for value in flat],
        out_specs=[pl.BlockSpec((out.shape[0], block), lambda i: (0, i)) for out in outs],
        out_shape=outs,
        compiler_params=pltpu.CompilerParams(vmem_limit_bytes=VMEM_LIMIT),
        cost_estimate=SMALL,
    )(grad_arrived, arrived, *flat)


def column_kernel(*refs, held):
    row_refs = refs[:held]
    lying_ref, out_ref = refs[held:]
    start, total = 0, None
    for row_ref in row_refs:
        rows = row_ref.shape[0]
        part = contract(row_ref[...], lying_ref[start : start + rows, :], 0, 0)
        total = part if total is None else total + part
        start += rows
    out_ref[...] = total.astype(BF16)


def column_terms(row_blocks, grad_lying):
    width = row_blocks[0].shape[1]
    block = 256
    out = jax.ShapeDtypeStruct((width, 3 * LANES), BF16)
    return pl.pallas_call(
        functools.partial(column_kernel, held=len(row_blocks)),
        grid=(width // block,),
        in_specs=[
            pl.BlockSpec((value.shape[0], block), lambda i: (0, i)) for value in row_blocks
        ]
        + [whole(grad_lying)],
        out_specs=rows_spec(out, block),
        out_shape=out,
        compiler_params=pltpu.CompilerParams(vmem_limit_bytes=VMEM_LIMIT),
        cost_estimate=SMALL,
    )(*row_blocks, grad_lying)


def close_kernel(
    pieces_ref, matrix_ref, tokens_ref, gain_ref, residual_ref, out_ref, part_ref, sum_ref, *, starts
):
    width = tokens_ref.shape[1]
    lane = lax.broadcasted_iota(jnp.int32, (tokens_ref.shape[0], LANES), 1)
    sum_ref[...] = jnp.zeros_like(sum_ref)
    for device, start in enumerate(starts):
        for part in range(3):
            piece = pieces_ref[device, :, part * LANES : (part + 1) * LANES].astype(F32)
            column = part * width + start
            if column % LANES == 0:
                sum_ref[:, column : column + LANES] += piece
            else:
                turned = pltpu.roll(piece, HALF, 1)
                low, high = column - HALF, column + HALF
                sum_ref[:, low : low + LANES] += jnp.where(lane >= HALF, turned, 0.0)
                sum_ref[:, high : high + LANES] += jnp.where(lane < HALF, turned, 0.0)
    grad = contract(sum_ref[...].astype(BF16), matrix_ref[...], 1, 1)
    inputs = tokens_ref[...].astype(F32)
    scale = lax.rsqrt(jnp.mean(inputs * inputs, axis=-1, keepdims=True) + EPSILON)
    normed = inputs * scale
    scaled = grad * gain_ref[...]
    mean = jnp.mean(scaled * normed, axis=-1, keepdims=True)
    out_ref[...] = residual_ref[...] + scale * (scaled - normed * mean)
    part_ref[...] = jnp.sum(grad * normed, axis=0, keepdims=True)


def close_norm(pieces, starts, matrix, tokens, gain, residual):
    rows, width = tokens.shape
    outs = [
        jax.ShapeDtypeStruct((rows, width), F32),
        jax.ShapeDtypeStruct((1, width), F32),
    ]
    return pl.pallas_call(
        functools.partial(close_kernel, starts=starts),
        in_specs=[pl.BlockSpec(memory_space=pltpu.VMEM)] * 5,
        out_specs=[pl.BlockSpec(memory_space=pltpu.VMEM)] * 2,
        out_shape=outs,
        scratch_shapes=[pltpu.VMEM((rows, 3 * width), F32)],
        compiler_params=pltpu.CompilerParams(vmem_limit_bytes=VMEM_LIMIT),
        cost_estimate=SMALL,
    )(pieces, matrix, tokens, gain, residual)


def dense_kernel(terms_ref, columns_ref, output_ref, square_ref, *, starts):
    width = output_ref.shape[1]
    columns_ref[...] = jnp.zeros_like(columns_ref)
    lane = lax.broadcasted_iota(jnp.int32, (columns_ref.shape[0], LANES), 1)
    output = jnp.zeros(output_ref.shape, F32)
    for device, start in enumerate(starts):
        output = output + terms_ref[device, :, 3 * LANES :].astype(F32)
        for part in range(3):
            piece = terms_ref[device, :, part * LANES : (part + 1) * LANES].astype(F32)
            column = part * width + start
            if column % LANES == 0:
                columns_ref[:, column : column + LANES] += piece
            else:
                turned = pltpu.roll(piece, HALF, 1)
                low, high = column - HALF, column + HALF
                columns_ref[:, low : low + LANES] += jnp.where(lane >= HALF, turned, 0.0)
                columns_ref[:, high : high + LANES] += jnp.where(lane < HALF, turned, 0.0)
    output_ref[...] = output
    columns = columns_ref[...]
    square_ref[...] = jnp.zeros_like(square_ref) + (
        jnp.sum(columns * columns) + jnp.sum(output * output)
    )


def dense_grads(terms, starts):
    unused, rows, lanes = terms.shape
    width = lanes - 3 * LANES
    outs = [jax.ShapeDtypeStruct((rows, columns), F32) for columns in (3 * width, width)]
    outs.append(jax.ShapeDtypeStruct((1, LANES), F32))
    return pl.pallas_call(
        functools.partial(dense_kernel, starts=starts),
        in_specs=[pl.BlockSpec(memory_space=pltpu.VMEM)],
        out_specs=[pl.BlockSpec(memory_space=pltpu.VMEM)] * 3,
        out_shape=outs,
        compiler_params=pltpu.CompilerParams(vmem_limit_bytes=VMEM_LIMIT),
        cost_estimate=SMALL,
    )(terms)


def adam_update(weight, grad, first, second, factor, rate, decay):
    clipped = grad * factor
    first_new = BETA_ONE * first + (1.0 - BETA_ONE) * clipped
    second_new = BETA_TWO * second + (1.0 - BETA_TWO) * clipped * clipped
    first_hat = first_new / (1.0 - BETA_ONE**STEP)
    second_hat = second_new / (1.0 - BETA_TWO**STEP)
    weight_new = weight - rate * (first_hat / (jnp.sqrt(second_hat) + ADAM_FLOOR) + decay * weight)
    return (first_new, second_new, weight_new)


def together(*values):
    return lax.optimization_barrier(values)


def swap(value, axes):
    return lax.all_to_all(value, axes, split_axis=0, concat_axis=0, tiled=True)


def adam_kernel(factor_ref, *refs, rates):
    count = len(rates)
    factor = factor_ref[0]
    for index, rate in enumerate(rates):
        weight, grad, first, second = [ref[...] for ref in refs[4 * index : 4 * index + 4]]
        outs = refs[4 * count + 3 * index : 4 * count + 3 * index + 3]
        for out, value in zip(
            outs, adam_update(weight, grad, first, second, factor, rate, DECAY), strict=True
        ):
            out[...] = value


def adam_all(factor, leaves, rates, steps):
    flat = [value.reshape(value.shape[-2:]) for leaf in leaves for value in leaf]

    def spec(value):
        rows, columns = value.shape
        if rows % (8 * steps) == 0:
            return pl.BlockSpec((rows // steps, columns), lambda i: (i, 0))
        lanes = columns // steps
        return pl.BlockSpec((rows, lanes), lambda i: (0, i))

    shapes = [jax.ShapeDtypeStruct(value.shape, F32) for value in flat[::4] for _ in range(3)]
    outs = pl.pallas_call(
        functools.partial(adam_kernel, rates=rates),
        grid=(steps,),
        in_specs=[pl.BlockSpec(memory_space=pltpu.SMEM)] + [spec(value) for value in flat],
        out_specs=[spec(shape) for shape in shapes],
        out_shape=shapes,
        compiler_params=pltpu.CompilerParams(vmem_limit_bytes=VMEM_LIMIT),
        cost_estimate=pl.CostEstimate(
            flops=20 * sum(value.size for value in flat[::4]),
            bytes_accessed=28 * sum(value.size for value in flat[::4]),
            transcendentals=0,
        ),
    )(factor.reshape(1), *flat)
    return [
        [out.reshape(leaf[0].shape) for out in outs[3 * index : 3 * index + 3]]
        for index, leaf in enumerate(leaves)
    ]


def flip(value, bits):
    count = lax.axis_size(SEQ)
    return lax.ppermute(value, SEQ, [(index, index ^ bits) for index in range(count)])


def others(value, axis):
    size = lax.axis_size(axis)
    parts = [
        lax.ppermute(value, axis, [((i + step) % size, i) for i in range(size)])
        for step in range(1, size)
    ]
    return parts[0] if size == 2 else jnp.concatenate(parts, axis=0)


def to_owners(blocks, axis):
    size = lax.axis_size(axis)
    return [
        lax.ppermute(block, axis, [(i, (i + step) % size) for i in range(size)])
        for step, block in enumerate(blocks, 1)
    ]


def add_all(own, parts):
    return functools.reduce(lambda total, part: total + part.astype(F32), parts, own.astype(F32))


def spread_sum(value):
    count = lax.axis_size(ALL)
    return jnp.sum(swap(jnp.broadcast_to(value[None], (count, *value.shape)), ALL), axis=0)


def body(
    tokens,
    cotangent,
    segment_ids,
    expert_ids,
    projection,
    output_weight,
    expert_up,
    expert_down,
    norm_gains,
    projection_first,
    projection_second,
    output_first,
    output_second,
    up_first,
    up_second,
    down_first,
    down_second,
    gains_first,
    gains_second,
):
    inputs = tokens[0].astype(F32)
    upstream = cotangent[0].astype(F32)
    row_count = inputs.shape[0]
    width = inputs.shape[1]
    head_size = width // HEADS
    scaling = head_size ** (-0.5)
    count = lax.axis_size(SEQ)
    groups = lax.axis_size("exp")
    team = lax.axis_size(TEAM)
    position = lax.axis_index(SEQ)
    length = count * row_count
    weight_rows = projection.shape[0]
    first_heads, active_table = head_plan(count)
    starts = [int(head) * head_size for head in first_heads]
    active = lax.dynamic_index_in_dim(jnp.asarray(active_table), position, 0, keepdims=False)
    gain_first = norm_gains[0]
    gain_second = norm_gains[1]
    used = active_table.any(axis=2)

    scale_first = lax.rsqrt(jnp.mean(inputs * inputs, axis=-1, keepdims=True) + EPSILON)
    normed_first = inputs * scale_first
    attend_in = (normed_first * gain_first).astype(BF16)
    slots = groups * CAP
    chosen = expert_ids[0, :, 0]
    one_hot = (chosen[:, None] == jnp.arange(groups, dtype=jnp.int32)[None, :]).astype(F32)
    token = jnp.arange(row_count, dtype=jnp.int32)
    earlier = (token[None, :] < token[:, None]).astype(BF16)
    counts = jnp.dot(earlier, one_hot.astype(BF16), preferred_element_type=F32)
    rank = jnp.sum(counts * one_hot, axis=1).astype(jnp.int32)
    target = chosen * CAP + rank
    placing = (target[:, None] == jnp.arange(slots, dtype=jnp.int32)[None, :]).astype(BF16)

    def to_slots(values):
        outgoing = jnp.einsum("ts,td->sd", placing, values, preferred_element_type=F32)
        return outgoing.astype(BF16)

    def dispatch(outgoing):
        outgoing = jnp.broadcast_to(
            outgoing.reshape(1, groups, CAP, width), (team, groups, CAP, width)
        )
        return swap(outgoing.reshape(team * groups, CAP, width), TEAM + EXP).reshape(
            team * slots, width
        )

    def send_back(values):
        return swap(values.reshape(team * groups, CAP, width), TEAM + EXP).reshape(
            team, slots, width
        )

    def collect(returned):
        return jnp.einsum("ts,jsd->td", placing, returned, preferred_element_type=F32)

    projection_low = projection.astype(BF16)
    sent_rows = weight_rows + 8
    own_documents = jnp.zeros((8, 3 * LANES + width), BF16)
    own_documents = own_documents.at[0, :row_count].set(segment_ids[0].astype(BF16))
    output_low = output_weight.astype(BF16)
    pieces = [
        jnp.concatenate(
            [projection_low[:, k * width + s : k * width + s + LANES] for k in range(3)]
            + [output_low],
            axis=1,
        )
        for s in starts
    ]
    pieces = jnp.stack([jnp.concatenate([piece, own_documents], axis=0) for piece in pieces])
    own_up = expert_up[0].astype(BF16)
    own_down = expert_down[0].astype(BF16)
    pairwise = count == 8
    if pairwise:
        order = jnp.arange(count, dtype=jnp.int32) ^ position
        beside, below, across = flip(attend_in, 1), flip(attend_in, 2), flip(attend_in, 4)
        got_rows, beside, below, across, own_up = together(
            swap(pieces, SEQ), beside, below, across, own_up
        )
        corner = flip(across, 2)
        row_blocks = [attend_in, beside]
        row_blocks += [part for block in (below, across, corner) for part in (block, flip(block, 1))]
    else:
        order = jnp.arange(count, dtype=jnp.int32)
        row_blocks = [lax.all_gather(attend_in, SEQ, axis=0, tiled=True)]
        got_rows = swap(pieces, SEQ)
    documents = jnp.broadcast_to(
        got_rows[:, weight_rows, :row_count].reshape(length, 1), (length, LANES)
    )
    own_copies = jnp.broadcast_to(
        got_rows[None, :, :weight_rows], (groups, count, weight_rows, 3 * LANES + width)
    )
    all_copies = swap(own_copies, EXP)

    peer_up = others(own_up, "hi")
    *row_blocks, all_copies, peer_up, own_up, own_down, slots_out, active, order, documents = (
        together(
            *row_blocks,
            all_copies,
            peer_up,
            own_up,
            own_down,
            to_slots(cotangent[0]),
            active,
            order,
            documents,
        )
    )
    columns = jnp.swapaxes(all_copies[..., : 3 * LANES], 0, 1).reshape(width, 3 * LANES)
    grad_arrived = dispatch(slots_out)
    peer_down = others(own_down, "hi")
    side_up = others(own_up, "in")
    side_down = others(own_down, "in")
    far_up = others(peer_up, "in")

    mixed_low, mixed_full, stat, pair = attend(
        active, order, row_blocks, columns, documents, row_count
    )

    def place_heads():
        index = np.arange(LANES)
        matrix = np.zeros((count, LANES, width), np.float32)
        for device in range(count):
            for slot in range(2):
                if used[device, slot]:
                    own = index[slot * HALF : (slot + 1) * HALF]
                    matrix[device, own, starts[device] + own] = 1.0
        return jnp.asarray(matrix, BF16)

    head_places = place_heads()

    def to_tokens(values):
        return swap(values.reshape(count, row_count, values.shape[1]), SEQ)

    mixed_low, grad_arrived, peer_down, side_up, side_down, far_up, all_copies = together(
        mixed_low, grad_arrived, peer_down, side_up, side_down, far_up, all_copies
    )
    output_full = jnp.swapaxes(all_copies[..., 3 * LANES :], 0, 1).reshape(width, width)
    far_down = others(peer_down, "in")
    mixed_pieces, projection_low, far_down = together(
        to_tokens(mixed_low), projection_low, far_down
    )
    projection_full = lax.all_gather(projection_low, ALL, axis=0, tiled=True)
    attend_out = jnp.einsum(
        "jtc,jcd->td", mixed_pieces, head_places, preferred_element_type=F32
    ).astype(BF16)
    branch = jnp.dot(attend_out, output_full, preferred_element_type=F32)
    middle = inputs + branch
    scale_second = lax.rsqrt(jnp.mean(middle * middle, axis=-1, keepdims=True) + EPSILON)
    normed_second = middle * scale_second
    expert_in = (normed_second * gain_second).astype(BF16)

    arrived = dispatch(to_slots(expert_in))
    ups, downs = (own_up, peer_up, side_up, far_up), (own_down, peer_down, side_down, far_down)
    grad_slots, actives, hiddens = expert_part(arrived, grad_arrived, ups, downs)
    returned_grad = send_back(grad_slots)

    blocks = list(zip(actives, hiddens, strict=True))
    down_far, up_far, down_peer, up_peer = unit_grads(
        grad_arrived, arrived, (blocks[3], blocks[1]), (BF16, F32)
    )
    (down_part,) = to_owners([down_far], "in")
    down_side, up_side, down_own, up_own = unit_grads(
        grad_arrived, arrived, (blocks[2], blocks[0]), (BF16, F32)
    )
    produced = produced_part(actives, downs)
    returned_grad, down_part, up_far, up_peer, projection_full, produced, down_side, up_own = (
        together(
            returned_grad, down_part, up_far, up_peer, projection_full, produced, down_side, up_own
        )
    )
    grad_expert_in = collect(returned_grad)
    (up_part,) = to_owners([up_far], "in")
    peers = lax.axis_size("hi")

    def hi_parts(value):
        return to_owners(list(value.astype(BF16).reshape(peers - 1, -1, width)), "hi")

    down_hi = hi_parts(add_all(down_peer, [down_part]))

    scaled_second = grad_expert_in * gain_second
    gain_second_part = jnp.sum(grad_expert_in * normed_second, axis=0)
    grad_middle = scale_second * (
        scaled_second
        - normed_second * jnp.mean(scaled_second * normed_second, axis=-1, keepdims=True)
    )
    residual_grad = upstream + grad_middle
    branch_grad = residual_grad.astype(BF16)
    grad_mixed = jnp.einsum(
        "td,ed->te", branch_grad, output_full, preferred_element_type=F32
    ).astype(BF16)

    sent_grad = jnp.stack([grad_mixed[:, s : s + LANES] for s in starts])
    row_grad = swap(sent_grad, SEQ).reshape(length, LANES)

    group = lax.axis_index(EXP)

    def group_rows(value):
        rows = value.reshape(count, groups, weight_rows, -1)
        own, *away = [
            lax.dynamic_index_in_dim(rows, lax.rem(group + step, groups), 1, keepdims=False)
            for step in range(groups)
        ]
        return own, away

    output_term = jnp.einsum("tc,te->ce", attend_out, branch_grad, preferred_element_type=F32)
    output_own, output_away = group_rows(output_term.astype(BF16))
    output_away = to_owners(output_away, "exp")
    row_grad, produced, down_side, up_side, up_part, *held = together(
        row_grad, produced, down_side, up_side, up_part, *down_hi, *output_away
    )
    down_hi, output_away = held[: peers - 1], held[peers - 1 :]
    (down_early,) = to_owners([down_side], "in")
    (up_early,) = to_owners([up_side], "in")
    up_hi = hi_parts(add_all(up_peer, [up_part]))
    returned = send_back(produced)
    grad_qkv, grad_lying = attend_back(
        active, order, pair, documents, stat, row_grad, mixed_full, row_count, scaling
    )
    grad_qkv, grad_lying, returned, down_early, up_early, *up_hi = together(
        grad_qkv, grad_lying, returned, down_early, up_early, *up_hi
    )
    down_grad = add_all(down_own, [down_early, *down_hi])[None]
    up_grad = add_all(up_own, [up_early, *up_hi])[None]
    block_output = (middle + collect(returned)).astype(BF16)[None]

    column_own, column_away = group_rows(column_terms(row_blocks, grad_lying))
    dense_rows = jnp.concatenate(
        [
            add_all(column_own, to_owners(column_away, "exp")).astype(BF16),
            add_all(output_own, output_away).astype(BF16),
        ],
        axis=2,
    )
    local_square = jnp.sum(up_grad * up_grad) + jnp.sum(down_grad * down_grad)
    grad_pieces, dense_rows, local_square = together(
        to_tokens(grad_qkv), dense_rows, local_square
    )
    projection_grad, output_grad, dense_square = dense_grads(swap(dense_rows, SEQ), starts)
    input_grad, gain_first_part = close_norm(
        grad_pieces, starts, projection_full, tokens[0], gain_first[None], residual_grad
    )
    input_grad, gain_first_part = input_grad[None], gain_first_part[0]
    summed = spread_sum(
        jnp.concatenate(
            [gain_first_part, gain_second_part, dense_square[0] + local_square]
        )[None]
    )[0]
    gains_grad = summed[: 2 * width].reshape(2, width)
    grad_norm = jnp.sqrt(summed[2 * width] + jnp.sum(gains_grad * gains_grad))
    factor = jnp.minimum(1.0, CLIP / (grad_norm + 1e-06))
    (
        (projection_moment, projection_square, projection_new),
        (output_moment, output_square, output_new),
        (up_moment, up_square, up_new),
        (down_moment, down_square, down_new),
    ) = adam_all(
        factor,
        [
            (projection, projection_grad, projection_first, projection_second),
            (output_weight, output_grad, output_first, output_second),
            (expert_up, up_grad, up_first, up_second),
            (expert_down, down_grad, down_first, down_second),
        ],
        (RATE_MATRIX, RATE_OUTPUT, RATE_MATRIX, RATE_MATRIX),
        3,
    )
    gains_moment, gains_square, gains_new = adam_update(
        norm_gains, gains_grad, gains_first, gains_second, factor, RATE_GAIN, 0.0
    )
    return (
        block_output,
        input_grad,
        grad_norm,
        projection_grad,
        projection_moment,
        projection_square,
        projection_new,
        output_grad,
        output_moment,
        output_square,
        output_new,
        up_grad,
        up_moment,
        up_square,
        up_new,
        down_grad,
        down_moment,
        down_square,
        down_new,
        gains_grad,
        gains_moment,
        gains_square,
        gains_new,
    )


def solution(mesh):
    token = P("exp", SEQ, None)
    dense = P(ALL, None)
    expert = P("exp", SEQ, None)
    in_specs = (
        (token, token, P("exp", SEQ), token)
        + (dense, dense, expert, expert, P())
        + (dense,) * 4
        + (expert,) * 4
        + (P(), P())
    )
    out_specs = (token, token, P()) + (dense,) * 8 + (expert,) * 8 + (P(),) * 4
    rows, groups = mesh.devices.shape
    fine = Mesh(mesh.devices.reshape(rows // 4, 2, 2, groups), ALL)
    return jax.shard_map(body, mesh=fine, in_specs=in_specs, out_specs=out_specs, check_vma=False)
```

```python
import functools
import math

import jax
import jax.numpy as jnp
import numpy as np
from jax import lax
from jax.experimental import pallas as pl
from jax.experimental.pallas import tpu as pltpu
from jax.sharding import Mesh
from jax.sharding import PartitionSpec as P

HEADS = 12
CAP = 128
STEP = 10


EPSILON = 1e-05
CLIP = 1.0
BETA_ONE = 0.9
BETA_TWO = 0.99
ADAM_FLOOR = 1e-08
DECAY = 0.1
RATE_MATRIX = 0.04
RATE_OUTPUT = 0.1
RATE_GAIN = 0.5

SEQ = ("hi", "lo", "in")
EXP = ("exp",)
ALL = SEQ + EXP
TEAM = ("lo",)
SHARE = ("hi", "in")
LANES = 128
HALF = 64
FAR = -1e30
BF16 = jnp.bfloat16
F32 = jnp.float32
VMEM_LIMIT = 60 * 1024 * 1024


def head_plan(count):
    whole = math.lcm(HEADS, count)
    units, parts = whole // count, whole // HEADS
    first = np.zeros((count,), np.int64)
    active = np.zeros((count, 2, count), np.int32)
    for device in range(count):
        first[device] = min(units * device // parts, HEADS - 2)
        for unit in range(units * device, units * (device + 1)):
            slot = unit // parts - first[device]
            for block in range(count):
                turn = block % (2 * parts)
                if min(turn, 2 * parts - 1 - turn) == unit % parts:
                    active[device, slot, block] = 1
    return first, active


def three_parts(value):
    high = value.astype(BF16).astype(F32)
    middle = (value - high).astype(BF16).astype(F32)
    return high, middle, value - high - middle


def contract(left, right, left_axis, right_axis):
    return lax.dot_general(
        left, right, (((left_axis,), (right_axis,)), ((), ())), preferred_element_type=F32
    )


def slot_arrays(packed, documents, kind, slot):
    spare = HALF - HALF * slot
    lane = lax.broadcasted_iota(jnp.int32, packed.shape, 1)
    own = (lane < HALF) if slot == 0 else (lane >= HALF)
    place = (lane - spare).astype(F32)
    ours = place == documents
    first = (lane >= spare) & (lane < spare + 3)
    if kind == "query":
        extra = jnp.where(first & jnp.logical_not(ours), FAR, 0.0)
    elif kind == "key":
        extra = jnp.where(ours | ((lane >= spare + 3) & (lane < spare + 6)), 1.0, 0.0)
    else:
        extra = jnp.where(first, 1.0, 0.0)
    return jnp.where(own, packed, extra).astype(BF16)


def fill_slots(packed_of, documents_ref, wide_ref, kinds, place):
    documents = documents_ref[place, :].astype(F32)
    for number, kind in enumerate(kinds):
        packed = packed_of(kind).astype(F32)
        if kind == "query":
            packed = packed * 0.125
        for slot in range(2):
            column = (2 * number + slot) * LANES
            wide_ref[place, column : column + LANES] = slot_arrays(packed, documents, kind, slot)


def attend_kernel(active_ref, order_ref, *refs, block, chunk, held):
    row_refs = refs[:held]
    columns_ref, documents_ref = refs[held : held + 2]
    low_ref, full_ref, stat_ref, pair_ref, mixed_ref, wide_ref = refs[held + 2 :]
    at = pl.program_id(0)

    @pl.when(at == 0)
    def _():
        def fill(tokens, index):
            place = pl.ds(pl.multiple_of(order_ref[index] * block, block), block)
            packed = contract(tokens, columns_ref[...], 1, 0).astype(BF16)
            pair_ref[place, :] = packed[:, LANES:]
            parts = {
                kind: packed[:, part * LANES : (part + 1) * LANES]
                for part, kind in enumerate(("query", "key", "value"))
            }
            fill_slots(parts.get, documents_ref, wide_ref, tuple(parts), place)

        if held > 1:
            for index, row_ref in enumerate(row_refs):
                fill(row_ref[...], index)
        else:

            @pl.loop(0, pl.num_programs(0))
            def _(index):
                fill(row_refs[0][pl.ds(pl.multiple_of(index * block, block), block), :], index)

    rows = pl.ds(pl.multiple_of(at * block, block), block)
    lane = lax.broadcasted_iota(jnp.int32, (block, LANES), 1)
    last = lax.div(at * block, chunk)
    for slot in range(2):
        spare = HALF - HALF * slot
        own = (lane < HALF) if slot == 0 else (lane >= HALF)
        columns = slice(slot * LANES, (slot + 1) * LANES)

        @pl.when(active_ref[slot, at] != 0)
        def _():
            query = wide_ref[rows, columns]

            def step(index, carry, edge):
                top, weighted = carry
                place = pl.ds(pl.multiple_of(index * chunk, chunk), chunk)
                keys = wide_ref[place, 2 * LANES + slot * LANES : 3 * LANES + slot * LANES]
                values = wide_ref[place, 4 * LANES + slot * LANES : 5 * LANES + slot * LANES]
                scores = contract(query, keys, 1, 1)
                if edge:
                    key_at = index * chunk + lax.broadcasted_iota(jnp.int32, (block, chunk), 1)
                    query_at = at * block + lax.broadcasted_iota(jnp.int32, (block, chunk), 0)
                    scores = jnp.where(key_at <= query_at, scores, FAR)
                new_top = jnp.maximum(top, jnp.max(scores, axis=1, keepdims=True))
                weights = jnp.exp(scores - new_top).astype(BF16)
                weighted = weighted * jnp.exp(top - new_top) + contract(weights, values, 1, 0)
                return new_top, weighted

            carry = (jnp.full((block, 1), FAR, F32), jnp.zeros((block, LANES), F32))
            carry = lax.fori_loop(0, last, lambda index, state: step(index, state, False), carry)
            top, weighted = step(last, carry, True)
            total = weighted[:, spare : spare + 1]
            mixed_ref[slot] = jnp.where(own, weighted / total, 0.0)
            log_total = top + jnp.log(total)
            high, middle, small = three_parts(log_total)
            extra = jnp.where(lane == spare + 3, -high, 0.0)
            extra = jnp.where(lane == spare + 4, -middle, extra)
            extra = jnp.where(lane == spare + 5, -small, extra)
            stat_ref[:, columns] = (query.astype(F32) + extra).astype(BF16)

        @pl.when(active_ref[slot, at] == 0)
        def _():
            mixed_ref[slot] = jnp.zeros((block, LANES), F32)
            stat_ref[:, columns] = jnp.zeros((block, LANES), BF16)

    mixed = mixed_ref[0] + mixed_ref[1]
    full_ref[...] = mixed
    low_ref[...] = mixed.astype(BF16)


def attend_back_kernel(
    active_ref,
    order_ref,
    pair_ref,
    documents_ref,
    stat_ref,
    grad_ref,
    mixed_ref,
    out_ref,
    lying_ref,
    key_sum_ref,
    value_sum_ref,
    query_sum_ref,
    wide_ref,
    *,
    block,
    chunk,
    scaling,
):
    at = pl.program_id(0)
    rows = pl.ds(pl.multiple_of(at * block, block), block)
    lane = lax.broadcasted_iota(jnp.int32, (block, LANES), 1)
    last = lax.div(at * block, chunk)

    @pl.when(at == 0)
    def _():
        @pl.loop(0, pl.num_programs(0))
        def _(index):
            place = pl.ds(pl.multiple_of(index * block, block), block)
            parts = {"key": pair_ref[place, :LANES], "value": pair_ref[place, LANES:]}
            fill_slots(parts.get, documents_ref, wide_ref, tuple(parts), place)

        key_sum_ref[...] = jnp.zeros_like(key_sum_ref)
        value_sum_ref[...] = jnp.zeros_like(value_sum_ref)

    for slot in range(2):
        spare = HALF - HALF * slot
        own = (lane < HALF) if slot == 0 else (lane >= HALF)
        columns = slice(slot * LANES, (slot + 1) * LANES)
        query_sum_ref[slot] = jnp.zeros((block, LANES), F32)

        @pl.when(active_ref[slot, at] != 0)
        def _():
            query = stat_ref[:, columns]
            grad = grad_ref[...].astype(F32)
            delta = jnp.sum(jnp.where(own, grad * mixed_ref[...], 0.0), axis=1, keepdims=True)
            high, middle, small = three_parts(delta)
            extra = jnp.where(lane == spare, -high, 0.0)
            extra = jnp.where(lane == spare + 1, -middle, extra)
            extra = jnp.where(lane == spare + 2, -small, extra)
            grad_low = jnp.where(own, grad, extra).astype(BF16)

            def step(index, edge):
                place = pl.ds(pl.multiple_of(index * chunk, chunk), chunk)
                keys = wide_ref[place, slot * LANES : (slot + 1) * LANES]
                values = wide_ref[place, (2 + slot) * LANES : (3 + slot) * LANES]
                scores = contract(keys, query, 1, 1)
                if edge:
                    key_at = index * chunk + lax.broadcasted_iota(jnp.int32, (chunk, block), 0)
                    query_at = at * block + lax.broadcasted_iota(jnp.int32, (chunk, block), 1)
                    scores = jnp.where(key_at <= query_at, scores, FAR)
                weights = jnp.exp(scores)
                grad_weights = contract(values, grad_low, 1, 1)
                grad_scores = (weights * grad_weights).astype(BF16)
                value_sum_ref[slot, place, :] += contract(weights.astype(BF16), grad_low, 1, 0)
                key_sum_ref[slot, place, :] += contract(grad_scores, query, 1, 0)
                query_sum_ref[slot] += contract(grad_scores, keys, 0, 0)

            @pl.loop(0, last)
            def _(index):
                step(index, False)

            step(last, True)

    first_half = lane < HALF
    query_grad = jnp.where(first_half, query_sum_ref[0], query_sum_ref[1]) * scaling
    out_ref[rows, :LANES] = query_grad.astype(BF16)
    lying = pl.ds(pl.multiple_of(order_ref[at] * block, block), block)
    lying_ref[lying, :LANES] = query_grad.astype(BF16)

    @pl.when(at == pl.num_programs(0) - 1)
    def _():
        @pl.loop(0, pl.num_programs(0))
        def _(index):
            place = pl.ds(pl.multiple_of(index * block, block), block)
            key_grad = jnp.where(first_half, key_sum_ref[0, place, :], key_sum_ref[1, place, :])
            value_grad = jnp.where(
                first_half, value_sum_ref[0, place, :], value_sum_ref[1, place, :]
            )
            out_ref[place, LANES : 2 * LANES] = key_grad.astype(BF16)
            out_ref[place, 2 * LANES :] = value_grad.astype(BF16)
            lying = pl.ds(pl.multiple_of(order_ref[index] * block, block), block)
            lying_ref[lying, LANES : 2 * LANES] = key_grad.astype(BF16)
            lying_ref[lying, 2 * LANES :] = value_grad.astype(BF16)


def whole(value):
    return pl.BlockSpec(value.shape, lambda i, *unused: (0, 0), pipeline_mode=pl.Buffered(1))


SMALL = pl.CostEstimate(flops=1, bytes_accessed=1, transcendentals=0)


def attend(active, order, row_blocks, columns, documents, block):
    length = documents.shape[0]
    pair = jax.ShapeDtypeStruct((length, 2 * LANES), BF16)
    return pl.pallas_call(
        functools.partial(attend_kernel, block=block, chunk=2 * block, held=len(row_blocks)),
        grid_spec=pltpu.PrefetchScalarGridSpec(
            num_scalar_prefetch=2,
            grid=(length // block,),
            in_specs=[whole(value) for value in (*row_blocks, columns, documents)],
            out_specs=[
                pl.BlockSpec((block, LANES), lambda i, a, o: (i, 0)),
                pl.BlockSpec((block, LANES), lambda i, a, o: (i, 0)),
                pl.BlockSpec((block, 2 * LANES), lambda i, a, o: (i, 0)),
                whole(pair),
            ],
            scratch_shapes=[
                pltpu.VMEM((2, block, LANES), F32),
                pltpu.VMEM((length, 6 * LANES), BF16),
            ],
        ),
        out_shape=[
            jax.ShapeDtypeStruct((length, LANES), BF16),
            jax.ShapeDtypeStruct((length, LANES), F32),
            jax.ShapeDtypeStruct((length, 2 * LANES), BF16),
            pair,
        ],
        compiler_params=pltpu.CompilerParams(vmem_limit_bytes=VMEM_LIMIT),
        cost_estimate=SMALL,
    )(active, order, *row_blocks, columns, documents)


def attend_back(active, order, pair, documents, stat, grad, mixed, block, scaling):
    length = pair.shape[0]
    count = length // block
    return pl.pallas_call(
        functools.partial(attend_back_kernel, block=block, chunk=2 * block, scaling=scaling),
        grid_spec=pltpu.PrefetchScalarGridSpec(
            num_scalar_prefetch=2,
            grid=(count,),
            in_specs=[
                whole(pair),
                whole(documents),
                pl.BlockSpec((block, 2 * LANES), lambda i, a, o: (i, 0)),
                pl.BlockSpec((block, LANES), lambda i, a, o: (i, 0)),
                pl.BlockSpec((block, LANES), lambda i, a, o: (i, 0)),
            ],
            out_specs=[
                pl.BlockSpec(
                    (length, 3 * LANES), lambda i, a, o: (0, 0), pipeline_mode=pl.Buffered(1)
                )
            ]
            * 2,
            scratch_shapes=[
                pltpu.VMEM((2, length, LANES), F32),
                pltpu.VMEM((2, length, LANES), F32),
                pltpu.VMEM((2, block, LANES), F32),
                pltpu.VMEM((length, 4 * LANES), BF16),
            ],
        ),
        out_shape=[jax.ShapeDtypeStruct((length, 3 * LANES), BF16)] * 2,
        compiler_params=pltpu.CompilerParams(vmem_limit_bytes=VMEM_LIMIT),
        cost_estimate=SMALL,
    )(active, order, pair, documents, stat, grad, mixed)


def expert_kernel(arrived_ref, grad_ref, *refs, count):
    up_refs, down_refs = refs[:count], refs[count : 2 * count]
    total_ref = refs[2 * count]
    active_refs, hidden_refs = refs[2 * count + 1 : 3 * count + 1], refs[3 * count + 1 :]
    arrived, grad_arrived = arrived_ref[...], grad_ref[...]
    scale = math.sqrt(2.0 / math.pi)
    total = jnp.zeros(total_ref.shape, F32)
    for up_ref, down_ref, active_ref, hidden_ref in zip(
        up_refs, down_refs, active_refs, hidden_refs, strict=True
    ):
        up = up_ref[...]
        hidden = contract(arrived, up, 1, 1)
        squared = hidden * hidden
        bend = jnp.tanh(scale * hidden * (1.0 + 0.044715 * squared))
        half = 0.5 + 0.5 * bend
        active_ref[...] = (hidden * half).astype(BF16)
        slope = half + (0.5 * scale) * hidden * (1.0 - bend * bend) * (1.0 + 3 * 0.044715 * squared)
        grad_hidden = (slope * contract(grad_arrived, down_ref[...], 1, 1)).astype(BF16)
        hidden_ref[...] = grad_hidden
        total = total + contract(grad_hidden, up, 1, 0)
    total_ref[...] = total.astype(BF16)


def rows_spec(value, block):
    return pl.BlockSpec((block, value.shape[1]), lambda i: (i, 0))


def expert_part(arrived, grad_arrived, ups, downs):
    slots, width = arrived.shape
    block = 256
    units = [jax.ShapeDtypeStruct((slots, up.shape[0]), BF16) for up in ups]
    outs = [jax.ShapeDtypeStruct((slots, width), BF16), *units, *units]
    total, *parts = pl.pallas_call(
        functools.partial(expert_kernel, count=len(ups)),
        grid=(slots // block,),
        in_specs=[rows_spec(arrived, block), rows_spec(grad_arrived, block)]
        + [whole(value) for value in (*ups, *downs)],
        out_specs=[rows_spec(out, block) for out in outs],
        out_shape=outs,
        compiler_params=pltpu.CompilerParams(vmem_limit_bytes=VMEM_LIMIT),
        cost_estimate=SMALL,
    )(arrived, grad_arrived, *ups, *downs)
    return total, parts[: len(ups)], parts[len(ups) :]


def produced_kernel(*refs, count):
    total = contract(refs[0][...], refs[count][...], 1, 0)
    for index in range(1, count):
        total = total + contract(refs[index][...], refs[count + index][...], 1, 0)
    refs[-1][...] = total.astype(BF16)


def produced_part(actives, downs):
    slots, width = actives[0].shape[0], downs[0].shape[1]
    block = 256
    out = jax.ShapeDtypeStruct((slots, width), BF16)
    return pl.pallas_call(
        functools.partial(produced_kernel, count=len(actives)),
        grid=(slots // block,),
        in_specs=[rows_spec(value, block) for value in actives] + [whole(down) for down in downs],
        out_specs=rows_spec(out, block),
        out_shape=out,
        compiler_params=pltpu.CompilerParams(vmem_limit_bytes=VMEM_LIMIT),
        cost_estimate=SMALL,
    )(*actives, *downs)


def unit_kernel(grad_ref, arrived_ref, *refs, count):
    for index in range(count):
        active_ref, hidden_ref = refs[2 * index : 2 * index + 2]
        down_ref, up_ref = refs[2 * count + 2 * index : 2 * count + 2 * index + 2]
        down_ref[...] = contract(active_ref[...], grad_ref[...], 0, 0).astype(down_ref.dtype)
        up_ref[...] = contract(hidden_ref[...], arrived_ref[...], 0, 0).astype(up_ref.dtype)


def unit_grads(grad_arrived, arrived, blocks, kinds):
    slots, width = arrived.shape
    block = 256
    right = pl.BlockSpec((slots, block), lambda i: (0, i))
    outs = [
        jax.ShapeDtypeStruct((active.shape[1], width), kind)
        for (active, unused), kind in zip(blocks, kinds, strict=True)
        for part in range(2)
    ]
    flat = [value for pair in blocks for value in pair]
    return pl.pallas_call(
        functools.partial(unit_kernel, count=len(blocks)),
        grid=(width // block,),
        in_specs=[right, right] + [whole(value) for value in flat],
        out_specs=[pl.BlockSpec((out.shape[0], block), lambda i: (0, i)) for out in outs],
        out_shape=outs,
        compiler_params=pltpu.CompilerParams(vmem_limit_bytes=VMEM_LIMIT),
        cost_estimate=SMALL,
    )(grad_arrived, arrived, *flat)


def column_kernel(*refs, held):
    row_refs = refs[:held]
    lying_ref, out_ref = refs[held:]
    start, total = 0, None
    for row_ref in row_refs:
        rows = row_ref.shape[0]
        part = contract(row_ref[...], lying_ref[start : start + rows, :], 0, 0)
        total = part if total is None else total + part
        start += rows
    out_ref[...] = total.astype(BF16)


def column_terms(row_blocks, grad_lying):
    width = row_blocks[0].shape[1]
    block = 256
    out = jax.ShapeDtypeStruct((width, 3 * LANES), BF16)
    return pl.pallas_call(
        functools.partial(column_kernel, held=len(row_blocks)),
        grid=(width // block,),
        in_specs=[
            pl.BlockSpec((value.shape[0], block), lambda i: (0, i)) for value in row_blocks
        ]
        + [whole(grad_lying)],
        out_specs=rows_spec(out, block),
        out_shape=out,
        compiler_params=pltpu.CompilerParams(vmem_limit_bytes=VMEM_LIMIT),
        cost_estimate=SMALL,
    )(*row_blocks, grad_lying)


def close_kernel(
    pieces_ref, matrix_ref, tokens_ref, gain_ref, residual_ref, out_ref, part_ref, sum_ref, *, starts
):
    width = tokens_ref.shape[1]
    lane = lax.broadcasted_iota(jnp.int32, (tokens_ref.shape[0], LANES), 1)
    sum_ref[...] = jnp.zeros_like(sum_ref)
    for device, start in enumerate(starts):
        for part in range(3):
            piece = pieces_ref[device, :, part * LANES : (part + 1) * LANES].astype(F32)
            column = part * width + start
            if column % LANES == 0:
                sum_ref[:, column : column + LANES] += piece
            else:
                turned = pltpu.roll(piece, HALF, 1)
                low, high = column - HALF, column + HALF
                sum_ref[:, low : low + LANES] += jnp.where(lane >= HALF, turned, 0.0)
                sum_ref[:, high : high + LANES] += jnp.where(lane < HALF, turned, 0.0)
    grad = contract(sum_ref[...].astype(BF16), matrix_ref[...], 1, 1)
    inputs = tokens_ref[...].astype(F32)
    scale = lax.rsqrt(jnp.mean(inputs * inputs, axis=-1, keepdims=True) + EPSILON)
    normed = inputs * scale
    scaled = grad * gain_ref[...]
    mean = jnp.mean(scaled * normed, axis=-1, keepdims=True)
    out_ref[...] = residual_ref[...] + scale * (scaled - normed * mean)
    part_ref[...] = jnp.sum(grad * normed, axis=0, keepdims=True)


def close_norm(pieces, starts, matrix, tokens, gain, residual):
    rows, width = tokens.shape
    outs = [
        jax.ShapeDtypeStruct((rows, width), F32),
        jax.ShapeDtypeStruct((1, width), F32),
    ]
    return pl.pallas_call(
        functools.partial(close_kernel, starts=starts),
        in_specs=[pl.BlockSpec(memory_space=pltpu.VMEM)] * 5,
        out_specs=[pl.BlockSpec(memory_space=pltpu.VMEM)] * 2,
        out_shape=outs,
        scratch_shapes=[pltpu.VMEM((rows, 3 * width), F32)],
        compiler_params=pltpu.CompilerParams(vmem_limit_bytes=VMEM_LIMIT),
        cost_estimate=SMALL,
    )(pieces, matrix, tokens, gain, residual)


def dense_kernel(terms_ref, columns_ref, output_ref, square_ref, *, starts):
    width = output_ref.shape[1]
    columns_ref[...] = jnp.zeros_like(columns_ref)
    lane = lax.broadcasted_iota(jnp.int32, (columns_ref.shape[0], LANES), 1)
    output = jnp.zeros(output_ref.shape, F32)
    for device, start in enumerate(starts):
        output = output + terms_ref[device, :, 3 * LANES :].astype(F32)
        for part in range(3):
            piece = terms_ref[device, :, part * LANES : (part + 1) * LANES].astype(F32)
            column = part * width + start
            if column % LANES == 0:
                columns_ref[:, column : column + LANES] += piece
            else:
                turned = pltpu.roll(piece, HALF, 1)
                low, high = column - HALF, column + HALF
                columns_ref[:, low : low + LANES] += jnp.where(lane >= HALF, turned, 0.0)
                columns_ref[:, high : high + LANES] += jnp.where(lane < HALF, turned, 0.0)
    output_ref[...] = output
    columns = columns_ref[...]
    square_ref[...] = jnp.zeros_like(square_ref) + (
        jnp.sum(columns * columns) + jnp.sum(output * output)
    )


def dense_grads(terms, starts):
    unused, rows, lanes = terms.shape
    width = lanes - 3 * LANES
    outs = [jax.ShapeDtypeStruct((rows, columns), F32) for columns in (3 * width, width)]
    outs.append(jax.ShapeDtypeStruct((1, LANES), F32))
    return pl.pallas_call(
        functools.partial(dense_kernel, starts=starts),
        in_specs=[pl.BlockSpec(memory_space=pltpu.VMEM)],
        out_specs=[pl.BlockSpec(memory_space=pltpu.VMEM)] * 3,
        out_shape=outs,
        compiler_params=pltpu.CompilerParams(vmem_limit_bytes=VMEM_LIMIT),
        cost_estimate=SMALL,
    )(terms)


def adam_update(weight, grad, first, second, factor, rate, decay):
    clipped = grad * factor
    first_new = BETA_ONE * first + (1.0 - BETA_ONE) * clipped
    second_new = BETA_TWO * second + (1.0 - BETA_TWO) * clipped * clipped
    first_hat = first_new / (1.0 - BETA_ONE**STEP)
    second_hat = second_new / (1.0 - BETA_TWO**STEP)
    weight_new = weight - rate * (first_hat / (jnp.sqrt(second_hat) + ADAM_FLOOR) + decay * weight)
    return (first_new, second_new, weight_new)


def together(*values):
    return lax.optimization_barrier(values)


def swap(value, axes):
    return lax.all_to_all(value, axes, split_axis=0, concat_axis=0, tiled=True)


def adam_kernel(factor_ref, *refs, rates):
    count = len(rates)
    factor = factor_ref[0]
    for index, rate in enumerate(rates):
        weight, grad, first, second = [ref[...] for ref in refs[4 * index : 4 * index + 4]]
        outs = refs[4 * count + 3 * index : 4 * count + 3 * index + 3]
        for out, value in zip(
            outs, adam_update(weight, grad, first, second, factor, rate, DECAY), strict=True
        ):
            out[...] = value


def adam_all(factor, leaves, rates, steps):
    flat = [value.reshape(value.shape[-2:]) for leaf in leaves for value in leaf]

    def spec(value):
        rows, columns = value.shape
        if rows % (8 * steps) == 0:
            return pl.BlockSpec((rows // steps, columns), lambda i: (i, 0))
        lanes = columns // steps
        return pl.BlockSpec((rows, lanes), lambda i: (0, i))

    shapes = [jax.ShapeDtypeStruct(value.shape, F32) for value in flat[::4] for _ in range(3)]
    outs = pl.pallas_call(
        functools.partial(adam_kernel, rates=rates),
        grid=(steps,),
        in_specs=[pl.BlockSpec(memory_space=pltpu.SMEM)] + [spec(value) for value in flat],
        out_specs=[spec(shape) for shape in shapes],
        out_shape=shapes,
        compiler_params=pltpu.CompilerParams(vmem_limit_bytes=VMEM_LIMIT),
        cost_estimate=pl.CostEstimate(
            flops=20 * sum(value.size for value in flat[::4]),
            bytes_accessed=28 * sum(value.size for value in flat[::4]),
            transcendentals=0,
        ),
    )(factor.reshape(1), *flat)
    return [
        [out.reshape(leaf[0].shape) for out in outs[3 * index : 3 * index + 3]]
        for index, leaf in enumerate(leaves)
    ]


def flip(value, bits):
    count = lax.axis_size(SEQ)
    return lax.ppermute(value, SEQ, [(index, index ^ bits) for index in range(count)])


def others(value, axis):
    size = lax.axis_size(axis)
    parts = [
        lax.ppermute(value, axis, [((i + step) % size, i) for i in range(size)])
        for step in range(1, size)
    ]
    return parts[0] if size == 2 else jnp.concatenate(parts, axis=0)


def to_owners(blocks, axis):
    size = lax.axis_size(axis)
    return [
        lax.ppermute(block, axis, [(i, (i + step) % size) for i in range(size)])
        for step, block in enumerate(blocks, 1)
    ]


def add_all(own, parts):
    return functools.reduce(lambda total, part: total + part.astype(F32), parts, own.astype(F32))


def spread_sum(value):
    count = lax.axis_size(ALL)
    return jnp.sum(swap(jnp.broadcast_to(value[None], (count, *value.shape)), ALL), axis=0)


def body(
    tokens,
    cotangent,
    segment_ids,
    expert_ids,
    projection,
    output_weight,
    expert_up,
    expert_down,
    norm_gains,
    projection_first,
    projection_second,
    output_first,
    output_second,
    up_first,
    up_second,
    down_first,
    down_second,
    gains_first,
    gains_second,
):
    inputs = tokens[0].astype(F32)
    upstream = cotangent[0].astype(F32)
    row_count = inputs.shape[0]
    width = inputs.shape[1]
    head_size = width // HEADS
    scaling = head_size ** (-0.5)
    count = lax.axis_size(SEQ)
    groups = lax.axis_size("exp")
    team = lax.axis_size(TEAM)
    position = lax.axis_index(SEQ)
    length = count * row_count
    weight_rows = projection.shape[0]
    first_heads, active_table = head_plan(count)
    starts = [int(head) * head_size for head in first_heads]
    active = lax.dynamic_index_in_dim(jnp.asarray(active_table), position, 0, keepdims=False)
    gain_first = norm_gains[0]
    gain_second = norm_gains[1]
    used = active_table.any(axis=2)

    scale_first = lax.rsqrt(jnp.mean(inputs * inputs, axis=-1, keepdims=True) + EPSILON)
    normed_first = inputs * scale_first
    attend_in = (normed_first * gain_first).astype(BF16)
    slots = groups * CAP
    chosen = expert_ids[0, :, 0]
    one_hot = (chosen[:, None] == jnp.arange(groups, dtype=jnp.int32)[None, :]).astype(F32)
    token = jnp.arange(row_count, dtype=jnp.int32)
    earlier = (token[None, :] < token[:, None]).astype(BF16)
    counts = jnp.dot(earlier, one_hot.astype(BF16), preferred_element_type=F32)
    rank = jnp.sum(counts * one_hot, axis=1).astype(jnp.int32)
    target = chosen * CAP + rank
    placing = (target[:, None] == jnp.arange(slots, dtype=jnp.int32)[None, :]).astype(BF16)

    def to_slots(values):
        outgoing = jnp.einsum("ts,td->sd", placing, values, preferred_element_type=F32)
        return outgoing.astype(BF16)

    def dispatch(outgoing):
        outgoing = jnp.broadcast_to(
            outgoing.reshape(1, groups, CAP, width), (team, groups, CAP, width)
        )
        return swap(outgoing.reshape(team * groups, CAP, width), TEAM + EXP).reshape(
            team * slots, width
        )

    def send_back(values):
        return swap(values.reshape(team * groups, CAP, width), TEAM + EXP).reshape(
            team, slots, width
        )

    def collect(returned):
        return jnp.einsum("ts,jsd->td", placing, returned, preferred_element_type=F32)

    projection_low = projection.astype(BF16)
    sent_rows = weight_rows + 8
    own_documents = jnp.zeros((8, 3 * LANES + width), BF16)
    own_documents = own_documents.at[0, :row_count].set(segment_ids[0].astype(BF16))
    output_low = output_weight.astype(BF16)
    pieces = [
        jnp.concatenate(
            [projection_low[:, k * width + s : k * width + s + LANES] for k in range(3)]
            + [output_low],
            axis=1,
        )
        for s in starts
    ]
    pieces = jnp.stack([jnp.concatenate([piece, own_documents], axis=0) for piece in pieces])
    own_up = expert_up[0].astype(BF16)
    own_down = expert_down[0].astype(BF16)
    pairwise = count == 8
    if pairwise:
        order = jnp.arange(count, dtype=jnp.int32) ^ position
        beside, below, across = flip(attend_in, 1), flip(attend_in, 2), flip(attend_in, 4)
        got_rows, beside, below, across, own_up = together(
            swap(pieces, SEQ), beside, below, across, own_up
        )
        corner = flip(across, 2)
        row_blocks = [attend_in, beside]
        row_blocks += [part for block in (below, across, corner) for part in (block, flip(block, 1))]
    else:
        order = jnp.arange(count, dtype=jnp.int32)
        row_blocks = [lax.all_gather(attend_in, SEQ, axis=0, tiled=True)]
        got_rows = swap(pieces, SEQ)
    documents = jnp.broadcast_to(
        got_rows[:, weight_rows, :row_count].reshape(length, 1), (length, LANES)
    )
    own_copies = jnp.broadcast_to(
        got_rows[None, :, :weight_rows], (groups, count, weight_rows, 3 * LANES + width)
    )
    all_copies = swap(own_copies, EXP)

    peer_up = others(own_up, "hi")
    *row_blocks, all_copies, peer_up, own_up, own_down, grad_slots_out = together(
        *row_blocks, all_copies, peer_up, own_up, own_down, to_slots(cotangent[0])
    )
    columns = jnp.swapaxes(all_copies[..., : 3 * LANES], 0, 1).reshape(width, 3 * LANES)
    grad_arrived = dispatch(grad_slots_out)
    peer_down = others(own_down, "hi")
    side_up = others(own_up, "in")
    side_down = others(own_down, "in")
    far_up = others(peer_up, "in")

    mixed_low, mixed_full, stat, pair = attend(
        active, order, row_blocks, columns, documents, row_count
    )

    def place_heads():
        index = np.arange(LANES)
        matrix = np.zeros((count, LANES, width), np.float32)
        for device in range(count):
            for slot in range(2):
                if used[device, slot]:
                    own = index[slot * HALF : (slot + 1) * HALF]
                    matrix[device, own, starts[device] + own] = 1.0
        return jnp.asarray(matrix, BF16)

    head_places = place_heads()

    def to_tokens(values):
        return swap(values.reshape(count, row_count, values.shape[1]), SEQ)

    mixed_low, grad_arrived, peer_down, side_up, side_down, far_up, all_copies = together(
        mixed_low, grad_arrived, peer_down, side_up, side_down, far_up, all_copies
    )
    output_full = jnp.swapaxes(all_copies[..., 3 * LANES :], 0, 1).reshape(width, width)
    far_down = others(peer_down, "in")
    mixed_pieces, projection_low, far_down = together(
        to_tokens(mixed_low), projection_low, far_down
    )
    projection_full = lax.all_gather(projection_low, ALL, axis=0, tiled=True)
    attend_out = jnp.einsum(
        "jtc,jcd->td", mixed_pieces, head_places, preferred_element_type=F32
    ).astype(BF16)
    branch = jnp.dot(attend_out, output_full, preferred_element_type=F32)
    middle = inputs + branch
    scale_second = lax.rsqrt(jnp.mean(middle * middle, axis=-1, keepdims=True) + EPSILON)
    normed_second = middle * scale_second
    expert_in = (normed_second * gain_second).astype(BF16)

    arrived = dispatch(to_slots(expert_in))
    ups, downs = (own_up, peer_up, side_up, far_up), (own_down, peer_down, side_down, far_down)
    grad_slots, actives, hiddens = expert_part(arrived, grad_arrived, ups, downs)
    returned_grad = send_back(grad_slots)

    blocks = list(zip(actives, hiddens, strict=True))
    down_far, up_far, down_peer, up_peer = unit_grads(
        grad_arrived, arrived, (blocks[3], blocks[1]), (BF16, F32)
    )
    (down_part,) = to_owners([down_far], "in")
    down_side, up_side, down_own, up_own = unit_grads(
        grad_arrived, arrived, (blocks[2], blocks[0]), (BF16, F32)
    )
    produced = produced_part(actives, downs)
    returned_grad, down_part, up_far, up_peer, projection_full, produced, down_side, up_own = (
        together(
            returned_grad, down_part, up_far, up_peer, projection_full, produced, down_side, up_own
        )
    )
    grad_expert_in = collect(returned_grad)
    (up_part,) = to_owners([up_far], "in")
    peers = lax.axis_size("hi")

    def hi_parts(value):
        return to_owners(list(value.astype(BF16).reshape(peers - 1, -1, width)), "hi")

    down_hi = hi_parts(add_all(down_peer, [down_part]))

    scaled_second = grad_expert_in * gain_second
    gain_second_part = jnp.sum(grad_expert_in * normed_second, axis=0)
    grad_middle = scale_second * (
        scaled_second
        - normed_second * jnp.mean(scaled_second * normed_second, axis=-1, keepdims=True)
    )
    residual_grad = upstream + grad_middle
    branch_grad = residual_grad.astype(BF16)
    grad_mixed = jnp.einsum(
        "td,ed->te", branch_grad, output_full, preferred_element_type=F32
    ).astype(BF16)

    sent_grad = jnp.stack([grad_mixed[:, s : s + LANES] for s in starts])
    row_grad = swap(sent_grad, SEQ).reshape(length, LANES)

    group = lax.axis_index(EXP)

    def group_rows(value):
        rows = value.reshape(count, groups, weight_rows, -1)
        own, *away = [
            lax.dynamic_index_in_dim(rows, lax.rem(group + step, groups), 1, keepdims=False)
            for step in range(groups)
        ]
        return own, away

    output_term = jnp.einsum("tc,te->ce", attend_out, branch_grad, preferred_element_type=F32)
    output_own, output_away = group_rows(output_term.astype(BF16))
    output_away = to_owners(output_away, "exp")
    row_grad, produced, down_side, up_side, up_part, *held = together(
        row_grad, produced, down_side, up_side, up_part, *down_hi, *output_away
    )
    down_hi, output_away = held[: peers - 1], held[peers - 1 :]
    (down_early,) = to_owners([down_side], "in")
    (up_early,) = to_owners([up_side], "in")
    up_hi = hi_parts(add_all(up_peer, [up_part]))
    returned = send_back(produced)
    grad_qkv, grad_lying = attend_back(
        active, order, pair, documents, stat, row_grad, mixed_full, row_count, scaling
    )
    grad_qkv, grad_lying, returned, down_early, up_early, *up_hi = together(
        grad_qkv, grad_lying, returned, down_early, up_early, *up_hi
    )
    down_grad = add_all(down_own, [down_early, *down_hi])[None]
    up_grad = add_all(up_own, [up_early, *up_hi])[None]
    block_output = (middle + collect(returned)).astype(BF16)[None]

    column_own, column_away = group_rows(column_terms(row_blocks, grad_lying))
    dense_rows = jnp.concatenate(
        [
            add_all(column_own, to_owners(column_away, "exp")).astype(BF16),
            add_all(output_own, output_away).astype(BF16),
        ],
        axis=2,
    )
    local_square = jnp.sum(up_grad * up_grad) + jnp.sum(down_grad * down_grad)
    grad_pieces, dense_rows, local_square = together(
        to_tokens(grad_qkv), dense_rows, local_square
    )
    projection_grad, output_grad, dense_square = dense_grads(swap(dense_rows, SEQ), starts)
    input_grad, gain_first_part = close_norm(
        grad_pieces, starts, projection_full, tokens[0], gain_first[None], residual_grad
    )
    input_grad, gain_first_part = input_grad[None], gain_first_part[0]
    summed = spread_sum(
        jnp.concatenate(
            [gain_first_part, gain_second_part, dense_square[0] + local_square]
        )[None]
    )[0]
    gains_grad = summed[: 2 * width].reshape(2, width)
    grad_norm = jnp.sqrt(summed[2 * width] + jnp.sum(gains_grad * gains_grad))
    factor = jnp.minimum(1.0, CLIP / (grad_norm + 1e-06))
    (
        (projection_moment, projection_square, projection_new),
        (output_moment, output_square, output_new),
        (up_moment, up_square, up_new),
        (down_moment, down_square, down_new),
    ) = adam_all(
        factor,
        [
            (projection, projection_grad, projection_first, projection_second),
            (output_weight, output_grad, output_first, output_second),
            (expert_up, up_grad, up_first, up_second),
            (expert_down, down_grad, down_first, down_second),
        ],
        (RATE_MATRIX, RATE_OUTPUT, RATE_MATRIX, RATE_MATRIX),
        6,
    )
    gains_moment, gains_square, gains_new = adam_update(
        norm_gains, gains_grad, gains_first, gains_second, factor, RATE_GAIN, 0.0
    )
    return (
        block_output,
        input_grad,
        grad_norm,
        projection_grad,
        projection_moment,
        projection_square,
        projection_new,
        output_grad,
        output_moment,
        output_square,
        output_new,
        up_grad,
        up_moment,
        up_square,
        up_new,
        down_grad,
        down_moment,
        down_square,
        down_new,
        gains_grad,
        gains_moment,
        gains_square,
        gains_new,
    )


def solution(mesh):
    token = P("exp", SEQ, None)
    dense = P(ALL, None)
    expert = P("exp", SEQ, None)
    in_specs = (
        (token, token, P("exp", SEQ), token)
        + (dense, dense, expert, expert, P())
        + (dense,) * 4
        + (expert,) * 4
        + (P(), P())
    )
    out_specs = (token, token, P()) + (dense,) * 8 + (expert,) * 8 + (P(),) * 4
    rows, groups = mesh.devices.shape
    fine = Mesh(mesh.devices.reshape(rows // 4, 2, 2, groups), ALL)
    return jax.shard_map(body, mesh=fine, in_specs=in_specs, out_specs=out_specs, check_vma=False)
```
